32 devices in a mesh: dp: 4 (over z), pipe: 4 (over x, core), tensor: 2 (over y).
Axes of the slice: x: 2, y: 2, z: 4, core: 2. Of those that a mesh axis runs over, the one named last changes fastest.
Arguments:
- residual: bfloat16 [4, 2, 256, 6144], P('pipe', None, 'dp', 'tensor'), may hold values from -6 to 6
- queries: bfloat16 [4, 2, 256, 6144], P('pipe', None, 'dp', 'tensor'), may hold values from -6 to 6
- keys_values: bfloat16 [4, 2, 2, 256, 6144], P('pipe', None, None, 'dp', 'tensor'), may hold values from -18 to 18
- global_kv: bfloat16 [4, 2, 2, 384, 6144], P('pipe', None, None, None, 'tensor'), may hold values from -6 to 6
- block_ids: int32 [4, 2, 4, 48], P('pipe', None, 'dp', 'tensor'), may hold values from 0 to 3, as said below
- lengths: int32 [4, 2], P('pipe'), may hold values from 1 to 4, as said below
- gain: bfloat16 [4, 2, 6144], P('pipe', None, 'tensor'), may hold values from 0.5 to 1.5
Outputs:
- normed: bfloat16 [4, 2, 256, 6144], P('pipe', None, 'dp', 'tensor')
The draws below stay inside these ranges and needn't reach their ends.
Inputs may be any that keep to these rules, and one draw needn't show every extreme that they name: `block_ids`: for one section and direction, the random blocks of the 1 query block of one index of dp in the 24 heads of one index of tensor lie at most 6 in the 1 block of any one index of dp, and exactly 6 for some index. `lengths`: for each section one of the two micro-batches has all 4 blocks live.
All inputs are finite; a program needn't handle non-finite values.
Results may differ from the reference program's by a relative error of at most 0.0053.
Values may be sent and summed in bfloat16 or wider, within the bound.
No kernel may reach another device: no remote copies, remote signals or barrier semaphores. Data moves between devices by JAX's collectives and lax.ppermute only.
A program may use at most 64 MiB of HBM per device.

```python
import math
import jax
import jax.numpy as jnp
from jax import lax

D = 6144
HEADS = 48
HD = 128
BLK = 64
GLOB = 384
SECTIONS = 4
QB_DEV = 1
NBLK = 4
TOKENS = 256
HEADS_DEV = 24
CAP = 6
N_DP = 4
N_TENSOR = 2


def draw_residual(key, part):
    shape = (SECTIONS, 2, TOKENS, D)
    row_scale = jnp.exp(jax.random.uniform(jax.random.fold_in(key, 21), (SECTIONS, 2, TOKENS, 1), minval=math.log(0.03), maxval=math.log(0.3)))
    values = jax.random.truncated_normal(jax.random.fold_in(key, 22), -6.0, 6.0, shape)
    column_scale = 1.0 + 2.0 * jnp.arange(D, dtype=jnp.float32) / D
    return (values * row_scale * column_scale).astype(jnp.bfloat16)


def draw_queries(key, part):
    shape = (SECTIONS, 2, TOKENS, D)
    values = jax.random.truncated_normal(jax.random.fold_in(key, 11), -6.0, 6.0, shape)
    return values.astype(jnp.bfloat16)


def draw_keys_values(key, part):
    shape = (SECTIONS, 2, TOKENS, D)
    key_part = jax.random.truncated_normal(jax.random.fold_in(key, 31), -6.0, 6.0, shape)
    value_part = 3.0 * jax.random.truncated_normal(jax.random.fold_in(key, 32), -6.0, 6.0, shape)
    return jnp.stack([key_part, value_part], axis=1).astype(jnp.bfloat16)


def draw_block_ids(key, part):
    per_group = QB_DEV * HEADS_DEV
    slot_total = N_DP * CAP
    group_count = SECTIONS * 2 * N_DP * N_TENSOR
    priority = jax.random.randint(jax.random.fold_in(key, 3), (group_count, slot_total), 0, 65536)
    priority = priority * slot_total + jnp.arange(slot_total, dtype=jnp.int32)[None, :]
    chosen = jnp.argsort(priority, axis=1)[:, :per_group]
    owner_dev = chosen // CAP
    local_block = jax.random.randint(jax.random.fold_in(key, 4), (group_count, per_group), 0, QB_DEV)
    block_index = owner_dev * QB_DEV + local_block
    block_index = block_index.reshape(SECTIONS, 2, N_DP, N_TENSOR, QB_DEV, HEADS_DEV).transpose(0, 1, 2, 4, 3, 5)
    return block_index.reshape(SECTIONS, 2, NBLK, HEADS).astype(jnp.int32)


def draw_lengths(key, part):
    full_side = jax.random.randint(jax.random.fold_in(key, 5), (SECTIONS, 1), 0, 2)
    shorter = jax.random.randint(jax.random.fold_in(key, 6), (SECTIONS, 2), max(1, NBLK // 4), NBLK + 1)
    is_full = jnp.arange(2, dtype=jnp.int32)[None, :] == full_side
    return jnp.where(is_full, NBLK, shorter).astype(jnp.int32)


def levels(rng, dims, pieces, least, high):
    def one(dim, shards_of):
        steps = jax.random.uniform(jax.random.fold_in(jax.random.fold_in(rng, 6), dim), (shards_of,), jnp.float32, least / len(pieces), high / len(pieces))
        return jnp.repeat(jnp.exp(steps), dims[dim] // shards_of).reshape((-1,) + (1,) * (len(dims) - dim - 1))

    factor_of = one(*pieces[0])
    for cut in pieces[1:]:
        factor_of = factor_of * one(*cut)
    return factor_of


def normal_values(rng, dims, width, limit, shards=(), kind=jnp.bfloat16):
    values = jax.random.normal(rng, dims, jnp.float32) * width
    if len(shards) > 0:
        values = levels(rng, dims, shards, -0.22, 0.18) * values
    return jnp.clip(values, min=-limit, max=limit).astype(kind)


def setup_inputs(seed: int = 0) -> dict:
    key_list = jax.random.split(jax.random.key(seed), 8)
    residual = draw_residual(jax.random.fold_in(key_list[7], 71), 0)
    queries = draw_queries(jax.random.fold_in(key_list[7], 71), 0)
    keys_values = draw_keys_values(jax.random.fold_in(key_list[7], 71), 0)
    global_kv = normal_values(key_list[3], (SECTIONS, 2, 2, GLOB, D), 1.0, 6.0, ((0, 4), (4, 2)))
    block_ids = draw_block_ids(jax.random.fold_in(key_list[7], 71), 0)
    lengths = draw_lengths(jax.random.fold_in(key_list[7], 71), 0)
    gain = jnp.clip(1.0 + 0.1 * jax.random.normal(key_list[6], (SECTIONS, 2, D), jnp.float32), 0.5, 1.5).astype(jnp.bfloat16)
    return {"residual": residual, "queries": queries, "keys_values": keys_values, "global_kv": global_kv, "block_ids": block_ids, "lengths": lengths, "gain": gain}


epsilon = 1e-05

def single_head(operands, seq_blocks):
    query_head, key_head, value_head, gkey_head, gvalue_head, index_head = operands
    zero_block = jnp.zeros((1, BLK, HD), jnp.float32)
    key_padded = jnp.concatenate([zero_block, key_head, zero_block], axis=0)
    value_padded = jnp.concatenate([zero_block, value_head, zero_block], axis=0)
    window_keys = jnp.concatenate([key_padded[offset:offset + NBLK] for offset in range(3)], axis=1)
    window_values = jnp.concatenate([value_padded[offset:offset + NBLK] for offset in range(3)], axis=1)
    random_keys = key_head[index_head]
    random_values = value_head[index_head]
    window_scores = jnp.einsum('nbe,nke->nbk', query_head, window_keys)
    global_scores = jnp.einsum('nbe,ke->nbk', query_head, gkey_head)
    random_scores = jnp.einsum('nbe,nke->nbk', query_head, random_keys)
    scores = jnp.concatenate([window_scores, global_scores, random_scores], axis=2) * HD ** (-0.5)
    block_number = jnp.arange(NBLK, dtype=jnp.int32)
    near_index = block_number[:, None] + jnp.arange(3, dtype=jnp.int32)[None, :] - 1
    near_valid = jnp.repeat((near_index >= 0) & (near_index < seq_blocks), BLK, axis=1)
    global_valid = jnp.ones((NBLK, GLOB), jnp.bool_)
    random_valid = jnp.repeat((index_head < seq_blocks)[:, None], BLK, axis=1)
    key_valid = jnp.concatenate([near_valid, global_valid, random_valid], axis=1)[:, None, :]
    scores = jnp.where(key_valid, scores, -jnp.inf)
    largest = lax.optimization_barrier(jnp.max(scores, axis=2, keepdims=True))
    weights = jnp.exp(scores - largest)
    weights = (weights / lax.optimization_barrier(jnp.sum(weights, axis=2, keepdims=True))).astype(jnp.bfloat16)
    weights = lax.optimization_barrier(weights).astype(jnp.float32)
    near_end = 3 * BLK
    glob_end = near_end + GLOB
    context = jnp.einsum('nbk,nke->nbe', weights[:, :, :near_end], window_values)
    context = context + jnp.einsum('nbk,ke->nbe', weights[:, :, near_end:glob_end], gvalue_head)
    context = context + jnp.einsum('nbk,nke->nbe', weights[:, :, glob_end:], random_values)
    query_valid = (block_number < seq_blocks)[:, None, None]
    return jnp.where(query_valid, context, 0.0)

def head_major(array):
    return array.astype(jnp.float32).reshape(array.shape[0] // BLK, BLK, HEADS, HD).transpose(2, 0, 1, 3)

def section_layer(operands):
    state, query, pair, global_pair, block_index, seq_blocks = operands
    query_heads = head_major(query)
    key_heads = head_major(pair[0])
    value_heads = head_major(pair[1])
    gkey_heads = global_pair[0].astype(jnp.float32).reshape(GLOB, HEADS, HD).transpose(1, 0, 2)
    gvalue_heads = global_pair[1].astype(jnp.float32).reshape(GLOB, HEADS, HD).transpose(1, 0, 2)
    index_heads = block_index.T
    context = lax.map(lambda items: single_head(items, seq_blocks), (query_heads, key_heads, value_heads, gkey_heads, gvalue_heads, index_heads))
    context = context.transpose(1, 2, 0, 3).reshape(TOKENS, D)
    return (state.astype(jnp.float32) + context).astype(jnp.bfloat16)

def reference(residual, queries, keys_values, global_kv, block_ids, lengths, gain):
    pair_count = SECTIONS * 2
    flat_state = residual.reshape(pair_count, TOKENS, D)
    flat_query = queries.reshape(pair_count, TOKENS, D)
    flat_pair = keys_values.transpose(0, 2, 1, 3, 4).reshape(pair_count, 2, TOKENS, D)
    flat_global = global_kv.transpose(0, 2, 1, 3, 4).reshape(pair_count, 2, GLOB, D)
    flat_index = block_ids.reshape(pair_count, NBLK, HEADS)
    flat_length = lengths.reshape(pair_count)
    updated = lax.map(section_layer, (flat_state, flat_query, flat_pair, flat_global, flat_index, flat_length))
    updated = updated.reshape(SECTIONS, 2, TOKENS, D)
    zero_section = jnp.zeros((1, TOKENS, D), jnp.bfloat16)
    from_above = jnp.concatenate([updated[1:, 0], zero_section], axis=0)
    from_below = jnp.concatenate([zero_section, updated[:-1, 1]], axis=0)
    arrived = jnp.stack([from_above, from_below], axis=1)
    wide = arrived.astype(jnp.float32)
    inverse = lax.rsqrt(lax.optimization_barrier(jnp.sum(wide * wide, axis=3, keepdims=True)) / D + epsilon)
    normed = (wide * inverse * gain.astype(jnp.float32)[:, :, None, :]).astype(jnp.bfloat16)
    return normed
```

```python
import functools

import jax
import jax.numpy as jnp
from jax import lax
from jax.experimental import pallas as pl
from jax.experimental.pallas import tpu as pltpu
from jax.sharding import PartitionSpec as P

D = 6144
HD = 128
BLK = 64
SCALE = HD ** (-0.5)
NEG = -1e30
VMEM_LIMIT = 40 * 1024 * 1024

epsilon = 1e-05


def dot_nt(a, b):
    return lax.dot_general(a, b, (((1,), (1,)), ((), ())), preferred_element_type=jnp.float32)


def dot_nn(a, b):
    return lax.dot_general(a, b, (((1,), (0,)), ((), ())), preferred_element_type=jnp.float32)


def head_group(heads):
    return max(g for g in range(1, 9) if heads % g == 0)


def far_classes(dp_count):
    if dp_count <= 4:
        return list(range(2, dp_count))
    return None


def partner_of(me, distance, dp_count):
    return jnp.where(me + distance < dp_count, me + distance, me - distance)


def pack_kernel(dp_count, ids_ref, kv_ref, slot_ref, *rest):
    outs, count_ref = rest[:-1], rest[-1]
    me = lax.axis_index("dp")
    heads = ids_ref.shape[2]
    classes = far_classes(dp_count)
    for out in outs:
        out[...] = jnp.zeros_like(out)
    for c in range(2):
        for owner in range(dp_count):
            count_ref[owner] = 0
        for h in range(heads):
            owner = ids_ref[me, c, h]
            slot = count_ref[owner]
            slot_ref[c, h] = slot
            count_ref[owner] = slot + 1

    def fill(out, place, asker, wanted):
        capacity = out.shape[2]
        for c in range(2):
            slot = jnp.int32(0)
            for h in range(heads):
                match = wanted & (ids_ref[asker, c, h] == me) & (slot < capacity)

                @pl.when(match)
                def _(slot=slot, h=h, c=c):
                    out[place, c, slot, 0] = kv_ref[0, c, :, h * HD : (h + 1) * HD]
                    out[place, c, slot, 1] = kv_ref[1, c, :, h * HD : (h + 1) * HD]

                slot = slot + match.astype(jnp.int32)

    if classes is None:

        @pl.loop(0, dp_count)
        def _(asker):
            fill(outs[0], asker, asker, jnp.abs(asker - me) >= 2)

    else:
        for out, distance in zip(outs, classes):
            asker = partner_of(me, distance, dp_count)
            inside = asker >= 0
            fill(out, 0, jnp.where(inside, asker, 0), inside)


def local_kernel(heads_step, ids_ref, len_ref, q_ref, kv_ref, gkv_ref, acc_ref, max_ref, sum_ref):
    me = lax.axis_index("dp")
    c = pl.program_id(0)
    g = pl.program_id(1)
    glob = gkv_ref.shape[2]
    lane = lax.broadcasted_iota(jnp.int32, (1, glob + BLK), 1)
    own_bias = jnp.where(me < len_ref[c], 0.0, NEG)
    bias = jnp.where(lane < glob, 0.0, own_bias)
    for n in range(heads_step):
        cols = slice(n * HD, (n + 1) * HD)
        q = q_ref[0, :, cols]
        k = jnp.concatenate([gkv_ref[0, 0, :, cols], kv_ref[0, 0, :, cols]], axis=0)
        v = jnp.concatenate([gkv_ref[1, 0, :, cols], kv_ref[1, 0, :, cols]], axis=0)
        twice = jnp.where(ids_ref[me, c, g * heads_step + n] == me, 2.0, 1.0)
        mult = jnp.where(lane < glob, 1.0, twice)
        s = dot_nt(q, k) * SCALE + bias
        m = jnp.max(s, axis=1, keepdims=True)
        p = jnp.exp(s - m) * mult
        acc_ref[0, :, cols] = dot_nn(p.astype(jnp.bfloat16), v)
        max_ref[0, 0, :, n : n + 1] = m
        sum_ref[0, 0, :, n : n + 1] = jnp.sum(p, axis=1, keepdims=True)


def merge_kernel(heads_step, dp_count, ids_ref, slot_ref, len_ref, q_ref, up_ref, down_ref, res_ref, acc_ref, max_ref, sum_ref, *rest):
    far_refs, (out_ref, sq_ref) = rest[:-2], rest[-2:]
    me = lax.axis_index("dp")
    c = pl.program_id(0)
    g = pl.program_id(1)
    length = len_ref[c]
    classes = far_classes(dp_count)
    lane = lax.broadcasted_iota(jnp.int32, (1, 3 * BLK), 1)
    up_bias = jnp.where((me >= 1) & (me - 1 < length), 0.0, NEG)
    down_bias = jnp.where(me + 1 < length, 0.0, NEG)
    alive = me < length
    squares = jnp.zeros((BLK, HD), jnp.float32)
    for n in range(heads_step):
        cols = slice(n * HD, (n + 1) * HD)
        head = g * heads_step + n
        block = ids_ref[me, c, head]
        slot = slot_ref[c, head]
        gap = jnp.abs(block - me)
        is_far = gap >= 2
        if classes is None:
            place = jnp.where(is_far, block, 0)
            far_slot = jnp.where(is_far, slot, 0)
            k_far = far_refs[0][place, 0, far_slot, 0]
            v_far = far_refs[0][place, 0, far_slot, 1]
        else:
            far_slot = jnp.where(is_far, slot, 0)
            k_far = far_refs[0][0, 0, far_slot, 0]
            v_far = far_refs[0][0, 0, far_slot, 1]
            for far_ref, distance in zip(far_refs[1:], classes[1:]):
                k_far = jnp.where(gap == distance, far_ref[0, 0, far_slot, 0], k_far)
                v_far = jnp.where(gap == distance, far_ref[0, 0, far_slot, 1], v_far)
        far_bias = jnp.where(is_far & (block < length), 0.0, NEG)
        bias = jnp.where(lane < BLK, up_bias, jnp.where(lane < 2 * BLK, down_bias, far_bias))
        up_mult = jnp.where(block == me - 1, 2.0, 1.0)
        down_mult = jnp.where(block == me + 1, 2.0, 1.0)
        mult = jnp.where(lane < BLK, up_mult, jnp.where(lane < 2 * BLK, down_mult, 1.0))
        q = q_ref[0, :, cols]
        k = jnp.concatenate([up_ref[0, 0, :, cols], down_ref[0, 0, :, cols], k_far], axis=0)
        v = jnp.concatenate([up_ref[1, 0, :, cols], down_ref[1, 0, :, cols], v_far], axis=0)
        s = dot_nt(q, k) * SCALE + bias
        m_old = max_ref[0, 0, :, n : n + 1]
        m = jnp.maximum(m_old, jnp.max(s, axis=1, keepdims=True))
        p = jnp.exp(s - m) * mult
        alpha = jnp.exp(m_old - m)
        total = alpha * sum_ref[0, 0, :, n : n + 1] + jnp.sum(p, axis=1, keepdims=True)
        acc = alpha * acc_ref[0, :, cols] + dot_nn(p.astype(jnp.bfloat16), v)
        context = jnp.where(alive, acc / total, 0.0)
        updated = (res_ref[0, :, cols].astype(jnp.float32) + context).astype(jnp.bfloat16)
        out_ref[0, :, cols] = updated
        wide = updated.astype(jnp.float32)
        squares = squares + wide * wide
    row = jnp.sum(squares, axis=1, keepdims=True)

    @pl.when(g == 0)
    def _():
        sq_ref[0] = jnp.zeros_like(sq_ref[0])

    sq_ref[0] += row


def smem():
    return pl.BlockSpec(memory_space=pltpu.SMEM)


def vmem():
    return pl.BlockSpec(memory_space=pltpu.VMEM)


def body(residual, queries, keys_values, global_kv, block_ids, lengths, gain):
    width = residual.shape[-1]
    heads = width // HD
    dp_count = lax.axis_size("dp")
    pipe_count = lax.axis_size("pipe")
    tensor_count = lax.axis_size("tensor")
    group = head_group(heads)
    steps = heads // group
    lanes = group * HD
    capacity = (heads + dp_count - 1) // dp_count
    classes = far_classes(dp_count)
    kv = keys_values[0]
    q = queries[0]
    res = residual[0]
    glob = global_kv[0]
    length = lengths[0]
    glob_count = glob.shape[2]
    params = pltpu.CompilerParams(vmem_limit_bytes=VMEM_LIMIT)

    ids = lax.all_gather(block_ids[0, :, 0], "dp")
    up = lax.ppermute(kv, "dp", [(i, i + 1) for i in range(dp_count - 1)])
    down = lax.ppermute(kv, "dp", [(i + 1, i) for i in range(dp_count - 1)])

    if classes is None:
        tile_shapes = [(dp_count, 2, capacity, 2, BLK, HD)]
    else:
        tile_shapes = [(1, 2, capacity, 2, BLK, HD)] * len(classes)
    slots, *tiles = pl.pallas_call(
        functools.partial(pack_kernel, dp_count),
        out_shape=[jax.ShapeDtypeStruct((2, heads), jnp.int32)]
        + [jax.ShapeDtypeStruct(shape, jnp.bfloat16) for shape in tile_shapes],
        in_specs=[smem(), vmem()],
        out_specs=[smem()] + [vmem() for _ in tile_shapes],
        scratch_shapes=[pltpu.SMEM((dp_count,), jnp.int32)],
        compiler_params=params,
    )(ids, kv)
    if classes is None:
        far = [lax.all_to_all(tiles[0], "dp", split_axis=0, concat_axis=0, tiled=True)]
    else:
        far = []
        for array, distance in zip(tiles, classes):
            pairs = [(i, i + distance) for i in range(dp_count - distance)]
            far.append(lax.ppermute(array, "dp", pairs + [(j, i) for i, j in pairs]))

    stat = jax.ShapeDtypeStruct((2, steps, BLK, group), jnp.float32)
    stat_spec = pl.BlockSpec((1, 1, BLK, group), lambda c, g: (c, g, 0, 0))
    row_spec = pl.BlockSpec((1, BLK, lanes), lambda c, g: (c, 0, g))
    pair_spec = pl.BlockSpec((2, 1, BLK, lanes), lambda c, g: (0, c, 0, g))
    acc, maxes, sums = pl.pallas_call(
        functools.partial(local_kernel, group),
        grid=(2, steps),
        out_shape=[jax.ShapeDtypeStruct((2, BLK, width), jnp.float32), stat, stat],
        in_specs=[
            smem(),
            smem(),
            row_spec,
            pair_spec,
            pl.BlockSpec((2, 1, glob_count, lanes), lambda c, g: (0, c, 0, g)),
        ],
        out_specs=[row_spec, stat_spec, stat_spec],
        compiler_params=params,
        cost_estimate=pl.CostEstimate(
            flops=4 * 2 * BLK * width * (glob_count + BLK), bytes_accessed=14 * 2**20, transcendentals=0
        ),
    )(ids, length, q, kv, glob)

    updated, squares = pl.pallas_call(
        functools.partial(merge_kernel, group, dp_count),
        grid=(2, steps),
        out_shape=[
            jax.ShapeDtypeStruct((2, BLK, width), jnp.bfloat16),
            jax.ShapeDtypeStruct((2, BLK, HD), jnp.float32),
        ],
        in_specs=[smem(), smem(), smem(), row_spec, pair_spec, pair_spec, row_spec, row_spec, stat_spec, stat_spec]
        + [pl.BlockSpec((shape[0], 1) + shape[2:], lambda c, g: (0, c, 0, 0, 0, 0)) for shape in tile_shapes],
        out_specs=[row_spec, pl.BlockSpec((1, BLK, HD), lambda c, g: (c, 0, 0))],
        compiler_params=params,
        cost_estimate=pl.CostEstimate(
            flops=4 * 2 * BLK * width * 3 * BLK, bytes_accessed=9 * 2**20, transcendentals=0
        ),
    )(ids, slots, length, q, up, down, res, acc, maxes, sums, *far)

    sq = squares[:, :, 0]
    normed = []
    for c, step in ((0, -1), (1, 1)):
        line = [(i, i + step) for i in range(pipe_count) if 0 <= i + step < pipe_count]
        arrived = lax.ppermute(updated[c], "pipe", line)
        total = lax.ppermute(sq[c], "pipe", line)
        for turn in range(1, tensor_count):
            cross = [
                (i * tensor_count + t, j * tensor_count + (t + turn) % tensor_count)
                for i, j in line
                for t in range(tensor_count)
            ]
            total = total + lax.ppermute(sq[c], ("pipe", "tensor"), cross)
        inverse = lax.rsqrt(total / D + epsilon)
        wide = arrived.astype(jnp.float32)
        normed.append((wide * inverse[:, None] * gain[0, c][None, :].astype(jnp.float32)).astype(jnp.bfloat16))
    return jnp.stack(normed)[None]


def solution(mesh):
    in_specs = (
        P("pipe", None, "dp", "tensor"),
        P("pipe", None, "dp", "tensor"),
        P("pipe", None, None, "dp", "tensor"),
        P("pipe", None, None, None, "tensor"),
        P("pipe", None, "dp", "tensor"),
        P("pipe", None),
        P("pipe", None, "tensor"),
    )
    out_specs = P("pipe", None, "dp", "tensor")
    return jax.shard_map(body, mesh=mesh, in_specs=in_specs, out_specs=out_specs, check_vma=False)
```

```python
import functools

import jax
import jax.numpy as jnp
from jax import lax
from jax.experimental import pallas as pl
from jax.experimental.pallas import tpu as pltpu
from jax.sharding import PartitionSpec as P

D = 6144
HD = 128
BLK = 64
LOG2E = 1.4426950408889634
SCALE = HD ** (-0.5) * LOG2E
NEG = -1e30
VMEM_LIMIT = 40 * 1024 * 1024

epsilon = 1e-05


def dot_nt(a, b):
    return lax.dot_general(a, b, (((1,), (1,)), ((), ())), preferred_element_type=jnp.float32)


def dot_nn(a, b):
    return lax.dot_general(a, b, (((1,), (0,)), ((), ())), preferred_element_type=jnp.float32)


def with_ones(v):
    return jnp.concatenate([v, jnp.ones((v.shape[0], HD), v.dtype)], axis=1)


def head_group(heads):
    return max(g for g in range(1, 9) if heads % g == 0)


def heads_wanted(table_ref, row, ids_ref, asker, block):
    heads, capacity = ids_ref.shape[2], table_ref.shape[2]
    for c in range(2):
        for s in range(capacity):
            table_ref[row, c, s] = -1
        slot = jnp.int32(0)
        for h in range(heads):
            match = (ids_ref[asker, c, h] == block) & (slot < capacity)

            @pl.when(match)
            def _(slot=slot, h=h, c=c):
                table_ref[row, c, slot] = h

            slot = slot + match.astype(jnp.int32)


def copy_tiles(out_ref, place, table_ref, row, source_ref):
    capacity = table_ref.shape[2]
    for c in range(2):
        for s in range(capacity):
            h = jnp.maximum(table_ref[row, c, s], 0)
            cols = pl.ds(pl.multiple_of(h * HD, HD), HD)
            out_ref[place, c, s, 0] = source_ref[0, c, :, cols]
            out_ref[place, c, s, 1] = source_ref[1, c, :, cols]


def plan_kernel(ids_ref, kv_ref, take_ref, give_ref, out_ref):
    me = lax.axis_index("dp")
    for row, gap in ((0, 2), (1, 3)):
        block = jnp.where(me + gap < 4, me + gap, me - gap)
        heads_wanted(take_ref, row, ids_ref, me, jnp.where(block < 0, 4, block))
    edge = (me == 0) | (me == 3)
    asker = jnp.where(me == 0, 2, jnp.where(me == 1, 0, jnp.where(me == 2, 3, 1)))
    block = jnp.where(edge, me, 3 - me)
    heads_wanted(give_ref, 0, ids_ref, asker, block)
    heads_wanted(give_ref, 1, ids_ref, 3 - me, jnp.where(edge, me, 4))

    @pl.when(edge)
    def _():
        copy_tiles(out_ref, 0, give_ref, 1, kv_ref)


def forward_kernel(give_ref, kv_ref, up_ref, down_ref, out_ref):
    me = lax.axis_index("dp")

    @pl.when((me == 0) | (me == 3))
    def _():
        copy_tiles(out_ref, 0, give_ref, 0, kv_ref)

    @pl.when(me == 1)
    def _():
        copy_tiles(out_ref, 0, give_ref, 0, down_ref)

    @pl.when(me == 2)
    def _():
        copy_tiles(out_ref, 0, give_ref, 0, up_ref)


def pack_kernel(ids_ref, kv_ref, take_ref, out_ref, list_ref):
    me = lax.axis_index("dp")

    @pl.loop(0, ids_ref.shape[0])
    def _(other):
        far = jnp.abs(other - me) >= 2
        heads_wanted(take_ref, other, ids_ref, me, jnp.where(far, other, -1))
        heads_wanted(list_ref, 0, ids_ref, other, jnp.where(far, me, -1))
        copy_tiles(out_ref, other, list_ref, 0, kv_ref)


def local_kernel(heads_step, ids_ref, len_ref, q_ref, kv_ref, gkv_ref, acc_ref, max_ref, sum_ref):
    me = lax.axis_index("dp")
    c = pl.program_id(0)
    g = pl.program_id(1)
    glob = gkv_ref.shape[2]
    lane = lax.broadcasted_iota(jnp.int32, (1, glob + BLK), 1)
    for n in range(heads_step):
        cols = slice(n * HD, (n + 1) * HD)
        q = q_ref[0, :, cols]
        k = jnp.concatenate([gkv_ref[0, 0, :, cols], kv_ref[0, 0, :, cols]], axis=0)
        v = jnp.concatenate([gkv_ref[1, 0, :, cols], kv_ref[1, 0, :, cols]], axis=0)
        twice = jnp.where(ids_ref[me, c, g * heads_step + n] == me, 1.0, 0.0)
        bias = jnp.where(lane < glob, 0.0, jnp.where(me < len_ref[c], twice, NEG))
        s = dot_nt(q, k) * SCALE + bias
        m = jnp.max(s, axis=1, keepdims=True)
        p = jnp.exp2(s - m).astype(jnp.bfloat16)
        pv = dot_nn(p, with_ones(v))
        acc_ref[0, :, cols] = pv[:, :HD]
        sum_ref[0, :, cols] = pv[:, HD:]
        max_ref[0, :, cols] = jnp.broadcast_to(m, (BLK, HD))


def merge(s, m_old, l_old, acc_old, v):
    m = jnp.maximum(m_old, jnp.max(s, axis=1, keepdims=True))
    p = jnp.exp2(s - m[:, : s.shape[1]]).astype(jnp.bfloat16)
    alpha = jnp.exp2(m_old - m)
    pv = dot_nn(p, with_ones(v))
    return m, alpha * l_old + pv[:, HD:], alpha * acc_old + pv[:, :HD]


def window_kernel(heads_step, ids_ref, len_ref, q_ref, up_ref, down_ref, res_ref, acc_ref, max_ref, sum_ref, new_acc_ref, new_max_ref, new_sum_ref, out_ref, sq_ref):
    me = lax.axis_index("dp")
    steps = q_ref.shape[2] // HD // heads_step
    lane = lax.broadcasted_iota(jnp.int32, (1, 2 * BLK), 1)
    for c in range(2):
        length = len_ref[c]
        alive = me < length
        up_live = (me >= 1) & (me - 1 < length)
        down_live = me + 1 < length

        def step(g, squares, c=c, alive=alive, up_live=up_live, down_live=down_live):
            for n in range(heads_step):
                head = g * heads_step + n
                cols = pl.ds(pl.multiple_of(head * HD, HD), HD)
                block = ids_ref[me, c, head]
                up_bias = jnp.where(up_live, jnp.where(block == me - 1, 1.0, 0.0), NEG)
                down_bias = jnp.where(down_live, jnp.where(block == me + 1, 1.0, 0.0), NEG)
                bias = jnp.where(lane < BLK, up_bias, down_bias)
                q = q_ref[c, :, cols]
                k = jnp.concatenate([up_ref[0, c, :, cols], down_ref[0, c, :, cols]], axis=0)
                v = jnp.concatenate([up_ref[1, c, :, cols], down_ref[1, c, :, cols]], axis=0)
                s = dot_nt(q, k) * SCALE + bias
                m, l, acc = merge(s, max_ref[c, :, cols], sum_ref[c, :, cols], acc_ref[c, :, cols], v)
                new_max_ref[c, :, cols] = m
                new_sum_ref[c, :, cols] = l
                new_acc_ref[c, :, cols] = acc
                context = jnp.where(alive, acc / l, 0.0)
                updated = (res_ref[c, :, cols].astype(jnp.float32) + context).astype(jnp.bfloat16)
                out_ref[c, :, cols] = updated
                wide = updated.astype(jnp.float32)
                near = jnp.where(jnp.abs(block - me) < 2, 1.0, 0.0)
                squares = squares + wide * wide * near
            return squares

        squares = lax.fori_loop(0, steps, step, jnp.zeros((BLK, HD), jnp.float32))
        sq_ref[c] = squares


def far_kernel(full, ids_ref, take_ref, len_ref, tile_ref, q_ref, res_ref, acc_ref, max_ref, sum_ref, old_ref, old_sq_ref, out_ref, sq_ref):
    del old_ref
    me = lax.axis_index("dp")
    owners, _, capacity = take_ref.shape
    sq_ref[...] = old_sq_ref[...]

    def one_owner(owner):
        for c in range(2):
            squares = jnp.zeros((BLK, HD), jnp.float32)
            for s in range(capacity):
                h = take_ref[owner, c, s]
                there = h >= 0
                h = jnp.maximum(h, 0)
                cols = pl.ds(pl.multiple_of(h * HD, HD), HD)
                bias = jnp.where(there & (ids_ref[me, c, h] < len_ref[c]), 0.0, NEG)
                score = dot_nt(q_ref[c, :, cols], tile_ref[owner, c, s, 0]) * SCALE + bias
                _, l, acc = merge(
                    score, max_ref[c, :, cols], sum_ref[c, :, cols], acc_ref[c, :, cols], tile_ref[owner, c, s, 1]
                )
                context = jnp.where(me < len_ref[c], acc / l, 0.0)
                updated = (res_ref[c, :, cols].astype(jnp.float32) + context).astype(jnp.bfloat16)
                if full:
                    out_ref[c, :, cols] = updated
                else:

                    @pl.when(there)
                    def _(c=c, cols=cols, updated=updated):
                        out_ref[c, :, cols] = updated

                wide = updated.astype(jnp.float32)
                squares = squares + wide * wide * jnp.where(there, 1.0, 0.0)
            sq_ref[c] += squares

    if full:

        @pl.when(take_ref[0, 0, 0] >= 0)
        def _():
            one_owner(0)

    else:
        pl.loop(0, owners)(one_owner)


def smem():
    return pl.BlockSpec(memory_space=pltpu.SMEM)


def vmem():
    return pl.BlockSpec(memory_space=pltpu.VMEM)


def body(residual, queries, keys_values, global_kv, block_ids, lengths, gain):
    width = residual.shape[-1]
    heads = width // HD
    dp_count = lax.axis_size("dp")
    pipe_count = lax.axis_size("pipe")
    tensor_count = lax.axis_size("tensor")
    group = head_group(heads)
    steps = heads // group
    lanes = group * HD
    capacity = (heads + dp_count - 1) // dp_count
    chain = dp_count == 4 and capacity * dp_count == heads
    q = queries[0]
    res = residual[0]
    glob = global_kv[0]
    length = lengths[0]
    glob_count = glob.shape[2]
    params = pltpu.CompilerParams(vmem_limit_bytes=VMEM_LIMIT)

    ids = lax.all_gather(block_ids[0, :, 0], "dp")
    kv, ids = lax.optimization_barrier((keys_values[0], ids))
    up = lax.ppermute(kv, "dp", [(i, i + 1) for i in range(dp_count - 1)])
    down = lax.ppermute(kv, "dp", [(i + 1, i) for i in range(dp_count - 1)])

    tile = (2, capacity, 2, BLK, HD)
    if chain:
        table = jax.ShapeDtypeStruct((2, 2, capacity), jnp.int32)
        tiles = jax.ShapeDtypeStruct((1,) + tile, jnp.bfloat16)
        take, give, tiles_3 = pl.pallas_call(
            plan_kernel,
            out_shape=[table, table, tiles],
            in_specs=[smem(), vmem()],
            out_specs=[smem(), smem(), vmem()],
            compiler_params=params,
        )(ids, kv)
        far_3 = lax.ppermute(tiles_3, "dp", [(0, 3), (3, 0)])
        tiles_2 = pl.pallas_call(
            forward_kernel,
            out_shape=tiles,
            in_specs=[smem(), vmem(), vmem(), vmem()],
            out_specs=vmem(),
            compiler_params=params,
        )(give, kv, up, down)
        far_2 = lax.ppermute(tiles_2, "dp", [(0, 2), (3, 1), (2, 3), (1, 0)])
        far = [(take[1:], far_3), (take[:1], far_2)]
    else:
        take, tiles_all = pl.pallas_call(
            pack_kernel,
            out_shape=[
                jax.ShapeDtypeStruct((dp_count, 2, capacity), jnp.int32),
                jax.ShapeDtypeStruct((dp_count,) + tile, jnp.bfloat16),
            ],
            in_specs=[smem(), vmem()],
            out_specs=[smem(), vmem()],
            scratch_shapes=[pltpu.SMEM((1, 2, capacity), jnp.int32)],
            compiler_params=params,
        )(ids, kv)
        far = [(take, lax.all_to_all(tiles_all, "dp", split_axis=0, concat_axis=0, tiled=True))]

    wide = jax.ShapeDtypeStruct((2, BLK, width), jnp.float32)
    row_spec = pl.BlockSpec((1, BLK, lanes), lambda c, g: (c, 0, g))
    pair_spec = pl.BlockSpec((2, 1, BLK, lanes), lambda c, g: (0, c, 0, g))
    acc, maxes, sums = pl.pallas_call(
        functools.partial(local_kernel, group),
        grid=(2, steps),
        out_shape=[wide] * 3,
        in_specs=[
            smem(),
            smem(),
            row_spec,
            pair_spec,
            pl.BlockSpec((2, 1, glob_count, lanes), lambda c, g: (0, c, 0, g)),
        ],
        out_specs=[row_spec] * 3,
        compiler_params=params,
        cost_estimate=pl.CostEstimate(
            flops=4 * 2 * BLK * width * (glob_count + BLK), bytes_accessed=14 * 2**20, transcendentals=0
        ),
    )(ids, length, q, kv, glob)

    acc, maxes, sums, updated, squares = pl.pallas_call(
        functools.partial(window_kernel, group),
        out_shape=[wide] * 3
        + [jax.ShapeDtypeStruct((2, BLK, width), jnp.bfloat16), jax.ShapeDtypeStruct((2, BLK, HD), jnp.float32)],
        in_specs=[smem(), smem()] + [vmem()] * 7,
        out_specs=[vmem()] * 5,
        compiler_params=params,
        cost_estimate=pl.CostEstimate(
            flops=4 * 2 * BLK * width * 2 * BLK, bytes_accessed=9 * 2**20, transcendentals=0
        ),
    )(ids, length, q, up, down, res, acc, maxes, sums)

    for heads_taken, tiles_got in far:
        updated, squares = pl.pallas_call(
            functools.partial(far_kernel, chain),
            out_shape=[
                jax.ShapeDtypeStruct((2, BLK, width), jnp.bfloat16),
                jax.ShapeDtypeStruct((2, BLK, HD), jnp.float32),
            ],
            in_specs=[smem(), smem(), smem()] + [vmem()] * 8,
            out_specs=[vmem()] * 2,
            input_output_aliases={9: 0},
            compiler_params=params,
        )(ids, heads_taken, length, tiles_got, q, res, acc, maxes, sums, updated, squares)

    line_0 = [(i + 1, i) for i in range(pipe_count - 1)]
    line_1 = [(i, i + 1) for i in range(pipe_count - 1)]
    arrived = [lax.ppermute(updated[c], "pipe", line) for c, line in ((0, line_0), (1, line_1))]
    sq = lax.all_gather(jnp.sum(squares, axis=2), ("pipe", "tensor"))
    sq = jnp.sum(sq.reshape(pipe_count, tensor_count, 2, BLK), axis=1)
    here = lax.axis_index("pipe")
    normed = []
    for c, source in ((0, jnp.minimum(here + 1, pipe_count - 1)), (1, jnp.maximum(here - 1, 0))):
        total = lax.dynamic_index_in_dim(sq[:, c], source, axis=0, keepdims=False)
        inverse = lax.rsqrt(total / D + epsilon)
        normed.append(
            (
                arrived[c].astype(jnp.float32) * inverse[:, None] * gain[0, c][None, :].astype(jnp.float32)
            ).astype(jnp.bfloat16)
        )
    return jnp.stack(normed)[None]


def solution(mesh):
    in_specs = (
        P("pipe", None, "dp", "tensor"),
        P("pipe", None, "dp", "tensor"),
        P("pipe", None, None, "dp", "tensor"),
        P("pipe", None, None, None, "tensor"),
        P("pipe", None, "dp", "tensor"),
        P("pipe", None),
        P("pipe", None, "tensor"),
    )
    out_specs = P("pipe", None, "dp", "tensor")
    return jax.shard_map(body, mesh=mesh, in_specs=in_specs, out_specs=out_specs, check_vma=False)
```

```python
import functools

import jax
import jax.numpy as jnp
from jax import lax
from jax.experimental import pallas as pl
from jax.experimental.pallas import tpu as pltpu
from jax.sharding import PartitionSpec as P

D = 6144
HD = 128
BLK = 64
LOG2E = 1.4426950408889634
SCALE = HD ** (-0.5) * LOG2E
NEG = -1e30
VMEM_LIMIT = 40 * 1024 * 1024

epsilon = 1e-05


def dot_nt(a, b):
    return lax.dot_general(a, b, (((1,), (1,)), ((), ())), preferred_element_type=jnp.float32)


def dot_nn(a, b):
    return lax.dot_general(a, b, (((1,), (0,)), ((), ())), preferred_element_type=jnp.float32)


def with_ones(v):
    return jnp.concatenate([v, jnp.ones((v.shape[0], HD), v.dtype)], axis=1)


def head_group(heads):
    return max(g for g in range(1, 9) if heads % g == 0)


def head_batch(heads):
    return max(g for g in range(1, 5) if heads % g == 0)


def heads_wanted(table_ref, row, ids_ref, asker, block):
    heads, capacity = ids_ref.shape[2], table_ref.shape[2]
    for c in range(2):
        for s in range(capacity):
            table_ref[row, c, s] = -1
        slot = jnp.int32(0)
        for h in range(heads):
            match = (ids_ref[asker, c, h] == block) & (slot < capacity)

            @pl.when(match)
            def _(slot=slot, h=h, c=c):
                table_ref[row, c, slot] = h

            slot = slot + match.astype(jnp.int32)


def copy_tiles(out_ref, place, table_ref, row, source_ref):
    capacity = table_ref.shape[2]
    for c in range(2):
        for s in range(capacity):
            h = jnp.maximum(table_ref[row, c, s], 0)
            cols = pl.ds(pl.multiple_of(h * HD, HD), HD)
            out_ref[place, c, s, 0] = source_ref[0, c, :, cols]
            out_ref[place, c, s, 1] = source_ref[1, c, :, cols]


def plan_kernel(ids_ref, kv_ref, take_ref, give_ref, out_ref):
    me = lax.axis_index("dp")
    for row, gap in ((0, 2), (1, 3)):
        block = jnp.where(me + gap < 4, me + gap, me - gap)
        heads_wanted(take_ref, row, ids_ref, me, jnp.where(block < 0, 4, block))
    edge = (me == 0) | (me == 3)
    asker = jnp.where(me == 0, 2, jnp.where(me == 1, 0, jnp.where(me == 2, 3, 1)))
    block = jnp.where(edge, me, 3 - me)
    heads_wanted(give_ref, 0, ids_ref, asker, block)
    heads_wanted(give_ref, 1, ids_ref, 3 - me, jnp.where(edge, me, 4))

    @pl.when(edge)
    def _():
        copy_tiles(out_ref, 0, give_ref, 1, kv_ref)


def forward_kernel(give_ref, kv_ref, up_ref, down_ref, out_ref):
    me = lax.axis_index("dp")

    @pl.when((me == 0) | (me == 3))
    def _():
        copy_tiles(out_ref, 0, give_ref, 0, kv_ref)

    @pl.when(me == 1)
    def _():
        copy_tiles(out_ref, 0, give_ref, 0, down_ref)

    @pl.when(me == 2)
    def _():
        copy_tiles(out_ref, 0, give_ref, 0, up_ref)


def pack_kernel(ids_ref, kv_ref, take_ref, out_ref, list_ref):
    me = lax.axis_index("dp")

    @pl.loop(0, ids_ref.shape[0])
    def _(other):
        far = jnp.abs(other - me) >= 2
        heads_wanted(take_ref, other, ids_ref, me, jnp.where(far, other, -1))
        heads_wanted(list_ref, 0, ids_ref, other, jnp.where(far, me, -1))
        copy_tiles(out_ref, other, list_ref, 0, kv_ref)


def local_kernel(heads_step, ids_ref, len_ref, q_ref, kv_ref, gkv_ref, acc_ref, max_ref, sum_ref):
    me = lax.axis_index("dp")
    c = pl.program_id(0)
    g = pl.program_id(1)
    glob = gkv_ref.shape[2]
    lane = lax.broadcasted_iota(jnp.int32, (1, glob + BLK), 1)
    batch = head_batch(heads_step)
    for start in range(0, heads_step, batch):
        cols = [slice(n * HD, (n + 1) * HD) for n in range(start, start + batch)]
        scores, values = [], []
        for n, col in zip(range(start, start + batch), cols):
            k = jnp.concatenate([gkv_ref[0, 0, :, col], kv_ref[0, 0, :, col]], axis=0)
            values.append(jnp.concatenate([gkv_ref[1, 0, :, col], kv_ref[1, 0, :, col]], axis=0))
            twice = jnp.where(ids_ref[me, c, g * heads_step + n] == me, 1.0, 0.0)
            bias = jnp.where(lane < glob, 0.0, jnp.where(me < len_ref[c], twice, NEG))
            scores.append(dot_nt(q_ref[0, :, col], k) * SCALE + bias)
        tops = [jnp.max(s, axis=1, keepdims=True) for s in scores]
        weights = [jnp.exp2(s - m).astype(jnp.bfloat16) for s, m in zip(scores, tops)]
        sums = [dot_nn(p, with_ones(v)) for p, v in zip(weights, values)]
        for col, m, pv in zip(cols, tops, sums):
            acc_ref[0, :, col] = pv[:, :HD]
            sum_ref[0, :, col] = pv[:, HD:]
            max_ref[0, :, col] = jnp.broadcast_to(m, (BLK, HD))


def merge(scores, olds, values):
    tops = [jnp.maximum(old[0], jnp.max(s, axis=1, keepdims=True)) for s, old in zip(scores, olds)]
    weights = [jnp.exp2(s - m[:, : s.shape[1]]).astype(jnp.bfloat16) for s, m in zip(scores, tops)]
    alphas = [jnp.exp2(old[0] - m) for old, m in zip(olds, tops)]
    added = [dot_nn(p, with_ones(v)) for p, v in zip(weights, values)]
    return [
        (m, alpha * old[1] + pv[:, HD:], alpha * old[2] + pv[:, :HD])
        for m, alpha, old, pv in zip(tops, alphas, olds, added)
    ]


def window_kernel(ids_ref, len_ref, q_ref, up_ref, down_ref, res_ref, acc_ref, max_ref, sum_ref, new_acc_ref, new_max_ref, new_sum_ref, out_ref, sq_ref):
    me = lax.axis_index("dp")
    heads = q_ref.shape[2] // HD
    batch = head_batch(heads)
    lane = lax.broadcasted_iota(jnp.int32, (1, 2 * BLK), 1)
    for c in range(2):
        length = len_ref[c]
        alive = me < length
        up_live = (me >= 1) & (me - 1 < length)
        down_live = me + 1 < length

        def step(g, squares, c=c, alive=alive, up_live=up_live, down_live=down_live):
            cols = [pl.ds(pl.multiple_of((g * batch + n) * HD, HD), HD) for n in range(batch)]
            blocks = [ids_ref[me, c, g * batch + n] for n in range(batch)]
            scores, values = [], []
            for block, col in zip(blocks, cols):
                up_bias = jnp.where(up_live, jnp.where(block == me - 1, 1.0, 0.0), NEG)
                down_bias = jnp.where(down_live, jnp.where(block == me + 1, 1.0, 0.0), NEG)
                bias = jnp.where(lane < BLK, up_bias, down_bias)
                k = jnp.concatenate([up_ref[0, c, :, col], down_ref[0, c, :, col]], axis=0)
                values.append(jnp.concatenate([up_ref[1, c, :, col], down_ref[1, c, :, col]], axis=0))
                scores.append(dot_nt(q_ref[c, :, col], k) * SCALE + bias)
            olds = [(max_ref[c, :, col], sum_ref[c, :, col], acc_ref[c, :, col]) for col in cols]
            residuals = [res_ref[c, :, col].astype(jnp.float32) for col in cols]
            news = merge(scores, olds, values)
            updates = [
                (res + jnp.where(alive, acc / l, 0.0)).astype(jnp.bfloat16) for res, (_, l, acc) in zip(residuals, news)
            ]
            for block, col, (m, l, acc), updated in zip(blocks, cols, news, updates):
                new_max_ref[c, :, col] = m
                new_sum_ref[c, :, col] = l
                new_acc_ref[c, :, col] = acc
                out_ref[c, :, col] = updated
                wide = updated.astype(jnp.float32)
                squares = squares + wide * wide * jnp.where(jnp.abs(block - me) < 2, 1.0, 0.0)
            return squares

        sq_ref[c] = lax.fori_loop(0, heads // batch, step, jnp.zeros((BLK, HD), jnp.float32))


def far_kernel(full, ids_ref, take_ref, len_ref, tile_ref, q_ref, res_ref, acc_ref, max_ref, sum_ref, old_ref, old_sq_ref, out_ref, sq_ref):
    del old_ref
    me = lax.axis_index("dp")
    owners, _, capacity = take_ref.shape
    sq_ref[...] = old_sq_ref[...]

    def one_owner(owner):
        places = [(c, s) for c in range(2) for s in range(capacity)]
        taken = [take_ref[owner, c, s] for c, s in places]
        chosen = [jnp.maximum(h, 0) for h in taken]
        cols = [pl.ds(pl.multiple_of(h * HD, HD), HD) for h in chosen]
        live = [(t >= 0) & (ids_ref[me, c, h] < len_ref[c]) for (c, _), t, h in zip(places, taken, chosen)]
        scores = [
            dot_nt(q_ref[c, :, col], tile_ref[owner, c, s, 0]) * SCALE + jnp.where(ok, 0.0, NEG)
            for (c, s), col, ok in zip(places, cols, live)
        ]
        olds = [(max_ref[c, :, col], sum_ref[c, :, col], acc_ref[c, :, col]) for (c, _), col in zip(places, cols)]
        residuals = [res_ref[c, :, col].astype(jnp.float32) for (c, _), col in zip(places, cols)]
        news = merge(scores, olds, [tile_ref[owner, c, s, 1] for c, s in places])
        updates = [
            (res + jnp.where(me < len_ref[c], acc / l, 0.0)).astype(jnp.bfloat16)
            for (c, _), res, (_, l, acc) in zip(places, residuals, news)
        ]
        squares = [jnp.zeros((BLK, HD), jnp.float32)] * 2
        for (c, _), t, updated in zip(places, taken, updates):
            wide = updated.astype(jnp.float32)
            squares[c] = squares[c] + wide * wide * jnp.where(t >= 0, 1.0, 0.0)
        for c in range(2):
            sq_ref[c] += squares[c]
        for (c, _), t, col, updated in zip(places, taken, cols, updates):
            if full:
                out_ref[c, :, col] = updated
            else:

                @pl.when(t >= 0)
                def _(c=c, col=col, updated=updated):
                    out_ref[c, :, col] = updated

    if full:

        @pl.when(take_ref[0, 0, 0] >= 0)
        def _():
            one_owner(0)

    else:
        pl.loop(0, owners)(one_owner)


def smem():
    return pl.BlockSpec(memory_space=pltpu.SMEM)


def vmem():
    return pl.BlockSpec(memory_space=pltpu.VMEM)


def body(residual, queries, keys_values, global_kv, block_ids, lengths, gain):
    width = residual.shape[-1]
    heads = width // HD
    dp_count = lax.axis_size("dp")
    pipe_count = lax.axis_size("pipe")
    tensor_count = lax.axis_size("tensor")
    group = head_group(heads)
    steps = heads // group
    lanes = group * HD
    capacity = (heads + dp_count - 1) // dp_count
    chain = dp_count == 4 and capacity * dp_count == heads
    q = queries[0]
    res = residual[0]
    glob = global_kv[0]
    length = lengths[0]
    glob_count = glob.shape[2]
    params = pltpu.CompilerParams(vmem_limit_bytes=VMEM_LIMIT)

    ids = block_ids[0, :, 0]
    ids = lax.all_to_all(jnp.broadcast_to(ids, (dp_count,) + ids.shape), "dp", split_axis=0, concat_axis=0, tiled=True)
    kv, ids = lax.optimization_barrier((keys_values[0], ids))
    up = lax.ppermute(kv, "dp", [(i, i + 1) for i in range(dp_count - 1)])
    down = lax.ppermute(kv, "dp", [(i + 1, i) for i in range(dp_count - 1)])

    lines = [[(i + 1, i) for i in range(pipe_count - 1)], [(i, i + 1) for i in range(pipe_count - 1)]]
    gains = [lax.ppermute(gain[0, c], "pipe", [(j, i) for i, j in lines[c]]) for c in range(2)]
    q, gains = lax.optimization_barrier((q, gains))
    wide = jax.ShapeDtypeStruct((2, BLK, width), jnp.float32)
    row_spec = pl.BlockSpec((1, BLK, lanes), lambda c, g: (c, 0, g))
    pair_spec = pl.BlockSpec((2, 1, BLK, lanes), lambda c, g: (0, c, 0, g))
    acc, maxes, sums = pl.pallas_call(
        functools.partial(local_kernel, group),
        grid=(2, steps),
        out_shape=[wide] * 3,
        in_specs=[
            smem(),
            smem(),
            row_spec,
            pair_spec,
            pl.BlockSpec((2, 1, glob_count, lanes), lambda c, g: (0, c, 0, g)),
        ],
        out_specs=[row_spec] * 3,
        compiler_params=params,
        cost_estimate=pl.CostEstimate(
            flops=4 * 2 * BLK * width * (glob_count + BLK), bytes_accessed=14 * 2**20, transcendentals=0
        ),
    )(ids, length, q, kv, glob)

    kv, acc = lax.optimization_barrier((kv, acc))

    tile = (2, capacity, 2, BLK, HD)
    if chain:
        table = jax.ShapeDtypeStruct((2, 2, capacity), jnp.int32)
        tiles = jax.ShapeDtypeStruct((1,) + tile, jnp.bfloat16)
        take, give, tiles_3 = pl.pallas_call(
            plan_kernel,
            out_shape=[table, table, tiles],
            in_specs=[smem(), vmem()],
            out_specs=[smem(), smem(), vmem()],
            compiler_params=params,
        )(ids, kv)
        far_3 = lax.ppermute(tiles_3, "dp", [(0, 3), (3, 0)])
        up, down, give = lax.optimization_barrier((up, down, give))
        tiles_2 = pl.pallas_call(
            forward_kernel,
            out_shape=tiles,
            in_specs=[smem(), vmem(), vmem(), vmem()],
            out_specs=vmem(),
            compiler_params=params,
        )(give, kv, up, down)
        far_2 = lax.ppermute(tiles_2, "dp", [(0, 2), (3, 1), (2, 3), (1, 0)])
        far = [(take[1:], far_3), (take[:1], far_2)]
    else:
        take, tiles_all = pl.pallas_call(
            pack_kernel,
            out_shape=[
                jax.ShapeDtypeStruct((dp_count, 2, capacity), jnp.int32),
                jax.ShapeDtypeStruct((dp_count,) + tile, jnp.bfloat16),
            ],
            in_specs=[smem(), vmem()],
            out_specs=[smem(), vmem()],
            scratch_shapes=[pltpu.SMEM((1, 2, capacity), jnp.int32)],
            compiler_params=params,
        )(ids, kv)
        far = [(take, lax.all_to_all(tiles_all, "dp", split_axis=0, concat_axis=0, tiled=True))]

    acc, maxes, sums, updated, squares = pl.pallas_call(
        window_kernel,
        out_shape=[wide] * 3
        + [jax.ShapeDtypeStruct((2, BLK, width), jnp.bfloat16), jax.ShapeDtypeStruct((2, BLK, HD), jnp.float32)],
        in_specs=[smem(), smem()] + [vmem()] * 7,
        out_specs=[vmem()] * 5,
        compiler_params=params,
        cost_estimate=pl.CostEstimate(
            flops=4 * 2 * BLK * width * 2 * BLK, bytes_accessed=9 * 2**20, transcendentals=0
        ),
    )(ids, length, q, up, down, res, acc, maxes, sums)

    for heads_taken, tiles_got in far:
        updated, squares = pl.pallas_call(
            functools.partial(far_kernel, chain),
            out_shape=[
                jax.ShapeDtypeStruct((2, BLK, width), jnp.bfloat16),
                jax.ShapeDtypeStruct((2, BLK, HD), jnp.float32),
            ],
            in_specs=[smem(), smem(), smem()] + [vmem()] * 8,
            out_specs=[vmem()] * 2,
            input_output_aliases={9: 0},
            compiler_params=params,
        )(ids, heads_taken, length, tiles_got, q, res, acc, maxes, sums, updated, squares)

    total = lax.psum(jnp.sum(squares, axis=2), "tensor")
    inverse = lax.rsqrt(total / D + epsilon)
    normed = [
        (updated[c].astype(jnp.float32) * inverse[c][:, None] * gains[c].astype(jnp.float32)).astype(jnp.bfloat16)
        for c in range(2)
    ]
    return jnp.stack([lax.ppermute(normed[c], "pipe", lines[c]) for c in range(2)])[None]


def solution(mesh):
    in_specs = (
        P("pipe", None, "dp", "tensor"),
        P("pipe", None, "dp", "tensor"),
        P("pipe", None, None, "dp", "tensor"),
        P("pipe", None, None, None, "tensor"),
        P("pipe", None, "dp", "tensor"),
        P("pipe", None),
        P("pipe", None, "tensor"),
    )
    out_specs = P("pipe", None, "dp", "tensor")
    return jax.shard_map(body, mesh=mesh, in_specs=in_specs, out_specs=out_specs, check_vma=False)
```

```python
import functools

import jax
import jax.numpy as jnp
from jax import lax
from jax.experimental import pallas as pl
from jax.experimental.pallas import tpu as pltpu
from jax.sharding import PartitionSpec as P

D = 6144
HD = 128
BLK = 64
LOG2E = 1.4426950408889634
SCALE = HD ** (-0.5) * LOG2E
NEG = -1e30
VMEM_LIMIT = 40 * 1024 * 1024

epsilon = 1e-05


def dot_nt(a, b):
    return lax.dot_general(a, b, (((1,), (1,)), ((), ())), preferred_element_type=jnp.float32)


def dot_nn(a, b):
    return lax.dot_general(a, b, (((1,), (0,)), ((), ())), preferred_element_type=jnp.float32)


def with_ones(v):
    return jnp.concatenate([v, jnp.ones((v.shape[0], HD), v.dtype)], axis=1)


def head_group(heads):
    return max(g for g in range(1, 9) if heads % g == 0)


def head_batch(heads):
    return max(g for g in range(1, 5) if heads % g == 0)


def heads_wanted(table_ref, row, ids_ref, asker, block):
    heads, capacity = ids_ref.shape[2], table_ref.shape[2]
    for c in range(2):
        for s in range(capacity):
            table_ref[row, c, s] = -1
        slot = jnp.int32(0)
        for h in range(heads):
            match = (ids_ref[asker, c, h] == block) & (slot < capacity)

            @pl.when(match)
            def _(slot=slot, h=h, c=c):
                table_ref[row, c, slot] = h

            slot = slot + match.astype(jnp.int32)


def copy_tiles(out_ref, list_ref, row, c, source_ref):
    for s in range(out_ref.shape[0]):
        cols = pl.ds(pl.multiple_of(jnp.maximum(list_ref[row, c, s], 0) * HD, HD), HD)
        out_ref[s, 0] = source_ref[0, :, cols]
        out_ref[s, 1] = source_ref[1, :, cols]


def pack_kernel(ids_ref, kv_ref, take_ref, out_ref, list_ref):
    me = lax.axis_index("dp")

    @pl.loop(0, ids_ref.shape[0])
    def _(other):
        far = jnp.abs(other - me) >= 2
        heads_wanted(take_ref, other, ids_ref, me, jnp.where(far, other, -1))
        heads_wanted(list_ref, 0, ids_ref, other, jnp.where(far, me, -1))
        for c in range(2):
            copy_tiles(out_ref.at[other, c], list_ref, 0, c, kv_ref.at[:, c])


def local_kernel(heads_step, ids_ref, len_ref, q_ref, kv_ref, gkv_ref, acc_ref, max_ref, sum_ref):
    me = lax.axis_index("dp")
    c = pl.program_id(0)
    g = pl.program_id(1)
    glob = gkv_ref.shape[2]
    lane = lax.broadcasted_iota(jnp.int32, (1, glob + BLK), 1)
    batch = head_batch(heads_step)
    for start in range(0, heads_step, batch):
        cols = [slice(n * HD, (n + 1) * HD) for n in range(start, start + batch)]
        scores, values = [], []
        for n, col in zip(range(start, start + batch), cols):
            k = jnp.concatenate([gkv_ref[0, 0, :, col], kv_ref[0, 0, :, col]], axis=0)
            values.append(jnp.concatenate([gkv_ref[1, 0, :, col], kv_ref[1, 0, :, col]], axis=0))
            twice = jnp.where(ids_ref[me, c, g * heads_step + n] == me, 1.0, 0.0)
            bias = jnp.where(lane < glob, 0.0, jnp.where(me < len_ref[c], twice, NEG))
            scores.append(dot_nt(q_ref[0, :, col], k) * SCALE + bias)
        tops = [jnp.max(s, axis=1, keepdims=True) for s in scores]
        weights = [jnp.exp2(s - m).astype(jnp.bfloat16) for s, m in zip(scores, tops)]
        sums = [dot_nn(p, with_ones(v)) for p, v in zip(weights, values)]
        for col, m, pv in zip(cols, tops, sums):
            acc_ref[0, :, col] = pv[:, :HD]
            sum_ref[0, :, col] = pv[:, HD:]
            max_ref[0, :, col] = jnp.broadcast_to(m, (BLK, HD))


def merge(scores, olds, values):
    tops = [jnp.maximum(old[0], jnp.max(s, axis=1, keepdims=True)) for s, old in zip(scores, olds)]
    weights = [jnp.exp2(s - m[:, : s.shape[1]]).astype(jnp.bfloat16) for s, m in zip(scores, tops)]
    alphas = [jnp.exp2(old[0] - m) for old, m in zip(olds, tops)]
    added = [dot_nn(p, with_ones(v)) for p, v in zip(weights, values)]
    return [
        (m, alpha * old[1] + pv[:, HD:], alpha * old[2] + pv[:, :HD])
        for m, alpha, old, pv in zip(tops, alphas, olds, added)
    ]


def window_kernel(ids_ref, len_ref, q_ref, up_ref, down_ref, res_ref, acc_ref, max_ref, sum_ref, new_acc_ref, new_max_ref, new_sum_ref, out_ref, sq_ref):
    me = lax.axis_index("dp")
    heads = q_ref.shape[2] // HD
    batch = head_batch(heads)
    lane = lax.broadcasted_iota(jnp.int32, (1, 2 * BLK), 1)
    for c in range(2):
        length = len_ref[c]
        alive = me < length
        up_live = (me >= 1) & (me - 1 < length)
        down_live = me + 1 < length

        def step(g, squares, c=c, alive=alive, up_live=up_live, down_live=down_live):
            cols = [pl.ds(pl.multiple_of((g * batch + n) * HD, HD), HD) for n in range(batch)]
            blocks = [ids_ref[me, c, g * batch + n] for n in range(batch)]
            scores, values = [], []
            for block, col in zip(blocks, cols):
                up_bias = jnp.where(up_live, jnp.where(block == me - 1, 1.0, 0.0), NEG)
                down_bias = jnp.where(down_live, jnp.where(block == me + 1, 1.0, 0.0), NEG)
                bias = jnp.where(lane < BLK, up_bias, down_bias)
                k = jnp.concatenate([up_ref[0, c, :, col], down_ref[0, c, :, col]], axis=0)
                values.append(jnp.concatenate([up_ref[1, c, :, col], down_ref[1, c, :, col]], axis=0))
                scores.append(dot_nt(q_ref[c, :, col], k) * SCALE + bias)
            olds = [(max_ref[c, :, col], sum_ref[c, :, col], acc_ref[c, :, col]) for col in cols]
            residuals = [res_ref[c, :, col].astype(jnp.float32) for col in cols]
            news = merge(scores, olds, values)
            updates = [
                (res + jnp.where(alive, acc / l, 0.0)).astype(jnp.bfloat16) for res, (_, l, acc) in zip(residuals, news)
            ]
            for block, col, (m, l, acc), updated in zip(blocks, cols, news, updates):
                new_max_ref[c, :, col] = m
                new_sum_ref[c, :, col] = l
                new_acc_ref[c, :, col] = acc
                out_ref[c, :, col] = updated
                wide = updated.astype(jnp.float32)
                squares = squares + wide * wide * jnp.where(jnp.abs(block - me) < 2, 1.0, 0.0)
            return squares

        sq_ref[c] = lax.fori_loop(0, heads // batch, step, jnp.zeros((BLK, HD), jnp.float32))


def far_kernel(ids_ref, take_ref, len_ref, tile_ref, q_ref, res_ref, acc_ref, max_ref, sum_ref, old_ref, old_sq_ref, out_ref, sq_ref):
    del old_ref
    me = lax.axis_index("dp")
    owners, _, capacity = take_ref.shape
    sq_ref[...] = old_sq_ref[...]

    def one_owner(owner):
        places = [(c, s) for c in range(2) for s in range(capacity)]
        taken = [take_ref[owner, c, s] for c, s in places]
        chosen = [jnp.maximum(h, 0) for h in taken]
        cols = [pl.ds(pl.multiple_of(h * HD, HD), HD) for h in chosen]
        live = [(t >= 0) & (ids_ref[me, c, h] < len_ref[c]) for (c, _), t, h in zip(places, taken, chosen)]
        scores = [
            dot_nt(q_ref[c, :, col], tile_ref[owner, c, s, 0]) * SCALE + jnp.where(ok, 0.0, NEG)
            for (c, s), col, ok in zip(places, cols, live)
        ]
        olds = [(max_ref[c, :, col], sum_ref[c, :, col], acc_ref[c, :, col]) for (c, _), col in zip(places, cols)]
        residuals = [res_ref[c, :, col].astype(jnp.float32) for (c, _), col in zip(places, cols)]
        news = merge(scores, olds, [tile_ref[owner, c, s, 1] for c, s in places])
        updates = [
            (res + jnp.where(me < len_ref[c], acc / l, 0.0)).astype(jnp.bfloat16)
            for (c, _), res, (_, l, acc) in zip(places, residuals, news)
        ]
        squares = [jnp.zeros((BLK, HD), jnp.float32)] * 2
        for (c, _), t, updated in zip(places, taken, updates):
            wide = updated.astype(jnp.float32)
            squares[c] = squares[c] + wide * wide * jnp.where(t >= 0, 1.0, 0.0)
        for c in range(2):
            sq_ref[c] += squares[c]
        for (c, _), t, col, updated in zip(places, taken, cols, updates):

            @pl.when(t >= 0)
            def _(c=c, col=col, updated=updated):
                out_ref[c, :, col] = updated

    pl.loop(0, owners)(one_owner)


def smem():
    return pl.BlockSpec(memory_space=pltpu.SMEM)


def vmem():
    return pl.BlockSpec(memory_space=pltpu.VMEM)


def body_any(residual, queries, keys_values, global_kv, block_ids, lengths, gain):
    width = residual.shape[-1]
    heads = width // HD
    dp_count = lax.axis_size("dp")
    pipe_count = lax.axis_size("pipe")
    tensor_count = lax.axis_size("tensor")
    group = head_group(heads)
    steps = heads // group
    lanes = group * HD
    capacity = (heads + dp_count - 1) // dp_count
    q = queries[0]
    res = residual[0]
    glob = global_kv[0]
    length = lengths[0]
    glob_count = glob.shape[2]
    params = pltpu.CompilerParams(vmem_limit_bytes=VMEM_LIMIT)

    ids = block_ids[0, :, 0]
    ids = lax.all_to_all(jnp.broadcast_to(ids, (dp_count,) + ids.shape), "dp", split_axis=0, concat_axis=0, tiled=True)
    kv, ids = lax.optimization_barrier((keys_values[0], ids))
    up = lax.ppermute(kv, "dp", [(i, i + 1) for i in range(dp_count - 1)])
    down = lax.ppermute(kv, "dp", [(i + 1, i) for i in range(dp_count - 1)])

    lines = [[(i + 1, i) for i in range(pipe_count - 1)], [(i, i + 1) for i in range(pipe_count - 1)]]
    gains = [lax.ppermute(gain[0, c], "pipe", [(j, i) for i, j in lines[c]]) for c in range(2)]
    q, gains = lax.optimization_barrier((q, gains))
    wide = jax.ShapeDtypeStruct((2, BLK, width), jnp.float32)
    row_spec = pl.BlockSpec((1, BLK, lanes), lambda c, g: (c, 0, g))
    pair_spec = pl.BlockSpec((2, 1, BLK, lanes), lambda c, g: (0, c, 0, g))
    acc, maxes, sums = pl.pallas_call(
        functools.partial(local_kernel, group),
        grid=(2, steps),
        out_shape=[wide] * 3,
        in_specs=[
            smem(),
            smem(),
            row_spec,
            pair_spec,
            pl.BlockSpec((2, 1, glob_count, lanes), lambda c, g: (0, c, 0, g)),
        ],
        out_specs=[row_spec] * 3,
        compiler_params=params,
        cost_estimate=pl.CostEstimate(
            flops=4 * 2 * BLK * width * (glob_count + BLK), bytes_accessed=14 * 2**20, transcendentals=0
        ),
    )(ids, length, q, kv, glob)

    kv, acc = lax.optimization_barrier((kv, acc))

    tile = (2, capacity, 2, BLK, HD)
    take, tiles_all = pl.pallas_call(
        pack_kernel,
        out_shape=[
            jax.ShapeDtypeStruct((dp_count, 2, capacity), jnp.int32),
            jax.ShapeDtypeStruct((dp_count,) + tile, jnp.bfloat16),
        ],
        in_specs=[smem(), vmem()],
        out_specs=[smem(), vmem()],
        scratch_shapes=[pltpu.SMEM((1, 2, capacity), jnp.int32)],
        compiler_params=params,
    )(ids, kv)
    far = [(take, lax.all_to_all(tiles_all, "dp", split_axis=0, concat_axis=0, tiled=True))]

    acc, maxes, sums, updated, squares = pl.pallas_call(
        window_kernel,
        out_shape=[wide] * 3
        + [jax.ShapeDtypeStruct((2, BLK, width), jnp.bfloat16), jax.ShapeDtypeStruct((2, BLK, HD), jnp.float32)],
        in_specs=[smem(), smem()] + [vmem()] * 7,
        out_specs=[vmem()] * 5,
        compiler_params=params,
        cost_estimate=pl.CostEstimate(
            flops=4 * 2 * BLK * width * 2 * BLK, bytes_accessed=9 * 2**20, transcendentals=0
        ),
    )(ids, length, q, up, down, res, acc, maxes, sums)

    for heads_taken, tiles_got in far:
        updated, squares = pl.pallas_call(
            far_kernel,
            out_shape=[
                jax.ShapeDtypeStruct((2, BLK, width), jnp.bfloat16),
                jax.ShapeDtypeStruct((2, BLK, HD), jnp.float32),
            ],
            in_specs=[smem(), smem(), smem()] + [vmem()] * 8,
            out_specs=[vmem()] * 2,
            input_output_aliases={9: 0},
            compiler_params=params,
        )(ids, heads_taken, length, tiles_got, q, res, acc, maxes, sums, updated, squares)

    total = lax.psum(jnp.sum(squares, axis=2), "tensor")
    inverse = lax.rsqrt(total / D + epsilon)
    normed = [
        (updated[c].astype(jnp.float32) * inverse[c][:, None] * gains[c].astype(jnp.float32)).astype(jnp.bfloat16)
        for c in range(2)
    ]
    return jnp.stack([lax.ppermute(normed[c], "pipe", lines[c]) for c in range(2)])[None]


LENGTH = 32


def sent_in(turn):
    parity = lax.rem(lax.axis_index("pipe"), 2)
    return parity if turn == 0 else 1 - parity


def copy_heads(out_ref, list_ref, row, source_ref):
    for s in range(out_ref.shape[0]):
        cols = pl.ds(pl.multiple_of(jnp.maximum(list_ref[row, s], 0) * HD, HD), HD)
        out_ref[s, 0] = source_ref[0, :, cols]
        out_ref[s, 1] = source_ref[1, :, cols]


def list_heads(list_ref, row, heads, block, block_of):
    capacity = list_ref.shape[1]
    for s in range(capacity):
        list_ref[row, s] = 0
    slot = jnp.int32(0)
    for h in range(heads):
        match = (block_of(h) == block) & (slot < capacity)

        @pl.when(match)
        def _(slot=slot, h=h):
            list_ref[row, slot] = h

        slot = slot + match.astype(jnp.int32)


def distant_kernel(ids_ref, kv0_ref, kv1_ref, tile0_ref, tile1_ref, list_ref):
    me = lax.axis_index("dp")
    heads = ids_ref.shape[2]

    @pl.when((me == 0) | (me == 3))
    def _():
        for turn, (kv_ref, tile_ref) in enumerate(((kv0_ref, tile0_ref), (kv1_ref, tile1_ref))):
            c = sent_in(turn)
            list_heads(list_ref, 0, heads, me, lambda h, c=c: ids_ref[3 - me, c, h])
            copy_heads(tile_ref, list_ref, 0, kv_ref)


def forward_kernel(turn, ids_ref, up_ids_ref, down_ids_ref, kv_ref, up_ref, down_ref, tile_ref, list_ref):
    me = lax.axis_index("dp")
    heads = ids_ref.shape[2]
    c = sent_in(turn)
    edge = (me == 0) | (me == 3)
    asker = jnp.where(me == 0, 2, 1)
    list_heads(
        list_ref,
        0,
        heads,
        jnp.where(edge, me, 3 - me),
        lambda h: jnp.where(edge, ids_ref[asker, c, h], jnp.where(me == 1, up_ids_ref[h], down_ids_ref[h])),
    )
    pl.when(edge)(lambda: copy_heads(tile_ref, list_ref, 0, kv_ref))
    pl.when(me == 1)(lambda: copy_heads(tile_ref, list_ref, 0, down_ref))
    pl.when(me == 2)(lambda: copy_heads(tile_ref, list_ref, 0, up_ref))


def message_kernel(heads_step, order_ref, ids_ref, len_ref, q_ref, res_ref, kv_ref, gkv_ref, *out_refs):
    me = lax.axis_index("dp")
    turn = pl.program_id(0)
    g = pl.program_id(1)
    c = order_ref[turn]
    glob = gkv_ref.shape[2]
    width = out_refs[0].shape[1] - HD
    heads = width // HD
    lane = lax.broadcasted_iota(jnp.int32, (1, glob + BLK), 1)
    place = lax.broadcasted_iota(jnp.int32, (1, HD), 1)
    batch = head_batch(heads_step)

    def start_state(out_ref):
        note = jnp.where(place == LENGTH, len_ref[c], 0)
        for h in range(heads):
            note = jnp.where(place == h, ids_ref[c, h], note)
        note = jnp.broadcast_to(note.astype(jnp.float32), (BLK, HD)).astype(jnp.bfloat16)
        out_ref[:BLK, width:] = note
        out_ref[BLK:, width:] = jnp.zeros((2 * BLK, HD), jnp.bfloat16)

    for n, out_ref in enumerate(out_refs):
        pl.when((g == 0) & (turn == n))(functools.partial(start_state, out_ref))

    parts = []
    for start in range(0, heads_step, batch):
        numbers = range(start, start + batch)
        cols = [slice(n * HD, (n + 1) * HD) for n in numbers]
        scores, values = [], []
        for n, col in zip(numbers, cols):
            k = jnp.concatenate([gkv_ref[0, 0, :, col], kv_ref[0, 0, :, col]], axis=0)
            values.append(jnp.concatenate([gkv_ref[1, 0, :, col], kv_ref[1, 0, :, col]], axis=0))
            twice = jnp.where(ids_ref[c, g * heads_step + n] == me, 1.0, 0.0)
            bias = jnp.where(lane < glob, 0.0, jnp.where(me < len_ref[c], twice, NEG))
            scores.append(dot_nt(q_ref[0, :, col], k) * SCALE + bias)
        tops = [jnp.max(s, axis=1, keepdims=True) for s in scores]
        weights = [jnp.exp2(s - m).astype(jnp.bfloat16) for s, m in zip(scores, tops)]
        sums = [dot_nn(p, with_ones(v)) for p, v in zip(weights, values)]
        contexts = [(pv[:, :HD] / pv[:, HD:]).astype(jnp.bfloat16) for pv in sums]
        levels = [m + jnp.log2(pv[:, HD:]) for m, pv in zip(tops, sums)]
        parts += list(zip(numbers, cols, contexts, levels))

    def write(out_ref):
        state = out_ref[2 * BLK :, width:].astype(jnp.float32)
        for n, col, context, level in parts:
            head = g * heads_step + n
            high = level.astype(jnp.bfloat16).astype(jnp.float32)
            middle = (level - high).astype(jnp.bfloat16).astype(jnp.float32)
            at = place - head
            state = jnp.where(at == 0, high, jnp.where(at == 32, middle, jnp.where(at == 64, level - high - middle, state)))
            out = pl.ds(pl.multiple_of(head * HD, HD), HD)
            out_ref[:BLK, out] = q_ref[0, :, col]
            out_ref[BLK : 2 * BLK, out] = res_ref[0, :, col]
            out_ref[2 * BLK :, out] = context
        out_ref[2 * BLK :, width:] = state.astype(jnp.bfloat16)

    for n, out_ref in enumerate(out_refs):
        pl.when(turn == n)(functools.partial(write, out_ref))


def near_kernel(info_ref, message_ref, up_ref, down_ref, acc_ref, max_ref, sum_ref, out_ref, sq_ref, take_ref):
    me = lax.axis_index("dp")
    width = out_ref.shape[1]
    heads = width // HD
    batch = head_batch(heads)
    length = info_ref[LENGTH]
    alive = me < length
    up_live = (me >= 1) & (me - 1 < length)
    down_live = me + 1 < length
    list_heads(take_ref, 0, heads, jnp.where(me < 2, me + 2, me - 2), lambda h: info_ref[h])
    list_heads(take_ref, 1, heads, 3 - me, lambda h: info_ref[h])
    lane = lax.broadcasted_iota(jnp.int32, (1, 2 * BLK), 1)
    state = message_ref[2 * BLK :, width:].astype(jnp.float32)
    state = state + pltpu.roll(state, 96, 1) + pltpu.roll(state, 64, 1)
    squares = jnp.zeros((BLK, HD), jnp.float32)
    for start in range(0, heads, batch):
        numbers = range(start, start + batch)
        cols = [slice(h * HD, (h + 1) * HD) for h in numbers]
        blocks = [info_ref[h] for h in numbers]
        scores, values = [], []
        for block, col in zip(blocks, cols):
            up_bias = jnp.where(up_live, jnp.where(block == me - 1, 1.0, 0.0), NEG)
            down_bias = jnp.where(down_live, jnp.where(block == me + 1, 1.0, 0.0), NEG)
            bias = jnp.where(lane < BLK, up_bias, down_bias)
            k = jnp.concatenate([up_ref[0, :, col], down_ref[0, :, col]], axis=0)
            values.append(jnp.concatenate([up_ref[1, :, col], down_ref[1, :, col]], axis=0))
            scores.append(dot_nt(message_ref[:BLK, col], k) * SCALE + bias)
        olds = [
            (jnp.broadcast_to(state[:, h : h + 1], (BLK, HD)), 1.0, message_ref[2 * BLK :, col].astype(jnp.float32))
            for h, col in zip(numbers, cols)
        ]
        residuals = [message_ref[BLK : 2 * BLK, col].astype(jnp.float32) for col in cols]
        news = merge(scores, olds, values)
        updates = [
            (res + jnp.where(alive, acc / l, 0.0)).astype(jnp.bfloat16) for res, (_, l, acc) in zip(residuals, news)
        ]
        for block, col, (m, l, acc), updated in zip(blocks, cols, news, updates):
            max_ref[:, col] = m
            sum_ref[:, col] = l
            acc_ref[:, col] = acc
            out_ref[:, col] = updated
            wide = updated.astype(jnp.float32)
            squares = squares + wide * wide * jnp.where(jnp.abs(block - me) < 2, 1.0, 0.0)
    sq_ref[...] = squares


def tile_kernel(row, last, *refs):
    infos, takes, messages, tiles, accs, maxes, sums, olds, old_sqs = [refs[2 * n : 2 * n + 2] for n in range(9)]
    me = lax.axis_index("dp")
    if last:
        outs = [refs[18].at[1 - sent_in(turn)] for turn in range(2)]
        sqs = [refs[19].at[1 - sent_in(turn)] for turn in range(2)]
        for turn in range(2):
            outs[turn][...] = olds[turn][...]
    else:
        outs, sqs = refs[18:20], refs[20:22]

    def work():
        places = [(t, s) for t in range(2) for s in range(tiles[0].shape[0])]
        chosen = [takes[t][row, s] for t, s in places]
        cols = [pl.ds(pl.multiple_of(h * HD, HD), HD) for h in chosen]
        live = [infos[t][h] < infos[t][LENGTH] for (t, _), h in zip(places, chosen)]
        scores = [
            dot_nt(messages[t][:BLK, col], tiles[t][s, 0]) * SCALE + jnp.where(ok, 0.0, NEG)
            for (t, s), col, ok in zip(places, cols, live)
        ]
        before = [(maxes[t][:, col], sums[t][:, col], accs[t][:, col]) for (t, _), col in zip(places, cols)]
        residuals = [messages[t][BLK : 2 * BLK, col].astype(jnp.float32) for (t, _), col in zip(places, cols)]
        news = merge(scores, before, [tiles[t][s, 1] for t, s in places])
        updates = [
            (res + jnp.where(me < infos[t][LENGTH], acc / l, 0.0)).astype(jnp.bfloat16)
            for (t, _), res, (_, l, acc) in zip(places, residuals, news)
        ]
        squares = [old_sqs[t][...] for t in range(2)]
        for (t, _), col, updated in zip(places, cols, updates):
            outs[t][:, col] = updated
            wide = updated.astype(jnp.float32)
            squares[t] = squares[t] + wide * wide
        for t in range(2):
            sqs[t][...] = squares[t]

    if last:
        work()
    else:
        for t in range(2):
            sqs[t][...] = old_sqs[t][...]
        pl.when((me == 0) | (me == 3))(work)


def body_chain(residual, queries, keys_values, global_kv, block_ids, lengths, gain):
    width = residual.shape[-1]
    heads = width // HD
    pipe_count = lax.axis_size("pipe")
    group = head_group(heads)
    steps = heads // group
    lanes = group * HD
    capacity = heads // 4
    q, res, glob, kv, length = queries[0], residual[0], global_kv[0], keys_values[0], lengths[0]
    own_ids = block_ids[0, :, 0]
    glob_count = glob.shape[2]
    params = pltpu.CompilerParams(vmem_limit_bytes=VMEM_LIMIT)
    order = jnp.stack([sent_in(0), sent_in(1)])

    def send(array, turn, moves):
        pairs = []
        for p in range(pipe_count):
            other = p ^ 1 if turn == 1 else ((p + 1) ^ 1) - 1
            if 0 <= other < pipe_count:
                pairs += [
                    ((i * pipe_count + p) if direct else (i * pipe_count + other), j * pipe_count + other)
                    for i, j, direct in moves
                ]
        return lax.ppermute(array, ("dp", "pipe"), pairs)

    ids = lax.all_to_all(jnp.broadcast_to(own_ids, (4,) + own_ids.shape), "dp", split_axis=0, concat_axis=0, tiled=True)
    kv, ids = lax.optimization_barrier((kv, ids))
    kvs, ups, downs = [], [], []
    for turn in range(2):
        c = order[turn]
        note = jnp.pad(lax.dynamic_index_in_dim(own_ids, c, 0, keepdims=False), (0, HD - heads)).astype(jnp.bfloat16)
        note = jnp.broadcast_to(note, (2, BLK, HD))
        kvs.append(jnp.concatenate([lax.dynamic_index_in_dim(kv, c, 1, keepdims=False), note], axis=2))
        ups.append(send(kvs[turn], turn, [(i, i + 1, True) for i in range(3)]))
        downs.append(send(kvs[turn], turn, [(i + 1, i, True) for i in range(3)]))

    message = jax.ShapeDtypeStruct((3 * BLK, width + HD), jnp.bfloat16)
    messages = pl.pallas_call(
        functools.partial(message_kernel, group),
        grid_spec=pltpu.PrefetchScalarGridSpec(
            num_scalar_prefetch=3,
            grid=(2, steps),
            in_specs=[
                pl.BlockSpec((1, BLK, lanes), lambda t, g, order, ids, length: (order[t], 0, g)),
                pl.BlockSpec((1, BLK, lanes), lambda t, g, order, ids, length: (order[t], 0, g)),
                pl.BlockSpec((2, 1, BLK, lanes), lambda t, g, order, ids, length: (0, order[t], 0, g)),
                pl.BlockSpec((2, 1, glob_count, lanes), lambda t, g, order, ids, length: (0, order[t], 0, g)),
            ],
            out_specs=[vmem(), vmem()],
        ),
        out_shape=[message, message],
        compiler_params=params,
    )(order, own_ids, length, q, res, kv, glob)

    same = [(i, i, True) for i in range(4)]
    messages = [send(messages[turn], turn, same) for turn in range(2)]
    tiles = jax.ShapeDtypeStruct((capacity, 2, BLK, HD), jnp.bfloat16)
    distant = pl.pallas_call(
        distant_kernel,
        out_shape=[tiles, tiles],
        in_specs=[smem(), vmem(), vmem()],
        out_specs=[vmem(), vmem()],
        scratch_shapes=[pltpu.SMEM((1, capacity), jnp.int32)],
        compiler_params=params,
    )(ids, *kvs)
    far_3 = [send(distant[turn], turn, [(0, 3, True), (3, 0, True)]) for turn in range(2)]

    far_2 = []
    for turn in range(2):
        array = pl.pallas_call(
            functools.partial(forward_kernel, turn),
            out_shape=tiles,
            in_specs=[smem()] * 3 + [vmem()] * 3,
            out_specs=vmem(),
            scratch_shapes=[pltpu.SMEM((1, capacity), jnp.int32)],
            compiler_params=params,
        )(
            ids,
            ups[turn][0, 0, width:].astype(jnp.int32),
            downs[turn][0, 0, width:].astype(jnp.int32),
            kvs[turn],
            ups[turn],
            downs[turn],
        )
        far_2.append(send(array, turn, [(0, 2, True), (3, 1, True), (2, 3, False), (1, 0, False)]))

    infos = [array[0, width:].astype(jnp.int32) for array in messages]
    wide = jax.ShapeDtypeStruct((BLK, width), jnp.float32)
    row = jax.ShapeDtypeStruct((BLK, width), jnp.bfloat16)
    square = jax.ShapeDtypeStruct((BLK, HD), jnp.float32)
    near = [
        pl.pallas_call(
            near_kernel,
            out_shape=[wide, wide, wide, row, square, jax.ShapeDtypeStruct((2, capacity), jnp.int32)],
            in_specs=[smem()] + [vmem()] * 3,
            out_specs=[vmem()] * 5 + [smem()],
            compiler_params=params,
        )(infos[turn], messages[turn], ups[turn], downs[turn])
        for turn in range(2)
    ]
    accs, maxes, sums, updates, squares, takes = [list(items) for items in zip(*near)]
    for index, got, last in ((1, far_3, False), (0, far_2, True)):
        pair = [jax.ShapeDtypeStruct((2,) + kind.shape, kind.dtype) for kind in (row, square)]
        results = pl.pallas_call(
            functools.partial(tile_kernel, index, last),
            out_shape=pair if last else [row, row, square, square],
            in_specs=[smem()] * 4 + [vmem()] * 14,
            out_specs=[vmem()] * (2 if last else 4),
            input_output_aliases={} if last else {14: 0, 15: 1},
            compiler_params=params,
        )(*infos, *takes, *messages, *got, *accs, *maxes, *sums, *updates, *squares)
        if not last:
            updates, squares = results[:2], results[2:]

    updated, squares = results
    total = lax.psum(jnp.sum(squares, axis=2), "tensor")
    inverse = lax.rsqrt(total / D + epsilon)
    normed = updated.astype(jnp.float32) * inverse[:, :, None] * gain[0][:, None, :].astype(jnp.float32)
    return normed.astype(jnp.bfloat16)[None]


def body(*arrays):
    heads = arrays[0].shape[-1] // HD
    chain = lax.axis_size("dp") == 4 and lax.axis_size("pipe") % 2 == 0 and heads % 4 == 0 and heads <= 32
    return (body_chain if chain else body_any)(*arrays)


def solution(mesh):
    in_specs = (
        P("pipe", None, "dp", "tensor"),
        P("pipe", None, "dp", "tensor"),
        P("pipe", None, None, "dp", "tensor"),
        P("pipe", None, None, None, "tensor"),
        P("pipe", None, "dp", "tensor"),
        P("pipe", None),
        P("pipe", None, "tensor"),
    )
    out_specs = P("pipe", None, "dp", "tensor")
    return jax.shard_map(body, mesh=mesh, in_specs=in_specs, out_specs=out_specs, check_vma=False)
```

```python
import functools

import jax
import jax.numpy as jnp
from jax import lax
from jax.experimental import pallas as pl
from jax.experimental.pallas import tpu as pltpu
from jax.sharding import PartitionSpec as P

D = 6144
HD = 128
BLK = 64
LOG2E = 1.4426950408889634
SCALE = HD ** (-0.5) * LOG2E
NEG = -1e30
VMEM_LIMIT = 40 * 1024 * 1024

epsilon = 1e-05


def dot_nt(a, b):
    return lax.dot_general(a, b, (((1,), (1,)), ((), ())), preferred_element_type=jnp.float32)


def dot_nn(a, b):
    return lax.dot_general(a, b, (((1,), (0,)), ((), ())), preferred_element_type=jnp.float32)


def with_ones(v):
    return jnp.concatenate([v, jnp.ones((v.shape[0], HD), v.dtype)], axis=1)


def head_group(heads):
    return max(g for g in range(1, 9) if heads % g == 0)


def head_batch(heads):
    return max(g for g in range(1, 5) if heads % g == 0)


def heads_wanted(table_ref, row, ids_ref, asker, block):
    heads, capacity = ids_ref.shape[2], table_ref.shape[2]
    for c in range(2):
        for s in range(capacity):
            table_ref[row, c, s] = -1
        slot = jnp.int32(0)
        for h in range(heads):
            match = (ids_ref[asker, c, h] == block) & (slot < capacity)

            @pl.when(match)
            def _(slot=slot, h=h, c=c):
                table_ref[row, c, slot] = h

            slot = slot + match.astype(jnp.int32)


def copy_tiles(out_ref, list_ref, row, c, source_ref):
    for s in range(out_ref.shape[0]):
        cols = pl.ds(pl.multiple_of(jnp.maximum(list_ref[row, c, s], 0) * HD, HD), HD)
        out_ref[s, 0] = source_ref[0, :, cols]
        out_ref[s, 1] = source_ref[1, :, cols]


def pack_kernel(ids_ref, kv_ref, take_ref, out_ref, list_ref):
    me = lax.axis_index("dp")

    @pl.loop(0, ids_ref.shape[0])
    def _(other):
        far = jnp.abs(other - me) >= 2
        heads_wanted(take_ref, other, ids_ref, me, jnp.where(far, other, -1))
        heads_wanted(list_ref, 0, ids_ref, other, jnp.where(far, me, -1))
        for c in range(2):
            copy_tiles(out_ref.at[other, c], list_ref, 0, c, kv_ref.at[:, c])


def local_kernel(heads_step, ids_ref, len_ref, q_ref, kv_ref, gkv_ref, acc_ref, max_ref, sum_ref):
    me = lax.axis_index("dp")
    c = pl.program_id(0)
    g = pl.program_id(1)
    glob = gkv_ref.shape[2]
    lane = lax.broadcasted_iota(jnp.int32, (1, glob + BLK), 1)
    batch = head_batch(heads_step)
    for start in range(0, heads_step, batch):
        cols = [slice(n * HD, (n + 1) * HD) for n in range(start, start + batch)]
        scores, values = [], []
        for n, col in zip(range(start, start + batch), cols):
            k = jnp.concatenate([gkv_ref[0, 0, :, col], kv_ref[0, 0, :, col]], axis=0)
            values.append(jnp.concatenate([gkv_ref[1, 0, :, col], kv_ref[1, 0, :, col]], axis=0))
            twice = jnp.where(ids_ref[me, c, g * heads_step + n] == me, 1.0, 0.0)
            bias = jnp.where(lane < glob, 0.0, jnp.where(me < len_ref[c], twice, NEG))
            scores.append(dot_nt(q_ref[0, :, col], k) * SCALE + bias)
        tops = [jnp.max(s, axis=1, keepdims=True) for s in scores]
        weights = [jnp.exp2(s - m).astype(jnp.bfloat16) for s, m in zip(scores, tops)]
        sums = [dot_nn(p, with_ones(v)) for p, v in zip(weights, values)]
        for col, m, pv in zip(cols, tops, sums):
            acc_ref[0, :, col] = pv[:, :HD]
            sum_ref[0, :, col] = pv[:, HD:]
            max_ref[0, :, col] = jnp.broadcast_to(m, (BLK, HD))


def merge(scores, olds, values):
    tops = [jnp.maximum(old[0], jnp.max(s, axis=1, keepdims=True)) for s, old in zip(scores, olds)]
    weights = [jnp.exp2(s - m[:, : s.shape[1]]).astype(jnp.bfloat16) for s, m in zip(scores, tops)]
    alphas = [jnp.exp2(old[0] - m) for old, m in zip(olds, tops)]
    added = [dot_nn(p, with_ones(v)) for p, v in zip(weights, values)]
    return [
        (m, alpha * old[1] + pv[:, HD:], alpha * old[2] + pv[:, :HD])
        for m, alpha, old, pv in zip(tops, alphas, olds, added)
    ]


def window_kernel(ids_ref, len_ref, q_ref, up_ref, down_ref, res_ref, acc_ref, max_ref, sum_ref, new_acc_ref, new_max_ref, new_sum_ref, out_ref, sq_ref):
    me = lax.axis_index("dp")
    heads = q_ref.shape[2] // HD
    batch = head_batch(heads)
    lane = lax.broadcasted_iota(jnp.int32, (1, 2 * BLK), 1)
    for c in range(2):
        length = len_ref[c]
        alive = me < length
        up_live = (me >= 1) & (me - 1 < length)
        down_live = me + 1 < length

        def step(g, squares, c=c, alive=alive, up_live=up_live, down_live=down_live):
            cols = [pl.ds(pl.multiple_of((g * batch + n) * HD, HD), HD) for n in range(batch)]
            blocks = [ids_ref[me, c, g * batch + n] for n in range(batch)]
            scores, values = [], []
            for block, col in zip(blocks, cols):
                up_bias = jnp.where(up_live, jnp.where(block == me - 1, 1.0, 0.0), NEG)
                down_bias = jnp.where(down_live, jnp.where(block == me + 1, 1.0, 0.0), NEG)
                bias = jnp.where(lane < BLK, up_bias, down_bias)
                k = jnp.concatenate([up_ref[0, c, :, col], down_ref[0, c, :, col]], axis=0)
                values.append(jnp.concatenate([up_ref[1, c, :, col], down_ref[1, c, :, col]], axis=0))
                scores.append(dot_nt(q_ref[c, :, col], k) * SCALE + bias)
            olds = [(max_ref[c, :, col], sum_ref[c, :, col], acc_ref[c, :, col]) for col in cols]
            residuals = [res_ref[c, :, col].astype(jnp.float32) for col in cols]
            news = merge(scores, olds, values)
            updates = [
                (res + jnp.where(alive, acc / l, 0.0)).astype(jnp.bfloat16) for res, (_, l, acc) in zip(residuals, news)
            ]
            for block, col, (m, l, acc), updated in zip(blocks, cols, news, updates):
                new_max_ref[c, :, col] = m
                new_sum_ref[c, :, col] = l
                new_acc_ref[c, :, col] = acc
                out_ref[c, :, col] = updated
                wide = updated.astype(jnp.float32)
                squares = squares + wide * wide * jnp.where(jnp.abs(block - me) < 2, 1.0, 0.0)
            return squares

        sq_ref[c] = lax.fori_loop(0, heads // batch, step, jnp.zeros((BLK, HD), jnp.float32))


def far_kernel(ids_ref, take_ref, len_ref, tile_ref, q_ref, res_ref, acc_ref, max_ref, sum_ref, old_ref, old_sq_ref, out_ref, sq_ref):
    del old_ref
    me = lax.axis_index("dp")
    owners, _, capacity = take_ref.shape
    sq_ref[...] = old_sq_ref[...]

    def one_owner(owner):
        places = [(c, s) for c in range(2) for s in range(capacity)]
        taken = [take_ref[owner, c, s] for c, s in places]
        chosen = [jnp.maximum(h, 0) for h in taken]
        cols = [pl.ds(pl.multiple_of(h * HD, HD), HD) for h in chosen]
        live = [(t >= 0) & (ids_ref[me, c, h] < len_ref[c]) for (c, _), t, h in zip(places, taken, chosen)]
        scores = [
            dot_nt(q_ref[c, :, col], tile_ref[owner, c, s, 0]) * SCALE + jnp.where(ok, 0.0, NEG)
            for (c, s), col, ok in zip(places, cols, live)
        ]
        olds = [(max_ref[c, :, col], sum_ref[c, :, col], acc_ref[c, :, col]) for (c, _), col in zip(places, cols)]
        residuals = [res_ref[c, :, col].astype(jnp.float32) for (c, _), col in zip(places, cols)]
        news = merge(scores, olds, [tile_ref[owner, c, s, 1] for c, s in places])
        updates = [
            (res + jnp.where(me < len_ref[c], acc / l, 0.0)).astype(jnp.bfloat16)
            for (c, _), res, (_, l, acc) in zip(places, residuals, news)
        ]
        squares = [jnp.zeros((BLK, HD), jnp.float32)] * 2
        for (c, _), t, updated in zip(places, taken, updates):
            wide = updated.astype(jnp.float32)
            squares[c] = squares[c] + wide * wide * jnp.where(t >= 0, 1.0, 0.0)
        for c in range(2):
            sq_ref[c] += squares[c]
        for (c, _), t, col, updated in zip(places, taken, cols, updates):

            @pl.when(t >= 0)
            def _(c=c, col=col, updated=updated):
                out_ref[c, :, col] = updated

    pl.loop(0, owners)(one_owner)


def smem():
    return pl.BlockSpec(memory_space=pltpu.SMEM)


def vmem():
    return pl.BlockSpec(memory_space=pltpu.VMEM)


def body_any(residual, queries, keys_values, global_kv, block_ids, lengths, gain):
    width = residual.shape[-1]
    heads = width // HD
    dp_count = lax.axis_size("dp")
    pipe_count = lax.axis_size("pipe")
    tensor_count = lax.axis_size("tensor")
    group = head_group(heads)
    steps = heads // group
    lanes = group * HD
    capacity = (heads + dp_count - 1) // dp_count
    q = queries[0]
    res = residual[0]
    glob = global_kv[0]
    length = lengths[0]
    glob_count = glob.shape[2]
    params = pltpu.CompilerParams(vmem_limit_bytes=VMEM_LIMIT)

    ids = block_ids[0, :, 0]
    ids = lax.all_to_all(jnp.broadcast_to(ids, (dp_count,) + ids.shape), "dp", split_axis=0, concat_axis=0, tiled=True)
    kv, ids = lax.optimization_barrier((keys_values[0], ids))
    up = lax.ppermute(kv, "dp", [(i, i + 1) for i in range(dp_count - 1)])
    down = lax.ppermute(kv, "dp", [(i + 1, i) for i in range(dp_count - 1)])

    lines = [[(i + 1, i) for i in range(pipe_count - 1)], [(i, i + 1) for i in range(pipe_count - 1)]]
    gains = [lax.ppermute(gain[0, c], "pipe", [(j, i) for i, j in lines[c]]) for c in range(2)]
    q, gains = lax.optimization_barrier((q, gains))
    wide = jax.ShapeDtypeStruct((2, BLK, width), jnp.float32)
    row_spec = pl.BlockSpec((1, BLK, lanes), lambda c, g: (c, 0, g))
    pair_spec = pl.BlockSpec((2, 1, BLK, lanes), lambda c, g: (0, c, 0, g))
    acc, maxes, sums = pl.pallas_call(
        functools.partial(local_kernel, group),
        grid=(2, steps),
        out_shape=[wide] * 3,
        in_specs=[
            smem(),
            smem(),
            row_spec,
            pair_spec,
            pl.BlockSpec((2, 1, glob_count, lanes), lambda c, g: (0, c, 0, g)),
        ],
        out_specs=[row_spec] * 3,
        compiler_params=params,
        cost_estimate=pl.CostEstimate(
            flops=4 * 2 * BLK * width * (glob_count + BLK), bytes_accessed=14 * 2**20, transcendentals=0
        ),
    )(ids, length, q, kv, glob)

    kv, acc = lax.optimization_barrier((kv, acc))

    tile = (2, capacity, 2, BLK, HD)
    take, tiles_all = pl.pallas_call(
        pack_kernel,
        out_shape=[
            jax.ShapeDtypeStruct((dp_count, 2, capacity), jnp.int32),
            jax.ShapeDtypeStruct((dp_count,) + tile, jnp.bfloat16),
        ],
        in_specs=[smem(), vmem()],
        out_specs=[smem(), vmem()],
        scratch_shapes=[pltpu.SMEM((1, 2, capacity), jnp.int32)],
        compiler_params=params,
    )(ids, kv)
    far = [(take, lax.all_to_all(tiles_all, "dp", split_axis=0, concat_axis=0, tiled=True))]

    acc, maxes, sums, updated, squares = pl.pallas_call(
        window_kernel,
        out_shape=[wide] * 3
        + [jax.ShapeDtypeStruct((2, BLK, width), jnp.bfloat16), jax.ShapeDtypeStruct((2, BLK, HD), jnp.float32)],
        in_specs=[smem(), smem()] + [vmem()] * 7,
        out_specs=[vmem()] * 5,
        compiler_params=params,
        cost_estimate=pl.CostEstimate(
            flops=4 * 2 * BLK * width * 2 * BLK, bytes_accessed=9 * 2**20, transcendentals=0
        ),
    )(ids, length, q, up, down, res, acc, maxes, sums)

    for heads_taken, tiles_got in far:
        updated, squares = pl.pallas_call(
            far_kernel,
            out_shape=[
                jax.ShapeDtypeStruct((2, BLK, width), jnp.bfloat16),
                jax.ShapeDtypeStruct((2, BLK, HD), jnp.float32),
            ],
            in_specs=[smem(), smem(), smem()] + [vmem()] * 8,
            out_specs=[vmem()] * 2,
            input_output_aliases={9: 0},
            compiler_params=params,
        )(ids, heads_taken, length, tiles_got, q, res, acc, maxes, sums, updated, squares)

    total = lax.psum(jnp.sum(squares, axis=2), "tensor")
    inverse = lax.rsqrt(total / D + epsilon)
    normed = [
        (updated[c].astype(jnp.float32) * inverse[c][:, None] * gains[c].astype(jnp.float32)).astype(jnp.bfloat16)
        for c in range(2)
    ]
    return jnp.stack([lax.ppermute(normed[c], "pipe", lines[c]) for c in range(2)])[None]


LENGTH = 32


def sent_in(turn):
    parity = lax.rem(lax.axis_index("pipe"), 2)
    return parity if turn == 0 else 1 - parity


def copy_heads(out_ref, list_ref, row, source_ref):
    for s in range(out_ref.shape[0]):
        cols = pl.ds(pl.multiple_of(jnp.maximum(list_ref[row, s], 0) * HD, HD), HD)
        out_ref[s, 0] = source_ref[0, :, cols]
        out_ref[s, 1] = source_ref[1, :, cols]


def list_heads(list_ref, row, heads, block, block_of):
    capacity = list_ref.shape[1]
    for s in range(capacity):
        list_ref[row, s] = 0
    slot = jnp.int32(0)
    for h in range(heads):
        match = (block_of(h) == block) & (slot < capacity)

        @pl.when(match)
        def _(slot=slot, h=h):
            list_ref[row, slot] = h

        slot = slot + match.astype(jnp.int32)


def distant_kernel(ids_ref, kv0_ref, kv1_ref, tile0_ref, tile1_ref, list_ref):
    me = lax.axis_index("dp")
    heads = ids_ref.shape[2]

    @pl.when((me == 0) | (me == 3))
    def _():
        for turn, (kv_ref, tile_ref) in enumerate(((kv0_ref, tile0_ref), (kv1_ref, tile1_ref))):
            c = sent_in(turn)
            list_heads(list_ref, 0, heads, me, lambda h, c=c: ids_ref[3 - me, c, h])
            copy_heads(tile_ref, list_ref, 0, kv_ref)


def forward_kernel(turn, ids_ref, up_ids_ref, down_ids_ref, kv_ref, up_ref, down_ref, tile_ref, list_ref):
    me = lax.axis_index("dp")
    heads = ids_ref.shape[2]
    c = sent_in(turn)
    edge = (me == 0) | (me == 3)
    asker = jnp.where(me == 0, 2, 1)
    list_heads(
        list_ref,
        0,
        heads,
        jnp.where(edge, me, 3 - me),
        lambda h: jnp.where(edge, ids_ref[asker, c, h], jnp.where(me == 1, up_ids_ref[h], down_ids_ref[h])),
    )
    pl.when(edge)(lambda: copy_heads(tile_ref, list_ref, 0, kv_ref))
    pl.when(me == 1)(lambda: copy_heads(tile_ref, list_ref, 0, down_ref))
    pl.when(me == 2)(lambda: copy_heads(tile_ref, list_ref, 0, up_ref))


def message_kernel(heads_step, order_ref, ids_ref, len_ref, q_ref, res_ref, kv_ref, gkv_ref, *out_refs):
    me = lax.axis_index("dp")
    turn = pl.program_id(0)
    g = pl.program_id(1)
    c = order_ref[turn]
    glob = gkv_ref.shape[2]
    width = out_refs[0].shape[1] - HD
    heads = width // HD
    lane = lax.broadcasted_iota(jnp.int32, (1, glob + BLK), 1)
    place = lax.broadcasted_iota(jnp.int32, (1, HD), 1)
    batch = head_batch(heads_step)

    def start_state(out_ref):
        note = jnp.where(place == LENGTH, len_ref[c], 0)
        for h in range(heads):
            note = jnp.where(place == h, ids_ref[c, h], note)
        note = jnp.broadcast_to(note.astype(jnp.float32), (BLK, HD)).astype(jnp.bfloat16)
        out_ref[:BLK, width:] = note
        out_ref[BLK:, width:] = jnp.zeros((2 * BLK, HD), jnp.bfloat16)

    for n, out_ref in enumerate(out_refs):
        pl.when((g == 0) & (turn == n))(functools.partial(start_state, out_ref))

    parts = []
    for start in range(0, heads_step, batch):
        numbers = range(start, start + batch)
        cols = [slice(n * HD, (n + 1) * HD) for n in numbers]
        scores, values = [], []
        for n, col in zip(numbers, cols):
            k = jnp.concatenate([gkv_ref[0, 0, :, col], kv_ref[0, 0, :, col]], axis=0)
            values.append(jnp.concatenate([gkv_ref[1, 0, :, col], kv_ref[1, 0, :, col]], axis=0))
            twice = jnp.where(ids_ref[c, g * heads_step + n] == me, 1.0, 0.0)
            bias = jnp.where(lane < glob, 0.0, jnp.where(me < len_ref[c], twice, NEG))
            scores.append(dot_nt(q_ref[0, :, col], k) * SCALE + bias)
        tops = [jnp.max(s, axis=1, keepdims=True) for s in scores]
        weights = [jnp.exp2(s - m).astype(jnp.bfloat16) for s, m in zip(scores, tops)]
        sums = [dot_nn(p, with_ones(v)) for p, v in zip(weights, values)]
        contexts = [(pv[:, :HD] / pv[:, HD:]).astype(jnp.bfloat16) for pv in sums]
        levels = [m + jnp.log2(pv[:, HD:]) for m, pv in zip(tops, sums)]
        parts += list(zip(numbers, cols, contexts, levels))

    def write(out_ref):
        state = out_ref[2 * BLK :, width:].astype(jnp.float32)
        for n, col, context, level in parts:
            head = g * heads_step + n
            high = level.astype(jnp.bfloat16).astype(jnp.float32)
            middle = (level - high).astype(jnp.bfloat16).astype(jnp.float32)
            at = place - head
            state = jnp.where(at == 0, high, jnp.where(at == 32, middle, jnp.where(at == 64, level - high - middle, state)))
            out = pl.ds(pl.multiple_of(head * HD, HD), HD)
            out_ref[:BLK, out] = q_ref[0, :, col]
            out_ref[BLK : 2 * BLK, out] = res_ref[0, :, col]
            out_ref[2 * BLK :, out] = context
        out_ref[2 * BLK :, width:] = state.astype(jnp.bfloat16)

    for n, out_ref in enumerate(out_refs):
        pl.when(turn == n)(functools.partial(write, out_ref))


def near_kernel(info_ref, message_ref, up_ref, down_ref, acc_ref, max_ref, sum_ref, out_ref, sq_ref, take_ref):
    me = lax.axis_index("dp")
    width = out_ref.shape[1]
    heads = width // HD
    batch = head_batch(heads)
    length = info_ref[LENGTH]
    alive = me < length
    up_live = (me >= 1) & (me - 1 < length)
    down_live = me + 1 < length
    list_heads(take_ref, 0, heads, jnp.where(me < 2, me + 2, me - 2), lambda h: info_ref[h])
    list_heads(take_ref, 1, heads, 3 - me, lambda h: info_ref[h])
    lane = lax.broadcasted_iota(jnp.int32, (1, 2 * BLK), 1)
    state = message_ref[2 * BLK :, width:].astype(jnp.float32)
    state = state + pltpu.roll(state, 96, 1) + pltpu.roll(state, 64, 1)
    squares = jnp.zeros((BLK, HD), jnp.float32)
    for start in range(0, heads, batch):
        numbers = range(start, start + batch)
        cols = [slice(h * HD, (h + 1) * HD) for h in numbers]
        blocks = [info_ref[h] for h in numbers]
        scores, values = [], []
        for block, col in zip(blocks, cols):
            up_bias = jnp.where(up_live, jnp.where(block == me - 1, 1.0, 0.0), NEG)
            down_bias = jnp.where(down_live, jnp.where(block == me + 1, 1.0, 0.0), NEG)
            bias = jnp.where(lane < BLK, up_bias, down_bias)
            k = jnp.concatenate([up_ref[0, :, col], down_ref[0, :, col]], axis=0)
            values.append(jnp.concatenate([up_ref[1, :, col], down_ref[1, :, col]], axis=0))
            scores.append(dot_nt(message_ref[:BLK, col], k) * SCALE + bias)
        olds = [
            (jnp.broadcast_to(state[:, h : h + 1], (BLK, HD)), 1.0, message_ref[2 * BLK :, col].astype(jnp.float32))
            for h, col in zip(numbers, cols)
        ]
        residuals = [message_ref[BLK : 2 * BLK, col].astype(jnp.float32) for col in cols]
        news = merge(scores, olds, values)
        updates = [
            (res + jnp.where(alive, acc / l, 0.0)).astype(jnp.bfloat16) for res, (_, l, acc) in zip(residuals, news)
        ]
        for block, col, (m, l, acc), updated in zip(blocks, cols, news, updates):
            max_ref[:, col] = m
            sum_ref[:, col] = l
            acc_ref[:, col] = acc
            out_ref[:, col] = updated
            wide = updated.astype(jnp.float32)
            squares = squares + wide * wide * jnp.where(jnp.abs(block - me) < 2, 1.0, 0.0)
    sq_ref[...] = squares


def tile_kernel(row, last, *refs):
    infos, takes, messages, tiles, accs, maxes, sums, olds, old_sqs = [refs[2 * n : 2 * n + 2] for n in range(9)]
    me = lax.axis_index("dp")
    if last:
        outs = [refs[18].at[1 - sent_in(turn)] for turn in range(2)]
        sqs = [refs[19].at[1 - sent_in(turn)] for turn in range(2)]
        for turn in range(2):
            outs[turn][...] = olds[turn][...]
    else:
        outs, sqs = refs[18:20], refs[20:22]

    def work():
        places = [(t, s) for t in range(2) for s in range(tiles[0].shape[0])]
        chosen = [takes[t][row, s] for t, s in places]
        cols = [pl.ds(pl.multiple_of(h * HD, HD), HD) for h in chosen]
        live = [infos[t][h] < infos[t][LENGTH] for (t, _), h in zip(places, chosen)]
        scores = [
            dot_nt(messages[t][:BLK, col], tiles[t][s, 0]) * SCALE + jnp.where(ok, 0.0, NEG)
            for (t, s), col, ok in zip(places, cols, live)
        ]
        before = [(maxes[t][:, col], sums[t][:, col], accs[t][:, col]) for (t, _), col in zip(places, cols)]
        residuals = [messages[t][BLK : 2 * BLK, col].astype(jnp.float32) for (t, _), col in zip(places, cols)]
        news = merge(scores, before, [tiles[t][s, 1] for t, s in places])
        updates = [
            (res + jnp.where(me < infos[t][LENGTH], acc / l, 0.0)).astype(jnp.bfloat16)
            for (t, _), res, (_, l, acc) in zip(places, residuals, news)
        ]
        squares = [old_sqs[t][...] for t in range(2)]
        for (t, _), col, updated in zip(places, cols, updates):
            outs[t][:, col] = updated
            wide = updated.astype(jnp.float32)
            squares[t] = squares[t] + wide * wide
        for t in range(2):
            sqs[t][...] = squares[t]

    if last:
        work()
    else:
        for t in range(2):
            sqs[t][...] = old_sqs[t][...]
        pl.when((me == 0) | (me == 3))(work)


def body_chain(residual, queries, keys_values, global_kv, block_ids, lengths, gain):
    width = residual.shape[-1]
    heads = width // HD
    pipe_count = lax.axis_size("pipe")
    group = head_group(heads)
    steps = heads // group
    lanes = group * HD
    capacity = heads // 4
    q, res, glob, kv, length = queries[0], residual[0], global_kv[0], keys_values[0], lengths[0]
    own_ids = block_ids[0, :, 0]
    glob_count = glob.shape[2]
    params = pltpu.CompilerParams(vmem_limit_bytes=VMEM_LIMIT)
    order = jnp.stack([sent_in(0), sent_in(1)])

    def send(array, turn, moves):
        pairs = []
        for p in range(pipe_count):
            other = p ^ 1 if turn == 1 else ((p + 1) ^ 1) - 1
            if 0 <= other < pipe_count:
                pairs += [
                    ((i * pipe_count + p) if direct else (i * pipe_count + other), j * pipe_count + other)
                    for i, j, direct in moves
                ]
        return lax.ppermute(array, ("dp", "pipe"), pairs)

    ids = lax.all_to_all(jnp.broadcast_to(own_ids, (4,) + own_ids.shape), "dp", split_axis=0, concat_axis=0, tiled=True)
    kvs, ups, downs = [], [], []
    for turn in range(2):
        c = order[turn]
        if turn == 1:
            kv, ids = lax.optimization_barrier((kv, ids))
        note = jnp.pad(lax.dynamic_index_in_dim(own_ids, c, 0, keepdims=False), (0, HD - heads)).astype(jnp.bfloat16)
        note = jnp.broadcast_to(note, (2, BLK, HD))
        kvs.append(jnp.concatenate([lax.dynamic_index_in_dim(kv, c, 1, keepdims=False), note], axis=2))
        ups.append(send(kvs[turn], turn, [(i, i + 1, True) for i in range(3)]))
        downs.append(send(kvs[turn], turn, [(i + 1, i, True) for i in range(3)]))

    message = jax.ShapeDtypeStruct((3 * BLK, width + HD), jnp.bfloat16)
    messages = pl.pallas_call(
        functools.partial(message_kernel, group),
        grid_spec=pltpu.PrefetchScalarGridSpec(
            num_scalar_prefetch=3,
            grid=(2, steps),
            in_specs=[
                pl.BlockSpec((1, BLK, lanes), lambda t, g, order, ids, length: (order[t], 0, g)),
                pl.BlockSpec((1, BLK, lanes), lambda t, g, order, ids, length: (order[t], 0, g)),
                pl.BlockSpec((2, 1, BLK, lanes), lambda t, g, order, ids, length: (0, order[t], 0, g)),
                pl.BlockSpec((2, 1, glob_count, lanes), lambda t, g, order, ids, length: (0, order[t], 0, g)),
            ],
            out_specs=[vmem(), vmem()],
        ),
        out_shape=[message, message],
        compiler_params=params,
    )(order, own_ids, length, q, res, kv, glob)

    same = [(i, i, True) for i in range(4)]
    messages = [send(messages[turn], turn, same) for turn in range(2)]
    tiles = jax.ShapeDtypeStruct((capacity, 2, BLK, HD), jnp.bfloat16)
    distant = pl.pallas_call(
        distant_kernel,
        out_shape=[tiles, tiles],
        in_specs=[smem(), vmem(), vmem()],
        out_specs=[vmem(), vmem()],
        scratch_shapes=[pltpu.SMEM((1, capacity), jnp.int32)],
        compiler_params=params,
    )(ids, *kvs)
    far_3 = [send(distant[turn], turn, [(0, 3, True), (3, 0, True)]) for turn in range(2)]

    far_2 = []
    for turn in range(2):
        array = pl.pallas_call(
            functools.partial(forward_kernel, turn),
            out_shape=tiles,
            in_specs=[smem()] * 3 + [vmem()] * 3,
            out_specs=vmem(),
            scratch_shapes=[pltpu.SMEM((1, capacity), jnp.int32)],
            compiler_params=params,
        )(
            ids,
            ups[turn][0, 0, width:].astype(jnp.int32),
            downs[turn][0, 0, width:].astype(jnp.int32),
            kvs[turn],
            ups[turn],
            downs[turn],
        )
        far_2.append(send(array, turn, [(0, 2, True), (3, 1, True), (2, 3, False), (1, 0, False)]))

    infos = [array[0, width:].astype(jnp.int32) for array in messages]
    wide = jax.ShapeDtypeStruct((BLK, width), jnp.float32)
    row = jax.ShapeDtypeStruct((BLK, width), jnp.bfloat16)
    square = jax.ShapeDtypeStruct((BLK, HD), jnp.float32)
    near = [
        pl.pallas_call(
            near_kernel,
            out_shape=[wide, wide, wide, row, square, jax.ShapeDtypeStruct((2, capacity), jnp.int32)],
            in_specs=[smem()] + [vmem()] * 3,
            out_specs=[vmem()] * 5 + [smem()],
            compiler_params=params,
        )(infos[turn], messages[turn], ups[turn], downs[turn])
        for turn in range(2)
    ]
    accs, maxes, sums, updates, squares, takes = [list(items) for items in zip(*near)]
    for index, got, last in ((1, far_3, False), (0, far_2, True)):
        pair = [jax.ShapeDtypeStruct((2,) + kind.shape, kind.dtype) for kind in (row, square)]
        results = pl.pallas_call(
            functools.partial(tile_kernel, index, last),
            out_shape=pair if last else [row, row, square, square],
            in_specs=[smem()] * 4 + [vmem()] * 14,
            out_specs=[vmem()] * (2 if last else 4),
            input_output_aliases={} if last else {14: 0, 15: 1},
            compiler_params=params,
        )(*infos, *takes, *messages, *got, *accs, *maxes, *sums, *updates, *squares)
        if not last:
            updates, squares = results[:2], results[2:]

    updated, squares = results
    total = lax.psum(jnp.sum(squares, axis=2), "tensor")
    inverse = lax.rsqrt(total / D + epsilon)
    normed = updated.astype(jnp.float32) * inverse[:, :, None] * gain[0][:, None, :].astype(jnp.float32)
    return normed.astype(jnp.bfloat16)[None]


def body(*arrays):
    heads = arrays[0].shape[-1] // HD
    chain = lax.axis_size("dp") == 4 and lax.axis_size("pipe") % 2 == 0 and heads % 4 == 0 and heads <= 32
    return (body_chain if chain else body_any)(*arrays)


def solution(mesh):
    in_specs = (
        P("pipe", None, "dp", "tensor"),
        P("pipe", None, "dp", "tensor"),
        P("pipe", None, None, "dp", "tensor"),
        P("pipe", None, None, None, "tensor"),
        P("pipe", None, "dp", "tensor"),
        P("pipe", None),
        P("pipe", None, "tensor"),
    )
    out_specs = P("pipe", None, "dp", "tensor")
    return jax.shard_map(body, mesh=mesh, in_specs=in_specs, out_specs=out_specs, check_vma=False)
```

```python
import functools

import jax
import jax.numpy as jnp
from jax import lax
from jax.experimental import pallas as pl
from jax.experimental.pallas import tpu as pltpu
from jax.sharding import PartitionSpec as P

D = 6144
HD = 128
BLK = 64
LOG2E = 1.4426950408889634
SCALE = HD ** (-0.5) * LOG2E
NEG = -1e30
VMEM_LIMIT = 40 * 1024 * 1024

epsilon = 1e-05


def dot_nt(a, b):
    return lax.dot_general(a, b, (((1,), (1,)), ((), ())), preferred_element_type=jnp.float32)


def dot_nn(a, b):
    return lax.dot_general(a, b, (((1,), (0,)), ((), ())), preferred_element_type=jnp.float32)


def with_ones(v):
    return jnp.concatenate([v, jnp.ones((v.shape[0], HD), v.dtype)], axis=1)


def head_group(heads):
    return max(g for g in range(1, 9) if heads % g == 0)


def head_batch(heads):
    return max(g for g in range(1, 5) if heads % g == 0)


def heads_wanted(table_ref, row, ids_ref, asker, block):
    heads, capacity = ids_ref.shape[2], table_ref.shape[2]
    for c in range(2):
        for s in range(capacity):
            table_ref[row, c, s] = -1
        slot = jnp.int32(0)
        for h in range(heads):
            match = (ids_ref[asker, c, h] == block) & (slot < capacity)

            @pl.when(match)
            def _(slot=slot, h=h, c=c):
                table_ref[row, c, slot] = h

            slot = slot + match.astype(jnp.int32)


def copy_tiles(out_ref, list_ref, row, c, source_ref):
    for s in range(out_ref.shape[0]):
        cols = pl.ds(pl.multiple_of(jnp.maximum(list_ref[row, c, s], 0) * HD, HD), HD)
        out_ref[s, 0] = source_ref[0, :, cols]
        out_ref[s, 1] = source_ref[1, :, cols]


def pack_kernel(ids_ref, kv_ref, take_ref, out_ref, list_ref):
    me = lax.axis_index("dp")

    @pl.loop(0, ids_ref.shape[0])
    def _(other):
        far = jnp.abs(other - me) >= 2
        heads_wanted(take_ref, other, ids_ref, me, jnp.where(far, other, -1))
        heads_wanted(list_ref, 0, ids_ref, other, jnp.where(far, me, -1))
        for c in range(2):
            copy_tiles(out_ref.at[other, c], list_ref, 0, c, kv_ref.at[:, c])


def local_kernel(heads_step, ids_ref, len_ref, q_ref, kv_ref, gkv_ref, acc_ref, max_ref, sum_ref):
    me = lax.axis_index("dp")
    c = pl.program_id(0)
    g = pl.program_id(1)
    glob = gkv_ref.shape[2]
    lane = lax.broadcasted_iota(jnp.int32, (1, glob + BLK), 1)
    batch = head_batch(heads_step)
    for start in range(0, heads_step, batch):
        cols = [slice(n * HD, (n + 1) * HD) for n in range(start, start + batch)]
        scores, values = [], []
        for n, col in zip(range(start, start + batch), cols):
            k = jnp.concatenate([gkv_ref[0, 0, :, col], kv_ref[0, 0, :, col]], axis=0)
            values.append(jnp.concatenate([gkv_ref[1, 0, :, col], kv_ref[1, 0, :, col]], axis=0))
            twice = jnp.where(ids_ref[me, c, g * heads_step + n] == me, 1.0, 0.0)
            bias = jnp.where(lane < glob, 0.0, jnp.where(me < len_ref[c], twice, NEG))
            scores.append(dot_nt(q_ref[0, :, col], k) * SCALE + bias)
        tops = [jnp.max(s, axis=1, keepdims=True) for s in scores]
        weights = [jnp.exp2(s - m).astype(jnp.bfloat16) for s, m in zip(scores, tops)]
        sums = [dot_nn(p, with_ones(v)) for p, v in zip(weights, values)]
        for col, m, pv in zip(cols, tops, sums):
            acc_ref[0, :, col] = pv[:, :HD]
            sum_ref[0, :, col] = pv[:, HD:]
            max_ref[0, :, col] = jnp.broadcast_to(m, (BLK, HD))


def merge(scores, olds, values):
    tops = [jnp.maximum(old[0], jnp.max(s, axis=1, keepdims=True)) for s, old in zip(scores, olds)]
    weights = [jnp.exp2(s - m[:, : s.shape[1]]).astype(jnp.bfloat16) for s, m in zip(scores, tops)]
    alphas = [jnp.exp2(old[0] - m) for old, m in zip(olds, tops)]
    added = [dot_nn(p, with_ones(v)) for p, v in zip(weights, values)]
    return [
        (m, alpha * old[1] + pv[:, HD:], alpha * old[2] + pv[:, :HD])
        for m, alpha, old, pv in zip(tops, alphas, olds, added)
    ]


def window_kernel(ids_ref, len_ref, q_ref, up_ref, down_ref, res_ref, acc_ref, max_ref, sum_ref, new_acc_ref, new_max_ref, new_sum_ref, out_ref, sq_ref):
    me = lax.axis_index("dp")
    heads = q_ref.shape[2] // HD
    batch = head_batch(heads)
    lane = lax.broadcasted_iota(jnp.int32, (1, 2 * BLK), 1)
    for c in range(2):
        length = len_ref[c]
        alive = me < length
        up_live = (me >= 1) & (me - 1 < length)
        down_live = me + 1 < length

        def step(g, squares, c=c, alive=alive, up_live=up_live, down_live=down_live):
            cols = [pl.ds(pl.multiple_of((g * batch + n) * HD, HD), HD) for n in range(batch)]
            blocks = [ids_ref[me, c, g * batch + n] for n in range(batch)]
            scores, values = [], []
            for block, col in zip(blocks, cols):
                up_bias = jnp.where(up_live, jnp.where(block == me - 1, 1.0, 0.0), NEG)
                down_bias = jnp.where(down_live, jnp.where(block == me + 1, 1.0, 0.0), NEG)
                bias = jnp.where(lane < BLK, up_bias, down_bias)
                k = jnp.concatenate([up_ref[0, c, :, col], down_ref[0, c, :, col]], axis=0)
                values.append(jnp.concatenate([up_ref[1, c, :, col], down_ref[1, c, :, col]], axis=0))
                scores.append(dot_nt(q_ref[c, :, col], k) * SCALE + bias)
            olds = [(max_ref[c, :, col], sum_ref[c, :, col], acc_ref[c, :, col]) for col in cols]
            residuals = [res_ref[c, :, col].astype(jnp.float32) for col in cols]
            news = merge(scores, olds, values)
            updates = [
                (res + jnp.where(alive, acc / l, 0.0)).astype(jnp.bfloat16) for res, (_, l, acc) in zip(residuals, news)
            ]
            for block, col, (m, l, acc), updated in zip(blocks, cols, news, updates):
                new_max_ref[c, :, col] = m
                new_sum_ref[c, :, col] = l
                new_acc_ref[c, :, col] = acc
                out_ref[c, :, col] = updated
                wide = updated.astype(jnp.float32)
                squares = squares + wide * wide * jnp.where(jnp.abs(block - me) < 2, 1.0, 0.0)
            return squares

        sq_ref[c] = lax.fori_loop(0, heads // batch, step, jnp.zeros((BLK, HD), jnp.float32))


def far_kernel(ids_ref, take_ref, len_ref, tile_ref, q_ref, res_ref, acc_ref, max_ref, sum_ref, old_ref, old_sq_ref, out_ref, sq_ref):
    del old_ref
    me = lax.axis_index("dp")
    owners, _, capacity = take_ref.shape
    sq_ref[...] = old_sq_ref[...]

    def one_owner(owner):
        places = [(c, s) for c in range(2) for s in range(capacity)]
        taken = [take_ref[owner, c, s] for c, s in places]
        chosen = [jnp.maximum(h, 0) for h in taken]
        cols = [pl.ds(pl.multiple_of(h * HD, HD), HD) for h in chosen]
        live = [(t >= 0) & (ids_ref[me, c, h] < len_ref[c]) for (c, _), t, h in zip(places, taken, chosen)]
        scores = [
            dot_nt(q_ref[c, :, col], tile_ref[owner, c, s, 0]) * SCALE + jnp.where(ok, 0.0, NEG)
            for (c, s), col, ok in zip(places, cols, live)
        ]
        olds = [(max_ref[c, :, col], sum_ref[c, :, col], acc_ref[c, :, col]) for (c, _), col in zip(places, cols)]
        residuals = [res_ref[c, :, col].astype(jnp.float32) for (c, _), col in zip(places, cols)]
        news = merge(scores, olds, [tile_ref[owner, c, s, 1] for c, s in places])
        updates = [
            (res + jnp.where(me < len_ref[c], acc / l, 0.0)).astype(jnp.bfloat16)
            for (c, _), res, (_, l, acc) in zip(places, residuals, news)
        ]
        squares = [jnp.zeros((BLK, HD), jnp.float32)] * 2
        for (c, _), t, updated in zip(places, taken, updates):
            wide = updated.astype(jnp.float32)
            squares[c] = squares[c] + wide * wide * jnp.where(t >= 0, 1.0, 0.0)
        for c in range(2):
            sq_ref[c] += squares[c]
        for (c, _), t, col, updated in zip(places, taken, cols, updates):

            @pl.when(t >= 0)
            def _(c=c, col=col, updated=updated):
                out_ref[c, :, col] = updated

    pl.loop(0, owners)(one_owner)


def smem():
    return pl.BlockSpec(memory_space=pltpu.SMEM)


def vmem():
    return pl.BlockSpec(memory_space=pltpu.VMEM)


def body_any(residual, queries, keys_values, global_kv, block_ids, lengths, gain):
    width = residual.shape[-1]
    heads = width // HD
    dp_count = lax.axis_size("dp")
    pipe_count = lax.axis_size("pipe")
    tensor_count = lax.axis_size("tensor")
    group = head_group(heads)
    steps = heads // group
    lanes = group * HD
    capacity = (heads + dp_count - 1) // dp_count
    q = queries[0]
    res = residual[0]
    glob = global_kv[0]
    length = lengths[0]
    glob_count = glob.shape[2]
    params = pltpu.CompilerParams(vmem_limit_bytes=VMEM_LIMIT)

    ids = block_ids[0, :, 0]
    ids = lax.all_to_all(jnp.broadcast_to(ids, (dp_count,) + ids.shape), "dp", split_axis=0, concat_axis=0, tiled=True)
    kv, ids = lax.optimization_barrier((keys_values[0], ids))
    up = lax.ppermute(kv, "dp", [(i, i + 1) for i in range(dp_count - 1)])
    down = lax.ppermute(kv, "dp", [(i + 1, i) for i in range(dp_count - 1)])

    lines = [[(i + 1, i) for i in range(pipe_count - 1)], [(i, i + 1) for i in range(pipe_count - 1)]]
    gains = [lax.ppermute(gain[0, c], "pipe", [(j, i) for i, j in lines[c]]) for c in range(2)]
    q, gains = lax.optimization_barrier((q, gains))
    wide = jax.ShapeDtypeStruct((2, BLK, width), jnp.float32)
    row_spec = pl.BlockSpec((1, BLK, lanes), lambda c, g: (c, 0, g))
    pair_spec = pl.BlockSpec((2, 1, BLK, lanes), lambda c, g: (0, c, 0, g))
    acc, maxes, sums = pl.pallas_call(
        functools.partial(local_kernel, group),
        grid=(2, steps),
        out_shape=[wide] * 3,
        in_specs=[
            smem(),
            smem(),
            row_spec,
            pair_spec,
            pl.BlockSpec((2, 1, glob_count, lanes), lambda c, g: (0, c, 0, g)),
        ],
        out_specs=[row_spec] * 3,
        compiler_params=params,
        cost_estimate=pl.CostEstimate(
            flops=4 * 2 * BLK * width * (glob_count + BLK), bytes_accessed=14 * 2**20, transcendentals=0
        ),
    )(ids, length, q, kv, glob)

    kv, acc = lax.optimization_barrier((kv, acc))

    tile = (2, capacity, 2, BLK, HD)
    take, tiles_all = pl.pallas_call(
        pack_kernel,
        out_shape=[
            jax.ShapeDtypeStruct((dp_count, 2, capacity), jnp.int32),
            jax.ShapeDtypeStruct((dp_count,) + tile, jnp.bfloat16),
        ],
        in_specs=[smem(), vmem()],
        out_specs=[smem(), vmem()],
        scratch_shapes=[pltpu.SMEM((1, 2, capacity), jnp.int32)],
        compiler_params=params,
    )(ids, kv)
    far = [(take, lax.all_to_all(tiles_all, "dp", split_axis=0, concat_axis=0, tiled=True))]

    acc, maxes, sums, updated, squares = pl.pallas_call(
        window_kernel,
        out_shape=[wide] * 3
        + [jax.ShapeDtypeStruct((2, BLK, width), jnp.bfloat16), jax.ShapeDtypeStruct((2, BLK, HD), jnp.float32)],
        in_specs=[smem(), smem()] + [vmem()] * 7,
        out_specs=[vmem()] * 5,
        compiler_params=params,
        cost_estimate=pl.CostEstimate(
            flops=4 * 2 * BLK * width * 2 * BLK, bytes_accessed=9 * 2**20, transcendentals=0
        ),
    )(ids, length, q, up, down, res, acc, maxes, sums)

    for heads_taken, tiles_got in far:
        updated, squares = pl.pallas_call(
            far_kernel,
            out_shape=[
                jax.ShapeDtypeStruct((2, BLK, width), jnp.bfloat16),
                jax.ShapeDtypeStruct((2, BLK, HD), jnp.float32),
            ],
            in_specs=[smem(), smem(), smem()] + [vmem()] * 8,
            out_specs=[vmem()] * 2,
            input_output_aliases={9: 0},
            compiler_params=params,
        )(ids, heads_taken, length, tiles_got, q, res, acc, maxes, sums, updated, squares)

    total = lax.psum(jnp.sum(squares, axis=2), "tensor")
    inverse = lax.rsqrt(total / D + epsilon)
    normed = [
        (updated[c].astype(jnp.float32) * inverse[c][:, None] * gains[c].astype(jnp.float32)).astype(jnp.bfloat16)
        for c in range(2)
    ]
    return jnp.stack([lax.ppermute(normed[c], "pipe", lines[c]) for c in range(2)])[None]


def pair_queries(first, second):
    none = jnp.zeros_like(first)
    return jnp.concatenate(
        [jnp.concatenate([first, none], axis=1), jnp.concatenate([none, second], axis=1)], axis=0
    )


def pair_rows(first, second, lanes):
    return jnp.concatenate([jnp.broadcast_to(first, (BLK, lanes)), jnp.broadcast_to(second, (BLK, lanes))], axis=0)


def pair_context(weights, values):
    both = dot_nn(weights.astype(jnp.bfloat16), values)
    return jnp.concatenate([both[:BLK, :HD], both[BLK:, HD:]], axis=0)


def pair_merge(scores, olds, values):
    tops = [jnp.maximum(old[0], jnp.max(s, axis=1, keepdims=True)) for s, old in zip(scores, olds)]
    weights = [jnp.exp2(s - m) for s, m in zip(scores, tops)]
    alphas = [jnp.exp2(old[0] - m) for old, m in zip(olds, tops)]
    sums = [alpha * old[1] + jnp.sum(p, axis=1, keepdims=True) for alpha, old, p in zip(alphas, olds, weights)]
    contexts = [alpha * old[2] + pair_context(p, v) for alpha, old, p, v in zip(alphas, olds, weights, values)]
    return list(zip(tops, sums, contexts))


LENGTH = 32


def sent_in(turn):
    parity = lax.rem(lax.axis_index("pipe"), 2)
    return parity if turn == 0 else 1 - parity


def copy_heads(out_ref, list_ref, row, source_ref):
    for s in range(out_ref.shape[0]):
        cols = pl.ds(pl.multiple_of(jnp.maximum(list_ref[row, s], 0) * HD, HD), HD)
        out_ref[s, 0] = source_ref[0, :, cols]
        out_ref[s, 1] = source_ref[1, :, cols]


def list_heads(list_ref, row, heads, block, block_of):
    capacity = list_ref.shape[1]
    for s in range(capacity):
        list_ref[row, s] = 0
    slot = jnp.int32(0)
    for h in range(heads):
        match = (block_of(h) == block) & (slot < capacity)

        @pl.when(match)
        def _(slot=slot, h=h):
            list_ref[row, slot] = h

        slot = slot + match.astype(jnp.int32)


def distant_kernel(ids_ref, kv0_ref, kv1_ref, tile0_ref, tile1_ref, list_ref):
    me = lax.axis_index("dp")
    heads = ids_ref.shape[2]

    @pl.when((me == 0) | (me == 3))
    def _():
        for turn, (kv_ref, tile_ref) in enumerate(((kv0_ref, tile0_ref), (kv1_ref, tile1_ref))):
            c = sent_in(turn)
            list_heads(list_ref, 0, heads, me, lambda h, c=c: ids_ref[3 - me, c, h])
            copy_heads(tile_ref, list_ref, 0, kv_ref)


def forward_kernel(turn, ids_ref, up_ids_ref, down_ids_ref, kv_ref, up_ref, down_ref, tile_ref, list_ref):
    me = lax.axis_index("dp")
    heads = ids_ref.shape[2]
    c = sent_in(turn)
    edge = (me == 0) | (me == 3)
    asker = jnp.where(me == 0, 2, 1)
    list_heads(
        list_ref,
        0,
        heads,
        jnp.where(edge, me, 3 - me),
        lambda h: jnp.where(edge, ids_ref[asker, c, h], jnp.where(me == 1, up_ids_ref[h], down_ids_ref[h])),
    )
    pl.when(edge)(lambda: copy_heads(tile_ref, list_ref, 0, kv_ref))
    pl.when(me == 1)(lambda: copy_heads(tile_ref, list_ref, 0, down_ref))
    pl.when(me == 2)(lambda: copy_heads(tile_ref, list_ref, 0, up_ref))


def message_kernel(turn, heads_step, order_ref, ids_ref, len_ref, q_ref, res_ref, kv_ref, gkv_ref, out_ref):
    me = lax.axis_index("dp")
    g = pl.program_id(0)
    c = order_ref[turn]
    glob = gkv_ref.shape[2]
    width = out_ref.shape[1] - HD
    heads = width // HD
    place = lax.broadcasted_iota(jnp.int32, (1, HD), 1)

    @pl.when(g == 0)
    def _():
        note = jnp.where(place == LENGTH, len_ref[c], 0)
        for h in range(heads):
            note = jnp.where(place == h, ids_ref[c, h], note)
        note = jnp.broadcast_to(note.astype(jnp.float32), (BLK, HD)).astype(jnp.bfloat16)
        out_ref[:BLK, width:] = note
        out_ref[BLK:, width:] = jnp.zeros((2 * BLK, HD), jnp.bfloat16)

    state = out_ref[2 * BLK :, width:].astype(jnp.float32)
    own_live = me < len_ref[c]
    numbers = range(0, heads_step, 2)
    scores, values = [], []
    for n in numbers:
        both = slice(n * HD, (n + 2) * HD)
        q = pair_queries(q_ref[0, :, n * HD : (n + 1) * HD], q_ref[0, :, (n + 1) * HD : (n + 2) * HD])
        k = jnp.concatenate([gkv_ref[0, 0, :, both], kv_ref[0, 0, :, both]], axis=0)
        values.append(jnp.concatenate([gkv_ref[1, 0, :, both], kv_ref[1, 0, :, both]], axis=0))
        own = [
            jnp.where(own_live, jnp.where(ids_ref[c, g * heads_step + n + i] == me, 1.0, 0.0), NEG) for i in range(2)
        ]
        s = dot_nt(q, k) * SCALE
        scores.append(jnp.concatenate([s[:, :glob], s[:, glob:] + pair_rows(*own, BLK)], axis=1))
    tops = [jnp.max(s, axis=1, keepdims=True) for s in scores]
    weights = [jnp.exp2(s - m) for s, m in zip(scores, tops)]
    sums = [jnp.sum(p, axis=1, keepdims=True) for p in weights]
    contexts = [(pair_context(p, v) / l).astype(jnp.bfloat16) for p, v, l in zip(weights, values, sums)]
    levels = [m + jnp.log2(l) for m, l in zip(tops, sums)]
    for n, context, level in zip(numbers, contexts, levels):
        high = level.astype(jnp.bfloat16).astype(jnp.float32)
        middle = (level - high).astype(jnp.bfloat16).astype(jnp.float32)
        low = level - high - middle
        for i in range(2):
            rows = slice(i * BLK, (i + 1) * BLK)
            head = g * heads_step + n + i
            at = place - head
            state = jnp.where(at == 0, high[rows], jnp.where(at == 32, middle[rows], jnp.where(at == 64, low[rows], state)))
            col = slice((n + i) * HD, (n + i + 1) * HD)
            out = pl.ds(pl.multiple_of(head * HD, HD), HD)
            out_ref[:BLK, out] = q_ref[0, :, col]
            out_ref[BLK : 2 * BLK, out] = res_ref[0, :, col]
            out_ref[2 * BLK :, out] = context[rows]
    out_ref[2 * BLK :, width:] = state.astype(jnp.bfloat16)


def near_kernel(info_ref, message_ref, up_ref, down_ref, acc_ref, max_ref, sum_ref, out_ref, sq_ref, take_ref):
    me = lax.axis_index("dp")
    width = out_ref.shape[1]
    heads = width // HD
    length = info_ref[LENGTH]
    alive = me < length
    up_live = (me >= 1) & (me - 1 < length)
    down_live = me + 1 < length
    list_heads(take_ref, 0, heads, jnp.where(me < 2, me + 2, me - 2), lambda h: info_ref[h])
    list_heads(take_ref, 1, heads, 3 - me, lambda h: info_ref[h])
    lane = lax.broadcasted_iota(jnp.int32, (1, 2 * BLK), 1)
    state = message_ref[2 * BLK :, width:].astype(jnp.float32)
    state = state + pltpu.roll(state, 96, 1) + pltpu.roll(state, 64, 1)
    squares = jnp.zeros((BLK, HD), jnp.float32)
    for start in range(0, heads, 4):
        numbers = range(start, start + 4, 2)
        scores, values, olds = [], [], []
        for h in numbers:
            both = slice(h * HD, (h + 2) * HD)
            biases = []
            for i in range(2):
                block = info_ref[h + i]
                up_bias = jnp.where(up_live, jnp.where(block == me - 1, 1.0, 0.0), NEG)
                down_bias = jnp.where(down_live, jnp.where(block == me + 1, 1.0, 0.0), NEG)
                biases.append(jnp.where(lane < BLK, up_bias, down_bias))
            q = pair_queries(message_ref[:BLK, h * HD : (h + 1) * HD], message_ref[:BLK, (h + 1) * HD : (h + 2) * HD])
            k = jnp.concatenate([up_ref[0, :, both], down_ref[0, :, both]], axis=0)
            values.append(jnp.concatenate([up_ref[1, :, both], down_ref[1, :, both]], axis=0))
            scores.append(dot_nt(q, k) * SCALE + pair_rows(*biases, 2 * BLK))
            level = jnp.concatenate([state[:, h : h + 1], state[:, h + 1 : h + 2]], axis=0)
            context = [message_ref[2 * BLK :, (h + i) * HD : (h + i + 1) * HD].astype(jnp.float32) for i in range(2)]
            olds.append((level, 1.0, jnp.concatenate(context, axis=0)))
        news = pair_merge(scores, olds, values)
        contexts = [jnp.where(alive, acc / l, 0.0) for _, l, acc in news]
        for h, (m, l, acc), context in zip(numbers, news, contexts):
            for i in range(2):
                rows = slice(i * BLK, (i + 1) * BLK)
                col = slice((h + i) * HD, (h + i + 1) * HD)
                max_ref[:, col] = jnp.broadcast_to(m[rows], (BLK, HD))
                sum_ref[:, col] = jnp.broadcast_to(l[rows], (BLK, HD))
                acc_ref[:, col] = acc[rows]
                updated = (message_ref[BLK : 2 * BLK, col].astype(jnp.float32) + context[rows]).astype(jnp.bfloat16)
                out_ref[:, col] = updated
                wide = updated.astype(jnp.float32)
                squares = squares + wide * wide * jnp.where(jnp.abs(info_ref[h + i] - me) < 2, 1.0, 0.0)
    sq_ref[...] = squares


def tile_kernel(row, last, *refs):
    infos, takes, messages, tiles, accs, maxes, sums, olds, old_sqs = [refs[2 * n : 2 * n + 2] for n in range(9)]
    me = lax.axis_index("dp")
    if last:
        outs = [refs[18].at[1 - sent_in(turn)] for turn in range(2)]
        sqs = [refs[19].at[1 - sent_in(turn)] for turn in range(2)]
        for turn in range(2):
            outs[turn][...] = olds[turn][...]
    else:
        outs, sqs = refs[18:20], refs[20:22]

    def work():
        capacity = tiles[0].shape[0]
        places = [(t, s) for t in range(2) for s in range(0, capacity, 2)]
        scores, values, before, cols = [], [], [], []
        for t, s in places:
            chosen = [takes[t][row, s + i] for i in range(2)]
            col = [pl.ds(pl.multiple_of(h * HD, HD), HD) for h in chosen]
            biases = [jnp.where(infos[t][h] < infos[t][LENGTH], 0.0, NEG) for h in chosen]
            q = pair_queries(messages[t][:BLK, col[0]], messages[t][:BLK, col[1]])
            k = jnp.concatenate([tiles[t][s, 0], tiles[t][s + 1, 0]], axis=1)
            values.append(jnp.concatenate([tiles[t][s, 1], tiles[t][s + 1, 1]], axis=1))
            scores.append(dot_nt(q, k) * SCALE + pair_rows(*biases, BLK))
            old = [jnp.concatenate([ref[t][:, one] for one in col], axis=0) for ref in (maxes, sums, accs)]
            before.append((old[0][:, :1], old[1][:, :1], old[2]))
            cols.append(col)
        residuals = [
            jnp.concatenate([messages[t][BLK : 2 * BLK, one] for one in col], axis=0).astype(jnp.float32)
            for (t, _), col in zip(places, cols)
        ]
        news = pair_merge(scores, before, values)
        updates = [
            (res + jnp.where(me < infos[t][LENGTH], acc / l, 0.0)).astype(jnp.bfloat16)
            for (t, _), res, (_, l, acc) in zip(places, residuals, news)
        ]
        squares = [old_sqs[t][...] for t in range(2)]
        for (t, _), col, updated in zip(places, cols, updates):
            for i in range(2):
                part = updated[i * BLK : (i + 1) * BLK]
                outs[t][:, col[i]] = part
                wide = part.astype(jnp.float32)
                squares[t] = squares[t] + wide * wide
        for t in range(2):
            sqs[t][...] = squares[t]

    if last:
        work()
    else:
        for t in range(2):
            sqs[t][...] = old_sqs[t][...]
        pl.when((me == 0) | (me == 3))(work)


def body_chain(residual, queries, keys_values, global_kv, block_ids, lengths, gain):
    width = residual.shape[-1]
    heads = width // HD
    pipe_count = lax.axis_size("pipe")
    group = head_group(heads)
    steps = heads // group
    lanes = group * HD
    capacity = heads // 4
    q, res, glob, kv, length = queries[0], residual[0], global_kv[0], keys_values[0], lengths[0]
    own_ids = block_ids[0, :, 0]
    glob_count = glob.shape[2]
    params = pltpu.CompilerParams(vmem_limit_bytes=VMEM_LIMIT)
    order = jnp.stack([sent_in(0), sent_in(1)])

    def send(array, turn, moves):
        pairs = []
        for p in range(pipe_count):
            other = p ^ 1 if turn == 1 else ((p + 1) ^ 1) - 1
            if 0 <= other < pipe_count:
                pairs += [
                    ((i * pipe_count + p) if direct else (i * pipe_count + other), j * pipe_count + other)
                    for i, j, direct in moves
                ]
        return lax.ppermute(array, ("dp", "pipe"), pairs)

    message = jax.ShapeDtypeStruct((3 * BLK, width + HD), jnp.bfloat16)

    def local_part(turn, kv):
        return pl.pallas_call(
            functools.partial(message_kernel, turn, group),
            grid_spec=pltpu.PrefetchScalarGridSpec(
                num_scalar_prefetch=3,
                grid=(steps,),
                in_specs=[
                    pl.BlockSpec((1, BLK, lanes), lambda g, order, ids, length: (order[turn], 0, g)),
                    pl.BlockSpec((1, BLK, lanes), lambda g, order, ids, length: (order[turn], 0, g)),
                    pl.BlockSpec((2, 1, BLK, lanes), lambda g, order, ids, length: (0, order[turn], 0, g)),
                    pl.BlockSpec((2, 1, glob_count, lanes), lambda g, order, ids, length: (0, order[turn], 0, g)),
                ],
                out_specs=vmem(),
            ),
            out_shape=message,
            compiler_params=params,
        )(order, own_ids, length, q, res, kv, glob)

    ids = lax.all_to_all(jnp.broadcast_to(own_ids, (4,) + own_ids.shape), "dp", split_axis=0, concat_axis=0, tiled=True)
    messages = [local_part(0, kv)]
    kv, ids, messages[0] = lax.optimization_barrier((kv, ids, messages[0]))
    kvs, ups, downs = [], [], []
    for turn in range(2):
        c = order[turn]
        note = jnp.pad(lax.dynamic_index_in_dim(own_ids, c, 0, keepdims=False), (0, HD - heads)).astype(jnp.bfloat16)
        note = jnp.broadcast_to(note, (2, BLK, HD))
        kvs.append(jnp.concatenate([lax.dynamic_index_in_dim(kv, c, 1, keepdims=False), note], axis=2))
        ups.append(send(kvs[turn], turn, [(i, i + 1, True) for i in range(3)]))
        downs.append(send(kvs[turn], turn, [(i + 1, i, True) for i in range(3)]))
    messages.append(local_part(1, kv))
    ups[0], downs[0], messages[1] = lax.optimization_barrier((ups[0], downs[0], messages[1]))
    same = [(i, i, True) for i in range(4)]
    messages = [send(messages[turn], turn, same) for turn in range(2)]
    tiles = jax.ShapeDtypeStruct((capacity, 2, BLK, HD), jnp.bfloat16)
    distant = pl.pallas_call(
        distant_kernel,
        out_shape=[tiles, tiles],
        in_specs=[smem(), vmem(), vmem()],
        out_specs=[vmem(), vmem()],
        scratch_shapes=[pltpu.SMEM((1, capacity), jnp.int32)],
        compiler_params=params,
    )(ids, *kvs)
    far_3 = [send(distant[turn], turn, [(0, 3, True), (3, 0, True)]) for turn in range(2)]

    far_2 = []
    for turn in range(2):
        array = pl.pallas_call(
            functools.partial(forward_kernel, turn),
            out_shape=tiles,
            in_specs=[smem()] * 3 + [vmem()] * 3,
            out_specs=vmem(),
            scratch_shapes=[pltpu.SMEM((1, capacity), jnp.int32)],
            compiler_params=params,
        )(
            ids,
            ups[turn][0, 0, width:].astype(jnp.int32),
            downs[turn][0, 0, width:].astype(jnp.int32),
            kvs[turn],
            ups[turn],
            downs[turn],
        )
        far_2.append(send(array, turn, [(0, 2, True), (3, 1, True), (2, 3, False), (1, 0, False)]))

    wide = jax.ShapeDtypeStruct((BLK, width), jnp.float32)
    row = jax.ShapeDtypeStruct((BLK, width), jnp.bfloat16)
    square = jax.ShapeDtypeStruct((BLK, HD), jnp.float32)
    near, infos = [], []
    for turn in range(2):
        if turn == 1:
            messages[1], near[0][4] = lax.optimization_barrier((messages[1], near[0][4]))
        infos.append(messages[turn][0, width:].astype(jnp.int32))
        near.append(
            list(pl.pallas_call(
                near_kernel,
                out_shape=[wide, wide, wide, row, square, jax.ShapeDtypeStruct((2, capacity), jnp.int32)],
                in_specs=[smem()] + [vmem()] * 3,
                out_specs=[vmem()] * 5 + [smem()],
                compiler_params=params,
            )(infos[turn], messages[turn], ups[turn], downs[turn]))
        )
    accs, maxes, sums, updates, squares, takes = [list(items) for items in zip(*near)]
    for index, got, last in ((1, far_3, False), (0, far_2, True)):
        pair = [jax.ShapeDtypeStruct((2,) + kind.shape, kind.dtype) for kind in (row, square)]
        results = pl.pallas_call(
            functools.partial(tile_kernel, index, last),
            out_shape=pair if last else [row, row, square, square],
            in_specs=[smem()] * 4 + [vmem()] * 14,
            out_specs=[vmem()] * (2 if last else 4),
            input_output_aliases={} if last else {14: 0, 15: 1},
            compiler_params=params,
        )(*infos, *takes, *messages, *got, *accs, *maxes, *sums, *updates, *squares)
        if not last:
            updates, squares = results[:2], results[2:]

    updated, squares = results
    total = lax.psum(jnp.sum(squares, axis=2), "tensor")
    inverse = lax.rsqrt(total / D + epsilon)
    normed = updated.astype(jnp.float32) * inverse[:, :, None] * gain[0][:, None, :].astype(jnp.float32)
    return normed.astype(jnp.bfloat16)[None]


def body(*arrays):
    heads = arrays[0].shape[-1] // HD
    chain = lax.axis_size("dp") == 4 and lax.axis_size("pipe") % 2 == 0 and heads % 8 == 0 and heads <= 32
    return (body_chain if chain else body_any)(*arrays)


def solution(mesh):
    in_specs = (
        P("pipe", None, "dp", "tensor"),
        P("pipe", None, "dp", "tensor"),
        P("pipe", None, None, "dp", "tensor"),
        P("pipe", None, None, None, "tensor"),
        P("pipe", None, "dp", "tensor"),
        P("pipe", None),
        P("pipe", None, "tensor"),
    )
    out_specs = P("pipe", None, "dp", "tensor")
    return jax.shard_map(body, mesh=mesh, in_specs=in_specs, out_specs=out_specs, check_vma=False)
```

```python
import functools

import jax
import jax.numpy as jnp
from jax import lax
from jax.experimental import pallas as pl
from jax.experimental.pallas import tpu as pltpu
from jax.sharding import PartitionSpec as P

D = 6144
HD = 128
BLK = 64
LOG2E = 1.4426950408889634
SCALE = HD ** (-0.5) * LOG2E
NEG = -1e30
VMEM_LIMIT = 40 * 1024 * 1024
LOCAL_LIMIT = 52 * 1024 * 1024

epsilon = 1e-05


def dot_nt(a, b):
    return lax.dot_general(a, b, (((1,), (1,)), ((), ())), preferred_element_type=jnp.float32)


def dot_nn(a, b):
    return lax.dot_general(a, b, (((1,), (0,)), ((), ())), preferred_element_type=jnp.float32)


def with_ones(v):
    return jnp.concatenate([v, jnp.ones((v.shape[0], HD), v.dtype)], axis=1)


def head_group(heads):
    return max(g for g in range(1, 9) if heads % g == 0)


def head_batch(heads):
    return max(g for g in range(1, 5) if heads % g == 0)


def heads_wanted(table_ref, row, ids_ref, asker, block):
    heads, capacity = ids_ref.shape[2], table_ref.shape[2]
    for c in range(2):
        for s in range(capacity):
            table_ref[row, c, s] = -1
        slot = jnp.int32(0)
        for h in range(heads):
            match = (ids_ref[asker, c, h] == block) & (slot < capacity)

            @pl.when(match)
            def _(slot=slot, h=h, c=c):
                table_ref[row, c, slot] = h

            slot = slot + match.astype(jnp.int32)


def copy_tiles(out_ref, list_ref, row, c, source_ref):
    for s in range(out_ref.shape[0]):
        cols = pl.ds(pl.multiple_of(jnp.maximum(list_ref[row, c, s], 0) * HD, HD), HD)
        out_ref[s, 0] = source_ref[0, :, cols]
        out_ref[s, 1] = source_ref[1, :, cols]


def pack_kernel(ids_ref, kv_ref, take_ref, out_ref, list_ref):
    me = lax.axis_index("dp")

    @pl.loop(0, ids_ref.shape[0])
    def _(other):
        far = jnp.abs(other - me) >= 2
        heads_wanted(take_ref, other, ids_ref, me, jnp.where(far, other, -1))
        heads_wanted(list_ref, 0, ids_ref, other, jnp.where(far, me, -1))
        for c in range(2):
            copy_tiles(out_ref.at[other, c], list_ref, 0, c, kv_ref.at[:, c])


def local_kernel(heads_step, ids_ref, len_ref, q_ref, kv_ref, gkv_ref, acc_ref, max_ref, sum_ref):
    me = lax.axis_index("dp")
    c = pl.program_id(0)
    g = pl.program_id(1)
    glob = gkv_ref.shape[2]
    lane = lax.broadcasted_iota(jnp.int32, (1, glob + BLK), 1)
    batch = head_batch(heads_step)
    for start in range(0, heads_step, batch):
        cols = [slice(n * HD, (n + 1) * HD) for n in range(start, start + batch)]
        scores, values = [], []
        for n, col in zip(range(start, start + batch), cols):
            k = jnp.concatenate([gkv_ref[0, 0, :, col], kv_ref[0, 0, :, col]], axis=0)
            values.append(jnp.concatenate([gkv_ref[1, 0, :, col], kv_ref[1, 0, :, col]], axis=0))
            twice = jnp.where(ids_ref[me, c, g * heads_step + n] == me, 1.0, 0.0)
            bias = jnp.where(lane < glob, 0.0, jnp.where(me < len_ref[c], twice, NEG))
            scores.append(dot_nt(q_ref[0, :, col], k) * SCALE + bias)
        tops = [jnp.max(s, axis=1, keepdims=True) for s in scores]
        weights = [jnp.exp2(s - m).astype(jnp.bfloat16) for s, m in zip(scores, tops)]
        sums = [dot_nn(p, with_ones(v)) for p, v in zip(weights, values)]
        for col, m, pv in zip(cols, tops, sums):
            acc_ref[0, :, col] = pv[:, :HD]
            sum_ref[0, :, col] = pv[:, HD:]
            max_ref[0, :, col] = jnp.broadcast_to(m, (BLK, HD))


def merge(scores, olds, values):
    tops = [jnp.maximum(old[0], jnp.max(s, axis=1, keepdims=True)) for s, old in zip(scores, olds)]
    weights = [jnp.exp2(s - m[:, : s.shape[1]]).astype(jnp.bfloat16) for s, m in zip(scores, tops)]
    alphas = [jnp.exp2(old[0] - m) for old, m in zip(olds, tops)]
    added = [dot_nn(p, with_ones(v)) for p, v in zip(weights, values)]
    return [
        (m, alpha * old[1] + pv[:, HD:], alpha * old[2] + pv[:, :HD])
        for m, alpha, old, pv in zip(tops, alphas, olds, added)
    ]


def window_kernel(ids_ref, len_ref, q_ref, up_ref, down_ref, res_ref, acc_ref, max_ref, sum_ref, new_acc_ref, new_max_ref, new_sum_ref, out_ref, sq_ref):
    me = lax.axis_index("dp")
    heads = q_ref.shape[2] // HD
    batch = head_batch(heads)
    lane = lax.broadcasted_iota(jnp.int32, (1, 2 * BLK), 1)
    for c in range(2):
        length = len_ref[c]
        alive = me < length
        up_live = (me >= 1) & (me - 1 < length)
        down_live = me + 1 < length

        def step(g, squares, c=c, alive=alive, up_live=up_live, down_live=down_live):
            cols = [pl.ds(pl.multiple_of((g * batch + n) * HD, HD), HD) for n in range(batch)]
            blocks = [ids_ref[me, c, g * batch + n] for n in range(batch)]
            scores, values = [], []
            for block, col in zip(blocks, cols):
                up_bias = jnp.where(up_live, jnp.where(block == me - 1, 1.0, 0.0), NEG)
                down_bias = jnp.where(down_live, jnp.where(block == me + 1, 1.0, 0.0), NEG)
                bias = jnp.where(lane < BLK, up_bias, down_bias)
                k = jnp.concatenate([up_ref[0, c, :, col], down_ref[0, c, :, col]], axis=0)
                values.append(jnp.concatenate([up_ref[1, c, :, col], down_ref[1, c, :, col]], axis=0))
                scores.append(dot_nt(q_ref[c, :, col], k) * SCALE + bias)
            olds = [(max_ref[c, :, col], sum_ref[c, :, col], acc_ref[c, :, col]) for col in cols]
            residuals = [res_ref[c, :, col].astype(jnp.float32) for col in cols]
            news = merge(scores, olds, values)
            updates = [
                (res + jnp.where(alive, acc / l, 0.0)).astype(jnp.bfloat16) for res, (_, l, acc) in zip(residuals, news)
            ]
            for block, col, (m, l, acc), updated in zip(blocks, cols, news, updates):
                new_max_ref[c, :, col] = m
                new_sum_ref[c, :, col] = l
                new_acc_ref[c, :, col] = acc
                out_ref[c, :, col] = updated
                wide = updated.astype(jnp.float32)
                squares = squares + wide * wide * jnp.where(jnp.abs(block - me) < 2, 1.0, 0.0)
            return squares

        sq_ref[c] = lax.fori_loop(0, heads // batch, step, jnp.zeros((BLK, HD), jnp.float32))


def far_kernel(ids_ref, take_ref, len_ref, tile_ref, q_ref, res_ref, acc_ref, max_ref, sum_ref, old_ref, old_sq_ref, out_ref, sq_ref):
    del old_ref
    me = lax.axis_index("dp")
    owners, _, capacity = take_ref.shape
    sq_ref[...] = old_sq_ref[...]

    def one_owner(owner):
        places = [(c, s) for c in range(2) for s in range(capacity)]
        taken = [take_ref[owner, c, s] for c, s in places]
        chosen = [jnp.maximum(h, 0) for h in taken]
        cols = [pl.ds(pl.multiple_of(h * HD, HD), HD) for h in chosen]
        live = [(t >= 0) & (ids_ref[me, c, h] < len_ref[c]) for (c, _), t, h in zip(places, taken, chosen)]
        scores = [
            dot_nt(q_ref[c, :, col], tile_ref[owner, c, s, 0]) * SCALE + jnp.where(ok, 0.0, NEG)
            for (c, s), col, ok in zip(places, cols, live)
        ]
        olds = [(max_ref[c, :, col], sum_ref[c, :, col], acc_ref[c, :, col]) for (c, _), col in zip(places, cols)]
        residuals = [res_ref[c, :, col].astype(jnp.float32) for (c, _), col in zip(places, cols)]
        news = merge(scores, olds, [tile_ref[owner, c, s, 1] for c, s in places])
        updates = [
            (res + jnp.where(me < len_ref[c], acc / l, 0.0)).astype(jnp.bfloat16)
            for (c, _), res, (_, l, acc) in zip(places, residuals, news)
        ]
        squares = [jnp.zeros((BLK, HD), jnp.float32)] * 2
        for (c, _), t, updated in zip(places, taken, updates):
            wide = updated.astype(jnp.float32)
            squares[c] = squares[c] + wide * wide * jnp.where(t >= 0, 1.0, 0.0)
        for c in range(2):
            sq_ref[c] += squares[c]
        for (c, _), t, col, updated in zip(places, taken, cols, updates):

            @pl.when(t >= 0)
            def _(c=c, col=col, updated=updated):
                out_ref[c, :, col] = updated

    pl.loop(0, owners)(one_owner)


def smem():
    return pl.BlockSpec(memory_space=pltpu.SMEM)


def vmem():
    return pl.BlockSpec(memory_space=pltpu.VMEM)


def body_any(residual, queries, keys_values, global_kv, block_ids, lengths, gain):
    width = residual.shape[-1]
    heads = width // HD
    dp_count = lax.axis_size("dp")
    pipe_count = lax.axis_size("pipe")
    tensor_count = lax.axis_size("tensor")
    group = head_group(heads)
    steps = heads // group
    lanes = group * HD
    capacity = (heads + dp_count - 1) // dp_count
    q = queries[0]
    res = residual[0]
    glob = global_kv[0]
    length = lengths[0]
    glob_count = glob.shape[2]
    params = pltpu.CompilerParams(vmem_limit_bytes=VMEM_LIMIT)

    ids = block_ids[0, :, 0]
    ids = lax.all_to_all(jnp.broadcast_to(ids, (dp_count,) + ids.shape), "dp", split_axis=0, concat_axis=0, tiled=True)
    kv, ids = lax.optimization_barrier((keys_values[0], ids))
    up = lax.ppermute(kv, "dp", [(i, i + 1) for i in range(dp_count - 1)])
    down = lax.ppermute(kv, "dp", [(i + 1, i) for i in range(dp_count - 1)])

    lines = [[(i + 1, i) for i in range(pipe_count - 1)], [(i, i + 1) for i in range(pipe_count - 1)]]
    gains = [lax.ppermute(gain[0, c], "pipe", [(j, i) for i, j in lines[c]]) for c in range(2)]
    q, gains = lax.optimization_barrier((q, gains))
    wide = jax.ShapeDtypeStruct((2, BLK, width), jnp.float32)
    row_spec = pl.BlockSpec((1, BLK, lanes), lambda c, g: (c, 0, g))
    pair_spec = pl.BlockSpec((2, 1, BLK, lanes), lambda c, g: (0, c, 0, g))
    acc, maxes, sums = pl.pallas_call(
        functools.partial(local_kernel, group),
        grid=(2, steps),
        out_shape=[wide] * 3,
        in_specs=[
            smem(),
            smem(),
            row_spec,
            pair_spec,
            pl.BlockSpec((2, 1, glob_count, lanes), lambda c, g: (0, c, 0, g)),
        ],
        out_specs=[row_spec] * 3,
        compiler_params=params,
        cost_estimate=pl.CostEstimate(
            flops=4 * 2 * BLK * width * (glob_count + BLK), bytes_accessed=14 * 2**20, transcendentals=0
        ),
    )(ids, length, q, kv, glob)

    kv, acc = lax.optimization_barrier((kv, acc))

    tile = (2, capacity, 2, BLK, HD)
    take, tiles_all = pl.pallas_call(
        pack_kernel,
        out_shape=[
            jax.ShapeDtypeStruct((dp_count, 2, capacity), jnp.int32),
            jax.ShapeDtypeStruct((dp_count,) + tile, jnp.bfloat16),
        ],
        in_specs=[smem(), vmem()],
        out_specs=[smem(), vmem()],
        scratch_shapes=[pltpu.SMEM((1, 2, capacity), jnp.int32)],
        compiler_params=params,
    )(ids, kv)
    far = [(take, lax.all_to_all(tiles_all, "dp", split_axis=0, concat_axis=0, tiled=True))]

    acc, maxes, sums, updated, squares = pl.pallas_call(
        window_kernel,
        out_shape=[wide] * 3
        + [jax.ShapeDtypeStruct((2, BLK, width), jnp.bfloat16), jax.ShapeDtypeStruct((2, BLK, HD), jnp.float32)],
        in_specs=[smem(), smem()] + [vmem()] * 7,
        out_specs=[vmem()] * 5,
        compiler_params=params,
        cost_estimate=pl.CostEstimate(
            flops=4 * 2 * BLK * width * 2 * BLK, bytes_accessed=9 * 2**20, transcendentals=0
        ),
    )(ids, length, q, up, down, res, acc, maxes, sums)

    for heads_taken, tiles_got in far:
        updated, squares = pl.pallas_call(
            far_kernel,
            out_shape=[
                jax.ShapeDtypeStruct((2, BLK, width), jnp.bfloat16),
                jax.ShapeDtypeStruct((2, BLK, HD), jnp.float32),
            ],
            in_specs=[smem(), smem(), smem()] + [vmem()] * 8,
            out_specs=[vmem()] * 2,
            input_output_aliases={9: 0},
            compiler_params=params,
        )(ids, heads_taken, length, tiles_got, q, res, acc, maxes, sums, updated, squares)

    total = lax.psum(jnp.sum(squares, axis=2), "tensor")
    inverse = lax.rsqrt(total / D + epsilon)
    normed = [
        (updated[c].astype(jnp.float32) * inverse[c][:, None] * gains[c].astype(jnp.float32)).astype(jnp.bfloat16)
        for c in range(2)
    ]
    return jnp.stack([lax.ppermute(normed[c], "pipe", lines[c]) for c in range(2)])[None]


def pair_queries(first, second):
    none = jnp.zeros_like(first)
    return jnp.concatenate(
        [jnp.concatenate([first, none], axis=1), jnp.concatenate([none, second], axis=1)], axis=0
    )


def pair_rows(first, second, lanes):
    return jnp.concatenate([jnp.broadcast_to(first, (BLK, lanes)), jnp.broadcast_to(second, (BLK, lanes))], axis=0)


def pair_context(weights, values):
    both = dot_nn(weights.astype(jnp.bfloat16), values)
    return jnp.concatenate([both[:BLK, :HD], both[BLK:, HD:]], axis=0)


LENGTH = 32


def sent_in(turn):
    parity = lax.rem(lax.axis_index("pipe"), 2)
    return parity if turn == 0 else 1 - parity


def copy_heads(out_ref, list_ref, row, source_ref):
    for s in range(out_ref.shape[0]):
        cols = pl.ds(pl.multiple_of(jnp.maximum(list_ref[row, s], 0) * HD, HD), HD)
        out_ref[s, 0] = source_ref[0, :, cols]
        out_ref[s, 1] = source_ref[1, :, cols]


def list_heads(list_ref, row, heads, block, block_of):
    capacity = list_ref.shape[1]
    for s in range(capacity):
        list_ref[row, s] = 0
    slot = jnp.int32(0)
    for h in range(heads):
        match = (block_of(h) == block) & (slot < capacity)

        @pl.when(match)
        def _(slot=slot, h=h):
            list_ref[row, slot] = h

        slot = slot + match.astype(jnp.int32)


def distant_kernel(ids_ref, kv0_ref, kv1_ref, tile0_ref, tile1_ref, list_ref):
    me = lax.axis_index("dp")
    heads = ids_ref.shape[2]

    @pl.when((me == 0) | (me == 3))
    def _():
        for turn, (kv_ref, tile_ref) in enumerate(((kv0_ref, tile0_ref), (kv1_ref, tile1_ref))):
            c = sent_in(turn)
            list_heads(list_ref, 0, heads, me, lambda h, c=c: ids_ref[3 - me, c, h])
            copy_heads(tile_ref, list_ref, 0, kv_ref)


def forward_kernel(turn, ids_ref, up_ids_ref, down_ids_ref, kv_ref, up_ref, down_ref, tile_ref, list_ref):
    me = lax.axis_index("dp")
    heads = ids_ref.shape[2]
    c = sent_in(turn)
    edge = (me == 0) | (me == 3)
    asker = jnp.where(me == 0, 2, 1)
    list_heads(
        list_ref,
        0,
        heads,
        jnp.where(edge, me, 3 - me),
        lambda h: jnp.where(edge, ids_ref[asker, c, h], jnp.where(me == 1, up_ids_ref[h], down_ids_ref[h])),
    )
    pl.when(edge)(lambda: copy_heads(tile_ref, list_ref, 0, kv_ref))
    pl.when(me == 1)(lambda: copy_heads(tile_ref, list_ref, 0, down_ref))
    pl.when(me == 2)(lambda: copy_heads(tile_ref, list_ref, 0, up_ref))


def message_kernel(turn, heads_step, order_ref, ids_ref, len_ref, q_ref, res_ref, kv_ref, gkv_ref, out_ref):
    me = lax.axis_index("dp")
    g = pl.program_id(0)
    c = order_ref[turn]
    glob = gkv_ref.shape[2]
    width = out_ref.shape[1] - HD
    heads = width // HD
    place = lax.broadcasted_iota(jnp.int32, (1, HD), 1)

    @pl.when(g == 0)
    def _():
        note = jnp.where(place == LENGTH, len_ref[c], 0)
        for h in range(heads):
            note = jnp.where(place == h, ids_ref[c, h], note)
        note = jnp.broadcast_to(note.astype(jnp.float32), (BLK, HD)).astype(jnp.bfloat16)
        out_ref[:BLK, width:] = note
        out_ref[BLK:, width:] = jnp.zeros((2 * BLK, HD), jnp.bfloat16)

    state = out_ref[2 * BLK :, width:].astype(jnp.float32)
    own_live = me < len_ref[c]
    numbers = range(0, heads_step, 2)
    scores, values = [], []
    for n in numbers:
        both = slice(n * HD, (n + 2) * HD)
        q = pair_queries(q_ref[0, :, n * HD : (n + 1) * HD], q_ref[0, :, (n + 1) * HD : (n + 2) * HD])
        k = jnp.concatenate([gkv_ref[0, 0, :, both], kv_ref[0, 0, :, both]], axis=0)
        values.append(jnp.concatenate([gkv_ref[1, 0, :, both], kv_ref[1, 0, :, both]], axis=0))
        own = [
            jnp.where(own_live, jnp.where(ids_ref[c, g * heads_step + n + i] == me, 1.0, 0.0), NEG) for i in range(2)
        ]
        s = dot_nt(q, k) * SCALE
        scores.append(jnp.concatenate([s[:, :glob], s[:, glob:] + pair_rows(*own, BLK)], axis=1))
    tops = [jnp.max(s, axis=1, keepdims=True) for s in scores]
    weights = [jnp.exp2(s - m) for s, m in zip(scores, tops)]
    sums = [jnp.sum(p, axis=1, keepdims=True) for p in weights]
    contexts = [(pair_context(p, v) / l).astype(jnp.bfloat16) for p, v, l in zip(weights, values, sums)]
    levels = [m + jnp.log2(l) for m, l in zip(tops, sums)]
    for n, context, level in zip(numbers, contexts, levels):
        high = level.astype(jnp.bfloat16).astype(jnp.float32)
        middle = (level - high).astype(jnp.bfloat16).astype(jnp.float32)
        low = level - high - middle
        for i in range(2):
            rows = slice(i * BLK, (i + 1) * BLK)
            head = g * heads_step + n + i
            at = place - head
            state = jnp.where(at == 0, high[rows], jnp.where(at == 32, middle[rows], jnp.where(at == 64, low[rows], state)))
            col = slice((n + i) * HD, (n + i + 1) * HD)
            out = pl.ds(pl.multiple_of(head * HD, HD), HD)
            out_ref[:BLK, out] = q_ref[0, :, col]
            out_ref[BLK : 2 * BLK, out] = res_ref[0, :, col]
            out_ref[2 * BLK :, out] = context[rows]
    out_ref[2 * BLK :, width:] = state.astype(jnp.bfloat16)


def near_kernel(info_ref, message_ref, up_ref, down_ref, acc_ref, max_ref, sum_ref, out_ref, sq_ref, take_ref):
    me = lax.axis_index("dp")
    width = out_ref.shape[1]
    heads = width // HD
    batch = head_batch(heads)
    length = info_ref[LENGTH]
    alive = me < length
    up_live = (me >= 1) & (me - 1 < length)
    down_live = me + 1 < length
    list_heads(take_ref, 0, heads, jnp.where(me < 2, me + 2, me - 2), lambda h: info_ref[h])
    list_heads(take_ref, 1, heads, 3 - me, lambda h: info_ref[h])
    lane = lax.broadcasted_iota(jnp.int32, (1, 2 * BLK), 1)
    state = message_ref[2 * BLK :, width:].astype(jnp.float32)
    state = state + pltpu.roll(state, 96, 1) + pltpu.roll(state, 64, 1)
    squares = jnp.zeros((BLK, HD), jnp.float32)
    for start in range(0, heads, batch):
        numbers = range(start, start + batch)
        cols = [slice(h * HD, (h + 1) * HD) for h in numbers]
        blocks = [info_ref[h] for h in numbers]
        scores, values = [], []
        for block, col in zip(blocks, cols):
            up_bias = jnp.where(up_live, jnp.where(block == me - 1, 1.0, 0.0), NEG)
            down_bias = jnp.where(down_live, jnp.where(block == me + 1, 1.0, 0.0), NEG)
            bias = jnp.where(lane < BLK, up_bias, down_bias)
            k = jnp.concatenate([up_ref[0, :, col], down_ref[0, :, col]], axis=0)
            values.append(jnp.concatenate([up_ref[1, :, col], down_ref[1, :, col]], axis=0))
            scores.append(dot_nt(message_ref[:BLK, col], k) * SCALE + bias)
        olds = [
            (jnp.broadcast_to(state[:, h : h + 1], (BLK, HD)), 1.0, message_ref[2 * BLK :, col].astype(jnp.float32))
            for h, col in zip(numbers, cols)
        ]
        residuals = [message_ref[BLK : 2 * BLK, col].astype(jnp.float32) for col in cols]
        news = merge(scores, olds, values)
        updates = [
            (res + jnp.where(alive, acc / l, 0.0)).astype(jnp.bfloat16) for res, (_, l, acc) in zip(residuals, news)
        ]
        for block, col, (m, l, acc), updated in zip(blocks, cols, news, updates):
            max_ref[:, col] = m
            sum_ref[:, col] = l
            acc_ref[:, col] = acc
            out_ref[:, col] = updated
            wide = updated.astype(jnp.float32)
            squares = squares + wide * wide * jnp.where(jnp.abs(block - me) < 2, 1.0, 0.0)
    sq_ref[...] = squares


def tile_kernel(row, last, *refs):
    infos, takes, messages, tiles, accs, maxes, sums, olds, old_sqs = [refs[2 * n : 2 * n + 2] for n in range(9)]
    me = lax.axis_index("dp")
    if last:
        outs = [refs[18].at[1 - sent_in(turn)] for turn in range(2)]
        sqs = [refs[19].at[1 - sent_in(turn)] for turn in range(2)]
        for turn in range(2):
            outs[turn][...] = olds[turn][...]
    else:
        outs, sqs = refs[18:20], refs[20:22]

    def work():
        places = [(t, s) for t in range(2) for s in range(tiles[0].shape[0])]
        chosen = [takes[t][row, s] for t, s in places]
        cols = [pl.ds(pl.multiple_of(h * HD, HD), HD) for h in chosen]
        live = [infos[t][h] < infos[t][LENGTH] for (t, _), h in zip(places, chosen)]
        scores = [
            dot_nt(messages[t][:BLK, col], tiles[t][s, 0]) * SCALE + jnp.where(ok, 0.0, NEG)
            for (t, s), col, ok in zip(places, cols, live)
        ]
        before = [(maxes[t][:, col], sums[t][:, col], accs[t][:, col]) for (t, _), col in zip(places, cols)]
        residuals = [messages[t][BLK : 2 * BLK, col].astype(jnp.float32) for (t, _), col in zip(places, cols)]
        news = merge(scores, before, [tiles[t][s, 1] for t, s in places])
        updates = [
            (res + jnp.where(me < infos[t][LENGTH], acc / l, 0.0)).astype(jnp.bfloat16)
            for (t, _), res, (_, l, acc) in zip(places, residuals, news)
        ]
        squares = [old_sqs[t][...] for t in range(2)]
        for (t, _), col, updated in zip(places, cols, updates):
            outs[t][:, col] = updated
            wide = updated.astype(jnp.float32)
            squares[t] = squares[t] + wide * wide
        for t in range(2):
            sqs[t][...] = squares[t]

    if last:
        work()
    else:
        for t in range(2):
            sqs[t][...] = old_sqs[t][...]
        pl.when((me == 0) | (me == 3))(work)


def body_chain(residual, queries, keys_values, global_kv, block_ids, lengths, gain):
    width = residual.shape[-1]
    heads = width // HD
    pipe_count = lax.axis_size("pipe")
    group = head_group(heads)
    steps = heads // group
    lanes = group * HD
    capacity = heads // 4
    q, res, glob, kv, length = queries[0], residual[0], global_kv[0], keys_values[0], lengths[0]
    own_ids = block_ids[0, :, 0]
    glob_count = glob.shape[2]
    params = pltpu.CompilerParams(vmem_limit_bytes=VMEM_LIMIT)
    order = jnp.stack([sent_in(0), sent_in(1)])

    def send(array, turn, moves):
        pairs = []
        for p in range(pipe_count):
            other = p ^ 1 if turn == 1 else ((p + 1) ^ 1) - 1
            if 0 <= other < pipe_count:
                pairs += [
                    ((i * pipe_count + p) if direct else (i * pipe_count + other), j * pipe_count + other)
                    for i, j, direct in moves
                ]
        return lax.ppermute(array, ("dp", "pipe"), pairs)

    message = jax.ShapeDtypeStruct((3 * BLK, width + HD), jnp.bfloat16)

    def local_part(turn, kv):
        return pl.pallas_call(
            functools.partial(message_kernel, turn, group),
            grid_spec=pltpu.PrefetchScalarGridSpec(
                num_scalar_prefetch=3,
                grid=(steps,),
                in_specs=[
                    pl.BlockSpec((1, BLK, lanes), lambda g, order, ids, length: (order[turn], 0, g)),
                    pl.BlockSpec((1, BLK, lanes), lambda g, order, ids, length: (order[turn], 0, g)),
                    pl.BlockSpec((2, 1, BLK, lanes), lambda g, order, ids, length: (0, order[turn], 0, g)),
                    pl.BlockSpec((2, 1, glob_count, lanes), lambda g, order, ids, length: (0, order[turn], 0, g)),
                ],
                out_specs=vmem(),
            ),
            out_shape=message,
            compiler_params=pltpu.CompilerParams(vmem_limit_bytes=LOCAL_LIMIT),
        )(order, own_ids, length, q, res, kv, glob)

    ids = lax.all_to_all(jnp.broadcast_to(own_ids, (4,) + own_ids.shape), "dp", split_axis=0, concat_axis=0, tiled=True)
    messages = [local_part(0, kv)]
    kv, ids = lax.optimization_barrier((kv, ids))
    kvs, ups, downs = [], [], []
    for turn in range(2):
        c = order[turn]
        note = jnp.pad(lax.dynamic_index_in_dim(own_ids, c, 0, keepdims=False), (0, HD - heads)).astype(jnp.bfloat16)
        note = jnp.broadcast_to(note, (2, BLK, HD))
        kvs.append(jnp.concatenate([lax.dynamic_index_in_dim(kv, c, 1, keepdims=False), note], axis=2))
        ups.append(send(kvs[turn], turn, [(i, i + 1, True) for i in range(3)]))
        downs.append(send(kvs[turn], turn, [(i + 1, i, True) for i in range(3)]))
    kv, ups[0], downs[0] = lax.optimization_barrier((kv, ups[0], downs[0]))
    messages.append(local_part(1, kv))
    same = [(i, i, True) for i in range(4)]
    messages = [send(messages[turn], turn, same) for turn in range(2)]
    tiles = jax.ShapeDtypeStruct((capacity, 2, BLK, HD), jnp.bfloat16)
    distant = pl.pallas_call(
        distant_kernel,
        out_shape=[tiles, tiles],
        in_specs=[smem(), vmem(), vmem()],
        out_specs=[vmem(), vmem()],
        scratch_shapes=[pltpu.SMEM((1, capacity), jnp.int32)],
        compiler_params=params,
    )(ids, *kvs)
    far_3 = [send(distant[turn], turn, [(0, 3, True), (3, 0, True)]) for turn in range(2)]

    far_2 = []
    for turn in range(2):
        array = pl.pallas_call(
            functools.partial(forward_kernel, turn),
            out_shape=tiles,
            in_specs=[smem()] * 3 + [vmem()] * 3,
            out_specs=vmem(),
            scratch_shapes=[pltpu.SMEM((1, capacity), jnp.int32)],
            compiler_params=params,
        )(
            ids,
            ups[turn][0, 0, width:].astype(jnp.int32),
            downs[turn][0, 0, width:].astype(jnp.int32),
            kvs[turn],
            ups[turn],
            downs[turn],
        )
        far_2.append(send(array, turn, [(0, 2, True), (3, 1, True), (2, 3, False), (1, 0, False)]))

    wide = jax.ShapeDtypeStruct((BLK, width), jnp.float32)
    row = jax.ShapeDtypeStruct((BLK, width), jnp.bfloat16)
    square = jax.ShapeDtypeStruct((BLK, HD), jnp.float32)
    near, infos = [], []
    for turn in range(2):
        if turn == 1:
            messages[1], near[0][4] = lax.optimization_barrier((messages[1], near[0][4]))
        infos.append(messages[turn][0, width:].astype(jnp.int32))
        near.append(
            list(pl.pallas_call(
                near_kernel,
                out_shape=[wide, wide, wide, row, square, jax.ShapeDtypeStruct((2, capacity), jnp.int32)],
                in_specs=[smem()] + [vmem()] * 3,
                out_specs=[vmem()] * 5 + [smem()],
                compiler_params=params,
            )(infos[turn], messages[turn], ups[turn], downs[turn]))
        )
    accs, maxes, sums, updates, squares, takes = [list(items) for items in zip(*near)]
    for index, got, last in ((1, far_3, False), (0, far_2, True)):
        pair = [jax.ShapeDtypeStruct((2,) + kind.shape, kind.dtype) for kind in (row, square)]
        results = pl.pallas_call(
            functools.partial(tile_kernel, index, last),
            out_shape=pair if last else [row, row, square, square],
            in_specs=[smem()] * 4 + [vmem()] * 14,
            out_specs=[vmem()] * (2 if last else 4),
            input_output_aliases={} if last else {14: 0, 15: 1},
            compiler_params=params,
        )(*infos, *takes, *messages, *got, *accs, *maxes, *sums, *updates, *squares)
        if not last:
            updates, squares = results[:2], results[2:]

    updated, squares = results
    total = lax.psum(jnp.sum(squares, axis=2), "tensor")
    inverse = lax.rsqrt(total / D + epsilon)
    normed = updated.astype(jnp.float32) * inverse[:, :, None] * gain[0][:, None, :].astype(jnp.float32)
    return normed.astype(jnp.bfloat16)[None]


def body(*arrays):
    heads = arrays[0].shape[-1] // HD
    chain = lax.axis_size("dp") == 4 and lax.axis_size("pipe") % 2 == 0 and heads % 8 == 0 and heads <= 32
    return (body_chain if chain else body_any)(*arrays)


def solution(mesh):
    in_specs = (
        P("pipe", None, "dp", "tensor"),
        P("pipe", None, "dp", "tensor"),
        P("pipe", None, None, "dp", "tensor"),
        P("pipe", None, None, None, "tensor"),
        P("pipe", None, "dp", "tensor"),
        P("pipe", None),
        P("pipe", None, "tensor"),
    )
    out_specs = P("pipe", None, "dp", "tensor")
    return jax.shard_map(body, mesh=mesh, in_specs=in_specs, out_specs=out_specs, check_vma=False)
```

```python
import functools

import jax
import jax.numpy as jnp
from jax import lax
from jax.experimental import pallas as pl
from jax.experimental.pallas import tpu as pltpu
from jax.sharding import PartitionSpec as P

D = 6144
HD = 128
BLK = 64
LOG2E = 1.4426950408889634
SCALE = HD ** (-0.5) * LOG2E
NEG = -1e30
VMEM_LIMIT = 40 * 1024 * 1024

epsilon = 1e-05


def dot_nt(a, b):
    return lax.dot_general(a, b, (((1,), (1,)), ((), ())), preferred_element_type=jnp.float32)


def dot_nn(a, b):
    return lax.dot_general(a, b, (((1,), (0,)), ((), ())), preferred_element_type=jnp.float32)


def with_ones(v):
    return jnp.concatenate([v, jnp.ones((v.shape[0], HD), v.dtype)], axis=1)


def head_group(heads):
    return max(g for g in range(1, 9) if heads % g == 0)


def head_batch(heads):
    return max(g for g in range(1, 5) if heads % g == 0)


def heads_wanted(table_ref, row, ids_ref, asker, block):
    heads, capacity = ids_ref.shape[2], table_ref.shape[2]
    for c in range(2):
        for s in range(capacity):
            table_ref[row, c, s] = -1
        slot = jnp.int32(0)
        for h in range(heads):
            match = (ids_ref[asker, c, h] == block) & (slot < capacity)

            @pl.when(match)
            def _(slot=slot, h=h, c=c):
                table_ref[row, c, slot] = h

            slot = slot + match.astype(jnp.int32)


def copy_tiles(out_ref, list_ref, row, c, source_ref):
    for s in range(out_ref.shape[0]):
        cols = pl.ds(pl.multiple_of(jnp.maximum(list_ref[row, c, s], 0) * HD, HD), HD)
        out_ref[s, 0] = source_ref[0, :, cols]
        out_ref[s, 1] = source_ref[1, :, cols]


def pack_kernel(ids_ref, kv_ref, take_ref, out_ref, list_ref):
    me = lax.axis_index("dp")

    @pl.loop(0, ids_ref.shape[0])
    def _(other):
        far = jnp.abs(other - me) >= 2
        heads_wanted(take_ref, other, ids_ref, me, jnp.where(far, other, -1))
        heads_wanted(list_ref, 0, ids_ref, other, jnp.where(far, me, -1))
        for c in range(2):
            copy_tiles(out_ref.at[other, c], list_ref, 0, c, kv_ref.at[:, c])


def local_kernel(heads_step, ids_ref, len_ref, q_ref, kv_ref, gkv_ref, acc_ref, max_ref, sum_ref):
    me = lax.axis_index("dp")
    c = pl.program_id(0)
    g = pl.program_id(1)
    glob = gkv_ref.shape[2]
    lane = lax.broadcasted_iota(jnp.int32, (1, glob + BLK), 1)
    batch = head_batch(heads_step)
    for start in range(0, heads_step, batch):
        cols = [slice(n * HD, (n + 1) * HD) for n in range(start, start + batch)]
        scores, values = [], []
        for n, col in zip(range(start, start + batch), cols):
            k = jnp.concatenate([gkv_ref[0, 0, :, col], kv_ref[0, 0, :, col]], axis=0)
            values.append(jnp.concatenate([gkv_ref[1, 0, :, col], kv_ref[1, 0, :, col]], axis=0))
            twice = jnp.where(ids_ref[me, c, g * heads_step + n] == me, 1.0, 0.0)
            bias = jnp.where(lane < glob, 0.0, jnp.where(me < len_ref[c], twice, NEG))
            scores.append(dot_nt(q_ref[0, :, col], k) * SCALE + bias)
        tops = [jnp.max(s, axis=1, keepdims=True) for s in scores]
        weights = [jnp.exp2(s - m).astype(jnp.bfloat16) for s, m in zip(scores, tops)]
        sums = [dot_nn(p, with_ones(v)) for p, v in zip(weights, values)]
        for col, m, pv in zip(cols, tops, sums):
            acc_ref[0, :, col] = pv[:, :HD]
            sum_ref[0, :, col] = pv[:, HD:]
            max_ref[0, :, col] = jnp.broadcast_to(m, (BLK, HD))


def merge(scores, olds, values):
    tops = [jnp.maximum(old[0], jnp.max(s, axis=1, keepdims=True)) for s, old in zip(scores, olds)]
    weights = [jnp.exp2(s - m[:, : s.shape[1]]).astype(jnp.bfloat16) for s, m in zip(scores, tops)]
    alphas = [jnp.exp2(old[0] - m) for old, m in zip(olds, tops)]
    added = [dot_nn(p, with_ones(v)) for p, v in zip(weights, values)]
    return [
        (m, alpha * old[1] + pv[:, HD:], alpha * old[2] + pv[:, :HD])
        for m, alpha, old, pv in zip(tops, alphas, olds, added)
    ]


def window_kernel(ids_ref, len_ref, q_ref, up_ref, down_ref, res_ref, acc_ref, max_ref, sum_ref, new_acc_ref, new_max_ref, new_sum_ref, out_ref, sq_ref):
    me = lax.axis_index("dp")
    heads = q_ref.shape[2] // HD
    batch = head_batch(heads)
    lane = lax.broadcasted_iota(jnp.int32, (1, 2 * BLK), 1)
    for c in range(2):
        length = len_ref[c]
        alive = me < length
        up_live = (me >= 1) & (me - 1 < length)
        down_live = me + 1 < length

        def step(g, squares, c=c, alive=alive, up_live=up_live, down_live=down_live):
            cols = [pl.ds(pl.multiple_of((g * batch + n) * HD, HD), HD) for n in range(batch)]
            blocks = [ids_ref[me, c, g * batch + n] for n in range(batch)]
            scores, values = [], []
            for block, col in zip(blocks, cols):
                up_bias = jnp.where(up_live, jnp.where(block == me - 1, 1.0, 0.0), NEG)
                down_bias = jnp.where(down_live, jnp.where(block == me + 1, 1.0, 0.0), NEG)
                bias = jnp.where(lane < BLK, up_bias, down_bias)
                k = jnp.concatenate([up_ref[0, c, :, col], down_ref[0, c, :, col]], axis=0)
                values.append(jnp.concatenate([up_ref[1, c, :, col], down_ref[1, c, :, col]], axis=0))
                scores.append(dot_nt(q_ref[c, :, col], k) * SCALE + bias)
            olds = [(max_ref[c, :, col], sum_ref[c, :, col], acc_ref[c, :, col]) for col in cols]
            residuals = [res_ref[c, :, col].astype(jnp.float32) for col in cols]
            news = merge(scores, olds, values)
            updates = [
                (res + jnp.where(alive, acc / l, 0.0)).astype(jnp.bfloat16) for res, (_, l, acc) in zip(residuals, news)
            ]
            for block, col, (m, l, acc), updated in zip(blocks, cols, news, updates):
                new_max_ref[c, :, col] = m
                new_sum_ref[c, :, col] = l
                new_acc_ref[c, :, col] = acc
                out_ref[c, :, col] = updated
                wide = updated.astype(jnp.float32)
                squares = squares + wide * wide * jnp.where(jnp.abs(block - me) < 2, 1.0, 0.0)
            return squares

        sq_ref[c] = lax.fori_loop(0, heads // batch, step, jnp.zeros((BLK, HD), jnp.float32))


def far_kernel(ids_ref, take_ref, len_ref, tile_ref, q_ref, res_ref, acc_ref, max_ref, sum_ref, old_ref, old_sq_ref, out_ref, sq_ref):
    del old_ref
    me = lax.axis_index("dp")
    owners, _, capacity = take_ref.shape
    sq_ref[...] = old_sq_ref[...]

    def one_owner(owner):
        places = [(c, s) for c in range(2) for s in range(capacity)]
        taken = [take_ref[owner, c, s] for c, s in places]
        chosen = [jnp.maximum(h, 0) for h in taken]
        cols = [pl.ds(pl.multiple_of(h * HD, HD), HD) for h in chosen]
        live = [(t >= 0) & (ids_ref[me, c, h] < len_ref[c]) for (c, _), t, h in zip(places, taken, chosen)]
        scores = [
            dot_nt(q_ref[c, :, col], tile_ref[owner, c, s, 0]) * SCALE + jnp.where(ok, 0.0, NEG)
            for (c, s), col, ok in zip(places, cols, live)
        ]
        olds = [(max_ref[c, :, col], sum_ref[c, :, col], acc_ref[c, :, col]) for (c, _), col in zip(places, cols)]
        residuals = [res_ref[c, :, col].astype(jnp.float32) for (c, _), col in zip(places, cols)]
        news = merge(scores, olds, [tile_ref[owner, c, s, 1] for c, s in places])
        updates = [
            (res + jnp.where(me < len_ref[c], acc / l, 0.0)).astype(jnp.bfloat16)
            for (c, _), res, (_, l, acc) in zip(places, residuals, news)
        ]
        squares = [jnp.zeros((BLK, HD), jnp.float32)] * 2
        for (c, _), t, updated in zip(places, taken, updates):
            wide = updated.astype(jnp.float32)
            squares[c] = squares[c] + wide * wide * jnp.where(t >= 0, 1.0, 0.0)
        for c in range(2):
            sq_ref[c] += squares[c]
        for (c, _), t, col, updated in zip(places, taken, cols, updates):

            @pl.when(t >= 0)
            def _(c=c, col=col, updated=updated):
                out_ref[c, :, col] = updated

    pl.loop(0, owners)(one_owner)


def smem():
    return pl.BlockSpec(memory_space=pltpu.SMEM)


def vmem():
    return pl.BlockSpec(memory_space=pltpu.VMEM)


def body_any(residual, queries, keys_values, global_kv, block_ids, lengths, gain):
    width = residual.shape[-1]
    heads = width // HD
    dp_count = lax.axis_size("dp")
    pipe_count = lax.axis_size("pipe")
    tensor_count = lax.axis_size("tensor")
    group = head_group(heads)
    steps = heads // group
    lanes = group * HD
    capacity = (heads + dp_count - 1) // dp_count
    q = queries[0]
    res = residual[0]
    glob = global_kv[0]
    length = lengths[0]
    glob_count = glob.shape[2]
    params = pltpu.CompilerParams(vmem_limit_bytes=VMEM_LIMIT)

    ids = block_ids[0, :, 0]
    ids = lax.all_to_all(jnp.broadcast_to(ids, (dp_count,) + ids.shape), "dp", split_axis=0, concat_axis=0, tiled=True)
    kv, ids = lax.optimization_barrier((keys_values[0], ids))
    up = lax.ppermute(kv, "dp", [(i, i + 1) for i in range(dp_count - 1)])
    down = lax.ppermute(kv, "dp", [(i + 1, i) for i in range(dp_count - 1)])

    lines = [[(i + 1, i) for i in range(pipe_count - 1)], [(i, i + 1) for i in range(pipe_count - 1)]]
    gains = [lax.ppermute(gain[0, c], "pipe", [(j, i) for i, j in lines[c]]) for c in range(2)]
    q, gains = lax.optimization_barrier((q, gains))
    wide = jax.ShapeDtypeStruct((2, BLK, width), jnp.float32)
    row_spec = pl.BlockSpec((1, BLK, lanes), lambda c, g: (c, 0, g))
    pair_spec = pl.BlockSpec((2, 1, BLK, lanes), lambda c, g: (0, c, 0, g))
    acc, maxes, sums = pl.pallas_call(
        functools.partial(local_kernel, group),
        grid=(2, steps),
        out_shape=[wide] * 3,
        in_specs=[
            smem(),
            smem(),
            row_spec,
            pair_spec,
            pl.BlockSpec((2, 1, glob_count, lanes), lambda c, g: (0, c, 0, g)),
        ],
        out_specs=[row_spec] * 3,
        compiler_params=params,
        cost_estimate=pl.CostEstimate(
            flops=4 * 2 * BLK * width * (glob_count + BLK), bytes_accessed=14 * 2**20, transcendentals=0
        ),
    )(ids, length, q, kv, glob)

    kv, acc = lax.optimization_barrier((kv, acc))

    tile = (2, capacity, 2, BLK, HD)
    take, tiles_all = pl.pallas_call(
        pack_kernel,
        out_shape=[
            jax.ShapeDtypeStruct((dp_count, 2, capacity), jnp.int32),
            jax.ShapeDtypeStruct((dp_count,) + tile, jnp.bfloat16),
        ],
        in_specs=[smem(), vmem()],
        out_specs=[smem(), vmem()],
        scratch_shapes=[pltpu.SMEM((1, 2, capacity), jnp.int32)],
        compiler_params=params,
    )(ids, kv)
    far = [(take, lax.all_to_all(tiles_all, "dp", split_axis=0, concat_axis=0, tiled=True))]

    acc, maxes, sums, updated, squares = pl.pallas_call(
        window_kernel,
        out_shape=[wide] * 3
        + [jax.ShapeDtypeStruct((2, BLK, width), jnp.bfloat16), jax.ShapeDtypeStruct((2, BLK, HD), jnp.float32)],
        in_specs=[smem(), smem()] + [vmem()] * 7,
        out_specs=[vmem()] * 5,
        compiler_params=params,
        cost_estimate=pl.CostEstimate(
            flops=4 * 2 * BLK * width * 2 * BLK, bytes_accessed=9 * 2**20, transcendentals=0
        ),
    )(ids, length, q, up, down, res, acc, maxes, sums)

    for heads_taken, tiles_got in far:
        updated, squares = pl.pallas_call(
            far_kernel,
            out_shape=[
                jax.ShapeDtypeStruct((2, BLK, width), jnp.bfloat16),
                jax.ShapeDtypeStruct((2, BLK, HD), jnp.float32),
            ],
            in_specs=[smem(), smem(), smem()] + [vmem()] * 8,
            out_specs=[vmem()] * 2,
            input_output_aliases={9: 0},
            compiler_params=params,
        )(ids, heads_taken, length, tiles_got, q, res, acc, maxes, sums, updated, squares)

    total = lax.psum(jnp.sum(squares, axis=2), "tensor")
    inverse = lax.rsqrt(total / D + epsilon)
    normed = [
        (updated[c].astype(jnp.float32) * inverse[c][:, None] * gains[c].astype(jnp.float32)).astype(jnp.bfloat16)
        for c in range(2)
    ]
    return jnp.stack([lax.ppermute(normed[c], "pipe", lines[c]) for c in range(2)])[None]


def pair_queries(first, second):
    none = jnp.zeros_like(first)
    return jnp.concatenate(
        [jnp.concatenate([first, none], axis=1), jnp.concatenate([none, second], axis=1)], axis=0
    )


def pair_rows(first, second, lanes):
    return jnp.concatenate([jnp.broadcast_to(first, (BLK, lanes)), jnp.broadcast_to(second, (BLK, lanes))], axis=0)


def pair_context(weights, values):
    both = dot_nn(weights.astype(jnp.bfloat16), values)
    return jnp.concatenate([both[:BLK, :HD], both[BLK:, HD:]], axis=0)


LENGTH = 32


def sent_in(turn):
    parity = lax.rem(lax.axis_index("pipe"), 2)
    return parity if turn == 0 else 1 - parity


def copy_heads(out_ref, list_ref, row, source_ref):
    for s in range(out_ref.shape[0]):
        cols = pl.ds(pl.multiple_of(jnp.maximum(list_ref[row, s], 0) * HD, HD), HD)
        out_ref[s, 0] = source_ref[0, :, cols]
        out_ref[s, 1] = source_ref[1, :, cols]


def list_heads(list_ref, row, heads, block, block_of):
    capacity = list_ref.shape[1]
    for s in range(capacity):
        list_ref[row, s] = 0
    slot = jnp.int32(0)
    for h in range(heads):
        match = (block_of(h) == block) & (slot < capacity)

        @pl.when(match)
        def _(slot=slot, h=h):
            list_ref[row, slot] = h

        slot = slot + match.astype(jnp.int32)


def distant_kernel(ids_ref, kv0_ref, kv1_ref, tile0_ref, tile1_ref, list_ref):
    me = lax.axis_index("dp")
    heads = ids_ref.shape[1]

    @pl.when((me == 0) | (me == 3))
    def _():
        for turn, (kv_ref, tile_ref) in enumerate(((kv0_ref, tile0_ref), (kv1_ref, tile1_ref))):
            c = sent_in(turn)
            list_heads(list_ref, 0, heads, me, lambda h, c=c: ids_ref[c, h])
            copy_heads(tile_ref, list_ref, 0, kv_ref)


def forward_kernel(turn, ids_ref, up_ids_ref, down_ids_ref, kv_ref, up_ref, down_ref, tile_ref, list_ref):
    me = lax.axis_index("dp")
    heads = ids_ref.shape[1]
    c = sent_in(turn)
    edge = (me == 0) | (me == 3)
    list_heads(
        list_ref,
        0,
        heads,
        jnp.where(edge, me, 3 - me),
        lambda h: jnp.where(edge, ids_ref[c, h], jnp.where(me == 1, up_ids_ref[h], down_ids_ref[h])),
    )
    pl.when(edge)(lambda: copy_heads(tile_ref, list_ref, 0, kv_ref))
    pl.when(me == 1)(lambda: copy_heads(tile_ref, list_ref, 0, down_ref))
    pl.when(me == 2)(lambda: copy_heads(tile_ref, list_ref, 0, up_ref))


def message_kernel(heads_step, order_ref, ids_ref, len_ref, q_ref, res_ref, kv_ref, gkv_ref, *out_refs):
    me = lax.axis_index("dp")
    turn = pl.program_id(0)
    g = pl.program_id(1)
    c = order_ref[turn]
    glob = gkv_ref.shape[2]
    width = out_refs[0].shape[1] - HD
    heads = width // HD
    place = lax.broadcasted_iota(jnp.int32, (1, HD), 1)

    def start_state(out_ref):
        note = jnp.where(place == LENGTH, len_ref[c], 0)
        for h in range(heads):
            note = jnp.where(place == h, ids_ref[c, h], note)
        note = jnp.broadcast_to(note.astype(jnp.float32), (BLK, HD)).astype(jnp.bfloat16)
        out_ref[:BLK, width:] = note
        out_ref[BLK:, width:] = jnp.zeros((2 * BLK, HD), jnp.bfloat16)

    for n, out_ref in enumerate(out_refs):
        pl.when((g == 0) & (turn == n))(functools.partial(start_state, out_ref))

    own_live = me < len_ref[c]
    numbers = range(0, heads_step, 2)
    scores, values = [], []
    for n in numbers:
        both = slice(n * HD, (n + 2) * HD)
        q = pair_queries(q_ref[0, :, n * HD : (n + 1) * HD], q_ref[0, :, (n + 1) * HD : (n + 2) * HD])
        k = jnp.concatenate([gkv_ref[0, 0, :, both], kv_ref[0, 0, :, both]], axis=0)
        values.append(jnp.concatenate([gkv_ref[1, 0, :, both], kv_ref[1, 0, :, both]], axis=0))
        own = [
            jnp.where(own_live, jnp.where(ids_ref[c, g * heads_step + n + i] == me, 1.0, 0.0), NEG) for i in range(2)
        ]
        s = dot_nt(q, k) * SCALE
        scores.append(jnp.concatenate([s[:, :glob], s[:, glob:] + pair_rows(*own, BLK)], axis=1))
    tops = [jnp.max(s, axis=1, keepdims=True) for s in scores]
    weights = [jnp.exp2(s - m) for s, m in zip(scores, tops)]
    sums = [jnp.sum(p, axis=1, keepdims=True) for p in weights]
    contexts = [(pair_context(p, v) / l).astype(jnp.bfloat16) for p, v, l in zip(weights, values, sums)]
    levels = [m + jnp.log2(l) for m, l in zip(tops, sums)]

    def write(out_ref):
        state = out_ref[2 * BLK :, width:].astype(jnp.float32)
        for n, context, level in zip(numbers, contexts, levels):
            high = level.astype(jnp.bfloat16).astype(jnp.float32)
            middle = (level - high).astype(jnp.bfloat16).astype(jnp.float32)
            low = level - high - middle
            for i in range(2):
                rows = slice(i * BLK, (i + 1) * BLK)
                head = g * heads_step + n + i
                at = place - head
                state = jnp.where(
                    at == 0, high[rows], jnp.where(at == 32, middle[rows], jnp.where(at == 64, low[rows], state))
                )
                col = slice((n + i) * HD, (n + i + 1) * HD)
                out = pl.ds(pl.multiple_of(head * HD, HD), HD)
                out_ref[:BLK, out] = q_ref[0, :, col]
                out_ref[BLK : 2 * BLK, out] = res_ref[0, :, col]
                out_ref[2 * BLK :, out] = context[rows]
        out_ref[2 * BLK :, width:] = state.astype(jnp.bfloat16)

    for n, out_ref in enumerate(out_refs):
        pl.when(turn == n)(functools.partial(write, out_ref))


def near_kernel(info_ref, message_ref, up_ref, down_ref, acc_ref, max_ref, sum_ref, out_ref, sq_ref, take_ref):
    me = lax.axis_index("dp")
    width = out_ref.shape[1]
    heads = width // HD
    batch = head_batch(heads)
    length = info_ref[LENGTH]
    alive = me < length
    up_live = (me >= 1) & (me - 1 < length)
    down_live = me + 1 < length
    list_heads(take_ref, 0, heads, jnp.where(me < 2, me + 2, me - 2), lambda h: info_ref[h])
    list_heads(take_ref, 1, heads, 3 - me, lambda h: info_ref[h])
    lane = lax.broadcasted_iota(jnp.int32, (1, 2 * BLK), 1)
    state = message_ref[2 * BLK :, width:].astype(jnp.float32)
    state = state + pltpu.roll(state, 96, 1) + pltpu.roll(state, 64, 1)
    squares = jnp.zeros((BLK, HD), jnp.float32)
    for start in range(0, heads, batch):
        numbers = range(start, start + batch)
        cols = [slice(h * HD, (h + 1) * HD) for h in numbers]
        blocks = [info_ref[h] for h in numbers]
        scores, values = [], []
        for block, col in zip(blocks, cols):
            up_bias = jnp.where(up_live, jnp.where(block == me - 1, 1.0, 0.0), NEG)
            down_bias = jnp.where(down_live, jnp.where(block == me + 1, 1.0, 0.0), NEG)
            bias = jnp.where(lane < BLK, up_bias, down_bias)
            k = jnp.concatenate([up_ref[0, :, col], down_ref[0, :, col]], axis=0)
            values.append(jnp.concatenate([up_ref[1, :, col], down_ref[1, :, col]], axis=0))
            scores.append(dot_nt(message_ref[:BLK, col], k) * SCALE + bias)
        olds = [
            (jnp.broadcast_to(state[:, h : h + 1], (BLK, HD)), 1.0, message_ref[2 * BLK :, col].astype(jnp.float32))
            for h, col in zip(numbers, cols)
        ]
        residuals = [message_ref[BLK : 2 * BLK, col].astype(jnp.float32) for col in cols]
        news = merge(scores, olds, values)
        updates = [
            (res + jnp.where(alive, acc / l, 0.0)).astype(jnp.bfloat16) for res, (_, l, acc) in zip(residuals, news)
        ]
        for block, col, (m, l, acc), updated in zip(blocks, cols, news, updates):
            max_ref[:, col] = m
            sum_ref[:, col] = l
            acc_ref[:, col] = acc
            out_ref[:, col] = updated
            wide = updated.astype(jnp.float32)
            squares = squares + wide * wide * jnp.where(jnp.abs(block - me) < 2, 1.0, 0.0)
    sq_ref[...] = squares


def tile_kernel(row, last, *refs):
    infos, takes, messages, tiles, accs, maxes, sums, olds, old_sqs = [refs[2 * n : 2 * n + 2] for n in range(9)]
    me = lax.axis_index("dp")
    if last:
        outs = [refs[18].at[1 - sent_in(turn)] for turn in range(2)]
        sqs = [refs[19].at[1 - sent_in(turn)] for turn in range(2)]
        for turn in range(2):
            outs[turn][...] = olds[turn][...]
    else:
        outs, sqs = refs[18:20], refs[20:22]

    def work():
        places = [(t, s) for t in range(2) for s in range(tiles[0].shape[0])]
        chosen = [takes[t][row, s] for t, s in places]
        cols = [pl.ds(pl.multiple_of(h * HD, HD), HD) for h in chosen]
        live = [infos[t][h] < infos[t][LENGTH] for (t, _), h in zip(places, chosen)]
        scores = [
            dot_nt(messages[t][:BLK, col], tiles[t][s, 0]) * SCALE + jnp.where(ok, 0.0, NEG)
            for (t, s), col, ok in zip(places, cols, live)
        ]
        before = [(maxes[t][:, col], sums[t][:, col], accs[t][:, col]) for (t, _), col in zip(places, cols)]
        residuals = [messages[t][BLK : 2 * BLK, col].astype(jnp.float32) for (t, _), col in zip(places, cols)]
        news = merge(scores, before, [tiles[t][s, 1] for t, s in places])
        updates = [
            (res + jnp.where(me < infos[t][LENGTH], acc / l, 0.0)).astype(jnp.bfloat16)
            for (t, _), res, (_, l, acc) in zip(places, residuals, news)
        ]
        squares = [old_sqs[t][...] for t in range(2)]
        for (t, _), col, updated in zip(places, cols, updates):
            outs[t][:, col] = updated
            wide = updated.astype(jnp.float32)
            squares[t] = squares[t] + wide * wide
        for t in range(2):
            sqs[t][...] = squares[t]

    if last:
        work()
    else:
        for t in range(2):
            sqs[t][...] = old_sqs[t][...]
        pl.when((me == 0) | (me == 3))(work)


def body_chain(residual, queries, keys_values, global_kv, block_ids, lengths, gain):
    width = residual.shape[-1]
    heads = width // HD
    pipe_count = lax.axis_size("pipe")
    group = head_group(heads)
    steps = heads // group
    lanes = group * HD
    capacity = heads // 4
    q, res, glob, kv, length = queries[0], residual[0], global_kv[0], keys_values[0], lengths[0]
    own_ids = block_ids[0, :, 0]
    glob_count = glob.shape[2]
    params = pltpu.CompilerParams(vmem_limit_bytes=VMEM_LIMIT)
    order = jnp.stack([sent_in(0), sent_in(1)])

    def send(array, turn, moves):
        pairs = []
        for p in range(pipe_count):
            other = p ^ 1 if turn == 1 else ((p + 1) ^ 1) - 1
            if 0 <= other < pipe_count:
                pairs += [
                    ((i * pipe_count + p) if direct else (i * pipe_count + other), j * pipe_count + other)
                    for i, j, direct in moves
                ]
        return lax.ppermute(array, ("dp", "pipe"), pairs)

    ids_3 = lax.ppermute(own_ids, "dp", [(0, 3), (3, 0)])
    ids_2 = lax.ppermute(own_ids, "dp", [(2, 0), (1, 3)])
    kvs, ups, downs = [], [], []
    for turn in range(2):
        c = order[turn]
        note = jnp.pad(lax.dynamic_index_in_dim(own_ids, c, 0, keepdims=False), (0, HD - heads)).astype(jnp.bfloat16)
        note = jnp.broadcast_to(note, (2, BLK, HD))
        kvs.append(jnp.concatenate([lax.dynamic_index_in_dim(kv, c, 1, keepdims=False), note], axis=2))
    kv, ids_3, ids_2, *kvs = lax.optimization_barrier((kv, ids_3, ids_2, *kvs))
    for turn in range(2):
        ups.append(send(kvs[turn], turn, [(i, i + 1, True) for i in range(3)]))
        downs.append(send(kvs[turn], turn, [(i + 1, i, True) for i in range(3)]))

    message = jax.ShapeDtypeStruct((3 * BLK, width + HD), jnp.bfloat16)
    messages = pl.pallas_call(
        functools.partial(message_kernel, group),
        grid_spec=pltpu.PrefetchScalarGridSpec(
            num_scalar_prefetch=3,
            grid=(2, steps),
            in_specs=[
                pl.BlockSpec((1, BLK, lanes), lambda t, g, order, ids, length: (order[t], 0, g)),
                pl.BlockSpec((1, BLK, lanes), lambda t, g, order, ids, length: (order[t], 0, g)),
                pl.BlockSpec((2, 1, BLK, lanes), lambda t, g, order, ids, length: (0, order[t], 0, g)),
                pl.BlockSpec((2, 1, glob_count, lanes), lambda t, g, order, ids, length: (0, order[t], 0, g)),
            ],
            out_specs=[vmem(), vmem()],
        ),
        out_shape=[message, message],
        compiler_params=params,
    )(order, own_ids, length, q, res, kv, glob)

    same = [(i, i, True) for i in range(4)]
    messages = [send(messages[turn], turn, same) for turn in range(2)]
    tiles = jax.ShapeDtypeStruct((capacity, 2, BLK, HD), jnp.bfloat16)
    distant = pl.pallas_call(
        distant_kernel,
        out_shape=[tiles, tiles],
        in_specs=[smem(), vmem(), vmem()],
        out_specs=[vmem(), vmem()],
        scratch_shapes=[pltpu.SMEM((1, capacity), jnp.int32)],
        compiler_params=params,
    )(ids_3, *kvs)
    far_3 = [send(distant[turn], turn, [(0, 3, True), (3, 0, True)]) for turn in range(2)]

    far_2 = []
    for turn in range(2):
        array = pl.pallas_call(
            functools.partial(forward_kernel, turn),
            out_shape=tiles,
            in_specs=[smem()] * 3 + [vmem()] * 3,
            out_specs=vmem(),
            scratch_shapes=[pltpu.SMEM((1, capacity), jnp.int32)],
            compiler_params=params,
        )(
            ids_2,
            ups[turn][0, 0, width:].astype(jnp.int32),
            downs[turn][0, 0, width:].astype(jnp.int32),
            kvs[turn],
            ups[turn],
            downs[turn],
        )
        far_2.append(send(array, turn, [(0, 2, True), (3, 1, True), (2, 3, False), (1, 0, False)]))

    infos = [array[0, width:].astype(jnp.int32) for array in messages]
    wide = jax.ShapeDtypeStruct((BLK, width), jnp.float32)
    row = jax.ShapeDtypeStruct((BLK, width), jnp.bfloat16)
    square = jax.ShapeDtypeStruct((BLK, HD), jnp.float32)
    near = [
        pl.pallas_call(
            near_kernel,
            out_shape=[wide, wide, wide, row, square, jax.ShapeDtypeStruct((2, capacity), jnp.int32)],
            in_specs=[smem()] + [vmem()] * 3,
            out_specs=[vmem()] * 5 + [smem()],
            compiler_params=params,
        )(infos[turn], messages[turn], ups[turn], downs[turn])
        for turn in range(2)
    ]
    accs, maxes, sums, updates, squares, takes = [list(items) for items in zip(*near)]
    for index, got, last in ((1, far_3, False), (0, far_2, True)):
        pair = [jax.ShapeDtypeStruct((2,) + kind.shape, kind.dtype) for kind in (row, square)]
        results = pl.pallas_call(
            functools.partial(tile_kernel, index, last),
            out_shape=pair if last else [row, row, square, square],
            in_specs=[smem()] * 4 + [vmem()] * 14,
            out_specs=[vmem()] * (2 if last else 4),
            input_output_aliases={} if last else {14: 0, 15: 1},
            compiler_params=params,
        )(*infos, *takes, *messages, *got, *accs, *maxes, *sums, *updates, *squares)
        if not last:
            updates, squares = results[:2], results[2:]

    updated, squares = results
    total = lax.psum(jnp.sum(squares, axis=2), "tensor")
    inverse = lax.rsqrt(total / D + epsilon)
    normed = updated.astype(jnp.float32) * inverse[:, :, None] * gain[0][:, None, :].astype(jnp.float32)
    return normed.astype(jnp.bfloat16)[None]


def body(*arrays):
    heads = arrays[0].shape[-1] // HD
    chain = lax.axis_size("dp") == 4 and lax.axis_size("pipe") % 2 == 0 and heads % 8 == 0 and heads <= 32
    return (body_chain if chain else body_any)(*arrays)


def solution(mesh):
    in_specs = (
        P("pipe", None, "dp", "tensor"),
        P("pipe", None, "dp", "tensor"),
        P("pipe", None, None, "dp", "tensor"),
        P("pipe", None, None, None, "tensor"),
        P("pipe", None, "dp", "tensor"),
        P("pipe", None),
        P("pipe", None, "tensor"),
    )
    out_specs = P("pipe", None, "dp", "tensor")
    return jax.shard_map(body, mesh=mesh, in_specs=in_specs, out_specs=out_specs, check_vma=False)
```

```python
import functools

import jax
import jax.numpy as jnp
from jax import lax
from jax.experimental import pallas as pl
from jax.experimental.pallas import tpu as pltpu
from jax.sharding import PartitionSpec as P

D = 6144
HD = 128
BLK = 64
LOG2E = 1.4426950408889634
SCALE = HD ** (-0.5) * LOG2E
NEG = -1e30
VMEM_LIMIT = 40 * 1024 * 1024

epsilon = 1e-05


def dot_nt(a, b):
    return lax.dot_general(a, b, (((1,), (1,)), ((), ())), preferred_element_type=jnp.float32)


def dot_nn(a, b):
    return lax.dot_general(a, b, (((1,), (0,)), ((), ())), preferred_element_type=jnp.float32)


def with_ones(v):
    return jnp.concatenate([v, jnp.ones((v.shape[0], HD), v.dtype)], axis=1)


def head_group(heads):
    return max(g for g in range(1, 9) if heads % g == 0)


def head_batch(heads):
    return max(g for g in range(1, 5) if heads % g == 0)


def heads_wanted(table_ref, row, ids_ref, asker, block):
    heads, capacity = ids_ref.shape[2], table_ref.shape[2]
    for c in range(2):
        for s in range(capacity):
            table_ref[row, c, s] = -1
        slot = jnp.int32(0)
        for h in range(heads):
            match = (ids_ref[asker, c, h] == block) & (slot < capacity)

            @pl.when(match)
            def _(slot=slot, h=h, c=c):
                table_ref[row, c, slot] = h

            slot = slot + match.astype(jnp.int32)


def copy_tiles(out_ref, list_ref, row, c, source_ref):
    for s in range(out_ref.shape[0]):
        cols = pl.ds(pl.multiple_of(jnp.maximum(list_ref[row, c, s], 0) * HD, HD), HD)
        out_ref[s, 0] = source_ref[0, :, cols]
        out_ref[s, 1] = source_ref[1, :, cols]


def pack_kernel(ids_ref, kv_ref, take_ref, out_ref, list_ref):
    me = lax.axis_index("dp")

    @pl.loop(0, ids_ref.shape[0])
    def _(other):
        far = jnp.abs(other - me) >= 2
        heads_wanted(take_ref, other, ids_ref, me, jnp.where(far, other, -1))
        heads_wanted(list_ref, 0, ids_ref, other, jnp.where(far, me, -1))
        for c in range(2):
            copy_tiles(out_ref.at[other, c], list_ref, 0, c, kv_ref.at[:, c])


def local_kernel(heads_step, ids_ref, len_ref, q_ref, kv_ref, gkv_ref, acc_ref, max_ref, sum_ref):
    me = lax.axis_index("dp")
    c = pl.program_id(0)
    g = pl.program_id(1)
    glob = gkv_ref.shape[2]
    lane = lax.broadcasted_iota(jnp.int32, (1, glob + BLK), 1)
    batch = head_batch(heads_step)
    for start in range(0, heads_step, batch):
        cols = [slice(n * HD, (n + 1) * HD) for n in range(start, start + batch)]
        scores, values = [], []
        for n, col in zip(range(start, start + batch), cols):
            k = jnp.concatenate([gkv_ref[0, 0, :, col], kv_ref[0, 0, :, col]], axis=0)
            values.append(jnp.concatenate([gkv_ref[1, 0, :, col], kv_ref[1, 0, :, col]], axis=0))
            twice = jnp.where(ids_ref[me, c, g * heads_step + n] == me, 1.0, 0.0)
            bias = jnp.where(lane < glob, 0.0, jnp.where(me < len_ref[c], twice, NEG))
            scores.append(dot_nt(q_ref[0, :, col], k) * SCALE + bias)
        tops = [jnp.max(s, axis=1, keepdims=True) for s in scores]
        weights = [jnp.exp2(s - m).astype(jnp.bfloat16) for s, m in zip(scores, tops)]
        sums = [dot_nn(p, with_ones(v)) for p, v in zip(weights, values)]
        for col, m, pv in zip(cols, tops, sums):
            acc_ref[0, :, col] = pv[:, :HD]
            sum_ref[0, :, col] = pv[:, HD:]
            max_ref[0, :, col] = jnp.broadcast_to(m, (BLK, HD))


def merge(scores, olds, values):
    tops = [jnp.maximum(old[0], jnp.max(s, axis=1, keepdims=True)) for s, old in zip(scores, olds)]
    weights = [jnp.exp2(s - m[:, : s.shape[1]]).astype(jnp.bfloat16) for s, m in zip(scores, tops)]
    alphas = [jnp.exp2(old[0] - m) for old, m in zip(olds, tops)]
    added = [dot_nn(p, with_ones(v)) for p, v in zip(weights, values)]
    return [
        (m, alpha * old[1] + pv[:, HD:], alpha * old[2] + pv[:, :HD])
        for m, alpha, old, pv in zip(tops, alphas, olds, added)
    ]


def window_kernel(ids_ref, len_ref, q_ref, up_ref, down_ref, res_ref, acc_ref, max_ref, sum_ref, new_acc_ref, new_max_ref, new_sum_ref, out_ref, sq_ref):
    me = lax.axis_index("dp")
    heads = q_ref.shape[2] // HD
    batch = head_batch(heads)
    lane = lax.broadcasted_iota(jnp.int32, (1, 2 * BLK), 1)
    for c in range(2):
        length = len_ref[c]
        alive = me < length
        up_live = (me >= 1) & (me - 1 < length)
        down_live = me + 1 < length

        def step(g, squares, c=c, alive=alive, up_live=up_live, down_live=down_live):
            cols = [pl.ds(pl.multiple_of((g * batch + n) * HD, HD), HD) for n in range(batch)]
            blocks = [ids_ref[me, c, g * batch + n] for n in range(batch)]
            scores, values = [], []
            for block, col in zip(blocks, cols):
                up_bias = jnp.where(up_live, jnp.where(block == me - 1, 1.0, 0.0), NEG)
                down_bias = jnp.where(down_live, jnp.where(block == me + 1, 1.0, 0.0), NEG)
                bias = jnp.where(lane < BLK, up_bias, down_bias)
                k = jnp.concatenate([up_ref[0, c, :, col], down_ref[0, c, :, col]], axis=0)
                values.append(jnp.concatenate([up_ref[1, c, :, col], down_ref[1, c, :, col]], axis=0))
                scores.append(dot_nt(q_ref[c, :, col], k) * SCALE + bias)
            olds = [(max_ref[c, :, col], sum_ref[c, :, col], acc_ref[c, :, col]) for col in cols]
            residuals = [res_ref[c, :, col].astype(jnp.float32) for col in cols]
            news = merge(scores, olds, values)
            updates = [
                (res + jnp.where(alive, acc / l, 0.0)).astype(jnp.bfloat16) for res, (_, l, acc) in zip(residuals, news)
            ]
            for block, col, (m, l, acc), updated in zip(blocks, cols, news, updates):
                new_max_ref[c, :, col] = m
                new_sum_ref[c, :, col] = l
                new_acc_ref[c, :, col] = acc
                out_ref[c, :, col] = updated
                wide = updated.astype(jnp.float32)
                squares = squares + wide * wide * jnp.where(jnp.abs(block - me) < 2, 1.0, 0.0)
            return squares

        sq_ref[c] = lax.fori_loop(0, heads // batch, step, jnp.zeros((BLK, HD), jnp.float32))


def far_kernel(ids_ref, take_ref, len_ref, tile_ref, q_ref, res_ref, acc_ref, max_ref, sum_ref, old_ref, old_sq_ref, out_ref, sq_ref):
    del old_ref
    me = lax.axis_index("dp")
    owners, _, capacity = take_ref.shape
    sq_ref[...] = old_sq_ref[...]

    def one_owner(owner):
        places = [(c, s) for c in range(2) for s in range(capacity)]
        taken = [take_ref[owner, c, s] for c, s in places]
        chosen = [jnp.maximum(h, 0) for h in taken]
        cols = [pl.ds(pl.multiple_of(h * HD, HD), HD) for h in chosen]
        live = [(t >= 0) & (ids_ref[me, c, h] < len_ref[c]) for (c, _), t, h in zip(places, taken, chosen)]
        scores = [
            dot_nt(q_ref[c, :, col], tile_ref[owner, c, s, 0]) * SCALE + jnp.where(ok, 0.0, NEG)
            for (c, s), col, ok in zip(places, cols, live)
        ]
        olds = [(max_ref[c, :, col], sum_ref[c, :, col], acc_ref[c, :, col]) for (c, _), col in zip(places, cols)]
        residuals = [res_ref[c, :, col].astype(jnp.float32) for (c, _), col in zip(places, cols)]
        news = merge(scores, olds, [tile_ref[owner, c, s, 1] for c, s in places])
        updates = [
            (res + jnp.where(me < len_ref[c], acc / l, 0.0)).astype(jnp.bfloat16)
            for (c, _), res, (_, l, acc) in zip(places, residuals, news)
        ]
        squares = [jnp.zeros((BLK, HD), jnp.float32)] * 2
        for (c, _), t, updated in zip(places, taken, updates):
            wide = updated.astype(jnp.float32)
            squares[c] = squares[c] + wide * wide * jnp.where(t >= 0, 1.0, 0.0)
        for c in range(2):
            sq_ref[c] += squares[c]
        for (c, _), t, col, updated in zip(places, taken, cols, updates):

            @pl.when(t >= 0)
            def _(c=c, col=col, updated=updated):
                out_ref[c, :, col] = updated

    pl.loop(0, owners)(one_owner)


def smem():
    return pl.BlockSpec(memory_space=pltpu.SMEM)


def vmem():
    return pl.BlockSpec(memory_space=pltpu.VMEM)


def body_any(residual, queries, keys_values, global_kv, block_ids, lengths, gain):
    width = residual.shape[-1]
    heads = width // HD
    dp_count = lax.axis_size("dp")
    pipe_count = lax.axis_size("pipe")
    tensor_count = lax.axis_size("tensor")
    group = head_group(heads)
    steps = heads // group
    lanes = group * HD
    capacity = (heads + dp_count - 1) // dp_count
    q = queries[0]
    res = residual[0]
    glob = global_kv[0]
    length = lengths[0]
    glob_count = glob.shape[2]
    params = pltpu.CompilerParams(vmem_limit_bytes=VMEM_LIMIT)

    ids = block_ids[0, :, 0]
    ids = lax.all_to_all(jnp.broadcast_to(ids, (dp_count,) + ids.shape), "dp", split_axis=0, concat_axis=0, tiled=True)
    kv, ids = lax.optimization_barrier((keys_values[0], ids))
    up = lax.ppermute(kv, "dp", [(i, i + 1) for i in range(dp_count - 1)])
    down = lax.ppermute(kv, "dp", [(i + 1, i) for i in range(dp_count - 1)])

    lines = [[(i + 1, i) for i in range(pipe_count - 1)], [(i, i + 1) for i in range(pipe_count - 1)]]
    gains = [lax.ppermute(gain[0, c], "pipe", [(j, i) for i, j in lines[c]]) for c in range(2)]
    q, gains = lax.optimization_barrier((q, gains))
    wide = jax.ShapeDtypeStruct((2, BLK, width), jnp.float32)
    row_spec = pl.BlockSpec((1, BLK, lanes), lambda c, g: (c, 0, g))
    pair_spec = pl.BlockSpec((2, 1, BLK, lanes), lambda c, g: (0, c, 0, g))
    acc, maxes, sums = pl.pallas_call(
        functools.partial(local_kernel, group),
        grid=(2, steps),
        out_shape=[wide] * 3,
        in_specs=[
            smem(),
            smem(),
            row_spec,
            pair_spec,
            pl.BlockSpec((2, 1, glob_count, lanes), lambda c, g: (0, c, 0, g)),
        ],
        out_specs=[row_spec] * 3,
        compiler_params=params,
        cost_estimate=pl.CostEstimate(
            flops=4 * 2 * BLK * width * (glob_count + BLK), bytes_accessed=14 * 2**20, transcendentals=0
        ),
    )(ids, length, q, kv, glob)

    kv, acc = lax.optimization_barrier((kv, acc))

    tile = (2, capacity, 2, BLK, HD)
    take, tiles_all = pl.pallas_call(
        pack_kernel,
        out_shape=[
            jax.ShapeDtypeStruct((dp_count, 2, capacity), jnp.int32),
            jax.ShapeDtypeStruct((dp_count,) + tile, jnp.bfloat16),
        ],
        in_specs=[smem(), vmem()],
        out_specs=[smem(), vmem()],
        scratch_shapes=[pltpu.SMEM((1, 2, capacity), jnp.int32)],
        compiler_params=params,
    )(ids, kv)
    far = [(take, lax.all_to_all(tiles_all, "dp", split_axis=0, concat_axis=0, tiled=True))]

    acc, maxes, sums, updated, squares = pl.pallas_call(
        window_kernel,
        out_shape=[wide] * 3
        + [jax.ShapeDtypeStruct((2, BLK, width), jnp.bfloat16), jax.ShapeDtypeStruct((2, BLK, HD), jnp.float32)],
        in_specs=[smem(), smem()] + [vmem()] * 7,
        out_specs=[vmem()] * 5,
        compiler_params=params,
        cost_estimate=pl.CostEstimate(
            flops=4 * 2 * BLK * width * 2 * BLK, bytes_accessed=9 * 2**20, transcendentals=0
        ),
    )(ids, length, q, up, down, res, acc, maxes, sums)

    for heads_taken, tiles_got in far:
        updated, squares = pl.pallas_call(
            far_kernel,
            out_shape=[
                jax.ShapeDtypeStruct((2, BLK, width), jnp.bfloat16),
                jax.ShapeDtypeStruct((2, BLK, HD), jnp.float32),
            ],
            in_specs=[smem(), smem(), smem()] + [vmem()] * 8,
            out_specs=[vmem()] * 2,
            input_output_aliases={9: 0},
            compiler_params=params,
        )(ids, heads_taken, length, tiles_got, q, res, acc, maxes, sums, updated, squares)

    total = lax.psum(jnp.sum(squares, axis=2), "tensor")
    inverse = lax.rsqrt(total / D + epsilon)
    normed = [
        (updated[c].astype(jnp.float32) * inverse[c][:, None] * gains[c].astype(jnp.float32)).astype(jnp.bfloat16)
        for c in range(2)
    ]
    return jnp.stack([lax.ppermute(normed[c], "pipe", lines[c]) for c in range(2)])[None]


def pair_queries(first, second):
    none = jnp.zeros_like(first)
    return jnp.concatenate(
        [jnp.concatenate([first, none], axis=1), jnp.concatenate([none, second], axis=1)], axis=0
    )


def pair_rows(first, second, lanes):
    return jnp.concatenate([jnp.broadcast_to(first, (BLK, lanes)), jnp.broadcast_to(second, (BLK, lanes))], axis=0)


def pair_context(weights, values):
    both = dot_nn(weights.astype(jnp.bfloat16), values)
    return jnp.concatenate([both[:BLK, :HD], both[BLK:, HD:]], axis=0)


LENGTH = 32


def sent_in(turn):
    parity = lax.rem(lax.axis_index("pipe"), 2)
    return parity if turn == 0 else 1 - parity


def copy_heads(out_ref, list_ref, row, source_ref):
    for s in range(out_ref.shape[0]):
        cols = pl.ds(pl.multiple_of(jnp.maximum(list_ref[row, s], 0) * HD, HD), HD)
        out_ref[s, 0] = source_ref[0, :, cols]
        out_ref[s, 1] = source_ref[1, :, cols]


def list_heads(list_ref, row, heads, block, block_of):
    capacity = list_ref.shape[1]
    for s in range(capacity):
        list_ref[row, s] = 0
    slot = jnp.int32(0)
    for h in range(heads):
        match = (block_of(h) == block) & (slot < capacity)

        @pl.when(match)
        def _(slot=slot, h=h):
            list_ref[row, slot] = h

        slot = slot + match.astype(jnp.int32)


def distant_kernel(ids_ref, kv0_ref, kv1_ref, tile0_ref, tile1_ref, list_ref):
    me = lax.axis_index("dp")
    heads = ids_ref.shape[1]

    @pl.when((me == 0) | (me == 3))
    def _():
        for turn, (kv_ref, tile_ref) in enumerate(((kv0_ref, tile0_ref), (kv1_ref, tile1_ref))):
            c = sent_in(turn)
            list_heads(list_ref, 0, heads, me, lambda h, c=c: ids_ref[c, h])
            copy_heads(tile_ref, list_ref, 0, kv_ref)


def forward_kernel(turn, ids_ref, up_ids_ref, down_ids_ref, kv_ref, up_ref, down_ref, tile_ref, list_ref):
    me = lax.axis_index("dp")
    heads = ids_ref.shape[1]
    c = sent_in(turn)
    edge = (me == 0) | (me == 3)
    list_heads(
        list_ref,
        0,
        heads,
        jnp.where(edge, me, 3 - me),
        lambda h: jnp.where(edge, ids_ref[c, h], jnp.where(me == 1, up_ids_ref[h], down_ids_ref[h])),
    )
    pl.when(edge)(lambda: copy_heads(tile_ref, list_ref, 0, kv_ref))
    pl.when(me == 1)(lambda: copy_heads(tile_ref, list_ref, 0, down_ref))
    pl.when(me == 2)(lambda: copy_heads(tile_ref, list_ref, 0, up_ref))


def message_kernel(heads_step, order_ref, ids_ref, len_ref, q_ref, res_ref, kv_ref, gkv_ref, *out_refs):
    me = lax.axis_index("dp")
    turn = pl.program_id(0)
    g = pl.program_id(1)
    c = order_ref[turn]
    glob = gkv_ref.shape[2]
    width = out_refs[0].shape[1] - HD
    heads = width // HD
    place = lax.broadcasted_iota(jnp.int32, (1, HD), 1)

    def start_state(out_ref):
        note = jnp.where(place == LENGTH, len_ref[c], 0)
        for h in range(heads):
            note = jnp.where(place == h, ids_ref[c, h], note)
        note = jnp.broadcast_to(note.astype(jnp.float32), (BLK, HD)).astype(jnp.bfloat16)
        out_ref[:BLK, width:] = note
        out_ref[BLK:, width:] = jnp.zeros((2 * BLK, HD), jnp.bfloat16)

    for n, out_ref in enumerate(out_refs):
        pl.when((g == 0) & (turn == n))(functools.partial(start_state, out_ref))

    own_live = me < len_ref[c]
    numbers = range(0, heads_step, 2)

    def score(n):
        both = slice(n * HD, (n + 2) * HD)
        q = pair_queries(q_ref[0, :, n * HD : (n + 1) * HD], q_ref[0, :, (n + 1) * HD : (n + 2) * HD])
        k = jnp.concatenate([gkv_ref[0, 0, :, both], kv_ref[0, 0, :, both]], axis=0)
        own = [
            jnp.where(own_live, jnp.where(ids_ref[c, g * heads_step + n + i] == me, 1.0, 0.0), NEG) for i in range(2)
        ]
        s = dot_nt(q, k) * SCALE
        return jnp.concatenate([s[:, :glob], s[:, glob:] + pair_rows(*own, BLK)], axis=1)

    def weigh(s):
        m = jnp.max(s, axis=1, keepdims=True)
        p = jnp.exp2(s - m)
        l = jnp.sum(p, axis=1, keepdims=True)
        return p.astype(jnp.bfloat16), l, m + jnp.log2(l)

    def finish(n, p, l):
        both = slice(n * HD, (n + 2) * HD)
        v = jnp.concatenate([gkv_ref[1, 0, :, both], kv_ref[1, 0, :, both]], axis=0)
        return (pair_context(p, v) / l).astype(jnp.bfloat16)

    contexts, levels = [], []
    scored = weighed = None
    for t in range(len(numbers) + 2):
        fresh = score(numbers[t]) if t < len(numbers) else None
        ready = None
        if scored is not None:
            p, l, level = weigh(scored)
            ready = (p, l)
            levels.append(level)
        if weighed is not None:
            contexts.append(finish(numbers[t - 2], *weighed))
        scored, weighed = fresh, ready

    def write(out_ref):
        state = out_ref[2 * BLK :, width:].astype(jnp.float32)
        for n, context, level in zip(numbers, contexts, levels):
            high = level.astype(jnp.bfloat16).astype(jnp.float32)
            middle = (level - high).astype(jnp.bfloat16).astype(jnp.float32)
            low = level - high - middle
            for i in range(2):
                rows = slice(i * BLK, (i + 1) * BLK)
                head = g * heads_step + n + i
                at = place - head
                state = jnp.where(
                    at == 0, high[rows], jnp.where(at == 32, middle[rows], jnp.where(at == 64, low[rows], state))
                )
                col = slice((n + i) * HD, (n + i + 1) * HD)
                out = pl.ds(pl.multiple_of(head * HD, HD), HD)
                out_ref[:BLK, out] = q_ref[0, :, col]
                out_ref[BLK : 2 * BLK, out] = res_ref[0, :, col]
                out_ref[2 * BLK :, out] = context[rows]
        out_ref[2 * BLK :, width:] = state.astype(jnp.bfloat16)

    for n, out_ref in enumerate(out_refs):
        pl.when(turn == n)(functools.partial(write, out_ref))


def near_kernel(info_ref, message_ref, up_ref, down_ref, acc_ref, max_ref, sum_ref, out_ref, sq_ref, take_ref):
    me = lax.axis_index("dp")
    width = out_ref.shape[1]
    heads = width // HD
    batch = head_batch(heads)
    length = info_ref[LENGTH]
    alive = me < length
    up_live = (me >= 1) & (me - 1 < length)
    down_live = me + 1 < length
    list_heads(take_ref, 0, heads, jnp.where(me < 2, me + 2, me - 2), lambda h: info_ref[h])
    list_heads(take_ref, 1, heads, 3 - me, lambda h: info_ref[h])
    lane = lax.broadcasted_iota(jnp.int32, (1, 2 * BLK), 1)
    state = message_ref[2 * BLK :, width:].astype(jnp.float32)
    state = state + pltpu.roll(state, 96, 1) + pltpu.roll(state, 64, 1)
    squares = jnp.zeros((BLK, HD), jnp.float32)

    def score(numbers):
        items = []
        for h in numbers:
            col = slice(h * HD, (h + 1) * HD)
            block = info_ref[h]
            up_bias = jnp.where(up_live, jnp.where(block == me - 1, 1.0, 0.0), NEG)
            down_bias = jnp.where(down_live, jnp.where(block == me + 1, 1.0, 0.0), NEG)
            bias = jnp.where(lane < BLK, up_bias, down_bias)
            k = jnp.concatenate([up_ref[0, :, col], down_ref[0, :, col]], axis=0)
            v = jnp.concatenate([up_ref[1, :, col], down_ref[1, :, col]], axis=0)
            s = dot_nt(message_ref[:BLK, col], k) * SCALE + bias
            level = jnp.broadcast_to(state[:, h : h + 1], (BLK, HD))
            near = jnp.where(jnp.abs(block - me) < 2, 1.0, 0.0)
            items.append((col, s, v, level, message_ref[BLK : 2 * BLK, col], message_ref[2 * BLK :, col], near))
        return items

    def weigh(items):
        outs = []
        for col, s, v, level, res, context, near in items:
            m = jnp.maximum(level, jnp.max(s, axis=1, keepdims=True))
            p = jnp.exp2(s - m).astype(jnp.bfloat16)
            outs.append((col, m, p, v, jnp.exp2(level - m), res, context, near))
        return outs

    def finish(items, squares):
        outs = []
        for col, m, p, v, alpha, res, context, near in items:
            pv = dot_nn(p, with_ones(v))
            l = alpha + pv[:, HD:]
            acc = alpha * context.astype(jnp.float32) + pv[:, :HD]
            updated = (res.astype(jnp.float32) + jnp.where(alive, acc / l, 0.0)).astype(jnp.bfloat16)
            wide = updated.astype(jnp.float32)
            squares = squares + wide * wide * near
            outs.append((col, m, l, acc, updated))
        for col, m, l, acc, updated in outs:
            max_ref[:, col] = m
            sum_ref[:, col] = l
            acc_ref[:, col] = acc
            out_ref[:, col] = updated
        return squares

    batches = [range(start, start + batch) for start in range(0, heads, batch)]
    scored = weighed = None
    for turn in range(len(batches) + 2):
        fresh = score(batches[turn]) if turn < len(batches) else None
        ready = weigh(scored) if scored else None
        if weighed:
            squares = finish(weighed, squares)
        scored, weighed = fresh, ready
    sq_ref[...] = squares


def tile_kernel(row, last, *refs):
    infos, takes, messages, tiles, accs, maxes, sums, olds, old_sqs = [refs[2 * n : 2 * n + 2] for n in range(9)]
    me = lax.axis_index("dp")
    if last:
        outs = [refs[18].at[1 - sent_in(turn)] for turn in range(2)]
        sqs = [refs[19].at[1 - sent_in(turn)] for turn in range(2)]
        for turn in range(2):
            outs[turn][...] = olds[turn][...]
    else:
        outs, sqs = refs[18:20], refs[20:22]

    def work():
        places = [(t, s) for t in range(2) for s in range(tiles[0].shape[0])]
        chosen = [takes[t][row, s] for t, s in places]
        cols = [pl.ds(pl.multiple_of(h * HD, HD), HD) for h in chosen]
        live = [infos[t][h] < infos[t][LENGTH] for (t, _), h in zip(places, chosen)]
        scores = [
            dot_nt(messages[t][:BLK, col], tiles[t][s, 0]) * SCALE + jnp.where(ok, 0.0, NEG)
            for (t, s), col, ok in zip(places, cols, live)
        ]
        before = [(maxes[t][:, col], sums[t][:, col], accs[t][:, col]) for (t, _), col in zip(places, cols)]
        residuals = [messages[t][BLK : 2 * BLK, col].astype(jnp.float32) for (t, _), col in zip(places, cols)]
        news = merge(scores, before, [tiles[t][s, 1] for t, s in places])
        updates = [
            (res + jnp.where(me < infos[t][LENGTH], acc / l, 0.0)).astype(jnp.bfloat16)
            for (t, _), res, (_, l, acc) in zip(places, residuals, news)
        ]
        squares = [old_sqs[t][...] for t in range(2)]
        for (t, _), col, updated in zip(places, cols, updates):
            outs[t][:, col] = updated
            wide = updated.astype(jnp.float32)
            squares[t] = squares[t] + wide * wide
        for t in range(2):
            sqs[t][...] = squares[t]

    if last:
        work()
    else:
        for t in range(2):
            sqs[t][...] = old_sqs[t][...]
        pl.when((me == 0) | (me == 3))(work)


def body_chain(residual, queries, keys_values, global_kv, block_ids, lengths, gain):
    width = residual.shape[-1]
    heads = width // HD
    pipe_count = lax.axis_size("pipe")
    group = head_group(heads)
    steps = heads // group
    lanes = group * HD
    capacity = heads // 4
    q, res, glob, kv, length = queries[0], residual[0], global_kv[0], keys_values[0], lengths[0]
    own_ids = block_ids[0, :, 0]
    glob_count = glob.shape[2]
    params = pltpu.CompilerParams(vmem_limit_bytes=VMEM_LIMIT)
    order = jnp.stack([sent_in(0), sent_in(1)])

    def send(array, turn, moves):
        pairs = []
        for p in range(pipe_count):
            other = p ^ 1 if turn == 1 else ((p + 1) ^ 1) - 1
            if 0 <= other < pipe_count:
                pairs += [
                    ((i * pipe_count + p) if direct else (i * pipe_count + other), j * pipe_count + other)
                    for i, j, direct in moves
                ]
        return lax.ppermute(array, ("dp", "pipe"), pairs)

    ids_3 = lax.ppermute(own_ids, "dp", [(0, 3), (3, 0)])
    ids_2 = lax.ppermute(own_ids, "dp", [(2, 0), (1, 3)])
    kvs, ups, downs = [], [], []
    for turn in range(2):
        c = order[turn]
        note = jnp.pad(lax.dynamic_index_in_dim(own_ids, c, 0, keepdims=False), (0, HD - heads)).astype(jnp.bfloat16)
        note = jnp.broadcast_to(note, (2, BLK, HD))
        kvs.append(jnp.concatenate([lax.dynamic_index_in_dim(kv, c, 1, keepdims=False), note], axis=2))
    kv, ids_3, ids_2, *kvs = lax.optimization_barrier((kv, ids_3, ids_2, *kvs))
    for turn in range(2):
        ups.append(send(kvs[turn], turn, [(i, i + 1, True) for i in range(3)]))
        downs.append(send(kvs[turn], turn, [(i + 1, i, True) for i in range(3)]))

    message = jax.ShapeDtypeStruct((3 * BLK, width + HD), jnp.bfloat16)
    messages = pl.pallas_call(
        functools.partial(message_kernel, group),
        grid_spec=pltpu.PrefetchScalarGridSpec(
            num_scalar_prefetch=3,
            grid=(2, steps),
            in_specs=[
                pl.BlockSpec((1, BLK, lanes), lambda t, g, order, ids, length: (order[t], 0, g)),
                pl.BlockSpec((1, BLK, lanes), lambda t, g, order, ids, length: (order[t], 0, g)),
                pl.BlockSpec((2, 1, BLK, lanes), lambda t, g, order, ids, length: (0, order[t], 0, g)),
                pl.BlockSpec((2, 1, glob_count, lanes), lambda t, g, order, ids, length: (0, order[t], 0, g)),
            ],
            out_specs=[vmem(), vmem()],
        ),
        out_shape=[message, message],
        compiler_params=params,
    )(order, own_ids, length, q, res, kv, glob)

    same = [(i, i, True) for i in range(4)]
    messages = [send(messages[turn], turn, same) for turn in range(2)]
    tiles = jax.ShapeDtypeStruct((capacity, 2, BLK, HD), jnp.bfloat16)
    distant = pl.pallas_call(
        distant_kernel,
        out_shape=[tiles, tiles],
        in_specs=[smem(), vmem(), vmem()],
        out_specs=[vmem(), vmem()],
        scratch_shapes=[pltpu.SMEM((1, capacity), jnp.int32)],
        compiler_params=params,
    )(ids_3, *kvs)
    far_3 = [send(distant[turn], turn, [(0, 3, True), (3, 0, True)]) for turn in range(2)]

    far_2 = []
    for turn in range(2):
        array = pl.pallas_call(
            functools.partial(forward_kernel, turn),
            out_shape=tiles,
            in_specs=[smem()] * 3 + [vmem()] * 3,
            out_specs=vmem(),
            scratch_shapes=[pltpu.SMEM((1, capacity), jnp.int32)],
            compiler_params=params,
        )(
            ids_2,
            ups[turn][0, 0, width:].astype(jnp.int32),
            downs[turn][0, 0, width:].astype(jnp.int32),
            kvs[turn],
            ups[turn],
            downs[turn],
        )
        far_2.append(send(array, turn, [(0, 2, True), (3, 1, True), (2, 3, False), (1, 0, False)]))

    wide = jax.ShapeDtypeStruct((BLK, width), jnp.float32)
    row = jax.ShapeDtypeStruct((BLK, width), jnp.bfloat16)
    square = jax.ShapeDtypeStruct((BLK, HD), jnp.float32)
    near, infos = [None, None], [None, None]
    for turn in (1, 0):
        if turn == 0:
            messages[0], near[1][4] = lax.optimization_barrier((messages[0], near[1][4]))
        infos[turn] = messages[turn][0, width:].astype(jnp.int32)
        near[turn] = list(
            pl.pallas_call(
                near_kernel,
                out_shape=[wide, wide, wide, row, square, jax.ShapeDtypeStruct((2, capacity), jnp.int32)],
                in_specs=[smem()] + [vmem()] * 3,
                out_specs=[vmem()] * 5 + [smem()],
                compiler_params=params,
            )(infos[turn], messages[turn], ups[turn], downs[turn])
        )
    accs, maxes, sums, updates, squares, takes = [list(items) for items in zip(*near)]
    for index, got, last in ((1, far_3, False), (0, far_2, True)):
        pair = [jax.ShapeDtypeStruct((2,) + kind.shape, kind.dtype) for kind in (row, square)]
        results = pl.pallas_call(
            functools.partial(tile_kernel, index, last),
            out_shape=pair if last else [row, row, square, square],
            in_specs=[smem()] * 4 + [vmem()] * 14,
            out_specs=[vmem()] * (2 if last else 4),
            input_output_aliases={} if last else {14: 0, 15: 1},
            compiler_params=params,
        )(*infos, *takes, *messages, *got, *accs, *maxes, *sums, *updates, *squares)
        if not last:
            updates, squares = results[:2], results[2:]

    updated, squares = results
    total = lax.psum(jnp.sum(squares, axis=2), "tensor")
    inverse = lax.rsqrt(total / D + epsilon)
    normed = updated.astype(jnp.float32) * inverse[:, :, None] * gain[0][:, None, :].astype(jnp.float32)
    return normed.astype(jnp.bfloat16)[None]


def body(*arrays):
    heads = arrays[0].shape[-1] // HD
    chain = lax.axis_size("dp") == 4 and lax.axis_size("pipe") % 2 == 0 and heads % 8 == 0 and heads <= 32
    return (body_chain if chain else body_any)(*arrays)


def solution(mesh):
    in_specs = (
        P("pipe", None, "dp", "tensor"),
        P("pipe", None, "dp", "tensor"),
        P("pipe", None, None, "dp", "tensor"),
        P("pipe", None, None, None, "tensor"),
        P("pipe", None, "dp", "tensor"),
        P("pipe", None),
        P("pipe", None, "tensor"),
    )
    out_specs = P("pipe", None, "dp", "tensor")
    return jax.shard_map(body, mesh=mesh, in_specs=in_specs, out_specs=out_specs, check_vma=False)
```

```python
import functools

import jax
import jax.numpy as jnp
from jax import lax
from jax.experimental import pallas as pl
from jax.experimental.pallas import tpu as pltpu
from jax.sharding import PartitionSpec as P

D = 6144
HD = 128
BLK = 64
LOG2E = 1.4426950408889634
SCALE = HD ** (-0.5) * LOG2E
NEG = -1e30
VMEM_LIMIT = 20 * 1024 * 1024

epsilon = 1e-05


def dot_nt(a, b):
    return lax.dot_general(a, b, (((1,), (1,)), ((), ())), preferred_element_type=jnp.float32)


def dot_nn(a, b):
    return lax.dot_general(a, b, (((1,), (0,)), ((), ())), preferred_element_type=jnp.float32)


def with_ones(v):
    return jnp.concatenate([v, jnp.ones((v.shape[0], HD), v.dtype)], axis=1)


def head_group(heads):
    return max(g for g in range(1, 9) if heads % g == 0)


def head_batch(heads):
    return max(g for g in range(1, 5) if heads % g == 0)


def heads_wanted(table_ref, row, ids_ref, asker, block):
    heads, capacity = ids_ref.shape[2], table_ref.shape[2]
    for c in range(2):
        for s in range(capacity):
            table_ref[row, c, s] = -1
        slot = jnp.int32(0)
        for h in range(heads):
            match = (ids_ref[asker, c, h] == block) & (slot < capacity)

            @pl.when(match)
            def _(slot=slot, h=h, c=c):
                table_ref[row, c, slot] = h

            slot = slot + match.astype(jnp.int32)


def copy_tiles(out_ref, list_ref, row, c, source_ref):
    for s in range(out_ref.shape[0]):
        cols = pl.ds(pl.multiple_of(jnp.maximum(list_ref[row, c, s], 0) * HD, HD), HD)
        out_ref[s, 0] = source_ref[0, :, cols]
        out_ref[s, 1] = source_ref[1, :, cols]


def pack_kernel(ids_ref, kv_ref, take_ref, out_ref, list_ref):
    me = lax.axis_index("dp")

    @pl.loop(0, ids_ref.shape[0])
    def _(other):
        far = jnp.abs(other - me) >= 2
        heads_wanted(take_ref, other, ids_ref, me, jnp.where(far, other, -1))
        heads_wanted(list_ref, 0, ids_ref, other, jnp.where(far, me, -1))
        for c in range(2):
            copy_tiles(out_ref.at[other, c], list_ref, 0, c, kv_ref.at[:, c])


def local_kernel(heads_step, ids_ref, len_ref, q_ref, kv_ref, gkv_ref, acc_ref, max_ref, sum_ref):
    me = lax.axis_index("dp")
    c = pl.program_id(0)
    g = pl.program_id(1)
    glob = gkv_ref.shape[2]
    lane = lax.broadcasted_iota(jnp.int32, (1, glob + BLK), 1)
    batch = head_batch(heads_step)
    for start in range(0, heads_step, batch):
        cols = [slice(n * HD, (n + 1) * HD) for n in range(start, start + batch)]
        scores, values = [], []
        for n, col in zip(range(start, start + batch), cols):
            k = jnp.concatenate([gkv_ref[0, 0, :, col], kv_ref[0, 0, :, col]], axis=0)
            values.append(jnp.concatenate([gkv_ref[1, 0, :, col], kv_ref[1, 0, :, col]], axis=0))
            twice = jnp.where(ids_ref[me, c, g * heads_step + n] == me, 1.0, 0.0)
            bias = jnp.where(lane < glob, 0.0, jnp.where(me < len_ref[c], twice, NEG))
            scores.append(dot_nt(q_ref[0, :, col], k) * SCALE + bias)
        tops = [jnp.max(s, axis=1, keepdims=True) for s in scores]
        weights = [jnp.exp2(s - m).astype(jnp.bfloat16) for s, m in zip(scores, tops)]
        sums = [dot_nn(p, with_ones(v)) for p, v in zip(weights, values)]
        for col, m, pv in zip(cols, tops, sums):
            acc_ref[0, :, col] = pv[:, :HD]
            sum_ref[0, :, col] = pv[:, HD:]
            max_ref[0, :, col] = jnp.broadcast_to(m, (BLK, HD))


def merge(scores, olds, values):
    tops = [jnp.maximum(old[0], jnp.max(s, axis=1, keepdims=True)) for s, old in zip(scores, olds)]
    weights = [jnp.exp2(s - m[:, : s.shape[1]]).astype(jnp.bfloat16) for s, m in zip(scores, tops)]
    alphas = [jnp.exp2(old[0] - m) for old, m in zip(olds, tops)]
    added = [dot_nn(p, with_ones(v)) for p, v in zip(weights, values)]
    return [
        (m, alpha * old[1] + pv[:, HD:], alpha * old[2] + pv[:, :HD])
        for m, alpha, old, pv in zip(tops, alphas, olds, added)
    ]


def window_kernel(ids_ref, len_ref, q_ref, up_ref, down_ref, res_ref, acc_ref, max_ref, sum_ref, new_acc_ref, new_max_ref, new_sum_ref, out_ref, sq_ref):
    me = lax.axis_index("dp")
    heads = q_ref.shape[2] // HD
    batch = head_batch(heads)
    lane = lax.broadcasted_iota(jnp.int32, (1, 2 * BLK), 1)
    for c in range(2):
        length = len_ref[c]
        alive = me < length
        up_live = (me >= 1) & (me - 1 < length)
        down_live = me + 1 < length

        def step(g, squares, c=c, alive=alive, up_live=up_live, down_live=down_live):
            cols = [pl.ds(pl.multiple_of((g * batch + n) * HD, HD), HD) for n in range(batch)]
            blocks = [ids_ref[me, c, g * batch + n] for n in range(batch)]
            scores, values = [], []
            for block, col in zip(blocks, cols):
                up_bias = jnp.where(up_live, jnp.where(block == me - 1, 1.0, 0.0), NEG)
                down_bias = jnp.where(down_live, jnp.where(block == me + 1, 1.0, 0.0), NEG)
                bias = jnp.where(lane < BLK, up_bias, down_bias)
                k = jnp.concatenate([up_ref[0, c, :, col], down_ref[0, c, :, col]], axis=0)
                values.append(jnp.concatenate([up_ref[1, c, :, col], down_ref[1, c, :, col]], axis=0))
                scores.append(dot_nt(q_ref[c, :, col], k) * SCALE + bias)
            olds = [(max_ref[c, :, col], sum_ref[c, :, col], acc_ref[c, :, col]) for col in cols]
            residuals = [res_ref[c, :, col].astype(jnp.float32) for col in cols]
            news = merge(scores, olds, values)
            updates = [
                (res + jnp.where(alive, acc / l, 0.0)).astype(jnp.bfloat16) for res, (_, l, acc) in zip(residuals, news)
            ]
            for block, col, (m, l, acc), updated in zip(blocks, cols, news, updates):
                new_max_ref[c, :, col] = m
                new_sum_ref[c, :, col] = l
                new_acc_ref[c, :, col] = acc
                out_ref[c, :, col] = updated
                wide = updated.astype(jnp.float32)
                squares = squares + wide * wide * jnp.where(jnp.abs(block - me) < 2, 1.0, 0.0)
            return squares

        sq_ref[c] = lax.fori_loop(0, heads // batch, step, jnp.zeros((BLK, HD), jnp.float32))


def far_kernel(ids_ref, take_ref, len_ref, tile_ref, q_ref, res_ref, acc_ref, max_ref, sum_ref, old_ref, old_sq_ref, out_ref, sq_ref):
    del old_ref
    me = lax.axis_index("dp")
    owners, _, capacity = take_ref.shape
    sq_ref[...] = old_sq_ref[...]

    def one_owner(owner):
        places = [(c, s) for c in range(2) for s in range(capacity)]
        taken = [take_ref[owner, c, s] for c, s in places]
        chosen = [jnp.maximum(h, 0) for h in taken]
        cols = [pl.ds(pl.multiple_of(h * HD, HD), HD) for h in chosen]
        live = [(t >= 0) & (ids_ref[me, c, h] < len_ref[c]) for (c, _), t, h in zip(places, taken, chosen)]
        scores = [
            dot_nt(q_ref[c, :, col], tile_ref[owner, c, s, 0]) * SCALE + jnp.where(ok, 0.0, NEG)
            for (c, s), col, ok in zip(places, cols, live)
        ]
        olds = [(max_ref[c, :, col], sum_ref[c, :, col], acc_ref[c, :, col]) for (c, _), col in zip(places, cols)]
        residuals = [res_ref[c, :, col].astype(jnp.float32) for (c, _), col in zip(places, cols)]
        news = merge(scores, olds, [tile_ref[owner, c, s, 1] for c, s in places])
        updates = [
            (res + jnp.where(me < len_ref[c], acc / l, 0.0)).astype(jnp.bfloat16)
            for (c, _), res, (_, l, acc) in zip(places, residuals, news)
        ]
        squares = [jnp.zeros((BLK, HD), jnp.float32)] * 2
        for (c, _), t, updated in zip(places, taken, updates):
            wide = updated.astype(jnp.float32)
            squares[c] = squares[c] + wide * wide * jnp.where(t >= 0, 1.0, 0.0)
        for c in range(2):
            sq_ref[c] += squares[c]
        for (c, _), t, col, updated in zip(places, taken, cols, updates):

            @pl.when(t >= 0)
            def _(c=c, col=col, updated=updated):
                out_ref[c, :, col] = updated

    pl.loop(0, owners)(one_owner)


def smem():
    return pl.BlockSpec(memory_space=pltpu.SMEM)


def vmem():
    return pl.BlockSpec(memory_space=pltpu.VMEM)


def body_any(residual, queries, keys_values, global_kv, block_ids, lengths, gain):
    width = residual.shape[-1]
    heads = width // HD
    dp_count = lax.axis_size("dp")
    pipe_count = lax.axis_size("pipe")
    tensor_count = lax.axis_size("tensor")
    group = head_group(heads)
    steps = heads // group
    lanes = group * HD
    capacity = (heads + dp_count - 1) // dp_count
    q = queries[0]
    res = residual[0]
    glob = global_kv[0]
    length = lengths[0]
    glob_count = glob.shape[2]
    params = pltpu.CompilerParams(vmem_limit_bytes=VMEM_LIMIT)

    ids = block_ids[0, :, 0]
    ids = lax.all_to_all(jnp.broadcast_to(ids, (dp_count,) + ids.shape), "dp", split_axis=0, concat_axis=0, tiled=True)
    kv, ids = lax.optimization_barrier((keys_values[0], ids))
    up = lax.ppermute(kv, "dp", [(i, i + 1) for i in range(dp_count - 1)])
    down = lax.ppermute(kv, "dp", [(i + 1, i) for i in range(dp_count - 1)])

    lines = [[(i + 1, i) for i in range(pipe_count - 1)], [(i, i + 1) for i in range(pipe_count - 1)]]
    gains = [lax.ppermute(gain[0, c], "pipe", [(j, i) for i, j in lines[c]]) for c in range(2)]
    q, gains = lax.optimization_barrier((q, gains))
    wide = jax.ShapeDtypeStruct((2, BLK, width), jnp.float32)
    row_spec = pl.BlockSpec((1, BLK, lanes), lambda c, g: (c, 0, g))
    pair_spec = pl.BlockSpec((2, 1, BLK, lanes), lambda c, g: (0, c, 0, g))
    acc, maxes, sums = pl.pallas_call(
        functools.partial(local_kernel, group),
        grid=(2, steps),
        out_shape=[wide] * 3,
        in_specs=[
            smem(),
            smem(),
            row_spec,
            pair_spec,
            pl.BlockSpec((2, 1, glob_count, lanes), lambda c, g: (0, c, 0, g)),
        ],
        out_specs=[row_spec] * 3,
        compiler_params=params,
        cost_estimate=pl.CostEstimate(
            flops=4 * 2 * BLK * width * (glob_count + BLK), bytes_accessed=14 * 2**20, transcendentals=0
        ),
    )(ids, length, q, kv, glob)

    kv, acc = lax.optimization_barrier((kv, acc))

    tile = (2, capacity, 2, BLK, HD)
    take, tiles_all = pl.pallas_call(
        pack_kernel,
        out_shape=[
            jax.ShapeDtypeStruct((dp_count, 2, capacity), jnp.int32),
            jax.ShapeDtypeStruct((dp_count,) + tile, jnp.bfloat16),
        ],
        in_specs=[smem(), vmem()],
        out_specs=[smem(), vmem()],
        scratch_shapes=[pltpu.SMEM((1, 2, capacity), jnp.int32)],
        compiler_params=params,
    )(ids, kv)
    far = [(take, lax.all_to_all(tiles_all, "dp", split_axis=0, concat_axis=0, tiled=True))]

    acc, maxes, sums, updated, squares = pl.pallas_call(
        window_kernel,
        out_shape=[wide] * 3
        + [jax.ShapeDtypeStruct((2, BLK, width), jnp.bfloat16), jax.ShapeDtypeStruct((2, BLK, HD), jnp.float32)],
        in_specs=[smem(), smem()] + [vmem()] * 7,
        out_specs=[vmem()] * 5,
        compiler_params=params,
        cost_estimate=pl.CostEstimate(
            flops=4 * 2 * BLK * width * 2 * BLK, bytes_accessed=9 * 2**20, transcendentals=0
        ),
    )(ids, length, q, up, down, res, acc, maxes, sums)

    for heads_taken, tiles_got in far:
        updated, squares = pl.pallas_call(
            far_kernel,
            out_shape=[
                jax.ShapeDtypeStruct((2, BLK, width), jnp.bfloat16),
                jax.ShapeDtypeStruct((2, BLK, HD), jnp.float32),
            ],
            in_specs=[smem(), smem(), smem()] + [vmem()] * 8,
            out_specs=[vmem()] * 2,
            input_output_aliases={9: 0},
            compiler_params=params,
        )(ids, heads_taken, length, tiles_got, q, res, acc, maxes, sums, updated, squares)

    total = lax.psum(jnp.sum(squares, axis=2), "tensor")
    inverse = lax.rsqrt(total / D + epsilon)
    normed = [
        (updated[c].astype(jnp.float32) * inverse[c][:, None] * gains[c].astype(jnp.float32)).astype(jnp.bfloat16)
        for c in range(2)
    ]
    return jnp.stack([lax.ppermute(normed[c], "pipe", lines[c]) for c in range(2)])[None]


def pair_queries(first, second):
    none = jnp.zeros_like(first)
    return jnp.concatenate(
        [jnp.concatenate([first, none], axis=1), jnp.concatenate([none, second], axis=1)], axis=0
    )


def pair_rows(first, second, lanes):
    return jnp.concatenate([jnp.broadcast_to(first, (BLK, lanes)), jnp.broadcast_to(second, (BLK, lanes))], axis=0)


def pair_context(weights, values):
    both = dot_nn(weights.astype(jnp.bfloat16), values)
    return jnp.concatenate([both[:BLK, :HD], both[BLK:, HD:]], axis=0)


LENGTH = 32


def sent_in(turn):
    parity = lax.rem(lax.axis_index("pipe"), 2)
    return parity if turn == 0 else 1 - parity


def copy_heads(out_ref, list_ref, row, source_ref):
    for s in range(out_ref.shape[0]):
        cols = pl.ds(pl.multiple_of(jnp.maximum(list_ref[row, s], 0) * HD, HD), HD)
        out_ref[s, 0] = source_ref[0, :, cols]
        out_ref[s, 1] = source_ref[1, :, cols]


def list_heads(list_ref, row, heads, block, block_of):
    capacity = list_ref.shape[1]
    for s in range(capacity):
        list_ref[row, s] = 0
    slot = jnp.int32(0)
    for h in range(heads):
        match = (block_of(h) == block) & (slot < capacity)

        @pl.when(match)
        def _(slot=slot, h=h):
            list_ref[row, slot] = h

        slot = slot + match.astype(jnp.int32)


def distant_kernel(ids_ref, kv0_ref, kv1_ref, tile0_ref, tile1_ref, list_ref):
    me = lax.axis_index("dp")
    heads = ids_ref.shape[1]

    @pl.when((me == 0) | (me == 3))
    def _():
        for turn, (kv_ref, tile_ref) in enumerate(((kv0_ref, tile0_ref), (kv1_ref, tile1_ref))):
            c = sent_in(turn)
            list_heads(list_ref, 0, heads, me, lambda h, c=c: ids_ref[c, h])
            copy_heads(tile_ref, list_ref, 0, kv_ref)


def forward_kernel(turn, ids_ref, up_ids_ref, down_ids_ref, kv_ref, up_ref, down_ref, tile_ref, list_ref):
    me = lax.axis_index("dp")
    heads = ids_ref.shape[1]
    c = sent_in(turn)
    edge = (me == 0) | (me == 3)
    list_heads(
        list_ref,
        0,
        heads,
        jnp.where(edge, me, 3 - me),
        lambda h: jnp.where(edge, ids_ref[c, h], jnp.where(me == 1, up_ids_ref[h], down_ids_ref[h])),
    )
    pl.when(edge)(lambda: copy_heads(tile_ref, list_ref, 0, kv_ref))
    pl.when(me == 1)(lambda: copy_heads(tile_ref, list_ref, 0, down_ref))
    pl.when(me == 2)(lambda: copy_heads(tile_ref, list_ref, 0, up_ref))


def message_kernel(heads_step, order_ref, ids_ref, len_ref, q_ref, res_ref, kv_ref, gkv_ref, *out_refs):
    me = lax.axis_index("dp")
    turn = pl.program_id(0)
    g = pl.program_id(1)
    c = order_ref[turn]
    glob = gkv_ref.shape[2]
    width = out_refs[0].shape[1] - HD
    heads = width // HD
    place = lax.broadcasted_iota(jnp.int32, (1, HD), 1)

    def start_state(out_ref):
        note = jnp.where(place == LENGTH, len_ref[c], 0)
        for h in range(heads):
            note = jnp.where(place == h, ids_ref[c, h], note)
        note = jnp.broadcast_to(note.astype(jnp.float32), (BLK, HD)).astype(jnp.bfloat16)
        out_ref[:BLK, width:] = note
        out_ref[BLK:, width:] = jnp.zeros((2 * BLK, HD), jnp.bfloat16)

    for n, out_ref in enumerate(out_refs):
        pl.when((g == 0) & (turn == n))(functools.partial(start_state, out_ref))

    own_live = me < len_ref[c]
    numbers = range(0, heads_step, 2)

    def score(n):
        both = slice(n * HD, (n + 2) * HD)
        q = pair_queries(q_ref[0, :, n * HD : (n + 1) * HD], q_ref[0, :, (n + 1) * HD : (n + 2) * HD])
        k = jnp.concatenate([gkv_ref[0, 0, :, both], kv_ref[0, 0, :, both]], axis=0)
        own = [
            jnp.where(own_live, jnp.where(ids_ref[c, g * heads_step + n + i] == me, 1.0, 0.0), NEG) for i in range(2)
        ]
        s = dot_nt(q, k) * SCALE
        return jnp.concatenate([s[:, :glob], s[:, glob:] + pair_rows(*own, BLK)], axis=1)

    def weigh(s):
        m = jnp.max(s, axis=1, keepdims=True)
        p = jnp.exp2(s - m)
        l = jnp.sum(p, axis=1, keepdims=True)
        return p.astype(jnp.bfloat16), l, m + jnp.log2(l)

    def finish(n, p, l):
        both = slice(n * HD, (n + 2) * HD)
        v = jnp.concatenate([gkv_ref[1, 0, :, both], kv_ref[1, 0, :, both]], axis=0)
        return (pair_context(p, v) / l).astype(jnp.bfloat16)

    contexts, levels = [], []
    scored = weighed = None
    for t in range(len(numbers) + 2):
        fresh = score(numbers[t]) if t < len(numbers) else None
        ready = None
        if scored is not None:
            p, l, level = weigh(scored)
            ready = (p, l)
            levels.append(level)
        if weighed is not None:
            contexts.append(finish(numbers[t - 2], *weighed))
        scored, weighed = fresh, ready

    def write(out_ref):
        state = out_ref[2 * BLK :, width:].astype(jnp.float32)
        for n, context, level in zip(numbers, contexts, levels):
            high = level.astype(jnp.bfloat16).astype(jnp.float32)
            middle = (level - high).astype(jnp.bfloat16).astype(jnp.float32)
            low = level - high - middle
            for i in range(2):
                rows = slice(i * BLK, (i + 1) * BLK)
                head = g * heads_step + n + i
                at = place - head
                state = jnp.where(
                    at == 0, high[rows], jnp.where(at == 32, middle[rows], jnp.where(at == 64, low[rows], state))
                )
                col = slice((n + i) * HD, (n + i + 1) * HD)
                out = pl.ds(pl.multiple_of(head * HD, HD), HD)
                out_ref[:BLK, out] = q_ref[0, :, col]
                out_ref[BLK : 2 * BLK, out] = res_ref[0, :, col]
                out_ref[2 * BLK :, out] = context[rows]
        out_ref[2 * BLK :, width:] = state.astype(jnp.bfloat16)

    for n, out_ref in enumerate(out_refs):
        pl.when(turn == n)(functools.partial(write, out_ref))


def near_kernel(info_ref, message_ref, up_ref, down_ref, acc_ref, max_ref, sum_ref, out_ref, sq_ref, take_ref):
    me = lax.axis_index("dp")
    width = out_ref.shape[1]
    heads = width // HD
    batch = head_batch(heads)
    length = info_ref[LENGTH]
    alive = me < length
    up_live = (me >= 1) & (me - 1 < length)
    down_live = me + 1 < length
    list_heads(take_ref, 0, heads, jnp.where(me < 2, me + 2, me - 2), lambda h: info_ref[h])
    list_heads(take_ref, 1, heads, 3 - me, lambda h: info_ref[h])
    lane = lax.broadcasted_iota(jnp.int32, (1, 2 * BLK), 1)
    state = message_ref[2 * BLK :, width:].astype(jnp.float32)
    state = state + pltpu.roll(state, 96, 1) + pltpu.roll(state, 64, 1)
    squares = jnp.zeros((BLK, HD), jnp.float32)

    def score(numbers):
        items = []
        for h in numbers:
            col = slice(h * HD, (h + 1) * HD)
            block = info_ref[h]
            up_bias = jnp.where(up_live, jnp.where(block == me - 1, 1.0, 0.0), NEG)
            down_bias = jnp.where(down_live, jnp.where(block == me + 1, 1.0, 0.0), NEG)
            bias = jnp.where(lane < BLK, up_bias, down_bias)
            k = jnp.concatenate([up_ref[0, :, col], down_ref[0, :, col]], axis=0)
            v = jnp.concatenate([up_ref[1, :, col], down_ref[1, :, col]], axis=0)
            s = dot_nt(message_ref[:BLK, col], k) * SCALE + bias
            level = jnp.broadcast_to(state[:, h : h + 1], (BLK, HD))
            near = jnp.where(jnp.abs(block - me) < 2, 1.0, 0.0)
            items.append((col, s, v, level, message_ref[BLK : 2 * BLK, col], message_ref[2 * BLK :, col], near))
        return items

    def weigh(items):
        outs = []
        for col, s, v, level, res, context, near in items:
            m = jnp.maximum(level, jnp.max(s, axis=1, keepdims=True))
            p = jnp.exp2(s - m).astype(jnp.bfloat16)
            outs.append((col, m, p, v, jnp.exp2(level - m), res, context, near))
        return outs

    def finish(items, squares):
        outs = []
        for col, m, p, v, alpha, res, context, near in items:
            pv = dot_nn(p, with_ones(v))
            l = alpha + pv[:, HD:]
            acc = alpha * context.astype(jnp.float32) + pv[:, :HD]
            updated = (res.astype(jnp.float32) + jnp.where(alive, acc / l, 0.0)).astype(jnp.bfloat16)
            wide = updated.astype(jnp.float32)
            squares = squares + wide * wide * near
            outs.append((col, m, l, acc, updated))
        for col, m, l, acc, updated in outs:
            max_ref[:, col] = m
            sum_ref[:, col] = l
            acc_ref[:, col] = acc
            out_ref[:, col] = updated
        return squares

    batches = [range(start, start + batch) for start in range(0, heads, batch)]
    scored = weighed = None
    for turn in range(len(batches) + 2):
        fresh = score(batches[turn]) if turn < len(batches) else None
        ready = weigh(scored) if scored else None
        if weighed:
            squares = finish(weighed, squares)
        scored, weighed = fresh, ready
    sq_ref[...] = squares


def tile_kernel(row, last, *refs):
    infos, takes, messages, tiles, accs, maxes, sums, olds, old_sqs = [refs[2 * n : 2 * n + 2] for n in range(9)]
    me = lax.axis_index("dp")
    if last:
        outs = [refs[18].at[1 - sent_in(turn)] for turn in range(2)]
        sqs = [refs[19].at[1 - sent_in(turn)] for turn in range(2)]
        for turn in range(2):
            outs[turn][...] = olds[turn][...]
    else:
        outs, sqs = refs[18:20], refs[20:22]

    def work():
        places = [(t, s) for t in range(2) for s in range(tiles[0].shape[0])]
        chosen = [takes[t][row, s] for t, s in places]
        cols = [pl.ds(pl.multiple_of(h * HD, HD), HD) for h in chosen]
        live = [infos[t][h] < infos[t][LENGTH] for (t, _), h in zip(places, chosen)]
        scores = [
            dot_nt(messages[t][:BLK, col], tiles[t][s, 0]) * SCALE + jnp.where(ok, 0.0, NEG)
            for (t, s), col, ok in zip(places, cols, live)
        ]
        before = [(maxes[t][:, col], sums[t][:, col], accs[t][:, col]) for (t, _), col in zip(places, cols)]
        residuals = [messages[t][BLK : 2 * BLK, col].astype(jnp.float32) for (t, _), col in zip(places, cols)]
        news = merge(scores, before, [tiles[t][s, 1] for t, s in places])
        updates = [
            (res + jnp.where(me < infos[t][LENGTH], acc / l, 0.0)).astype(jnp.bfloat16)
            for (t, _), res, (_, l, acc) in zip(places, residuals, news)
        ]
        squares = [old_sqs[t][...] for t in range(2)]
        for (t, _), col, updated in zip(places, cols, updates):
            outs[t][:, col] = updated
            wide = updated.astype(jnp.float32)
            squares[t] = squares[t] + wide * wide
        for t in range(2):
            sqs[t][...] = squares[t]

    if last:
        work()
    else:
        for t in range(2):
            sqs[t][...] = old_sqs[t][...]
        pl.when((me == 0) | (me == 3))(work)


def body_chain(residual, queries, keys_values, global_kv, block_ids, lengths, gain):
    width = residual.shape[-1]
    heads = width // HD
    pipe_count = lax.axis_size("pipe")
    group = head_group(heads)
    steps = heads // group
    lanes = group * HD
    capacity = heads // 4
    q, res, glob, kv, length = queries[0], residual[0], global_kv[0], keys_values[0], lengths[0]
    own_ids = block_ids[0, :, 0]
    glob_count = glob.shape[2]
    params = pltpu.CompilerParams(vmem_limit_bytes=VMEM_LIMIT)
    order = jnp.stack([sent_in(0), sent_in(1)])

    def send(array, turn, moves):
        pairs = []
        for p in range(pipe_count):
            other = p ^ 1 if turn == 1 else ((p + 1) ^ 1) - 1
            if 0 <= other < pipe_count:
                pairs += [
                    ((i * pipe_count + p) if direct else (i * pipe_count + other), j * pipe_count + other)
                    for i, j, direct in moves
                ]
        return lax.ppermute(array, ("dp", "pipe"), pairs)

    ids_3 = lax.ppermute(own_ids, "dp", [(0, 3), (3, 0)])
    ids_2 = lax.ppermute(own_ids, "dp", [(2, 0), (1, 3)])
    kvs, ups, downs = [], [], []
    for turn in range(2):
        c = order[turn]
        note = jnp.pad(lax.dynamic_index_in_dim(own_ids, c, 0, keepdims=False), (0, HD - heads)).astype(jnp.bfloat16)
        note = jnp.broadcast_to(note, (2, BLK, HD))
        kvs.append(jnp.concatenate([lax.dynamic_index_in_dim(kv, c, 1, keepdims=False), note], axis=2))
    kv, ids_3, ids_2, *kvs = lax.optimization_barrier((kv, ids_3, ids_2, *kvs))
    same = [(i, i, True) for i in range(4)]
    crossed = send(kvs[0], 0, same)
    for turn, source in enumerate((crossed, kvs[1])):
        ups.append(send(source, turn, [(i, i + 1, turn == 1) for i in range(3)]))
        downs.append(send(source, turn, [(i + 1, i, turn == 1) for i in range(3)]))

    message = jax.ShapeDtypeStruct((3 * BLK, width + HD), jnp.bfloat16)
    messages = pl.pallas_call(
        functools.partial(message_kernel, group),
        grid_spec=pltpu.PrefetchScalarGridSpec(
            num_scalar_prefetch=3,
            grid=(2, steps),
            in_specs=[
                pl.BlockSpec((1, BLK, lanes), lambda t, g, order, ids, length: (order[t], 0, g)),
                pl.BlockSpec((1, BLK, lanes), lambda t, g, order, ids, length: (order[t], 0, g)),
                pl.BlockSpec((2, 1, BLK, lanes), lambda t, g, order, ids, length: (0, order[t], 0, g)),
                pl.BlockSpec((2, 1, glob_count, lanes), lambda t, g, order, ids, length: (0, order[t], 0, g)),
            ],
            out_specs=[vmem(), vmem()],
        ),
        out_shape=[message, message],
        compiler_params=params,
    )(order, own_ids, length, q, res, kv, glob)

    messages = list(messages)
    messages[1], downs[1] = lax.optimization_barrier((messages[1], downs[1]))
    messages = [send(messages[turn], turn, same) for turn in range(2)]
    tiles = jax.ShapeDtypeStruct((capacity, 2, BLK, HD), jnp.bfloat16)
    distant = pl.pallas_call(
        distant_kernel,
        out_shape=[tiles, tiles],
        in_specs=[smem(), vmem(), vmem()],
        out_specs=[vmem(), vmem()],
        scratch_shapes=[pltpu.SMEM((1, capacity), jnp.int32)],
        compiler_params=params,
    )(ids_3, *kvs)
    far_3 = [send(distant[turn], turn, [(0, 3, True), (3, 0, True)]) for turn in range(2)]

    far_2 = []
    for turn in range(2):
        array = pl.pallas_call(
            functools.partial(forward_kernel, turn),
            out_shape=tiles,
            in_specs=[smem()] * 3 + [vmem()] * 3,
            out_specs=vmem(),
            scratch_shapes=[pltpu.SMEM((1, capacity), jnp.int32)],
            compiler_params=params,
        )(
            ids_2,
            ups[turn][0, 0, width:].astype(jnp.int32),
            downs[turn][0, 0, width:].astype(jnp.int32),
            kvs[turn],
            ups[turn],
            downs[turn],
        )
        far_2.append(send(array, turn, [(0, 2, True), (3, 1, True), (2, 3, False), (1, 0, False)]))

    wide = jax.ShapeDtypeStruct((BLK, width), jnp.float32)
    row = jax.ShapeDtypeStruct((BLK, width), jnp.bfloat16)
    square = jax.ShapeDtypeStruct((BLK, HD), jnp.float32)
    near, infos = [None, None], [None, None]
    for turn in (1, 0):
        if turn == 0:
            messages[0], near[1][4] = lax.optimization_barrier((messages[0], near[1][4]))
        infos[turn] = messages[turn][0, width:].astype(jnp.int32)
        near[turn] = list(
            pl.pallas_call(
                near_kernel,
                out_shape=[wide, wide, wide, row, square, jax.ShapeDtypeStruct((2, capacity), jnp.int32)],
                in_specs=[smem()] + [vmem()] * 3,
                out_specs=[vmem()] * 5 + [smem()],
                compiler_params=params,
            )(infos[turn], messages[turn], ups[turn], downs[turn])
        )
    accs, maxes, sums, updates, squares, takes = [list(items) for items in zip(*near)]
    for index, got, last in ((1, far_3, False), (0, far_2, True)):
        pair = [jax.ShapeDtypeStruct((2,) + kind.shape, kind.dtype) for kind in (row, square)]
        results = pl.pallas_call(
            functools.partial(tile_kernel, index, last),
            out_shape=pair if last else [row, row, square, square],
            in_specs=[smem()] * 4 + [vmem()] * 14,
            out_specs=[vmem()] * (2 if last else 4),
            input_output_aliases={} if last else {14: 0, 15: 1},
            compiler_params=params,
        )(*infos, *takes, *messages, *got, *accs, *maxes, *sums, *updates, *squares)
        if not last:
            updates, squares = results[:2], results[2:]

    updated, squares = results
    total = lax.psum(jnp.sum(squares, axis=2), "tensor")
    inverse = lax.rsqrt(total / D + epsilon)
    normed = updated.astype(jnp.float32) * inverse[:, :, None] * gain[0][:, None, :].astype(jnp.float32)
    return normed.astype(jnp.bfloat16)[None]


def body(*arrays):
    heads = arrays[0].shape[-1] // HD
    chain = lax.axis_size("dp") == 4 and lax.axis_size("pipe") % 2 == 0 and heads % 8 == 0 and heads <= 32
    return (body_chain if chain else body_any)(*arrays)


def solution(mesh):
    in_specs = (
        P("pipe", None, "dp", "tensor"),
        P("pipe", None, "dp", "tensor"),
        P("pipe", None, None, "dp", "tensor"),
        P("pipe", None, None, None, "tensor"),
        P("pipe", None, "dp", "tensor"),
        P("pipe", None),
        P("pipe", None, "tensor"),
    )
    out_specs = P("pipe", None, "dp", "tensor")
    return jax.shard_map(body, mesh=mesh, in_specs=in_specs, out_specs=out_specs, check_vma=False)
```

```python
import functools

import jax
import jax.numpy as jnp
from jax import lax
from jax.experimental import pallas as pl
from jax.experimental.pallas import tpu as pltpu
from jax.sharding import PartitionSpec as P

D = 6144
HD = 128
BLK = 64
LOG2E = 1.4426950408889634
SCALE = HD ** (-0.5) * LOG2E
NEG = -1e30
VMEM_LIMIT = 20 * 1024 * 1024
LOCAL_LIMIT = 52 * 1024 * 1024

epsilon = 1e-05


def dot_nt(a, b):
    return lax.dot_general(a, b, (((1,), (1,)), ((), ())), preferred_element_type=jnp.float32)


def dot_nn(a, b):
    return lax.dot_general(a, b, (((1,), (0,)), ((), ())), preferred_element_type=jnp.float32)


def with_ones(v):
    return jnp.concatenate([v, jnp.ones((v.shape[0], HD), v.dtype)], axis=1)


def head_group(heads):
    return max(g for g in range(1, 9) if heads % g == 0)


def head_batch(heads):
    return max(g for g in range(1, 5) if heads % g == 0)


def heads_wanted(table_ref, row, ids_ref, asker, block):
    heads, capacity = ids_ref.shape[2], table_ref.shape[2]
    for c in range(2):
        for s in range(capacity):
            table_ref[row, c, s] = -1
        slot = jnp.int32(0)
        for h in range(heads):
            match = (ids_ref[asker, c, h] == block) & (slot < capacity)

            @pl.when(match)
            def _(slot=slot, h=h, c=c):
                table_ref[row, c, slot] = h

            slot = slot + match.astype(jnp.int32)


def copy_tiles(out_ref, list_ref, row, c, source_ref):
    for s in range(out_ref.shape[0]):
        cols = pl.ds(pl.multiple_of(jnp.maximum(list_ref[row, c, s], 0) * HD, HD), HD)
        out_ref[s, 0] = source_ref[0, :, cols]
        out_ref[s, 1] = source_ref[1, :, cols]


def pack_kernel(ids_ref, kv_ref, take_ref, out_ref, list_ref):
    me = lax.axis_index("dp")

    @pl.loop(0, ids_ref.shape[0])
    def _(other):
        far = jnp.abs(other - me) >= 2
        heads_wanted(take_ref, other, ids_ref, me, jnp.where(far, other, -1))
        heads_wanted(list_ref, 0, ids_ref, other, jnp.where(far, me, -1))
        for c in range(2):
            copy_tiles(out_ref.at[other, c], list_ref, 0, c, kv_ref.at[:, c])


def local_kernel(heads_step, ids_ref, len_ref, q_ref, kv_ref, gkv_ref, acc_ref, max_ref, sum_ref):
    me = lax.axis_index("dp")
    c = pl.program_id(0)
    g = pl.program_id(1)
    glob = gkv_ref.shape[2]
    lane = lax.broadcasted_iota(jnp.int32, (1, glob + BLK), 1)
    batch = head_batch(heads_step)
    for start in range(0, heads_step, batch):
        cols = [slice(n * HD, (n + 1) * HD) for n in range(start, start + batch)]
        scores, values = [], []
        for n, col in zip(range(start, start + batch), cols):
            k = jnp.concatenate([gkv_ref[0, 0, :, col], kv_ref[0, 0, :, col]], axis=0)
            values.append(jnp.concatenate([gkv_ref[1, 0, :, col], kv_ref[1, 0, :, col]], axis=0))
            twice = jnp.where(ids_ref[me, c, g * heads_step + n] == me, 1.0, 0.0)
            bias = jnp.where(lane < glob, 0.0, jnp.where(me < len_ref[c], twice, NEG))
            scores.append(dot_nt(q_ref[0, :, col], k) * SCALE + bias)
        tops = [jnp.max(s, axis=1, keepdims=True) for s in scores]
        weights = [jnp.exp2(s - m).astype(jnp.bfloat16) for s, m in zip(scores, tops)]
        sums = [dot_nn(p, with_ones(v)) for p, v in zip(weights, values)]
        for col, m, pv in zip(cols, tops, sums):
            acc_ref[0, :, col] = pv[:, :HD]
            sum_ref[0, :, col] = pv[:, HD:]
            max_ref[0, :, col] = jnp.broadcast_to(m, (BLK, HD))


def merge(scores, olds, values):
    tops = [jnp.maximum(old[0], jnp.max(s, axis=1, keepdims=True)) for s, old in zip(scores, olds)]
    weights = [jnp.exp2(s - m[:, : s.shape[1]]).astype(jnp.bfloat16) for s, m in zip(scores, tops)]
    alphas = [jnp.exp2(old[0] - m) for old, m in zip(olds, tops)]
    added = [dot_nn(p, with_ones(v)) for p, v in zip(weights, values)]
    return [
        (m, alpha * old[1] + pv[:, HD:], alpha * old[2] + pv[:, :HD])
        for m, alpha, old, pv in zip(tops, alphas, olds, added)
    ]


def window_kernel(ids_ref, len_ref, q_ref, up_ref, down_ref, res_ref, acc_ref, max_ref, sum_ref, new_acc_ref, new_max_ref, new_sum_ref, out_ref, sq_ref):
    me = lax.axis_index("dp")
    heads = q_ref.shape[2] // HD
    batch = head_batch(heads)
    lane = lax.broadcasted_iota(jnp.int32, (1, 2 * BLK), 1)
    for c in range(2):
        length = len_ref[c]
        alive = me < length
        up_live = (me >= 1) & (me - 1 < length)
        down_live = me + 1 < length

        def step(g, squares, c=c, alive=alive, up_live=up_live, down_live=down_live):
            cols = [pl.ds(pl.multiple_of((g * batch + n) * HD, HD), HD) for n in range(batch)]
            blocks = [ids_ref[me, c, g * batch + n] for n in range(batch)]
            scores, values = [], []
            for block, col in zip(blocks, cols):
                up_bias = jnp.where(up_live, jnp.where(block == me - 1, 1.0, 0.0), NEG)
                down_bias = jnp.where(down_live, jnp.where(block == me + 1, 1.0, 0.0), NEG)
                bias = jnp.where(lane < BLK, up_bias, down_bias)
                k = jnp.concatenate([up_ref[0, c, :, col], down_ref[0, c, :, col]], axis=0)
                values.append(jnp.concatenate([up_ref[1, c, :, col], down_ref[1, c, :, col]], axis=0))
                scores.append(dot_nt(q_ref[c, :, col], k) * SCALE + bias)
            olds = [(max_ref[c, :, col], sum_ref[c, :, col], acc_ref[c, :, col]) for col in cols]
            residuals = [res_ref[c, :, col].astype(jnp.float32) for col in cols]
            news = merge(scores, olds, values)
            updates = [
                (res + jnp.where(alive, acc / l, 0.0)).astype(jnp.bfloat16) for res, (_, l, acc) in zip(residuals, news)
            ]
            for block, col, (m, l, acc), updated in zip(blocks, cols, news, updates):
                new_max_ref[c, :, col] = m
                new_sum_ref[c, :, col] = l
                new_acc_ref[c, :, col] = acc
                out_ref[c, :, col] = updated
                wide = updated.astype(jnp.float32)
                squares = squares + wide * wide * jnp.where(jnp.abs(block - me) < 2, 1.0, 0.0)
            return squares

        sq_ref[c] = lax.fori_loop(0, heads // batch, step, jnp.zeros((BLK, HD), jnp.float32))


def far_kernel(ids_ref, take_ref, len_ref, tile_ref, q_ref, res_ref, acc_ref, max_ref, sum_ref, old_ref, old_sq_ref, out_ref, sq_ref):
    del old_ref
    me = lax.axis_index("dp")
    owners, _, capacity = take_ref.shape
    sq_ref[...] = old_sq_ref[...]

    def one_owner(owner):
        places = [(c, s) for c in range(2) for s in range(capacity)]
        taken = [take_ref[owner, c, s] for c, s in places]
        chosen = [jnp.maximum(h, 0) for h in taken]
        cols = [pl.ds(pl.multiple_of(h * HD, HD), HD) for h in chosen]
        live = [(t >= 0) & (ids_ref[me, c, h] < len_ref[c]) for (c, _), t, h in zip(places, taken, chosen)]
        scores = [
            dot_nt(q_ref[c, :, col], tile_ref[owner, c, s, 0]) * SCALE + jnp.where(ok, 0.0, NEG)
            for (c, s), col, ok in zip(places, cols, live)
        ]
        olds = [(max_ref[c, :, col], sum_ref[c, :, col], acc_ref[c, :, col]) for (c, _), col in zip(places, cols)]
        residuals = [res_ref[c, :, col].astype(jnp.float32) for (c, _), col in zip(places, cols)]
        news = merge(scores, olds, [tile_ref[owner, c, s, 1] for c, s in places])
        updates = [
            (res + jnp.where(me < len_ref[c], acc / l, 0.0)).astype(jnp.bfloat16)
            for (c, _), res, (_, l, acc) in zip(places, residuals, news)
        ]
        squares = [jnp.zeros((BLK, HD), jnp.float32)] * 2
        for (c, _), t, updated in zip(places, taken, updates):
            wide = updated.astype(jnp.float32)
            squares[c] = squares[c] + wide * wide * jnp.where(t >= 0, 1.0, 0.0)
        for c in range(2):
            sq_ref[c] += squares[c]
        for (c, _), t, col, updated in zip(places, taken, cols, updates):

            @pl.when(t >= 0)
            def _(c=c, col=col, updated=updated):
                out_ref[c, :, col] = updated

    pl.loop(0, owners)(one_owner)


def smem():
    return pl.BlockSpec(memory_space=pltpu.SMEM)


def vmem():
    return pl.BlockSpec(memory_space=pltpu.VMEM)


def body_any(residual, queries, keys_values, global_kv, block_ids, lengths, gain):
    width = residual.shape[-1]
    heads = width // HD
    dp_count = lax.axis_size("dp")
    pipe_count = lax.axis_size("pipe")
    tensor_count = lax.axis_size("tensor")
    group = head_group(heads)
    steps = heads // group
    lanes = group * HD
    capacity = (heads + dp_count - 1) // dp_count
    q = queries[0]
    res = residual[0]
    glob = global_kv[0]
    length = lengths[0]
    glob_count = glob.shape[2]
    params = pltpu.CompilerParams(vmem_limit_bytes=VMEM_LIMIT)

    ids = block_ids[0, :, 0]
    ids = lax.all_to_all(jnp.broadcast_to(ids, (dp_count,) + ids.shape), "dp", split_axis=0, concat_axis=0, tiled=True)
    kv, ids = lax.optimization_barrier((keys_values[0], ids))
    up = lax.ppermute(kv, "dp", [(i, i + 1) for i in range(dp_count - 1)])
    down = lax.ppermute(kv, "dp", [(i + 1, i) for i in range(dp_count - 1)])

    lines = [[(i + 1, i) for i in range(pipe_count - 1)], [(i, i + 1) for i in range(pipe_count - 1)]]
    gains = [lax.ppermute(gain[0, c], "pipe", [(j, i) for i, j in lines[c]]) for c in range(2)]
    q, gains = lax.optimization_barrier((q, gains))
    wide = jax.ShapeDtypeStruct((2, BLK, width), jnp.float32)
    row_spec = pl.BlockSpec((1, BLK, lanes), lambda c, g: (c, 0, g))
    pair_spec = pl.BlockSpec((2, 1, BLK, lanes), lambda c, g: (0, c, 0, g))
    acc, maxes, sums = pl.pallas_call(
        functools.partial(local_kernel, group),
        grid=(2, steps),
        out_shape=[wide] * 3,
        in_specs=[
            smem(),
            smem(),
            row_spec,
            pair_spec,
            pl.BlockSpec((2, 1, glob_count, lanes), lambda c, g: (0, c, 0, g)),
        ],
        out_specs=[row_spec] * 3,
        compiler_params=params,
        cost_estimate=pl.CostEstimate(
            flops=4 * 2 * BLK * width * (glob_count + BLK), bytes_accessed=14 * 2**20, transcendentals=0
        ),
    )(ids, length, q, kv, glob)

    kv, acc = lax.optimization_barrier((kv, acc))

    tile = (2, capacity, 2, BLK, HD)
    take, tiles_all = pl.pallas_call(
        pack_kernel,
        out_shape=[
            jax.ShapeDtypeStruct((dp_count, 2, capacity), jnp.int32),
            jax.ShapeDtypeStruct((dp_count,) + tile, jnp.bfloat16),
        ],
        in_specs=[smem(), vmem()],
        out_specs=[smem(), vmem()],
        scratch_shapes=[pltpu.SMEM((1, 2, capacity), jnp.int32)],
        compiler_params=params,
    )(ids, kv)
    far = [(take, lax.all_to_all(tiles_all, "dp", split_axis=0, concat_axis=0, tiled=True))]

    acc, maxes, sums, updated, squares = pl.pallas_call(
        window_kernel,
        out_shape=[wide] * 3
        + [jax.ShapeDtypeStruct((2, BLK, width), jnp.bfloat16), jax.ShapeDtypeStruct((2, BLK, HD), jnp.float32)],
        in_specs=[smem(), smem()] + [vmem()] * 7,
        out_specs=[vmem()] * 5,
        compiler_params=params,
        cost_estimate=pl.CostEstimate(
            flops=4 * 2 * BLK * width * 2 * BLK, bytes_accessed=9 * 2**20, transcendentals=0
        ),
    )(ids, length, q, up, down, res, acc, maxes, sums)

    for heads_taken, tiles_got in far:
        updated, squares = pl.pallas_call(
            far_kernel,
            out_shape=[
                jax.ShapeDtypeStruct((2, BLK, width), jnp.bfloat16),
                jax.ShapeDtypeStruct((2, BLK, HD), jnp.float32),
            ],
            in_specs=[smem(), smem(), smem()] + [vmem()] * 8,
            out_specs=[vmem()] * 2,
            input_output_aliases={9: 0},
            compiler_params=params,
        )(ids, heads_taken, length, tiles_got, q, res, acc, maxes, sums, updated, squares)

    total = lax.psum(jnp.sum(squares, axis=2), "tensor")
    inverse = lax.rsqrt(total / D + epsilon)
    normed = [
        (updated[c].astype(jnp.float32) * inverse[c][:, None] * gains[c].astype(jnp.float32)).astype(jnp.bfloat16)
        for c in range(2)
    ]
    return jnp.stack([lax.ppermute(normed[c], "pipe", lines[c]) for c in range(2)])[None]


def pair_queries(first, second):
    none = jnp.zeros_like(first)
    return jnp.concatenate(
        [jnp.concatenate([first, none], axis=1), jnp.concatenate([none, second], axis=1)], axis=0
    )


def pair_rows(first, second, lanes):
    return jnp.concatenate([jnp.broadcast_to(first, (BLK, lanes)), jnp.broadcast_to(second, (BLK, lanes))], axis=0)


def pair_context(weights, values):
    both = dot_nn(weights.astype(jnp.bfloat16), values)
    return jnp.concatenate([both[:BLK, :HD], both[BLK:, HD:]], axis=0)


LENGTH = 32


def sent_in(turn):
    parity = lax.rem(lax.axis_index("pipe"), 2)
    return parity if turn == 0 else 1 - parity


def copy_heads(out_ref, list_ref, row, source_ref):
    for s in range(out_ref.shape[0]):
        cols = pl.ds(pl.multiple_of(jnp.maximum(list_ref[row, s], 0) * HD, HD), HD)
        out_ref[s, 0] = source_ref[0, :, cols]
        out_ref[s, 1] = source_ref[1, :, cols]


def list_heads(list_ref, row, heads, block, block_of):
    capacity = list_ref.shape[1]
    for s in range(capacity):
        list_ref[row, s] = 0
    slot = jnp.int32(0)
    for h in range(heads):
        match = (block_of(h) == block) & (slot < capacity)

        @pl.when(match)
        def _(slot=slot, h=h):
            list_ref[row, slot] = h

        slot = slot + match.astype(jnp.int32)


def distant_kernel(ids_ref, kv0_ref, kv1_ref, tile0_ref, tile1_ref, list_ref):
    me = lax.axis_index("dp")
    heads = ids_ref.shape[1]

    @pl.when((me == 0) | (me == 3))
    def _():
        for turn, (kv_ref, tile_ref) in enumerate(((kv0_ref, tile0_ref), (kv1_ref, tile1_ref))):
            c = sent_in(turn)
            list_heads(list_ref, 0, heads, me, lambda h, c=c: ids_ref[c, h])
            copy_heads(tile_ref, list_ref, 0, kv_ref)


def forward_kernel(turn, ids_ref, up_ids_ref, down_ids_ref, kv_ref, up_ref, down_ref, tile_ref, list_ref):
    me = lax.axis_index("dp")
    heads = ids_ref.shape[1]
    c = sent_in(turn)
    edge = (me == 0) | (me == 3)
    list_heads(
        list_ref,
        0,
        heads,
        jnp.where(edge, me, 3 - me),
        lambda h: jnp.where(edge, ids_ref[c, h], jnp.where(me == 1, up_ids_ref[h], down_ids_ref[h])),
    )
    pl.when(edge)(lambda: copy_heads(tile_ref, list_ref, 0, kv_ref))
    pl.when(me == 1)(lambda: copy_heads(tile_ref, list_ref, 0, down_ref))
    pl.when(me == 2)(lambda: copy_heads(tile_ref, list_ref, 0, up_ref))


def message_kernel(turn, order_ref, ids_ref, len_ref, q_ref, res_ref, kv_ref, gkv_ref, out_ref, glob_ref, sems):
    me = lax.axis_index("dp")
    c = order_ref[turn]
    glob = gkv_ref.shape[2]
    width = out_ref.shape[1] - HD
    heads = width // HD
    parts = sems.shape[0]
    copies = []
    for n in range(parts):
        cols = slice(n * (width // parts), (n + 1) * (width // parts))
        copies.append(pltpu.make_async_copy(gkv_ref.at[:, c, :, cols], glob_ref.at[:, :, cols], sems.at[n]))
        copies[-1].start()
    place = lax.broadcasted_iota(jnp.int32, (1, HD), 1)
    note = jnp.where(place == LENGTH, len_ref[c], 0)
    for h in range(heads):
        note = jnp.where(place == h, ids_ref[c, h], note)
    out_ref[:BLK, width:] = jnp.broadcast_to(note.astype(jnp.float32), (BLK, HD)).astype(jnp.bfloat16)
    out_ref[BLK : 2 * BLK, width:] = jnp.zeros((BLK, HD), jnp.bfloat16)
    out_ref[:BLK, :width] = q_ref[c]
    out_ref[BLK : 2 * BLK, :width] = res_ref[c]
    own_live = me < len_ref[c]

    def score(n):
        both = slice(n * HD, (n + 2) * HD)
        q = pair_queries(q_ref[c, :, n * HD : (n + 1) * HD], q_ref[c, :, (n + 1) * HD : (n + 2) * HD])
        k = jnp.concatenate([glob_ref[0, :, both], kv_ref[0, c, :, both]], axis=0)
        own = [jnp.where(own_live, jnp.where(ids_ref[c, n + i] == me, 1.0, 0.0), NEG) for i in range(2)]
        s = dot_nt(q, k) * SCALE
        return jnp.concatenate([s[:, :glob], s[:, glob:] + pair_rows(*own, BLK)], axis=1)

    def weigh(s):
        m = jnp.max(s, axis=1, keepdims=True)
        p = jnp.exp2(s - m)
        l = jnp.sum(p, axis=1, keepdims=True)
        return p.astype(jnp.bfloat16), l, m + jnp.log2(l)

    def finish(n, p, l):
        both = slice(n * HD, (n + 2) * HD)
        v = jnp.concatenate([glob_ref[1, :, both], kv_ref[1, c, :, both]], axis=0)
        return (pair_context(p, v) / l).astype(jnp.bfloat16)

    state = jnp.zeros((BLK, HD), jnp.float32)
    pairs = heads // 2
    scored = weighed = None
    for t in range(pairs + 2):
        fresh = ready = None
        if t < pairs:
            if t % (pairs // parts) == 0:
                copies[t // (pairs // parts)].wait()
            fresh = score(2 * t)
        if scored is not None:
            p, l, level = weigh(scored)
            ready = (p, l)
            high = level.astype(jnp.bfloat16).astype(jnp.float32)
            middle = (level - high).astype(jnp.bfloat16).astype(jnp.float32)
            low = level - high - middle
            for i in range(2):
                rows = slice(i * BLK, (i + 1) * BLK)
                at = place - (2 * (t - 1) + i)
                state = jnp.where(
                    at == 0, high[rows], jnp.where(at == 32, middle[rows], jnp.where(at == 64, low[rows], state))
                )
        if weighed is not None:
            h = 2 * (t - 2)
            context = finish(h, *weighed)
            for i in range(2):
                out_ref[2 * BLK :, (h + i) * HD : (h + i + 1) * HD] = context[i * BLK : (i + 1) * BLK]
        scored, weighed = fresh, ready
    out_ref[2 * BLK :, width:] = state.astype(jnp.bfloat16)


def near_kernel(info_ref, message_ref, up_ref, down_ref, acc_ref, max_ref, sum_ref, out_ref, sq_ref, take_ref):
    me = lax.axis_index("dp")
    width = out_ref.shape[1]
    heads = width // HD
    batch = head_batch(heads)
    length = info_ref[LENGTH]
    alive = me < length
    up_live = (me >= 1) & (me - 1 < length)
    down_live = me + 1 < length
    list_heads(take_ref, 0, heads, jnp.where(me < 2, me + 2, me - 2), lambda h: info_ref[h])
    list_heads(take_ref, 1, heads, 3 - me, lambda h: info_ref[h])
    lane = lax.broadcasted_iota(jnp.int32, (1, 2 * BLK), 1)
    state = message_ref[2 * BLK :, width:].astype(jnp.float32)
    state = state + pltpu.roll(state, 96, 1) + pltpu.roll(state, 64, 1)
    squares = jnp.zeros((BLK, HD), jnp.float32)

    def score(numbers):
        items = []
        for h in numbers:
            col = slice(h * HD, (h + 1) * HD)
            block = info_ref[h]
            up_bias = jnp.where(up_live, jnp.where(block == me - 1, 1.0, 0.0), NEG)
            down_bias = jnp.where(down_live, jnp.where(block == me + 1, 1.0, 0.0), NEG)
            bias = jnp.where(lane < BLK, up_bias, down_bias)
            k = jnp.concatenate([up_ref[0, :, col], down_ref[0, :, col]], axis=0)
            v = jnp.concatenate([up_ref[1, :, col], down_ref[1, :, col]], axis=0)
            s = dot_nt(message_ref[:BLK, col], k) * SCALE + bias
            level = jnp.broadcast_to(state[:, h : h + 1], (BLK, HD))
            near = jnp.where(jnp.abs(block - me) < 2, 1.0, 0.0)
            items.append((col, s, v, level, message_ref[BLK : 2 * BLK, col], message_ref[2 * BLK :, col], near))
        return items

    def weigh(items):
        outs = []
        for col, s, v, level, res, context, near in items:
            m = jnp.maximum(level, jnp.max(s, axis=1, keepdims=True))
            p = jnp.exp2(s - m).astype(jnp.bfloat16)
            outs.append((col, m, p, v, jnp.exp2(level - m), res, context, near))
        return outs

    def finish(items, squares):
        outs = []
        for col, m, p, v, alpha, res, context, near in items:
            pv = dot_nn(p, with_ones(v))
            l = alpha + pv[:, HD:]
            acc = alpha * context.astype(jnp.float32) + pv[:, :HD]
            updated = (res.astype(jnp.float32) + jnp.where(alive, acc / l, 0.0)).astype(jnp.bfloat16)
            wide = updated.astype(jnp.float32)
            squares = squares + wide * wide * near
            outs.append((col, m, l, acc, updated))
        for col, m, l, acc, updated in outs:
            max_ref[:, col] = m
            sum_ref[:, col] = l
            acc_ref[:, col] = acc
            out_ref[:, col] = updated
        return squares

    batches = [range(start, start + batch) for start in range(0, heads, batch)]
    scored = weighed = None
    for turn in range(len(batches) + 2):
        fresh = score(batches[turn]) if turn < len(batches) else None
        ready = weigh(scored) if scored else None
        if weighed:
            squares = finish(weighed, squares)
        scored, weighed = fresh, ready
    sq_ref[...] = squares


def tile_kernel(row, last, *refs):
    infos, takes, messages, tiles, accs, maxes, sums, olds, old_sqs = [refs[2 * n : 2 * n + 2] for n in range(9)]
    me = lax.axis_index("dp")
    if last:
        outs = [refs[18].at[1 - sent_in(turn)] for turn in range(2)]
        sqs = [refs[19].at[1 - sent_in(turn)] for turn in range(2)]
        for turn in range(2):
            outs[turn][...] = olds[turn][...]
    else:
        outs, sqs = refs[18:20], refs[20:22]

    def work():
        places = [(t, s) for t in range(2) for s in range(tiles[0].shape[0])]
        chosen = [takes[t][row, s] for t, s in places]
        cols = [pl.ds(pl.multiple_of(h * HD, HD), HD) for h in chosen]
        live = [infos[t][h] < infos[t][LENGTH] for (t, _), h in zip(places, chosen)]
        scores = [
            dot_nt(messages[t][:BLK, col], tiles[t][s, 0]) * SCALE + jnp.where(ok, 0.0, NEG)
            for (t, s), col, ok in zip(places, cols, live)
        ]
        before = [(maxes[t][:, col], sums[t][:, col], accs[t][:, col]) for (t, _), col in zip(places, cols)]
        residuals = [messages[t][BLK : 2 * BLK, col].astype(jnp.float32) for (t, _), col in zip(places, cols)]
        news = merge(scores, before, [tiles[t][s, 1] for t, s in places])
        updates = [
            (res + jnp.where(me < infos[t][LENGTH], acc / l, 0.0)).astype(jnp.bfloat16)
            for (t, _), res, (_, l, acc) in zip(places, residuals, news)
        ]
        squares = [old_sqs[t][...] for t in range(2)]
        for (t, _), col, updated in zip(places, cols, updates):
            outs[t][:, col] = updated
            wide = updated.astype(jnp.float32)
            squares[t] = squares[t] + wide * wide
        for t in range(2):
            sqs[t][...] = squares[t]

    if last:
        work()
    else:
        for t in range(2):
            sqs[t][...] = old_sqs[t][...]
        pl.when((me == 0) | (me == 3))(work)


def body_chain(residual, queries, keys_values, global_kv, block_ids, lengths, gain):
    width = residual.shape[-1]
    heads = width // HD
    pipe_count = lax.axis_size("pipe")
    capacity = heads // 4
    q, res, glob, kv, length = queries[0], residual[0], global_kv[0], keys_values[0], lengths[0]
    own_ids = block_ids[0, :, 0]
    glob_count = glob.shape[2]
    params = pltpu.CompilerParams(vmem_limit_bytes=VMEM_LIMIT)
    order = jnp.stack([sent_in(0), sent_in(1)])

    def send(array, turn, moves):
        pairs = []
        for p in range(pipe_count):
            other = p ^ 1 if turn == 1 else ((p + 1) ^ 1) - 1
            if 0 <= other < pipe_count:
                pairs += [
                    ((i * pipe_count + p) if direct else (i * pipe_count + other), j * pipe_count + other)
                    for i, j, direct in moves
                ]
        return lax.ppermute(array, ("dp", "pipe"), pairs)

    ids_3 = lax.ppermute(own_ids, "dp", [(0, 3), (3, 0)])
    ids_2 = lax.ppermute(own_ids, "dp", [(2, 0), (1, 3)])
    kvs, ups, downs = [], [], []
    for turn in range(2):
        c = order[turn]
        note = jnp.pad(lax.dynamic_index_in_dim(own_ids, c, 0, keepdims=False), (0, HD - heads)).astype(jnp.bfloat16)
        note = jnp.broadcast_to(note, (2, BLK, HD))
        kvs.append(jnp.concatenate([lax.dynamic_index_in_dim(kv, c, 1, keepdims=False), note], axis=2))
    kv, ids_3, ids_2, *kvs = lax.optimization_barrier((kv, ids_3, ids_2, *kvs))
    same = [(i, i, True) for i in range(4)]
    crossed = send(kvs[0], 0, same)
    for turn, source in enumerate((crossed, kvs[1])):
        ups.append(send(source, turn, [(i, i + 1, turn == 1) for i in range(3)]))
        downs.append(send(source, turn, [(i + 1, i, turn == 1) for i in range(3)]))

    message = jax.ShapeDtypeStruct((3 * BLK, width + HD), jnp.bfloat16)

    def local_part(turn, kv):
        return pl.pallas_call(
            functools.partial(message_kernel, turn),
            out_shape=message,
            in_specs=[smem()] * 3 + [vmem()] * 3 + [pl.BlockSpec(memory_space=pl.ANY)],
            out_specs=vmem(),
            scratch_shapes=[
                pltpu.VMEM((2, glob_count, width), jnp.bfloat16),
                pltpu.SemaphoreType.DMA((3,)),
            ],
            compiler_params=pltpu.CompilerParams(vmem_limit_bytes=LOCAL_LIMIT),
        )(order, own_ids, length, q, res, kv, glob)

    messages = [local_part(0, kv)]
    kv, crossed = lax.optimization_barrier((kv, crossed))
    messages.append(local_part(1, kv))
    messages = [send(messages[turn], turn, same) for turn in range(2)]
    tiles = jax.ShapeDtypeStruct((capacity, 2, BLK, HD), jnp.bfloat16)
    distant = pl.pallas_call(
        distant_kernel,
        out_shape=[tiles, tiles],
        in_specs=[smem(), vmem(), vmem()],
        out_specs=[vmem(), vmem()],
        scratch_shapes=[pltpu.SMEM((1, capacity), jnp.int32)],
        compiler_params=params,
    )(ids_3, *kvs)
    distant = list(distant)
    distant[1], downs[0] = lax.optimization_barrier((distant[1], downs[0]))
    far_3 = [send(distant[turn], turn, [(0, 3, True), (3, 0, True)]) for turn in range(2)]

    far_2 = []
    for turn in range(2):
        array = pl.pallas_call(
            functools.partial(forward_kernel, turn),
            out_shape=tiles,
            in_specs=[smem()] * 3 + [vmem()] * 3,
            out_specs=vmem(),
            scratch_shapes=[pltpu.SMEM((1, capacity), jnp.int32)],
            compiler_params=params,
        )(
            ids_2,
            ups[turn][0, 0, width:].astype(jnp.int32),
            downs[turn][0, 0, width:].astype(jnp.int32),
            kvs[turn],
            ups[turn],
            downs[turn],
        )
        far_2.append(send(array, turn, [(0, 2, True), (3, 1, True), (2, 3, False), (1, 0, False)]))

    wide = jax.ShapeDtypeStruct((BLK, width), jnp.float32)
    row = jax.ShapeDtypeStruct((BLK, width), jnp.bfloat16)
    square = jax.ShapeDtypeStruct((BLK, HD), jnp.float32)
    near, infos = [None, None], [None, None]
    for turn in (1, 0):
        if turn == 0:
            messages[0], near[1][4] = lax.optimization_barrier((messages[0], near[1][4]))
        infos[turn] = messages[turn][0, width:].astype(jnp.int32)
        near[turn] = list(
            pl.pallas_call(
                near_kernel,
                out_shape=[wide, wide, wide, row, square, jax.ShapeDtypeStruct((2, capacity), jnp.int32)],
                in_specs=[smem()] + [vmem()] * 3,
                out_specs=[vmem()] * 5 + [smem()],
                compiler_params=params,
            )(infos[turn], messages[turn], ups[turn], downs[turn])
        )
    accs, maxes, sums, updates, squares, takes = [list(items) for items in zip(*near)]
    for index, got, last in ((1, far_3, False), (0, far_2, True)):
        pair = [jax.ShapeDtypeStruct((2,) + kind.shape, kind.dtype) for kind in (row, square)]
        results = pl.pallas_call(
            functools.partial(tile_kernel, index, last),
            out_shape=pair if last else [row, row, square, square],
            in_specs=[smem()] * 4 + [vmem()] * 14,
            out_specs=[vmem()] * (2 if last else 4),
            input_output_aliases={} if last else {14: 0, 15: 1},
            compiler_params=params,
        )(*infos, *takes, *messages, *got, *accs, *maxes, *sums, *updates, *squares)
        if not last:
            updates, squares = results[:2], results[2:]

    updated, squares = results
    total = lax.psum(jnp.sum(squares, axis=2), "tensor")
    inverse = lax.rsqrt(total / D + epsilon)
    normed = updated.astype(jnp.float32) * inverse[:, :, None] * gain[0][:, None, :].astype(jnp.float32)
    return normed.astype(jnp.bfloat16)[None]


def body(*arrays):
    heads = arrays[0].shape[-1] // HD
    chain = lax.axis_size("dp") == 4 and lax.axis_size("pipe") % 2 == 0 and heads % 24 == 0 and heads <= 32
    return (body_chain if chain else body_any)(*arrays)


def solution(mesh):
    in_specs = (
        P("pipe", None, "dp", "tensor"),
        P("pipe", None, "dp", "tensor"),
        P("pipe", None, None, "dp", "tensor"),
        P("pipe", None, None, None, "tensor"),
        P("pipe", None, "dp", "tensor"),
        P("pipe", None),
        P("pipe", None, "tensor"),
    )
    out_specs = P("pipe", None, "dp", "tensor")
    return jax.shard_map(body, mesh=mesh, in_specs=in_specs, out_specs=out_specs, check_vma=False)
```

```python
import functools

import jax
import jax.numpy as jnp
from jax import lax
from jax.experimental import pallas as pl
from jax.experimental.pallas import tpu as pltpu
from jax.sharding import PartitionSpec as P

D = 6144
HD = 128
BLK = 64
LOG2E = 1.4426950408889634
SCALE = HD ** (-0.5) * LOG2E
NEG = -1e30
VMEM_LIMIT = 40 * 1024 * 1024

epsilon = 1e-05


def dot_nt(a, b):
    return lax.dot_general(a, b, (((1,), (1,)), ((), ())), preferred_element_type=jnp.float32)


def dot_nn(a, b):
    return lax.dot_general(a, b, (((1,), (0,)), ((), ())), preferred_element_type=jnp.float32)


def with_ones(v):
    return jnp.concatenate([v, jnp.ones((v.shape[0], HD), v.dtype)], axis=1)


def head_group(heads):
    return max(g for g in range(1, 9) if heads % g == 0)


def head_batch(heads):
    return max(g for g in range(1, 5) if heads % g == 0)


def heads_wanted(table_ref, row, ids_ref, asker, block):
    heads, capacity = ids_ref.shape[2], table_ref.shape[2]
    for c in range(2):
        for s in range(capacity):
            table_ref[row, c, s] = -1
        slot = jnp.int32(0)
        for h in range(heads):
            match = (ids_ref[asker, c, h] == block) & (slot < capacity)

            @pl.when(match)
            def _(slot=slot, h=h, c=c):
                table_ref[row, c, slot] = h

            slot = slot + match.astype(jnp.int32)


def copy_tiles(out_ref, list_ref, row, c, source_ref):
    for s in range(out_ref.shape[0]):
        cols = pl.ds(pl.multiple_of(jnp.maximum(list_ref[row, c, s], 0) * HD, HD), HD)
        out_ref[s, 0] = source_ref[0, :, cols]
        out_ref[s, 1] = source_ref[1, :, cols]


def pack_kernel(ids_ref, kv_ref, take_ref, out_ref, list_ref):
    me = lax.axis_index("dp")

    @pl.loop(0, ids_ref.shape[0])
    def _(other):
        far = jnp.abs(other - me) >= 2
        heads_wanted(take_ref, other, ids_ref, me, jnp.where(far, other, -1))
        heads_wanted(list_ref, 0, ids_ref, other, jnp.where(far, me, -1))
        for c in range(2):
            copy_tiles(out_ref.at[other, c], list_ref, 0, c, kv_ref.at[:, c])


def local_kernel(heads_step, ids_ref, len_ref, q_ref, kv_ref, gkv_ref, acc_ref, max_ref, sum_ref):
    me = lax.axis_index("dp")
    c = pl.program_id(0)
    g = pl.program_id(1)
    glob = gkv_ref.shape[2]
    lane = lax.broadcasted_iota(jnp.int32, (1, glob + BLK), 1)
    batch = head_batch(heads_step)
    for start in range(0, heads_step, batch):
        cols = [slice(n * HD, (n + 1) * HD) for n in range(start, start + batch)]
        scores, values = [], []
        for n, col in zip(range(start, start + batch), cols):
            k = jnp.concatenate([gkv_ref[0, 0, :, col], kv_ref[0, 0, :, col]], axis=0)
            values.append(jnp.concatenate([gkv_ref[1, 0, :, col], kv_ref[1, 0, :, col]], axis=0))
            twice = jnp.where(ids_ref[me, c, g * heads_step + n] == me, 1.0, 0.0)
            bias = jnp.where(lane < glob, 0.0, jnp.where(me < len_ref[c], twice, NEG))
            scores.append(dot_nt(q_ref[0, :, col], k) * SCALE + bias)
        tops = [jnp.max(s, axis=1, keepdims=True) for s in scores]
        weights = [jnp.exp2(s - m).astype(jnp.bfloat16) for s, m in zip(scores, tops)]
        sums = [dot_nn(p, with_ones(v)) for p, v in zip(weights, values)]
        for col, m, pv in zip(cols, tops, sums):
            acc_ref[0, :, col] = pv[:, :HD]
            sum_ref[0, :, col] = pv[:, HD:]
            max_ref[0, :, col] = jnp.broadcast_to(m, (BLK, HD))


def merge(scores, olds, values):
    tops = [jnp.maximum(old[0], jnp.max(s, axis=1, keepdims=True)) for s, old in zip(scores, olds)]
    weights = [jnp.exp2(s - m[:, : s.shape[1]]).astype(jnp.bfloat16) for s, m in zip(scores, tops)]
    alphas = [jnp.exp2(old[0] - m) for old, m in zip(olds, tops)]
    added = [dot_nn(p, with_ones(v)) for p, v in zip(weights, values)]
    return [
        (m, alpha * old[1] + pv[:, HD:], alpha * old[2] + pv[:, :HD])
        for m, alpha, old, pv in zip(tops, alphas, olds, added)
    ]


def window_kernel(ids_ref, len_ref, q_ref, up_ref, down_ref, res_ref, acc_ref, max_ref, sum_ref, new_acc_ref, new_max_ref, new_sum_ref, out_ref, sq_ref):
    me = lax.axis_index("dp")
    heads = q_ref.shape[2] // HD
    batch = head_batch(heads)
    lane = lax.broadcasted_iota(jnp.int32, (1, 2 * BLK), 1)
    for c in range(2):
        length = len_ref[c]
        alive = me < length
        up_live = (me >= 1) & (me - 1 < length)
        down_live = me + 1 < length

        def step(g, squares, c=c, alive=alive, up_live=up_live, down_live=down_live):
            cols = [pl.ds(pl.multiple_of((g * batch + n) * HD, HD), HD) for n in range(batch)]
            blocks = [ids_ref[me, c, g * batch + n] for n in range(batch)]
            scores, values = [], []
            for block, col in zip(blocks, cols):
                up_bias = jnp.where(up_live, jnp.where(block == me - 1, 1.0, 0.0), NEG)
                down_bias = jnp.where(down_live, jnp.where(block == me + 1, 1.0, 0.0), NEG)
                bias = jnp.where(lane < BLK, up_bias, down_bias)
                k = jnp.concatenate([up_ref[0, c, :, col], down_ref[0, c, :, col]], axis=0)
                values.append(jnp.concatenate([up_ref[1, c, :, col], down_ref[1, c, :, col]], axis=0))
                scores.append(dot_nt(q_ref[c, :, col], k) * SCALE + bias)
            olds = [(max_ref[c, :, col], sum_ref[c, :, col], acc_ref[c, :, col]) for col in cols]
            residuals = [res_ref[c, :, col].astype(jnp.float32) for col in cols]
            news = merge(scores, olds, values)
            updates = [
                (res + jnp.where(alive, acc / l, 0.0)).astype(jnp.bfloat16) for res, (_, l, acc) in zip(residuals, news)
            ]
            for block, col, (m, l, acc), updated in zip(blocks, cols, news, updates):
                new_max_ref[c, :, col] = m
                new_sum_ref[c, :, col] = l
                new_acc_ref[c, :, col] = acc
                out_ref[c, :, col] = updated
                wide = updated.astype(jnp.float32)
                squares = squares + wide * wide * jnp.where(jnp.abs(block - me) < 2, 1.0, 0.0)
            return squares

        sq_ref[c] = lax.fori_loop(0, heads // batch, step, jnp.zeros((BLK, HD), jnp.float32))


def far_kernel(ids_ref, take_ref, len_ref, tile_ref, q_ref, res_ref, acc_ref, max_ref, sum_ref, old_ref, old_sq_ref, out_ref, sq_ref):
    del old_ref
    me = lax.axis_index("dp")
    owners, _, capacity = take_ref.shape
    sq_ref[...] = old_sq_ref[...]

    def one_owner(owner):
        places = [(c, s) for c in range(2) for s in range(capacity)]
        taken = [take_ref[owner, c, s] for c, s in places]
        chosen = [jnp.maximum(h, 0) for h in taken]
        cols = [pl.ds(pl.multiple_of(h * HD, HD), HD) for h in chosen]
        live = [(t >= 0) & (ids_ref[me, c, h] < len_ref[c]) for (c, _), t, h in zip(places, taken, chosen)]
        scores = [
            dot_nt(q_ref[c, :, col], tile_ref[owner, c, s, 0]) * SCALE + jnp.where(ok, 0.0, NEG)
            for (c, s), col, ok in zip(places, cols, live)
        ]
        olds = [(max_ref[c, :, col], sum_ref[c, :, col], acc_ref[c, :, col]) for (c, _), col in zip(places, cols)]
        residuals = [res_ref[c, :, col].astype(jnp.float32) for (c, _), col in zip(places, cols)]
        news = merge(scores, olds, [tile_ref[owner, c, s, 1] for c, s in places])
        updates = [
            (res + jnp.where(me < len_ref[c], acc / l, 0.0)).astype(jnp.bfloat16)
            for (c, _), res, (_, l, acc) in zip(places, residuals, news)
        ]
        squares = [jnp.zeros((BLK, HD), jnp.float32)] * 2
        for (c, _), t, updated in zip(places, taken, updates):
            wide = updated.astype(jnp.float32)
            squares[c] = squares[c] + wide * wide * jnp.where(t >= 0, 1.0, 0.0)
        for c in range(2):
            sq_ref[c] += squares[c]
        for (c, _), t, col, updated in zip(places, taken, cols, updates):

            @pl.when(t >= 0)
            def _(c=c, col=col, updated=updated):
                out_ref[c, :, col] = updated

    pl.loop(0, owners)(one_owner)


def smem():
    return pl.BlockSpec(memory_space=pltpu.SMEM)


def vmem():
    return pl.BlockSpec(memory_space=pltpu.VMEM)


def body_any(residual, queries, keys_values, global_kv, block_ids, lengths, gain):
    width = residual.shape[-1]
    heads = width // HD
    dp_count = lax.axis_size("dp")
    pipe_count = lax.axis_size("pipe")
    tensor_count = lax.axis_size("tensor")
    group = head_group(heads)
    steps = heads // group
    lanes = group * HD
    capacity = (heads + dp_count - 1) // dp_count
    q = queries[0]
    res = residual[0]
    glob = global_kv[0]
    length = lengths[0]
    glob_count = glob.shape[2]
    params = pltpu.CompilerParams(vmem_limit_bytes=VMEM_LIMIT)

    ids = block_ids[0, :, 0]
    ids = lax.all_to_all(jnp.broadcast_to(ids, (dp_count,) + ids.shape), "dp", split_axis=0, concat_axis=0, tiled=True)
    kv, ids = lax.optimization_barrier((keys_values[0], ids))
    up = lax.ppermute(kv, "dp", [(i, i + 1) for i in range(dp_count - 1)])
    down = lax.ppermute(kv, "dp", [(i + 1, i) for i in range(dp_count - 1)])

    lines = [[(i + 1, i) for i in range(pipe_count - 1)], [(i, i + 1) for i in range(pipe_count - 1)]]
    gains = [lax.ppermute(gain[0, c], "pipe", [(j, i) for i, j in lines[c]]) for c in range(2)]
    q, gains = lax.optimization_barrier((q, gains))
    wide = jax.ShapeDtypeStruct((2, BLK, width), jnp.float32)
    row_spec = pl.BlockSpec((1, BLK, lanes), lambda c, g: (c, 0, g))
    pair_spec = pl.BlockSpec((2, 1, BLK, lanes), lambda c, g: (0, c, 0, g))
    acc, maxes, sums = pl.pallas_call(
        functools.partial(local_kernel, group),
        grid=(2, steps),
        out_shape=[wide] * 3,
        in_specs=[
            smem(),
            smem(),
            row_spec,
            pair_spec,
            pl.BlockSpec((2, 1, glob_count, lanes), lambda c, g: (0, c, 0, g)),
        ],
        out_specs=[row_spec] * 3,
        compiler_params=params,
        cost_estimate=pl.CostEstimate(
            flops=4 * 2 * BLK * width * (glob_count + BLK), bytes_accessed=14 * 2**20, transcendentals=0
        ),
    )(ids, length, q, kv, glob)

    kv, acc = lax.optimization_barrier((kv, acc))

    tile = (2, capacity, 2, BLK, HD)
    take, tiles_all = pl.pallas_call(
        pack_kernel,
        out_shape=[
            jax.ShapeDtypeStruct((dp_count, 2, capacity), jnp.int32),
            jax.ShapeDtypeStruct((dp_count,) + tile, jnp.bfloat16),
        ],
        in_specs=[smem(), vmem()],
        out_specs=[smem(), vmem()],
        scratch_shapes=[pltpu.SMEM((1, 2, capacity), jnp.int32)],
        compiler_params=params,
    )(ids, kv)
    far = [(take, lax.all_to_all(tiles_all, "dp", split_axis=0, concat_axis=0, tiled=True))]

    acc, maxes, sums, updated, squares = pl.pallas_call(
        window_kernel,
        out_shape=[wide] * 3
        + [jax.ShapeDtypeStruct((2, BLK, width), jnp.bfloat16), jax.ShapeDtypeStruct((2, BLK, HD), jnp.float32)],
        in_specs=[smem(), smem()] + [vmem()] * 7,
        out_specs=[vmem()] * 5,
        compiler_params=params,
        cost_estimate=pl.CostEstimate(
            flops=4 * 2 * BLK * width * 2 * BLK, bytes_accessed=9 * 2**20, transcendentals=0
        ),
    )(ids, length, q, up, down, res, acc, maxes, sums)

    for heads_taken, tiles_got in far:
        updated, squares = pl.pallas_call(
            far_kernel,
            out_shape=[
                jax.ShapeDtypeStruct((2, BLK, width), jnp.bfloat16),
                jax.ShapeDtypeStruct((2, BLK, HD), jnp.float32),
            ],
            in_specs=[smem(), smem(), smem()] + [vmem()] * 8,
            out_specs=[vmem()] * 2,
            input_output_aliases={9: 0},
            compiler_params=params,
        )(ids, heads_taken, length, tiles_got, q, res, acc, maxes, sums, updated, squares)

    total = lax.psum(jnp.sum(squares, axis=2), "tensor")
    inverse = lax.rsqrt(total / D + epsilon)
    normed = [
        (updated[c].astype(jnp.float32) * inverse[c][:, None] * gains[c].astype(jnp.float32)).astype(jnp.bfloat16)
        for c in range(2)
    ]
    return jnp.stack([lax.ppermute(normed[c], "pipe", lines[c]) for c in range(2)])[None]


def pair_queries(first, second):
    none = jnp.zeros_like(first)
    return jnp.concatenate(
        [jnp.concatenate([first, none], axis=1), jnp.concatenate([none, second], axis=1)], axis=0
    )


def pair_rows(first, second, lanes):
    return jnp.concatenate([jnp.broadcast_to(first, (BLK, lanes)), jnp.broadcast_to(second, (BLK, lanes))], axis=0)


def pair_context(weights, values):
    both = dot_nn(weights.astype(jnp.bfloat16), values)
    return jnp.concatenate([both[:BLK, :HD], both[BLK:, HD:]], axis=0)


LENGTH = 32


def sent_in(turn):
    parity = lax.rem(lax.axis_index("pipe"), 2)
    return parity if turn == 0 else 1 - parity


def copy_heads(out_ref, list_ref, row, source_ref):
    for s in range(out_ref.shape[0]):
        cols = pl.ds(pl.multiple_of(jnp.maximum(list_ref[row, s], 0) * HD, HD), HD)
        out_ref[s, 0] = source_ref[0, :, cols]
        out_ref[s, 1] = source_ref[1, :, cols]


def list_heads(list_ref, row, heads, block, block_of):
    capacity = list_ref.shape[1]
    for s in range(capacity):
        list_ref[row, s] = 0
    slot = jnp.int32(0)
    for h in range(heads):
        match = (block_of(h) == block) & (slot < capacity)

        @pl.when(match)
        def _(slot=slot, h=h):
            list_ref[row, slot] = h

        slot = slot + match.astype(jnp.int32)


def distant_kernel(ids_ref, kv0_ref, kv1_ref, tile0_ref, tile1_ref, list_ref):
    me = lax.axis_index("dp")
    heads = ids_ref.shape[1]

    @pl.when((me == 0) | (me == 3))
    def _():
        for turn, (kv_ref, tile_ref) in enumerate(((kv0_ref, tile0_ref), (kv1_ref, tile1_ref))):
            c = sent_in(turn)
            list_heads(list_ref, 0, heads, me, lambda h, c=c: ids_ref[c, h])
            copy_heads(tile_ref, list_ref, 0, kv_ref)


def forward_kernel(turn, ids_ref, up_ids_ref, down_ids_ref, kv_ref, up_ref, down_ref, tile_ref, list_ref):
    me = lax.axis_index("dp")
    heads = ids_ref.shape[1]
    c = sent_in(turn)
    edge = (me == 0) | (me == 3)
    list_heads(
        list_ref,
        0,
        heads,
        jnp.where(edge, me, 3 - me),
        lambda h: jnp.where(edge, ids_ref[c, h], jnp.where(me == 1, up_ids_ref[h], down_ids_ref[h])),
    )
    pl.when(edge)(lambda: copy_heads(tile_ref, list_ref, 0, kv_ref))
    pl.when(me == 1)(lambda: copy_heads(tile_ref, list_ref, 0, down_ref))
    pl.when(me == 2)(lambda: copy_heads(tile_ref, list_ref, 0, up_ref))


def message_kernel(heads_step, order_ref, ids_ref, len_ref, q_ref, res_ref, kv_ref, gkv_ref, *out_refs):
    me = lax.axis_index("dp")
    turn = pl.program_id(0)
    g = pl.program_id(1)
    c = order_ref[turn]
    glob = gkv_ref.shape[2]
    width = out_refs[0].shape[1] - HD
    heads = width // HD
    place = lax.broadcasted_iota(jnp.int32, (1, HD), 1)

    def start_state(out_ref):
        note = jnp.where(place == LENGTH, len_ref[c], 0)
        for h in range(heads):
            note = jnp.where(place == h, ids_ref[c, h], note)
        note = jnp.broadcast_to(note.astype(jnp.float32), (BLK, HD)).astype(jnp.bfloat16)
        out_ref[:BLK, width:] = note
        out_ref[BLK:, width:] = jnp.zeros((2 * BLK, HD), jnp.bfloat16)

    for n, out_ref in enumerate(out_refs):
        pl.when((g == 0) & (turn == n))(functools.partial(start_state, out_ref))

    own_live = me < len_ref[c]
    numbers = range(0, heads_step, 2)

    def score(n):
        both = slice(n * HD, (n + 2) * HD)
        q = pair_queries(q_ref[0, :, n * HD : (n + 1) * HD], q_ref[0, :, (n + 1) * HD : (n + 2) * HD])
        k = jnp.concatenate([gkv_ref[0, 0, :, both], kv_ref[0, 0, :, both]], axis=0)
        own = [
            jnp.where(own_live, jnp.where(ids_ref[c, g * heads_step + n + i] == me, 1.0, 0.0), NEG) for i in range(2)
        ]
        s = dot_nt(q, k) * SCALE
        return jnp.concatenate([s[:, :glob], s[:, glob:] + pair_rows(*own, BLK)], axis=1)

    def weigh(s):
        m = jnp.max(s, axis=1, keepdims=True)
        p = jnp.exp2(s - m)
        l = jnp.sum(p, axis=1, keepdims=True)
        return p.astype(jnp.bfloat16), l, m + jnp.log2(l)

    def finish(n, p, l):
        both = slice(n * HD, (n + 2) * HD)
        v = jnp.concatenate([gkv_ref[1, 0, :, both], kv_ref[1, 0, :, both]], axis=0)
        return (pair_context(p, v) / l).astype(jnp.bfloat16)

    contexts, levels = [], []
    scored = weighed = None
    for t in range(len(numbers) + 2):
        fresh = score(numbers[t]) if t < len(numbers) else None
        ready = None
        if scored is not None:
            p, l, level = weigh(scored)
            ready = (p, l)
            levels.append(level)
        if weighed is not None:
            contexts.append(finish(numbers[t - 2], *weighed))
        scored, weighed = fresh, ready

    def write(out_ref):
        state = out_ref[2 * BLK :, width:].astype(jnp.float32)
        for n, context, level in zip(numbers, contexts, levels):
            high = level.astype(jnp.bfloat16).astype(jnp.float32)
            middle = (level - high).astype(jnp.bfloat16).astype(jnp.float32)
            low = level - high - middle
            for i in range(2):
                rows = slice(i * BLK, (i + 1) * BLK)
                head = g * heads_step + n + i
                at = place - head
                state = jnp.where(
                    at == 0, high[rows], jnp.where(at == 32, middle[rows], jnp.where(at == 64, low[rows], state))
                )
                col = slice((n + i) * HD, (n + i + 1) * HD)
                out = pl.ds(pl.multiple_of(head * HD, HD), HD)
                out_ref[:BLK, out] = q_ref[0, :, col]
                out_ref[BLK : 2 * BLK, out] = res_ref[0, :, col]
                out_ref[2 * BLK :, out] = context[rows]
        out_ref[2 * BLK :, width:] = state.astype(jnp.bfloat16)

    for n, out_ref in enumerate(out_refs):
        pl.when(turn == n)(functools.partial(write, out_ref))


def near_kernel(info_ref, message_ref, up_ref, down_ref, acc_ref, max_ref, sum_ref, out_ref, sq_ref, take_ref):
    me = lax.axis_index("dp")
    width = out_ref.shape[1]
    heads = width // HD
    batch = head_batch(heads)
    length = info_ref[LENGTH]
    alive = me < length
    up_live = (me >= 1) & (me - 1 < length)
    down_live = me + 1 < length
    list_heads(take_ref, 0, heads, jnp.where(me < 2, me + 2, me - 2), lambda h: info_ref[h])
    list_heads(take_ref, 1, heads, 3 - me, lambda h: info_ref[h])
    lane = lax.broadcasted_iota(jnp.int32, (1, 2 * BLK), 1)
    state = message_ref[2 * BLK :, width:].astype(jnp.float32)
    state = state + pltpu.roll(state, 96, 1) + pltpu.roll(state, 64, 1)
    squares = jnp.zeros((BLK, HD), jnp.float32)

    def score(numbers):
        items = []
        for h in numbers:
            col = slice(h * HD, (h + 1) * HD)
            block = info_ref[h]
            up_bias = jnp.where(up_live, jnp.where(block == me - 1, 1.0, 0.0), NEG)
            down_bias = jnp.where(down_live, jnp.where(block == me + 1, 1.0, 0.0), NEG)
            bias = jnp.where(lane < BLK, up_bias, down_bias)
            k = jnp.concatenate([up_ref[0, :, col], down_ref[0, :, col]], axis=0)
            v = jnp.concatenate([up_ref[1, :, col], down_ref[1, :, col]], axis=0)
            s = dot_nt(message_ref[:BLK, col], k) * SCALE + bias
            level = jnp.broadcast_to(state[:, h : h + 1], (BLK, HD))
            near = jnp.where(jnp.abs(block - me) < 2, 1.0, 0.0)
            items.append((col, s, v, level, message_ref[BLK : 2 * BLK, col], message_ref[2 * BLK :, col], near))
        return items

    def weigh(items):
        outs = []
        for col, s, v, level, res, context, near in items:
            m = jnp.maximum(level, jnp.max(s, axis=1, keepdims=True))
            p = jnp.exp2(s - m).astype(jnp.bfloat16)
            outs.append((col, m, p, v, jnp.exp2(level - m), res, context, near))
        return outs

    def finish(items, squares):
        outs = []
        for col, m, p, v, alpha, res, context, near in items:
            pv = dot_nn(p, with_ones(v))
            l = alpha + pv[:, HD:]
            acc = alpha * context.astype(jnp.float32) + pv[:, :HD]
            updated = (res.astype(jnp.float32) + jnp.where(alive, acc / l, 0.0)).astype(jnp.bfloat16)
            wide = updated.astype(jnp.float32)
            squares = squares + wide * wide * near
            outs.append((col, m, l, acc, updated))
        for col, m, l, acc, updated in outs:
            max_ref[:, col] = m
            sum_ref[:, col] = l
            acc_ref[:, col] = acc
            out_ref[:, col] = updated
        return squares

    batches = [range(start, start + batch) for start in range(0, heads, batch)]
    scored = weighed = None
    for turn in range(len(batches) + 2):
        fresh = score(batches[turn]) if turn < len(batches) else None
        ready = weigh(scored) if scored else None
        if weighed:
            squares = finish(weighed, squares)
        scored, weighed = fresh, ready
    sq_ref[...] = squares


def tile_kernel(crossing, info_ref, take_ref, message_ref, tile2_ref, tile3_ref, acc_ref, max_ref, sum_ref, old_ref, old_sq_ref, out_ref, sq_ref):
    me = lax.axis_index("dp")
    width = old_ref.shape[1]
    out_ref[:, :width] = old_ref[...]
    sq_ref[...] = old_sq_ref[...]

    def work(row, tile_ref):
        slots = range(tile_ref.shape[0])
        chosen = [take_ref[row, s] for s in slots]
        cols = [pl.ds(pl.multiple_of(h * HD, HD), HD) for h in chosen]
        live = [info_ref[h] < info_ref[LENGTH] for h in chosen]
        scores = [
            dot_nt(message_ref[:BLK, col], tile_ref[s, 0]) * SCALE + jnp.where(ok, 0.0, NEG)
            for s, col, ok in zip(slots, cols, live)
        ]
        before = [(max_ref[:, col], sum_ref[:, col], acc_ref[:, col]) for col in cols]
        residuals = [message_ref[BLK : 2 * BLK, col].astype(jnp.float32) for col in cols]
        news = merge(scores, before, [tile_ref[s, 1] for s in slots])
        updates = [
            (res + jnp.where(me < info_ref[LENGTH], acc / l, 0.0)).astype(jnp.bfloat16)
            for res, (_, l, acc) in zip(residuals, news)
        ]
        squares = jnp.zeros((BLK, HD), jnp.float32)
        for col, updated in zip(cols, updates):
            out_ref[:, col] = updated
            wide = updated.astype(jnp.float32)
            squares = squares + wide * wide
        sq_ref[...] += squares

    pl.when((me == 0) | (me == 3))(lambda: work(1, tile3_ref))
    work(0, tile2_ref)
    if crossing:
        total = jnp.sum(sq_ref[...], axis=1, keepdims=True)
        high = total.astype(jnp.bfloat16).astype(jnp.float32)
        middle = (total - high).astype(jnp.bfloat16).astype(jnp.float32)
        lane = lax.broadcasted_iota(jnp.int32, (1, HD), 1)
        parts = jnp.where(lane == 0, high, jnp.where(lane == 1, middle, jnp.where(lane == 2, total - high - middle, 0.0)))
        out_ref[:, width:] = parts.astype(jnp.bfloat16)


def body_chain(residual, queries, keys_values, global_kv, block_ids, lengths, gain):
    width = residual.shape[-1]
    heads = width // HD
    pipe_count = lax.axis_size("pipe")
    group = head_group(heads)
    steps = heads // group
    lanes = group * HD
    capacity = heads // 4
    q, res, glob, kv, length = queries[0], residual[0], global_kv[0], keys_values[0], lengths[0]
    own_ids = block_ids[0, :, 0]
    glob_count = glob.shape[2]
    params = pltpu.CompilerParams(vmem_limit_bytes=VMEM_LIMIT)
    order = jnp.stack([sent_in(0), sent_in(1)])

    def send(array, turn, moves):
        pairs = []
        for p in range(pipe_count):
            if turn == 1:
                pairs += [(i * pipe_count + (p if direct else p ^ 1), j * pipe_count + (p ^ 1)) for i, j, direct in moves]
            elif 0 <= ((p + 1) ^ 1) - 1 < pipe_count:
                pairs += [(i * pipe_count + p, j * pipe_count + p) for i, j, _ in moves]
        return lax.ppermute(array, ("dp", "pipe"), pairs)

    ids_3 = lax.ppermute(own_ids, "dp", [(0, 3), (3, 0)])
    ids_2 = lax.ppermute(own_ids, "dp", [(2, 0), (1, 3)])
    kvs, ups, downs = [], [], []
    for turn in range(2):
        c = order[turn]
        note = jnp.pad(lax.dynamic_index_in_dim(own_ids, c, 0, keepdims=False), (0, HD - heads)).astype(jnp.bfloat16)
        note = jnp.broadcast_to(note, (2, BLK, HD))
        kvs.append(jnp.concatenate([lax.dynamic_index_in_dim(kv, c, 1, keepdims=False), note], axis=2))
    kv, ids_3, ids_2, *kvs = lax.optimization_barrier((kv, ids_3, ids_2, *kvs))
    for turn in range(2):
        ups.append(send(kvs[turn], turn, [(i, i + 1, True) for i in range(3)]))
        downs.append(send(kvs[turn], turn, [(i + 1, i, True) for i in range(3)]))

    message = jax.ShapeDtypeStruct((3 * BLK, width + HD), jnp.bfloat16)
    messages = pl.pallas_call(
        functools.partial(message_kernel, group),
        grid_spec=pltpu.PrefetchScalarGridSpec(
            num_scalar_prefetch=3,
            grid=(2, steps),
            in_specs=[
                pl.BlockSpec((1, BLK, lanes), lambda t, g, order, ids, length: (order[t], 0, g)),
                pl.BlockSpec((1, BLK, lanes), lambda t, g, order, ids, length: (order[t], 0, g)),
                pl.BlockSpec((2, 1, BLK, lanes), lambda t, g, order, ids, length: (0, order[t], 0, g)),
                pl.BlockSpec((2, 1, glob_count, lanes), lambda t, g, order, ids, length: (0, order[t], 0, g)),
            ],
            out_specs=[vmem(), vmem()],
        ),
        out_shape=[message, message],
        compiler_params=params,
    )(order, own_ids, length, q, res, kv, glob)

    messages = list(messages)
    messages[1], downs[1] = lax.optimization_barrier((messages[1], downs[1]))
    messages[1] = send(messages[1], 1, [(i, i, True) for i in range(4)])
    tiles = jax.ShapeDtypeStruct((capacity, 2, BLK, HD), jnp.bfloat16)
    distant = pl.pallas_call(
        distant_kernel,
        out_shape=[tiles, tiles],
        in_specs=[smem(), vmem(), vmem()],
        out_specs=[vmem(), vmem()],
        scratch_shapes=[pltpu.SMEM((1, capacity), jnp.int32)],
        compiler_params=params,
    )(ids_3, *kvs)
    distant = list(distant)
    distant[1], downs[0], ups[0], downs[1], ups[1] = lax.optimization_barrier((distant[1], downs[0], ups[0], downs[1], ups[1]))
    far_3 = [send(distant[turn], turn, [(0, 3, True), (3, 0, True)]) for turn in range(2)]

    far_2 = []
    for turn in range(2):
        array = pl.pallas_call(
            functools.partial(forward_kernel, turn),
            out_shape=tiles,
            in_specs=[smem()] * 3 + [vmem()] * 3,
            out_specs=vmem(),
            scratch_shapes=[pltpu.SMEM((1, capacity), jnp.int32)],
            compiler_params=params,
        )(
            ids_2,
            ups[turn][0, 0, width:].astype(jnp.int32),
            downs[turn][0, 0, width:].astype(jnp.int32),
            kvs[turn],
            ups[turn],
            downs[turn],
        )
        far_2.append(send(array, turn, [(0, 2, True), (3, 1, True), (2, 3, False), (1, 0, False)]))

    wide = jax.ShapeDtypeStruct((BLK, width), jnp.float32)
    row = jax.ShapeDtypeStruct((BLK, width), jnp.bfloat16)
    square = jax.ShapeDtypeStruct((BLK, HD), jnp.float32)
    infos = [array[0, width:].astype(jnp.int32) for array in messages]
    near = [
        pl.pallas_call(
            near_kernel,
            out_shape=[wide, wide, wide, row, square, jax.ShapeDtypeStruct((2, capacity), jnp.int32)],
            in_specs=[smem()] + [vmem()] * 3,
            out_specs=[vmem()] * 5 + [smem()],
            compiler_params=params,
        )(infos[turn], messages[turn], ups[turn], downs[turn])
        for turn in range(2)
    ]
    near = [list(items) for items in near]
    far_2[0], near[1][4] = lax.optimization_barrier((far_2[0], near[1][4]))
    done = [None, None]
    for turn in range(2):
        acc, top, total, updated, squares, take = near[turn]
        done[turn] = pl.pallas_call(
            functools.partial(tile_kernel, turn == 0),
            out_shape=[jax.ShapeDtypeStruct((BLK, width + (HD if turn == 0 else 0)), jnp.bfloat16), square],
            in_specs=[smem()] * 2 + [vmem()] * 8,
            out_specs=[vmem()] * 2,
            compiler_params=params,
        )(infos[turn], take, messages[turn], far_2[turn], far_3[turn], acc, top, total, updated, squares)

    crossing = [(p, ((p + 1) ^ 1) - 1) for p in range(pipe_count)]
    crossed = lax.ppermute(done[0][0], "pipe", [(p, other) for p, other in crossing if 0 <= other < pipe_count])
    parts = jnp.sum(crossed[:, width : width + 3].astype(jnp.float32), axis=1)
    total = lax.psum(jnp.stack([parts, jnp.sum(done[1][1], axis=1)]), "tensor")
    even = lax.rem(lax.axis_index("pipe"), 2) == 0
    pair = (crossed[:, :width], done[1][0])
    normed = []
    for c in range(2):
        first = even == (c == 1)
        arrived = jnp.where(first, pair[0], pair[1]).astype(jnp.float32)
        inverse = lax.rsqrt(jnp.where(first, total[0], total[1]) / D + epsilon)
        normed.append((arrived * inverse[:, None] * gain[0, c][None, :].astype(jnp.float32)).astype(jnp.bfloat16))
    return jnp.stack(normed)[None]


def body(*arrays):
    heads = arrays[0].shape[-1] // HD
    chain = lax.axis_size("dp") == 4 and lax.axis_size("pipe") % 2 == 0 and heads % 8 == 0 and heads <= 32
    return (body_chain if chain else body_any)(*arrays)


def solution(mesh):
    in_specs = (
        P("pipe", None, "dp", "tensor"),
        P("pipe", None, "dp", "tensor"),
        P("pipe", None, None, "dp", "tensor"),
        P("pipe", None, None, None, "tensor"),
        P("pipe", None, "dp", "tensor"),
        P("pipe", None),
        P("pipe", None, "tensor"),
    )
    out_specs = P("pipe", None, "dp", "tensor")
    return jax.shard_map(body, mesh=mesh, in_specs=in_specs, out_specs=out_specs, check_vma=False)
```

```python
import functools

import jax
import jax.numpy as jnp
from jax import lax
from jax.experimental import pallas as pl
from jax.experimental.pallas import tpu as pltpu
from jax.sharding import PartitionSpec as P

D = 6144
HD = 128
BLK = 64
LOG2E = 1.4426950408889634
SCALE = HD ** (-0.5) * LOG2E
NEG = -1e30
VMEM_LIMIT = 20 * 1024 * 1024
LOCAL_LIMIT = 40 * 1024 * 1024

epsilon = 1e-05


def dot_nt(a, b):
    return lax.dot_general(a, b, (((1,), (1,)), ((), ())), preferred_element_type=jnp.float32)


def dot_nn(a, b):
    return lax.dot_general(a, b, (((1,), (0,)), ((), ())), preferred_element_type=jnp.float32)


def with_ones(v):
    return jnp.concatenate([v, jnp.ones((v.shape[0], HD), v.dtype)], axis=1)


def head_group(heads):
    return max(g for g in range(1, 9) if heads % g == 0)


def head_batch(heads):
    return max(g for g in range(1, 5) if heads % g == 0)


def heads_wanted(table_ref, row, ids_ref, asker, block):
    heads, capacity = ids_ref.shape[2], table_ref.shape[2]
    for c in range(2):
        for s in range(capacity):
            table_ref[row, c, s] = -1
        slot = jnp.int32(0)
        for h in range(heads):
            match = (ids_ref[asker, c, h] == block) & (slot < capacity)

            @pl.when(match)
            def _(slot=slot, h=h, c=c):
                table_ref[row, c, slot] = h

            slot = slot + match.astype(jnp.int32)


def copy_tiles(out_ref, list_ref, row, c, source_ref):
    for s in range(out_ref.shape[0]):
        cols = pl.ds(pl.multiple_of(jnp.maximum(list_ref[row, c, s], 0) * HD, HD), HD)
        out_ref[s, 0] = source_ref[0, :, cols]
        out_ref[s, 1] = source_ref[1, :, cols]


def pack_kernel(ids_ref, kv_ref, take_ref, out_ref, list_ref):
    me = lax.axis_index("dp")

    @pl.loop(0, ids_ref.shape[0])
    def _(other):
        far = jnp.abs(other - me) >= 2
        heads_wanted(take_ref, other, ids_ref, me, jnp.where(far, other, -1))
        heads_wanted(list_ref, 0, ids_ref, other, jnp.where(far, me, -1))
        for c in range(2):
            copy_tiles(out_ref.at[other, c], list_ref, 0, c, kv_ref.at[:, c])


def local_kernel(heads_step, ids_ref, len_ref, q_ref, kv_ref, gkv_ref, acc_ref, max_ref, sum_ref):
    me = lax.axis_index("dp")
    c = pl.program_id(0)
    g = pl.program_id(1)
    glob = gkv_ref.shape[2]
    lane = lax.broadcasted_iota(jnp.int32, (1, glob + BLK), 1)
    batch = head_batch(heads_step)
    for start in range(0, heads_step, batch):
        cols = [slice(n * HD, (n + 1) * HD) for n in range(start, start + batch)]
        scores, values = [], []
        for n, col in zip(range(start, start + batch), cols):
            k = jnp.concatenate([gkv_ref[0, 0, :, col], kv_ref[0, 0, :, col]], axis=0)
            values.append(jnp.concatenate([gkv_ref[1, 0, :, col], kv_ref[1, 0, :, col]], axis=0))
            twice = jnp.where(ids_ref[me, c, g * heads_step + n] == me, 1.0, 0.0)
            bias = jnp.where(lane < glob, 0.0, jnp.where(me < len_ref[c], twice, NEG))
            scores.append(dot_nt(q_ref[0, :, col], k) * SCALE + bias)
        tops = [jnp.max(s, axis=1, keepdims=True) for s in scores]
        weights = [jnp.exp2(s - m).astype(jnp.bfloat16) for s, m in zip(scores, tops)]
        sums = [dot_nn(p, with_ones(v)) for p, v in zip(weights, values)]
        for col, m, pv in zip(cols, tops, sums):
            acc_ref[0, :, col] = pv[:, :HD]
            sum_ref[0, :, col] = pv[:, HD:]
            max_ref[0, :, col] = jnp.broadcast_to(m, (BLK, HD))


def merge(scores, olds, values):
    tops = [jnp.maximum(old[0], jnp.max(s, axis=1, keepdims=True)) for s, old in zip(scores, olds)]
    weights = [jnp.exp2(s - m[:, : s.shape[1]]).astype(jnp.bfloat16) for s, m in zip(scores, tops)]
    alphas = [jnp.exp2(old[0] - m) for old, m in zip(olds, tops)]
    added = [dot_nn(p, with_ones(v)) for p, v in zip(weights, values)]
    return [
        (m, alpha * old[1] + pv[:, HD:], alpha * old[2] + pv[:, :HD])
        for m, alpha, old, pv in zip(tops, alphas, olds, added)
    ]


def window_kernel(ids_ref, len_ref, q_ref, up_ref, down_ref, res_ref, acc_ref, max_ref, sum_ref, new_acc_ref, new_max_ref, new_sum_ref, out_ref, sq_ref):
    me = lax.axis_index("dp")
    heads = q_ref.shape[2] // HD
    batch = head_batch(heads)
    lane = lax.broadcasted_iota(jnp.int32, (1, 2 * BLK), 1)
    for c in range(2):
        length = len_ref[c]
        alive = me < length
        up_live = (me >= 1) & (me - 1 < length)
        down_live = me + 1 < length

        def step(g, squares, c=c, alive=alive, up_live=up_live, down_live=down_live):
            cols = [pl.ds(pl.multiple_of((g * batch + n) * HD, HD), HD) for n in range(batch)]
            blocks = [ids_ref[me, c, g * batch + n] for n in range(batch)]
            scores, values = [], []
            for block, col in zip(blocks, cols):
                up_bias = jnp.where(up_live, jnp.where(block == me - 1, 1.0, 0.0), NEG)
                down_bias = jnp.where(down_live, jnp.where(block == me + 1, 1.0, 0.0), NEG)
                bias = jnp.where(lane < BLK, up_bias, down_bias)
                k = jnp.concatenate([up_ref[0, c, :, col], down_ref[0, c, :, col]], axis=0)
                values.append(jnp.concatenate([up_ref[1, c, :, col], down_ref[1, c, :, col]], axis=0))
                scores.append(dot_nt(q_ref[c, :, col], k) * SCALE + bias)
            olds = [(max_ref[c, :, col], sum_ref[c, :, col], acc_ref[c, :, col]) for col in cols]
            residuals = [res_ref[c, :, col].astype(jnp.float32) for col in cols]
            news = merge(scores, olds, values)
            updates = [
                (res + jnp.where(alive, acc / l, 0.0)).astype(jnp.bfloat16) for res, (_, l, acc) in zip(residuals, news)
            ]
            for block, col, (m, l, acc), updated in zip(blocks, cols, news, updates):
                new_max_ref[c, :, col] = m
                new_sum_ref[c, :, col] = l
                new_acc_ref[c, :, col] = acc
                out_ref[c, :, col] = updated
                wide = updated.astype(jnp.float32)
                squares = squares + wide * wide * jnp.where(jnp.abs(block - me) < 2, 1.0, 0.0)
            return squares

        sq_ref[c] = lax.fori_loop(0, heads // batch, step, jnp.zeros((BLK, HD), jnp.float32))


def far_kernel(ids_ref, take_ref, len_ref, tile_ref, q_ref, res_ref, acc_ref, max_ref, sum_ref, old_ref, old_sq_ref, out_ref, sq_ref):
    del old_ref
    me = lax.axis_index("dp")
    owners, _, capacity = take_ref.shape
    sq_ref[...] = old_sq_ref[...]

    def one_owner(owner):
        places = [(c, s) for c in range(2) for s in range(capacity)]
        taken = [take_ref[owner, c, s] for c, s in places]
        chosen = [jnp.maximum(h, 0) for h in taken]
        cols = [pl.ds(pl.multiple_of(h * HD, HD), HD) for h in chosen]
        live = [(t >= 0) & (ids_ref[me, c, h] < len_ref[c]) for (c, _), t, h in zip(places, taken, chosen)]
        scores = [
            dot_nt(q_ref[c, :, col], tile_ref[owner, c, s, 0]) * SCALE + jnp.where(ok, 0.0, NEG)
            for (c, s), col, ok in zip(places, cols, live)
        ]
        olds = [(max_ref[c, :, col], sum_ref[c, :, col], acc_ref[c, :, col]) for (c, _), col in zip(places, cols)]
        residuals = [res_ref[c, :, col].astype(jnp.float32) for (c, _), col in zip(places, cols)]
        news = merge(scores, olds, [tile_ref[owner, c, s, 1] for c, s in places])
        updates = [
            (res + jnp.where(me < len_ref[c], acc / l, 0.0)).astype(jnp.bfloat16)
            for (c, _), res, (_, l, acc) in zip(places, residuals, news)
        ]
        squares = [jnp.zeros((BLK, HD), jnp.float32)] * 2
        for (c, _), t, updated in zip(places, taken, updates):
            wide = updated.astype(jnp.float32)
            squares[c] = squares[c] + wide * wide * jnp.where(t >= 0, 1.0, 0.0)
        for c in range(2):
            sq_ref[c] += squares[c]
        for (c, _), t, col, updated in zip(places, taken, cols, updates):

            @pl.when(t >= 0)
            def _(c=c, col=col, updated=updated):
                out_ref[c, :, col] = updated

    pl.loop(0, owners)(one_owner)


def smem():
    return pl.BlockSpec(memory_space=pltpu.SMEM)


def vmem():
    return pl.BlockSpec(memory_space=pltpu.VMEM)


def body_any(residual, queries, keys_values, global_kv, block_ids, lengths, gain):
    width = residual.shape[-1]
    heads = width // HD
    dp_count = lax.axis_size("dp")
    pipe_count = lax.axis_size("pipe")
    tensor_count = lax.axis_size("tensor")
    group = head_group(heads)
    steps = heads // group
    lanes = group * HD
    capacity = (heads + dp_count - 1) // dp_count
    q = queries[0]
    res = residual[0]
    glob = global_kv[0]
    length = lengths[0]
    glob_count = glob.shape[2]
    params = pltpu.CompilerParams(vmem_limit_bytes=VMEM_LIMIT)

    ids = block_ids[0, :, 0]
    ids = lax.all_to_all(jnp.broadcast_to(ids, (dp_count,) + ids.shape), "dp", split_axis=0, concat_axis=0, tiled=True)
    kv, ids = lax.optimization_barrier((keys_values[0], ids))
    up = lax.ppermute(kv, "dp", [(i, i + 1) for i in range(dp_count - 1)])
    down = lax.ppermute(kv, "dp", [(i + 1, i) for i in range(dp_count - 1)])

    lines = [[(i + 1, i) for i in range(pipe_count - 1)], [(i, i + 1) for i in range(pipe_count - 1)]]
    gains = [lax.ppermute(gain[0, c], "pipe", [(j, i) for i, j in lines[c]]) for c in range(2)]
    q, gains = lax.optimization_barrier((q, gains))
    wide = jax.ShapeDtypeStruct((2, BLK, width), jnp.float32)
    row_spec = pl.BlockSpec((1, BLK, lanes), lambda c, g: (c, 0, g))
    pair_spec = pl.BlockSpec((2, 1, BLK, lanes), lambda c, g: (0, c, 0, g))
    acc, maxes, sums = pl.pallas_call(
        functools.partial(local_kernel, group),
        grid=(2, steps),
        out_shape=[wide] * 3,
        in_specs=[
            smem(),
            smem(),
            row_spec,
            pair_spec,
            pl.BlockSpec((2, 1, glob_count, lanes), lambda c, g: (0, c, 0, g)),
        ],
        out_specs=[row_spec] * 3,
        compiler_params=params,
        cost_estimate=pl.CostEstimate(
            flops=4 * 2 * BLK * width * (glob_count + BLK), bytes_accessed=14 * 2**20, transcendentals=0
        ),
    )(ids, length, q, kv, glob)

    kv, acc = lax.optimization_barrier((kv, acc))

    tile = (2, capacity, 2, BLK, HD)
    take, tiles_all = pl.pallas_call(
        pack_kernel,
        out_shape=[
            jax.ShapeDtypeStruct((dp_count, 2, capacity), jnp.int32),
            jax.ShapeDtypeStruct((dp_count,) + tile, jnp.bfloat16),
        ],
        in_specs=[smem(), vmem()],
        out_specs=[smem(), vmem()],
        scratch_shapes=[pltpu.SMEM((1, 2, capacity), jnp.int32)],
        compiler_params=params,
    )(ids, kv)
    far = [(take, lax.all_to_all(tiles_all, "dp", split_axis=0, concat_axis=0, tiled=True))]

    acc, maxes, sums, updated, squares = pl.pallas_call(
        window_kernel,
        out_shape=[wide] * 3
        + [jax.ShapeDtypeStruct((2, BLK, width), jnp.bfloat16), jax.ShapeDtypeStruct((2, BLK, HD), jnp.float32)],
        in_specs=[smem(), smem()] + [vmem()] * 7,
        out_specs=[vmem()] * 5,
        compiler_params=params,
        cost_estimate=pl.CostEstimate(
            flops=4 * 2 * BLK * width * 2 * BLK, bytes_accessed=9 * 2**20, transcendentals=0
        ),
    )(ids, length, q, up, down, res, acc, maxes, sums)

    for heads_taken, tiles_got in far:
        updated, squares = pl.pallas_call(
            far_kernel,
            out_shape=[
                jax.ShapeDtypeStruct((2, BLK, width), jnp.bfloat16),
                jax.ShapeDtypeStruct((2, BLK, HD), jnp.float32),
            ],
            in_specs=[smem(), smem(), smem()] + [vmem()] * 8,
            out_specs=[vmem()] * 2,
            input_output_aliases={9: 0},
            compiler_params=params,
        )(ids, heads_taken, length, tiles_got, q, res, acc, maxes, sums, updated, squares)

    total = lax.psum(jnp.sum(squares, axis=2), "tensor")
    inverse = lax.rsqrt(total / D + epsilon)
    normed = [
        (updated[c].astype(jnp.float32) * inverse[c][:, None] * gains[c].astype(jnp.float32)).astype(jnp.bfloat16)
        for c in range(2)
    ]
    return jnp.stack([lax.ppermute(normed[c], "pipe", lines[c]) for c in range(2)])[None]


def pair_queries(first, second):
    none = jnp.zeros_like(first)
    return jnp.concatenate(
        [jnp.concatenate([first, none], axis=1), jnp.concatenate([none, second], axis=1)], axis=0
    )


def pair_rows(first, second, lanes):
    return jnp.concatenate([jnp.broadcast_to(first, (BLK, lanes)), jnp.broadcast_to(second, (BLK, lanes))], axis=0)


def pair_context(weights, values):
    both = dot_nn(weights.astype(jnp.bfloat16), values)
    return jnp.concatenate([both[:BLK, :HD], both[BLK:, HD:]], axis=0)


LENGTH = 32


def sent_in(turn):
    parity = lax.rem(lax.axis_index("pipe"), 2)
    return parity if turn == 0 else 1 - parity


def copy_heads(out_ref, list_ref, row, source_ref):
    for s in range(out_ref.shape[0]):
        cols = pl.ds(pl.multiple_of(jnp.maximum(list_ref[row, s], 0) * HD, HD), HD)
        out_ref[s, 0] = source_ref[0, :, cols]
        out_ref[s, 1] = source_ref[1, :, cols]


def list_heads(list_ref, row, heads, block, block_of):
    capacity = list_ref.shape[1]
    for s in range(capacity):
        list_ref[row, s] = 0
    slot = jnp.int32(0)
    for h in range(heads):
        match = (block_of(h) == block) & (slot < capacity)

        @pl.when(match)
        def _(slot=slot, h=h):
            list_ref[row, slot] = h

        slot = slot + match.astype(jnp.int32)


def distant_kernel(ids_ref, kv0_ref, kv1_ref, tile0_ref, tile1_ref, list_ref):
    me = lax.axis_index("dp")
    heads = ids_ref.shape[1]

    @pl.when((me == 0) | (me == 3))
    def _():
        for turn, (kv_ref, tile_ref) in enumerate(((kv0_ref, tile0_ref), (kv1_ref, tile1_ref))):
            c = sent_in(turn)
            list_heads(list_ref, 0, heads, me, lambda h, c=c: ids_ref[c, h])
            copy_heads(tile_ref, list_ref, 0, kv_ref)


def forward_kernel(turn, ids_ref, up_ids_ref, down_ids_ref, kv_ref, up_ref, down_ref, tile_ref, list_ref):
    me = lax.axis_index("dp")
    heads = ids_ref.shape[1]
    c = sent_in(turn)
    edge = (me == 0) | (me == 3)
    list_heads(
        list_ref,
        0,
        heads,
        jnp.where(edge, me, 3 - me),
        lambda h: jnp.where(edge, ids_ref[c, h], jnp.where(me == 1, up_ids_ref[h], down_ids_ref[h])),
    )
    pl.when(edge)(lambda: copy_heads(tile_ref, list_ref, 0, kv_ref))
    pl.when(me == 1)(lambda: copy_heads(tile_ref, list_ref, 0, down_ref))
    pl.when(me == 2)(lambda: copy_heads(tile_ref, list_ref, 0, up_ref))


def message_kernel(heads_step, order_ref, ids_ref, len_ref, q_ref, res_ref, kv_ref, gkv_ref, *out_refs):
    me = lax.axis_index("dp")
    turn = pl.program_id(0)
    g = pl.program_id(1)
    c = order_ref[turn]
    glob = gkv_ref.shape[2]
    width = out_refs[0].shape[1] - HD
    heads = width // HD
    place = lax.broadcasted_iota(jnp.int32, (1, HD), 1)

    def start_state(out_ref):
        note = jnp.where(place == LENGTH, len_ref[c], 0)
        for h in range(heads):
            note = jnp.where(place == h, ids_ref[c, h], note)
        note = jnp.broadcast_to(note.astype(jnp.float32), (BLK, HD)).astype(jnp.bfloat16)
        out_ref[:BLK, width:] = note
        out_ref[BLK:, width:] = jnp.zeros((2 * BLK, HD), jnp.bfloat16)

    for n, out_ref in enumerate(out_refs):
        pl.when((g == 0) & (turn == n))(functools.partial(start_state, out_ref))

    own_live = me < len_ref[c]
    numbers = range(0, heads_step, 2)

    def score(n):
        both = slice(n * HD, (n + 2) * HD)
        q = pair_queries(q_ref[0, :, n * HD : (n + 1) * HD], q_ref[0, :, (n + 1) * HD : (n + 2) * HD])
        k = jnp.concatenate([gkv_ref[0, 0, :, both], kv_ref[0, 0, :, both]], axis=0)
        own = [
            jnp.where(own_live, jnp.where(ids_ref[c, g * heads_step + n + i] == me, 1.0, 0.0), NEG) for i in range(2)
        ]
        s = dot_nt(q, k) * SCALE
        return jnp.concatenate([s[:, :glob], s[:, glob:] + pair_rows(*own, BLK)], axis=1)

    def weigh(s):
        m = jnp.max(s, axis=1, keepdims=True)
        p = jnp.exp2(s - m)
        l = jnp.sum(p, axis=1, keepdims=True)
        return p.astype(jnp.bfloat16), l, m + jnp.log2(l)

    def finish(n, p, l):
        both = slice(n * HD, (n + 2) * HD)
        v = jnp.concatenate([gkv_ref[1, 0, :, both], kv_ref[1, 0, :, both]], axis=0)
        return (pair_context(p, v) / l).astype(jnp.bfloat16)

    contexts, levels = [], []
    scored = weighed = None
    for t in range(len(numbers) + 2):
        fresh = score(numbers[t]) if t < len(numbers) else None
        ready = None
        if scored is not None:
            p, l, level = weigh(scored)
            ready = (p, l)
            levels.append(level)
        if weighed is not None:
            contexts.append(finish(numbers[t - 2], *weighed))
        scored, weighed = fresh, ready

    def write(out_ref):
        state = out_ref[2 * BLK :, width:].astype(jnp.float32)
        for n, context, level in zip(numbers, contexts, levels):
            high = level.astype(jnp.bfloat16).astype(jnp.float32)
            middle = (level - high).astype(jnp.bfloat16).astype(jnp.float32)
            low = level - high - middle
            for i in range(2):
                rows = slice(i * BLK, (i + 1) * BLK)
                head = g * heads_step + n + i
                at = place - head
                state = jnp.where(
                    at == 0, high[rows], jnp.where(at == 32, middle[rows], jnp.where(at == 64, low[rows], state))
                )
                col = slice((n + i) * HD, (n + i + 1) * HD)
                out = pl.ds(pl.multiple_of(head * HD, HD), HD)
                out_ref[:BLK, out] = q_ref[0, :, col]
                out_ref[BLK : 2 * BLK, out] = res_ref[0, :, col]
                out_ref[2 * BLK :, out] = context[rows]
        out_ref[2 * BLK :, width:] = state.astype(jnp.bfloat16)

    for n, out_ref in enumerate(out_refs):
        pl.when(turn == n)(functools.partial(write, out_ref))


def near_kernel(info_ref, message_ref, up_ref, down_ref, acc_ref, max_ref, sum_ref, out_ref, sq_ref, take_ref):
    me = lax.axis_index("dp")
    width = out_ref.shape[1]
    heads = width // HD
    batch = head_batch(heads)
    length = info_ref[LENGTH]
    alive = me < length
    up_live = (me >= 1) & (me - 1 < length)
    down_live = me + 1 < length
    list_heads(take_ref, 0, heads, jnp.where(me < 2, me + 2, me - 2), lambda h: info_ref[h])
    list_heads(take_ref, 1, heads, 3 - me, lambda h: info_ref[h])
    lane = lax.broadcasted_iota(jnp.int32, (1, 2 * BLK), 1)
    state = message_ref[2 * BLK :, width:].astype(jnp.float32)
    state = state + pltpu.roll(state, 96, 1) + pltpu.roll(state, 64, 1)
    squares = jnp.zeros((BLK, HD), jnp.float32)

    def score(numbers):
        items = []
        for h in numbers:
            col = slice(h * HD, (h + 1) * HD)
            block = info_ref[h]
            up_bias = jnp.where(up_live, jnp.where(block == me - 1, 1.0, 0.0), NEG)
            down_bias = jnp.where(down_live, jnp.where(block == me + 1, 1.0, 0.0), NEG)
            bias = jnp.where(lane < BLK, up_bias, down_bias)
            k = jnp.concatenate([up_ref[0, :, col], down_ref[0, :, col]], axis=0)
            v = jnp.concatenate([up_ref[1, :, col], down_ref[1, :, col]], axis=0)
            s = dot_nt(message_ref[:BLK, col], k) * SCALE + bias
            level = jnp.broadcast_to(state[:, h : h + 1], (BLK, HD))
            near = jnp.where(jnp.abs(block - me) < 2, 1.0, 0.0)
            items.append((col, s, v, level, message_ref[BLK : 2 * BLK, col], message_ref[2 * BLK :, col], near))
        return items

    def weigh(items):
        outs = []
        for col, s, v, level, res, context, near in items:
            m = jnp.maximum(level, jnp.max(s, axis=1, keepdims=True))
            p = jnp.exp2(s - m).astype(jnp.bfloat16)
            outs.append((col, m, p, v, jnp.exp2(level - m), res, context, near))
        return outs

    def finish(items, squares):
        outs = []
        for col, m, p, v, alpha, res, context, near in items:
            pv = dot_nn(p, with_ones(v))
            l = alpha + pv[:, HD:]
            acc = alpha * context.astype(jnp.float32) + pv[:, :HD]
            updated = (res.astype(jnp.float32) + jnp.where(alive, acc / l, 0.0)).astype(jnp.bfloat16)
            wide = updated.astype(jnp.float32)
            squares = squares + wide * wide * near
            outs.append((col, m, l, acc, updated))
        for col, m, l, acc, updated in outs:
            max_ref[:, col] = m
            sum_ref[:, col] = l
            acc_ref[:, col] = acc
            out_ref[:, col] = updated
        return squares

    batches = [range(start, start + batch) for start in range(0, heads, batch)]
    scored = weighed = None
    for turn in range(len(batches) + 2):
        fresh = score(batches[turn]) if turn < len(batches) else None
        ready = weigh(scored) if scored else None
        if weighed:
            squares = finish(weighed, squares)
        scored, weighed = fresh, ready
    sq_ref[...] = squares


def tile_kernel(crossing, info_ref, take_ref, message_ref, tile2_ref, tile3_ref, acc_ref, max_ref, sum_ref, old_ref, old_sq_ref, *rest):
    out_ref, sq_ref = rest[-2:]
    me = lax.axis_index("dp")
    width = old_ref.shape[1]
    out_ref[:, :width] = old_ref[...]
    sq_ref[...] = old_sq_ref[...]

    def work(row, tile_ref):
        slots = range(tile_ref.shape[0])
        chosen = [take_ref[row, s] for s in slots]
        cols = [pl.ds(pl.multiple_of(h * HD, HD), HD) for h in chosen]
        live = [info_ref[h] < info_ref[LENGTH] for h in chosen]
        scores = [
            dot_nt(message_ref[:BLK, col], tile_ref[s, 0]) * SCALE + jnp.where(ok, 0.0, NEG)
            for s, col, ok in zip(slots, cols, live)
        ]
        before = [(max_ref[:, col], sum_ref[:, col], acc_ref[:, col]) for col in cols]
        residuals = [message_ref[BLK : 2 * BLK, col].astype(jnp.float32) for col in cols]
        news = merge(scores, before, [tile_ref[s, 1] for s in slots])
        updates = [
            (res + jnp.where(me < info_ref[LENGTH], acc / l, 0.0)).astype(jnp.bfloat16)
            for res, (_, l, acc) in zip(residuals, news)
        ]
        squares = jnp.zeros((BLK, HD), jnp.float32)
        for col, updated in zip(cols, updates):
            out_ref[:, col] = updated
            wide = updated.astype(jnp.float32)
            squares = squares + wide * wide
        sq_ref[...] += squares

    pl.when((me == 0) | (me == 3))(lambda: work(1, tile3_ref))
    work(0, tile2_ref)
    if crossing:
        total = jnp.sum(sq_ref[...], axis=1, keepdims=True)
        high = total.astype(jnp.bfloat16).astype(jnp.float32)
        middle = (total - high).astype(jnp.bfloat16).astype(jnp.float32)
        lane = lax.broadcasted_iota(jnp.int32, (1, HD), 1)
        parts = jnp.where(lane == 0, high, jnp.where(lane == 1, middle, jnp.where(lane == 2, total - high - middle, 0.0)))
        out_ref[:, width:] = parts.astype(jnp.bfloat16)


def body_chain(residual, queries, keys_values, global_kv, block_ids, lengths, gain):
    width = residual.shape[-1]
    heads = width // HD
    pipe_count = lax.axis_size("pipe")
    group = head_group(heads)
    steps = heads // group
    lanes = group * HD
    capacity = heads // 4
    q, res, glob, kv, length = queries[0], residual[0], global_kv[0], keys_values[0], lengths[0]
    own_ids = block_ids[0, :, 0]
    glob_count = glob.shape[2]
    params = pltpu.CompilerParams(vmem_limit_bytes=VMEM_LIMIT)
    order = jnp.stack([sent_in(0), sent_in(1)])

    def send(array, turn, moves):
        pairs = []
        for p in range(pipe_count):
            if turn == 1:
                pairs += [(i * pipe_count + (p if direct else p ^ 1), j * pipe_count + (p ^ 1)) for i, j, direct in moves]
            elif 0 <= ((p + 1) ^ 1) - 1 < pipe_count:
                pairs += [(i * pipe_count + p, j * pipe_count + p) for i, j, _ in moves]
        return lax.ppermute(array, ("dp", "pipe"), pairs)

    ids_3 = lax.ppermute(own_ids, "dp", [(0, 3), (3, 0)])
    ids_2 = lax.ppermute(own_ids, "dp", [(2, 0), (1, 3)])
    kvs, ups, downs = [], [], []
    for turn in range(2):
        c = order[turn]
        note = jnp.pad(lax.dynamic_index_in_dim(own_ids, c, 0, keepdims=False), (0, HD - heads)).astype(jnp.bfloat16)
        note = jnp.broadcast_to(note, (2, BLK, HD))
        kvs.append(jnp.concatenate([lax.dynamic_index_in_dim(kv, c, 1, keepdims=False), note], axis=2))
    kv, ids_3, ids_2, *kvs = lax.optimization_barrier((kv, ids_3, ids_2, *kvs))
    for turn in range(2):
        ups.append(send(kvs[turn], turn, [(i, i + 1, True) for i in range(3)]))
        downs.append(send(kvs[turn], turn, [(i + 1, i, True) for i in range(3)]))

    message = jax.ShapeDtypeStruct((3 * BLK, width + HD), jnp.bfloat16)
    messages = pl.pallas_call(
        functools.partial(message_kernel, group),
        grid_spec=pltpu.PrefetchScalarGridSpec(
            num_scalar_prefetch=3,
            grid=(2, steps),
            in_specs=[
                pl.BlockSpec((1, BLK, lanes), lambda t, g, order, ids, length: (order[t], 0, g)),
                pl.BlockSpec((1, BLK, lanes), lambda t, g, order, ids, length: (order[t], 0, g)),
                pl.BlockSpec((2, 1, BLK, lanes), lambda t, g, order, ids, length: (0, order[t], 0, g)),
                pl.BlockSpec((2, 1, glob_count, lanes), lambda t, g, order, ids, length: (0, order[t], 0, g)),
            ],
            out_specs=[vmem(), vmem()],
        ),
        out_shape=[message, message],
        compiler_params=pltpu.CompilerParams(vmem_limit_bytes=LOCAL_LIMIT),
    )(order, own_ids, length, q, res, kv, glob)

    messages = list(messages)
    messages[1], downs[0], ups[0] = lax.optimization_barrier((messages[1], downs[0], ups[0]))
    messages[1] = send(messages[1], 1, [(i, i, True) for i in range(4)])
    tiles = jax.ShapeDtypeStruct((capacity, 2, BLK, HD), jnp.bfloat16)
    distant = pl.pallas_call(
        distant_kernel,
        out_shape=[tiles, tiles],
        in_specs=[smem(), vmem(), vmem()],
        out_specs=[vmem(), vmem()],
        scratch_shapes=[pltpu.SMEM((1, capacity), jnp.int32)],
        compiler_params=params,
    )(ids_3, *kvs)
    distant = list(distant)
    far_3 = [send(distant[turn], turn, [(0, 3, True), (3, 0, True)]) for turn in range(2)]

    far_2 = []
    for turn in range(2):
        forwarded = pl.pallas_call(
            functools.partial(forward_kernel, turn),
            out_shape=tiles,
            in_specs=[smem()] * 3 + [vmem()] * 3,
            out_specs=vmem(),
            scratch_shapes=[pltpu.SMEM((1, capacity), jnp.int32)],
            compiler_params=params,
        )(
            ids_2,
            ups[turn][0, 0, width:].astype(jnp.int32),
            downs[turn][0, 0, width:].astype(jnp.int32),
            kvs[turn],
            ups[turn],
            downs[turn],
        )
        far_2.append(send(forwarded, turn, [(0, 2, True), (3, 1, True), (2, 3, False), (1, 0, False)]))

    wide = jax.ShapeDtypeStruct((BLK, width), jnp.float32)
    row = jax.ShapeDtypeStruct((BLK, width), jnp.bfloat16)
    square = jax.ShapeDtypeStruct((BLK, HD), jnp.float32)
    infos = [array[0, width:].astype(jnp.int32) for array in messages]
    near = [
        pl.pallas_call(
            near_kernel,
            out_shape=[wide, wide, wide, row, square, jax.ShapeDtypeStruct((2, capacity), jnp.int32)],
            in_specs=[smem()] + [vmem()] * 3,
            out_specs=[vmem()] * 5 + [smem()],
            compiler_params=params,
        )(infos[turn], messages[turn], ups[turn], downs[turn])
        for turn in range(2)
    ]
    near = [list(items) for items in near]
    done = [None, None]
    for turn in range(2):
        acc, top, total, updated, squares, take = near[turn]
        done[turn] = pl.pallas_call(
            functools.partial(tile_kernel, turn == 0),
            out_shape=[jax.ShapeDtypeStruct((BLK, width + (HD if turn == 0 else 0)), jnp.bfloat16), square],
            in_specs=[smem()] * 2 + [vmem()] * 8 + [pl.BlockSpec(memory_space=pl.ANY)] * (1 - turn),
            out_specs=[vmem()] * 2,
            compiler_params=params,
        )(
            *(infos[turn], take, messages[turn], far_2[turn], far_3[turn], acc, top, total, updated, squares),
            *([forwarded] if turn == 0 else []),
        )

    crossing = [(p, ((p + 1) ^ 1) - 1) for p in range(pipe_count)]
    crossed = lax.ppermute(done[0][0], "pipe", [(p, other) for p, other in crossing if 0 <= other < pipe_count])
    parts = jnp.sum(crossed[:, width : width + 3].astype(jnp.float32), axis=1)
    total = lax.psum(jnp.stack([parts, jnp.sum(done[1][1], axis=1)]), "tensor")
    first = jnp.arange(2, dtype=jnp.int32) != sent_in(0)
    inverse = lax.rsqrt(jnp.where(first[:, None], total[0], total[1]) / D + epsilon)
    arrived = jnp.where(first[:, None, None], crossed[None, :, :width], done[1][0][None]).astype(jnp.float32)
    normed = arrived * inverse[:, :, None] * gain[0][:, None, :].astype(jnp.float32)
    return normed.astype(jnp.bfloat16)[None]


def body(*arrays):
    heads = arrays[0].shape[-1] // HD
    chain = lax.axis_size("dp") == 4 and lax.axis_size("pipe") % 2 == 0 and heads % 8 == 0 and heads <= 32
    return (body_chain if chain else body_any)(*arrays)


def solution(mesh):
    in_specs = (
        P("pipe", None, "dp", "tensor"),
        P("pipe", None, "dp", "tensor"),
        P("pipe", None, None, "dp", "tensor"),
        P("pipe", None, None, None, "tensor"),
        P("pipe", None, "dp", "tensor"),
        P("pipe", None),
        P("pipe", None, "tensor"),
    )
    out_specs = P("pipe", None, "dp", "tensor")
    return jax.shard_map(body, mesh=mesh, in_specs=in_specs, out_specs=out_specs, check_vma=False)
```

```python
import functools

import jax
import jax.numpy as jnp
from jax import lax
from jax.experimental import pallas as pl
from jax.experimental.pallas import tpu as pltpu
from jax.sharding import PartitionSpec as P

D = 6144
HD = 128
BLK = 64
LOG2E = 1.4426950408889634
SCALE = HD ** (-0.5) * LOG2E
NEG = -1e30
VMEM_LIMIT = 20 * 1024 * 1024
LOCAL_LIMIT = 40 * 1024 * 1024

epsilon = 1e-05


def dot_nt(a, b):
    return lax.dot_general(a, b, (((1,), (1,)), ((), ())), preferred_element_type=jnp.float32)


def dot_nn(a, b):
    return lax.dot_general(a, b, (((1,), (0,)), ((), ())), preferred_element_type=jnp.float32)


def with_ones(v):
    return jnp.concatenate([v, jnp.ones((v.shape[0], HD), v.dtype)], axis=1)


def head_group(heads):
    return max(g for g in range(1, 9) if heads % g == 0)


def head_batch(heads):
    return max(g for g in range(1, 5) if heads % g == 0)


def heads_wanted(table_ref, row, ids_ref, asker, block):
    heads, capacity = ids_ref.shape[2], table_ref.shape[2]
    for c in range(2):
        for s in range(capacity):
            table_ref[row, c, s] = -1
        slot = jnp.int32(0)
        for h in range(heads):
            match = (ids_ref[asker, c, h] == block) & (slot < capacity)

            @pl.when(match)
            def _(slot=slot, h=h, c=c):
                table_ref[row, c, slot] = h

            slot = slot + match.astype(jnp.int32)


def copy_tiles(out_ref, list_ref, row, c, source_ref):
    for s in range(out_ref.shape[0]):
        cols = pl.ds(pl.multiple_of(jnp.maximum(list_ref[row, c, s], 0) * HD, HD), HD)
        out_ref[s, 0] = source_ref[0, :, cols]
        out_ref[s, 1] = source_ref[1, :, cols]


def pack_kernel(ids_ref, kv_ref, take_ref, out_ref, list_ref):
    me = lax.axis_index("dp")

    @pl.loop(0, ids_ref.shape[0])
    def _(other):
        far = jnp.abs(other - me) >= 2
        heads_wanted(take_ref, other, ids_ref, me, jnp.where(far, other, -1))
        heads_wanted(list_ref, 0, ids_ref, other, jnp.where(far, me, -1))
        for c in range(2):
            copy_tiles(out_ref.at[other, c], list_ref, 0, c, kv_ref.at[:, c])


def local_kernel(heads_step, ids_ref, len_ref, q_ref, kv_ref, gkv_ref, acc_ref, max_ref, sum_ref):
    me = lax.axis_index("dp")
    c = pl.program_id(0)
    g = pl.program_id(1)
    glob = gkv_ref.shape[2]
    lane = lax.broadcasted_iota(jnp.int32, (1, glob + BLK), 1)
    batch = head_batch(heads_step)
    for start in range(0, heads_step, batch):
        cols = [slice(n * HD, (n + 1) * HD) for n in range(start, start + batch)]
        scores, values = [], []
        for n, col in zip(range(start, start + batch), cols):
            k = jnp.concatenate([gkv_ref[0, 0, :, col], kv_ref[0, 0, :, col]], axis=0)
            values.append(jnp.concatenate([gkv_ref[1, 0, :, col], kv_ref[1, 0, :, col]], axis=0))
            twice = jnp.where(ids_ref[me, c, g * heads_step + n] == me, 1.0, 0.0)
            bias = jnp.where(lane < glob, 0.0, jnp.where(me < len_ref[c], twice, NEG))
            scores.append(dot_nt(q_ref[0, :, col], k) * SCALE + bias)
        tops = [jnp.max(s, axis=1, keepdims=True) for s in scores]
        weights = [jnp.exp2(s - m).astype(jnp.bfloat16) for s, m in zip(scores, tops)]
        sums = [dot_nn(p, with_ones(v)) for p, v in zip(weights, values)]
        for col, m, pv in zip(cols, tops, sums):
            acc_ref[0, :, col] = pv[:, :HD]
            sum_ref[0, :, col] = pv[:, HD:]
            max_ref[0, :, col] = jnp.broadcast_to(m, (BLK, HD))


def merge(scores, olds, values):
    tops = [jnp.maximum(old[0], jnp.max(s, axis=1, keepdims=True)) for s, old in zip(scores, olds)]
    weights = [jnp.exp2(s - m[:, : s.shape[1]]).astype(jnp.bfloat16) for s, m in zip(scores, tops)]
    alphas = [jnp.exp2(old[0] - m) for old, m in zip(olds, tops)]
    added = [dot_nn(p, with_ones(v)) for p, v in zip(weights, values)]
    return [
        (m, alpha * old[1] + pv[:, HD:], alpha * old[2] + pv[:, :HD])
        for m, alpha, old, pv in zip(tops, alphas, olds, added)
    ]


def window_kernel(ids_ref, len_ref, q_ref, up_ref, down_ref, res_ref, acc_ref, max_ref, sum_ref, new_acc_ref, new_max_ref, new_sum_ref, out_ref, sq_ref):
    me = lax.axis_index("dp")
    heads = q_ref.shape[2] // HD
    batch = head_batch(heads)
    lane = lax.broadcasted_iota(jnp.int32, (1, 2 * BLK), 1)
    for c in range(2):
        length = len_ref[c]
        alive = me < length
        up_live = (me >= 1) & (me - 1 < length)
        down_live = me + 1 < length

        def step(g, squares, c=c, alive=alive, up_live=up_live, down_live=down_live):
            cols = [pl.ds(pl.multiple_of((g * batch + n) * HD, HD), HD) for n in range(batch)]
            blocks = [ids_ref[me, c, g * batch + n] for n in range(batch)]
            scores, values = [], []
            for block, col in zip(blocks, cols):
                up_bias = jnp.where(up_live, jnp.where(block == me - 1, 1.0, 0.0), NEG)
                down_bias = jnp.where(down_live, jnp.where(block == me + 1, 1.0, 0.0), NEG)
                bias = jnp.where(lane < BLK, up_bias, down_bias)
                k = jnp.concatenate([up_ref[0, c, :, col], down_ref[0, c, :, col]], axis=0)
                values.append(jnp.concatenate([up_ref[1, c, :, col], down_ref[1, c, :, col]], axis=0))
                scores.append(dot_nt(q_ref[c, :, col], k) * SCALE + bias)
            olds = [(max_ref[c, :, col], sum_ref[c, :, col], acc_ref[c, :, col]) for col in cols]
            residuals = [res_ref[c, :, col].astype(jnp.float32) for col in cols]
            news = merge(scores, olds, values)
            updates = [
                (res + jnp.where(alive, acc / l, 0.0)).astype(jnp.bfloat16) for res, (_, l, acc) in zip(residuals, news)
            ]
            for block, col, (m, l, acc), updated in zip(blocks, cols, news, updates):
                new_max_ref[c, :, col] = m
                new_sum_ref[c, :, col] = l
                new_acc_ref[c, :, col] = acc
                out_ref[c, :, col] = updated
                wide = updated.astype(jnp.float32)
                squares = squares + wide * wide * jnp.where(jnp.abs(block - me) < 2, 1.0, 0.0)
            return squares

        sq_ref[c] = lax.fori_loop(0, heads // batch, step, jnp.zeros((BLK, HD), jnp.float32))


def far_kernel(ids_ref, take_ref, len_ref, tile_ref, q_ref, res_ref, acc_ref, max_ref, sum_ref, old_ref, old_sq_ref, out_ref, sq_ref):
    del old_ref
    me = lax.axis_index("dp")
    owners, _, capacity = take_ref.shape
    sq_ref[...] = old_sq_ref[...]

    def one_owner(owner):
        places = [(c, s) for c in range(2) for s in range(capacity)]
        taken = [take_ref[owner, c, s] for c, s in places]
        chosen = [jnp.maximum(h, 0) for h in taken]
        cols = [pl.ds(pl.multiple_of(h * HD, HD), HD) for h in chosen]
        live = [(t >= 0) & (ids_ref[me, c, h] < len_ref[c]) for (c, _), t, h in zip(places, taken, chosen)]
        scores = [
            dot_nt(q_ref[c, :, col], tile_ref[owner, c, s, 0]) * SCALE + jnp.where(ok, 0.0, NEG)
            for (c, s), col, ok in zip(places, cols, live)
        ]
        olds = [(max_ref[c, :, col], sum_ref[c, :, col], acc_ref[c, :, col]) for (c, _), col in zip(places, cols)]
        residuals = [res_ref[c, :, col].astype(jnp.float32) for (c, _), col in zip(places, cols)]
        news = merge(scores, olds, [tile_ref[owner, c, s, 1] for c, s in places])
        updates = [
            (res + jnp.where(me < len_ref[c], acc / l, 0.0)).astype(jnp.bfloat16)
            for (c, _), res, (_, l, acc) in zip(places, residuals, news)
        ]
        squares = [jnp.zeros((BLK, HD), jnp.float32)] * 2
        for (c, _), t, updated in zip(places, taken, updates):
            wide = updated.astype(jnp.float32)
            squares[c] = squares[c] + wide * wide * jnp.where(t >= 0, 1.0, 0.0)
        for c in range(2):
            sq_ref[c] += squares[c]
        for (c, _), t, col, updated in zip(places, taken, cols, updates):

            @pl.when(t >= 0)
            def _(c=c, col=col, updated=updated):
                out_ref[c, :, col] = updated

    pl.loop(0, owners)(one_owner)


def smem():
    return pl.BlockSpec(memory_space=pltpu.SMEM)


def vmem():
    return pl.BlockSpec(memory_space=pltpu.VMEM)


def body_any(residual, queries, keys_values, global_kv, block_ids, lengths, gain):
    width = residual.shape[-1]
    heads = width // HD
    dp_count = lax.axis_size("dp")
    pipe_count = lax.axis_size("pipe")
    tensor_count = lax.axis_size("tensor")
    group = head_group(heads)
    steps = heads // group
    lanes = group * HD
    capacity = (heads + dp_count - 1) // dp_count
    q = queries[0]
    res = residual[0]
    glob = global_kv[0]
    length = lengths[0]
    glob_count = glob.shape[2]
    params = pltpu.CompilerParams(vmem_limit_bytes=VMEM_LIMIT)

    ids = block_ids[0, :, 0]
    ids = lax.all_to_all(jnp.broadcast_to(ids, (dp_count,) + ids.shape), "dp", split_axis=0, concat_axis=0, tiled=True)
    kv, ids = lax.optimization_barrier((keys_values[0], ids))
    up = lax.ppermute(kv, "dp", [(i, i + 1) for i in range(dp_count - 1)])
    down = lax.ppermute(kv, "dp", [(i + 1, i) for i in range(dp_count - 1)])

    lines = [[(i + 1, i) for i in range(pipe_count - 1)], [(i, i + 1) for i in range(pipe_count - 1)]]
    gains = [lax.ppermute(gain[0, c], "pipe", [(j, i) for i, j in lines[c]]) for c in range(2)]
    q, gains = lax.optimization_barrier((q, gains))
    wide = jax.ShapeDtypeStruct((2, BLK, width), jnp.float32)
    row_spec = pl.BlockSpec((1, BLK, lanes), lambda c, g: (c, 0, g))
    pair_spec = pl.BlockSpec((2, 1, BLK, lanes), lambda c, g: (0, c, 0, g))
    acc, maxes, sums = pl.pallas_call(
        functools.partial(local_kernel, group),
        grid=(2, steps),
        out_shape=[wide] * 3,
        in_specs=[
            smem(),
            smem(),
            row_spec,
            pair_spec,
            pl.BlockSpec((2, 1, glob_count, lanes), lambda c, g: (0, c, 0, g)),
        ],
        out_specs=[row_spec] * 3,
        compiler_params=params,
        cost_estimate=pl.CostEstimate(
            flops=4 * 2 * BLK * width * (glob_count + BLK), bytes_accessed=14 * 2**20, transcendentals=0
        ),
    )(ids, length, q, kv, glob)

    kv, acc = lax.optimization_barrier((kv, acc))

    tile = (2, capacity, 2, BLK, HD)
    take, tiles_all = pl.pallas_call(
        pack_kernel,
        out_shape=[
            jax.ShapeDtypeStruct((dp_count, 2, capacity), jnp.int32),
            jax.ShapeDtypeStruct((dp_count,) + tile, jnp.bfloat16),
        ],
        in_specs=[smem(), vmem()],
        out_specs=[smem(), vmem()],
        scratch_shapes=[pltpu.SMEM((1, 2, capacity), jnp.int32)],
        compiler_params=params,
    )(ids, kv)
    far = [(take, lax.all_to_all(tiles_all, "dp", split_axis=0, concat_axis=0, tiled=True))]

    acc, maxes, sums, updated, squares = pl.pallas_call(
        window_kernel,
        out_shape=[wide] * 3
        + [jax.ShapeDtypeStruct((2, BLK, width), jnp.bfloat16), jax.ShapeDtypeStruct((2, BLK, HD), jnp.float32)],
        in_specs=[smem(), smem()] + [vmem()] * 7,
        out_specs=[vmem()] * 5,
        compiler_params=params,
        cost_estimate=pl.CostEstimate(
            flops=4 * 2 * BLK * width * 2 * BLK, bytes_accessed=9 * 2**20, transcendentals=0
        ),
    )(ids, length, q, up, down, res, acc, maxes, sums)

    for heads_taken, tiles_got in far:
        updated, squares = pl.pallas_call(
            far_kernel,
            out_shape=[
                jax.ShapeDtypeStruct((2, BLK, width), jnp.bfloat16),
                jax.ShapeDtypeStruct((2, BLK, HD), jnp.float32),
            ],
            in_specs=[smem(), smem(), smem()] + [vmem()] * 8,
            out_specs=[vmem()] * 2,
            input_output_aliases={9: 0},
            compiler_params=params,
        )(ids, heads_taken, length, tiles_got, q, res, acc, maxes, sums, updated, squares)

    total = lax.psum(jnp.sum(squares, axis=2), "tensor")
    inverse = lax.rsqrt(total / D + epsilon)
    normed = [
        (updated[c].astype(jnp.float32) * inverse[c][:, None] * gains[c].astype(jnp.float32)).astype(jnp.bfloat16)
        for c in range(2)
    ]
    return jnp.stack([lax.ppermute(normed[c], "pipe", lines[c]) for c in range(2)])[None]


def pair_queries(first, second):
    none = jnp.zeros_like(first)
    return jnp.concatenate(
        [jnp.concatenate([first, none], axis=1), jnp.concatenate([none, second], axis=1)], axis=0
    )


def pair_rows(first, second, lanes):
    return jnp.concatenate([jnp.broadcast_to(first, (BLK, lanes)), jnp.broadcast_to(second, (BLK, lanes))], axis=0)


def pair_context(weights, values):
    both = dot_nn(weights.astype(jnp.bfloat16), values)
    return jnp.concatenate([both[:BLK, :HD], both[BLK:, HD:]], axis=0)


LENGTH = 32


def sent_in(turn):
    parity = lax.rem(lax.axis_index("pipe"), 2)
    return parity if turn == 0 else 1 - parity


def copy_heads(out_ref, list_ref, row, source_ref):
    for s in range(out_ref.shape[0]):
        cols = pl.ds(pl.multiple_of(jnp.maximum(list_ref[row, s], 0) * HD, HD), HD)
        out_ref[s, 0] = source_ref[0, :, cols]
        out_ref[s, 1] = source_ref[1, :, cols]


def list_heads(list_ref, row, heads, block, block_of):
    capacity = list_ref.shape[1]
    for s in range(capacity):
        list_ref[row, s] = 0
    slot = jnp.int32(0)
    for h in range(heads):
        match = (block_of(h) == block) & (slot < capacity)

        @pl.when(match)
        def _(slot=slot, h=h):
            list_ref[row, slot] = h

        slot = slot + match.astype(jnp.int32)


def distant_kernel(ids_ref, kv0_ref, kv1_ref, tile0_ref, tile1_ref, list_ref):
    me = lax.axis_index("dp")
    heads = ids_ref.shape[1]

    @pl.when((me == 0) | (me == 3))
    def _():
        for turn, (kv_ref, tile_ref) in enumerate(((kv0_ref, tile0_ref), (kv1_ref, tile1_ref))):
            c = sent_in(turn)
            list_heads(list_ref, 0, heads, me, lambda h, c=c: ids_ref[c, h])
            copy_heads(tile_ref, list_ref, 0, kv_ref)


def forward_kernel(turn, ids_ref, up_ids_ref, down_ids_ref, kv_ref, up_ref, down_ref, tile_ref, list_ref):
    me = lax.axis_index("dp")
    heads = ids_ref.shape[1]
    c = sent_in(turn)
    edge = (me == 0) | (me == 3)
    list_heads(
        list_ref,
        0,
        heads,
        jnp.where(edge, me, 3 - me),
        lambda h: jnp.where(edge, ids_ref[c, h], jnp.where(me == 1, up_ids_ref[h], down_ids_ref[h])),
    )
    pl.when(edge)(lambda: copy_heads(tile_ref, list_ref, 0, kv_ref))
    pl.when(me == 1)(lambda: copy_heads(tile_ref, list_ref, 0, down_ref))
    pl.when(me == 2)(lambda: copy_heads(tile_ref, list_ref, 0, up_ref))


def message_kernel(heads_step, order_ref, ids_ref, len_ref, q_ref, res_ref, kv_ref, gkv_ref, *out_refs):
    me = lax.axis_index("dp")
    turn = pl.program_id(0)
    g = pl.program_id(1)
    c = order_ref[turn]
    glob = gkv_ref.shape[2]
    width = out_refs[0].shape[1] - HD
    heads = width // HD
    place = lax.broadcasted_iota(jnp.int32, (1, HD), 1)

    def start_state(out_ref):
        note = jnp.where(place == LENGTH, len_ref[c], 0)
        for h in range(heads):
            note = jnp.where(place == h, ids_ref[c, h], note)
        note = jnp.broadcast_to(note.astype(jnp.float32), (BLK, HD)).astype(jnp.bfloat16)
        out_ref[:BLK, width:] = note
        out_ref[BLK:, width:] = jnp.zeros((2 * BLK, HD), jnp.bfloat16)

    for n, out_ref in enumerate(out_refs):
        pl.when((g == 0) & (turn == n))(functools.partial(start_state, out_ref))

    own_live = me < len_ref[c]
    numbers = range(0, heads_step, 2)

    def score(n):
        both = slice(n * HD, (n + 2) * HD)
        q = pair_queries(q_ref[0, :, n * HD : (n + 1) * HD], q_ref[0, :, (n + 1) * HD : (n + 2) * HD])
        k = jnp.concatenate([gkv_ref[0, 0, :, both], kv_ref[0, 0, :, both]], axis=0)
        own = [
            jnp.where(own_live, jnp.where(ids_ref[c, g * heads_step + n + i] == me, 1.0, 0.0), NEG) for i in range(2)
        ]
        s = dot_nt(q, k) * SCALE
        return jnp.concatenate([s[:, :glob], s[:, glob:] + pair_rows(*own, BLK)], axis=1)

    def weigh(s):
        m = jnp.max(s, axis=1, keepdims=True)
        p = jnp.exp2(s - m)
        l = jnp.sum(p, axis=1, keepdims=True)
        return p.astype(jnp.bfloat16), l, m + jnp.log2(l)

    def finish(n, p, l):
        both = slice(n * HD, (n + 2) * HD)
        v = jnp.concatenate([gkv_ref[1, 0, :, both], kv_ref[1, 0, :, both]], axis=0)
        return (pair_context(p, v) / l).astype(jnp.bfloat16)

    contexts, levels = [], []
    scored = weighed = None
    for t in range(len(numbers) + 2):
        fresh = score(numbers[t]) if t < len(numbers) else None
        ready = None
        if scored is not None:
            p, l, level = weigh(scored)
            ready = (p, l)
            levels.append(level)
        if weighed is not None:
            contexts.append(finish(numbers[t - 2], *weighed))
        scored, weighed = fresh, ready

    def write(out_ref):
        state = out_ref[2 * BLK :, width:].astype(jnp.float32)
        for n, context, level in zip(numbers, contexts, levels):
            high = level.astype(jnp.bfloat16).astype(jnp.float32)
            middle = (level - high).astype(jnp.bfloat16).astype(jnp.float32)
            low = level - high - middle
            for i in range(2):
                rows = slice(i * BLK, (i + 1) * BLK)
                head = g * heads_step + n + i
                at = place - head
                state = jnp.where(
                    at == 0, high[rows], jnp.where(at == 32, middle[rows], jnp.where(at == 64, low[rows], state))
                )
                col = slice((n + i) * HD, (n + i + 1) * HD)
                out = pl.ds(pl.multiple_of(head * HD, HD), HD)
                out_ref[:BLK, out] = q_ref[0, :, col]
                out_ref[BLK : 2 * BLK, out] = res_ref[0, :, col]
                out_ref[2 * BLK :, out] = context[rows]
        out_ref[2 * BLK :, width:] = state.astype(jnp.bfloat16)

    for n, out_ref in enumerate(out_refs):
        pl.when(turn == n)(functools.partial(write, out_ref))


def near_kernel(info_ref, message_ref, up_ref, down_ref, acc_ref, max_ref, sum_ref, out_ref, sq_ref, take_ref):
    me = lax.axis_index("dp")
    width = out_ref.shape[1]
    heads = width // HD
    batch = head_batch(heads)
    length = info_ref[LENGTH]
    alive = me < length
    up_live = (me >= 1) & (me - 1 < length)
    down_live = me + 1 < length
    list_heads(take_ref, 0, heads, jnp.where(me < 2, me + 2, me - 2), lambda h: info_ref[h])
    list_heads(take_ref, 1, heads, 3 - me, lambda h: info_ref[h])
    lane = lax.broadcasted_iota(jnp.int32, (1, 2 * BLK), 1)
    state = message_ref[2 * BLK :, width:].astype(jnp.float32)
    state = state + pltpu.roll(state, 96, 1) + pltpu.roll(state, 64, 1)
    squares = jnp.zeros((BLK, HD), jnp.float32)

    def score(numbers):
        items = []
        for h in numbers:
            col = slice(h * HD, (h + 1) * HD)
            block = info_ref[h]
            up_bias = jnp.where(up_live, jnp.where(block == me - 1, 1.0, 0.0), NEG)
            down_bias = jnp.where(down_live, jnp.where(block == me + 1, 1.0, 0.0), NEG)
            bias = jnp.where(lane < BLK, up_bias, down_bias)
            k = jnp.concatenate([up_ref[0, :, col], down_ref[0, :, col]], axis=0)
            v = jnp.concatenate([up_ref[1, :, col], down_ref[1, :, col]], axis=0)
            s = dot_nt(message_ref[:BLK, col], k) * SCALE + bias
            level = jnp.broadcast_to(state[:, h : h + 1], (BLK, HD))
            near = jnp.where(jnp.abs(block - me) < 2, 1.0, 0.0)
            items.append((col, s, v, level, message_ref[BLK : 2 * BLK, col], message_ref[2 * BLK :, col], near))
        return items

    def weigh(items):
        outs = []
        for col, s, v, level, res, context, near in items:
            m = jnp.maximum(level, jnp.max(s, axis=1, keepdims=True))
            p = jnp.exp2(s - m).astype(jnp.bfloat16)
            outs.append((col, m, p, v, jnp.exp2(level - m), res, context, near))
        return outs

    def finish(items, squares):
        outs = []
        for col, m, p, v, alpha, res, context, near in items:
            pv = dot_nn(p, with_ones(v))
            l = alpha + pv[:, HD:]
            acc = alpha * context.astype(jnp.float32) + pv[:, :HD]
            updated = (res.astype(jnp.float32) + jnp.where(alive, acc / l, 0.0)).astype(jnp.bfloat16)
            wide = updated.astype(jnp.float32)
            squares = squares + wide * wide * near
            outs.append((col, m, l, acc, updated))
        for col, m, l, acc, updated in outs:
            max_ref[:, col] = m
            sum_ref[:, col] = l
            acc_ref[:, col] = acc
            out_ref[:, col] = updated
        return squares

    batches = [range(start, start + batch) for start in range(0, heads, batch)]
    scored = weighed = None
    for turn in range(len(batches) + 2):
        fresh = score(batches[turn]) if turn < len(batches) else None
        ready = weigh(scored) if scored else None
        if weighed:
            squares = finish(weighed, squares)
        scored, weighed = fresh, ready
    sq_ref[...] = squares


def tile_kernel(row, last, *refs):
    infos, takes, messages, tiles, accs, maxes, sums, olds, old_sqs = [refs[2 * n : 2 * n + 2] for n in range(9)]
    me = lax.axis_index("dp")
    if last:
        outs = [refs[18].at[1 - sent_in(turn)] for turn in range(2)]
        sqs = [refs[19].at[1 - sent_in(turn)] for turn in range(2)]
        for turn in range(2):
            outs[turn][...] = olds[turn][...]
    else:
        outs, sqs = refs[18:20], refs[20:22]

    def work():
        places = [(t, s) for t in range(2) for s in range(tiles[0].shape[0])]
        chosen = [takes[t][row, s] for t, s in places]
        cols = [pl.ds(pl.multiple_of(h * HD, HD), HD) for h in chosen]
        live = [infos[t][h] < infos[t][LENGTH] for (t, _), h in zip(places, chosen)]
        scores = [
            dot_nt(messages[t][:BLK, col], tiles[t][s, 0]) * SCALE + jnp.where(ok, 0.0, NEG)
            for (t, s), col, ok in zip(places, cols, live)
        ]
        before = [(maxes[t][:, col], sums[t][:, col], accs[t][:, col]) for (t, _), col in zip(places, cols)]
        residuals = [messages[t][BLK : 2 * BLK, col].astype(jnp.float32) for (t, _), col in zip(places, cols)]
        news = merge(scores, before, [tiles[t][s, 1] for t, s in places])
        updates = [
            (res + jnp.where(me < infos[t][LENGTH], acc / l, 0.0)).astype(jnp.bfloat16)
            for (t, _), res, (_, l, acc) in zip(places, residuals, news)
        ]
        squares = [old_sqs[t][...] for t in range(2)]
        for (t, _), col, updated in zip(places, cols, updates):
            outs[t][:, col] = updated
            wide = updated.astype(jnp.float32)
            squares[t] = squares[t] + wide * wide
        for t in range(2):
            sqs[t][...] = squares[t]

    if last:
        work()
    else:
        for t in range(2):
            sqs[t][...] = old_sqs[t][...]
        pl.when((me == 0) | (me == 3))(work)


def body_chain(residual, queries, keys_values, global_kv, block_ids, lengths, gain):
    width = residual.shape[-1]
    heads = width // HD
    pipe_count = lax.axis_size("pipe")
    group = head_group(heads)
    steps = heads // group
    lanes = group * HD
    capacity = heads // 4
    q, res, glob, kv, length = queries[0], residual[0], global_kv[0], keys_values[0], lengths[0]
    own_ids = block_ids[0, :, 0]
    glob_count = glob.shape[2]
    params = pltpu.CompilerParams(vmem_limit_bytes=VMEM_LIMIT)
    order = jnp.stack([sent_in(0), sent_in(1)])

    def send(array, turn, moves):
        pairs = []
        for p in range(pipe_count):
            other = p ^ 1 if turn == 1 else ((p + 1) ^ 1) - 1
            if 0 <= other < pipe_count:
                pairs += [
                    ((i * pipe_count + p) if direct else (i * pipe_count + other), j * pipe_count + other)
                    for i, j, direct in moves
                ]
        return lax.ppermute(array, ("dp", "pipe"), pairs)

    ids_3 = lax.ppermute(own_ids, "dp", [(0, 3), (3, 0)])
    ids_2 = lax.ppermute(own_ids, "dp", [(2, 0), (1, 3)])
    kvs, ups, downs = [], [], []
    for turn in range(2):
        c = order[turn]
        note = jnp.pad(lax.dynamic_index_in_dim(own_ids, c, 0, keepdims=False), (0, HD - heads)).astype(jnp.bfloat16)
        note = jnp.broadcast_to(note, (2, BLK, HD))
        kvs.append(jnp.concatenate([lax.dynamic_index_in_dim(kv, c, 1, keepdims=False), note], axis=2))
    kv, ids_3, ids_2, *kvs = lax.optimization_barrier((kv, ids_3, ids_2, *kvs))
    same = [(i, i, True) for i in range(4)]
    crossed = send(kvs[0], 0, same)
    kv, crossed = lax.optimization_barrier((kv, crossed))
    for turn, source in enumerate((crossed, kvs[1])):
        ups.append(send(source, turn, [(i, i + 1, turn == 1) for i in range(3)]))
        downs.append(send(source, turn, [(i + 1, i, turn == 1) for i in range(3)]))

    message = jax.ShapeDtypeStruct((3 * BLK, width + HD), jnp.bfloat16)
    messages = pl.pallas_call(
        functools.partial(message_kernel, group),
        grid_spec=pltpu.PrefetchScalarGridSpec(
            num_scalar_prefetch=3,
            grid=(2, steps),
            in_specs=[
                pl.BlockSpec((1, BLK, lanes), lambda t, g, order, ids, length: (order[t], 0, g)),
                pl.BlockSpec((1, BLK, lanes), lambda t, g, order, ids, length: (order[t], 0, g)),
                pl.BlockSpec((2, 1, BLK, lanes), lambda t, g, order, ids, length: (0, order[t], 0, g)),
                pl.BlockSpec((2, 1, glob_count, lanes), lambda t, g, order, ids, length: (0, order[t], 0, g)),
            ],
            out_specs=[vmem(), vmem()],
        ),
        out_shape=[message, message],
        compiler_params=pltpu.CompilerParams(vmem_limit_bytes=LOCAL_LIMIT),
    )(order, own_ids, length, q, res, kv, glob)

    messages = [send(messages[turn], turn, same) for turn in range(2)]
    tiles = jax.ShapeDtypeStruct((capacity, 2, BLK, HD), jnp.bfloat16)
    distant = pl.pallas_call(
        distant_kernel,
        out_shape=[tiles, tiles],
        in_specs=[smem(), vmem(), vmem()],
        out_specs=[vmem(), vmem()],
        scratch_shapes=[pltpu.SMEM((1, capacity), jnp.int32)],
        compiler_params=params,
    )(ids_3, *kvs)
    far_3 = [send(distant[turn], turn, [(0, 3, True), (3, 0, True)]) for turn in range(2)]

    far_2 = []
    for turn in range(2):
        array = pl.pallas_call(
            functools.partial(forward_kernel, turn),
            out_shape=tiles,
            in_specs=[smem()] * 3 + [vmem()] * 3,
            out_specs=vmem(),
            scratch_shapes=[pltpu.SMEM((1, capacity), jnp.int32)],
            compiler_params=params,
        )(
            ids_2,
            ups[turn][0, 0, width:].astype(jnp.int32),
            downs[turn][0, 0, width:].astype(jnp.int32),
            kvs[turn],
            ups[turn],
            downs[turn],
        )
        far_2.append(send(array, turn, [(0, 2, True), (3, 1, True), (2, 3, False), (1, 0, False)]))

    wide = jax.ShapeDtypeStruct((BLK, width), jnp.float32)
    row = jax.ShapeDtypeStruct((BLK, width), jnp.bfloat16)
    square = jax.ShapeDtypeStruct((BLK, HD), jnp.float32)
    near, infos = [None, None], [None, None]
    for turn in (1, 0):
        if turn == 0:
            messages[0], near[1][4] = lax.optimization_barrier((messages[0], near[1][4]))
        infos[turn] = messages[turn][0, width:].astype(jnp.int32)
        near[turn] = list(
            pl.pallas_call(
                near_kernel,
                out_shape=[wide, wide, wide, row, square, jax.ShapeDtypeStruct((2, capacity), jnp.int32)],
                in_specs=[smem()] + [vmem()] * 3,
                out_specs=[vmem()] * 5 + [smem()],
                compiler_params=params,
            )(infos[turn], messages[turn], ups[turn], downs[turn])
        )
    accs, maxes, sums, updates, squares, takes = [list(items) for items in zip(*near)]
    for index, got, last in ((1, far_3, False), (0, far_2, True)):
        pair = [jax.ShapeDtypeStruct((2,) + kind.shape, kind.dtype) for kind in (row, square)]
        results = pl.pallas_call(
            functools.partial(tile_kernel, index, last),
            out_shape=pair if last else [row, row, square, square],
            in_specs=[smem()] * 4 + [vmem()] * 14,
            out_specs=[vmem()] * (2 if last else 4),
            input_output_aliases={} if last else {14: 0, 15: 1},
            compiler_params=params,
        )(*infos, *takes, *messages, *got, *accs, *maxes, *sums, *updates, *squares)
        if not last:
            updates, squares = results[:2], results[2:]

    updated, squares = results
    total = lax.psum(jnp.sum(squares, axis=2), "tensor")
    inverse = lax.rsqrt(total / D + epsilon)
    normed = updated.astype(jnp.float32) * inverse[:, :, None] * gain[0][:, None, :].astype(jnp.float32)
    return normed.astype(jnp.bfloat16)[None]


def body(*arrays):
    heads = arrays[0].shape[-1] // HD
    chain = lax.axis_size("dp") == 4 and lax.axis_size("pipe") % 2 == 0 and heads % 8 == 0 and heads <= 32
    return (body_chain if chain else body_any)(*arrays)


def solution(mesh):
    in_specs = (
        P("pipe", None, "dp", "tensor"),
        P("pipe", None, "dp", "tensor"),
        P("pipe", None, None, "dp", "tensor"),
        P("pipe", None, None, None, "tensor"),
        P("pipe", None, "dp", "tensor"),
        P("pipe", None),
        P("pipe", None, "tensor"),
    )
    out_specs = P("pipe", None, "dp", "tensor")
    return jax.shard_map(body, mesh=mesh, in_specs=in_specs, out_specs=out_specs, check_vma=False)
```

```python
import functools

import jax
import jax.numpy as jnp
from jax import lax
from jax.experimental import pallas as pl
from jax.experimental.pallas import tpu as pltpu
from jax.sharding import PartitionSpec as P

D = 6144
HD = 128
BLK = 64
LOG2E = 1.4426950408889634
SCALE = HD ** (-0.5) * LOG2E
NEG = -1e30
VMEM_LIMIT = 20 * 1024 * 1024
LOCAL_LIMIT = 52 * 1024 * 1024

epsilon = 1e-05


def dot_nt(a, b):
    return lax.dot_general(a, b, (((1,), (1,)), ((), ())), preferred_element_type=jnp.float32)


def dot_nn(a, b):
    return lax.dot_general(a, b, (((1,), (0,)), ((), ())), preferred_element_type=jnp.float32)


def with_ones(v):
    return jnp.concatenate([v, jnp.ones((v.shape[0], HD), v.dtype)], axis=1)


def head_group(heads):
    return max(g for g in range(1, 9) if heads % g == 0)


def head_batch(heads):
    return max(g for g in range(1, 5) if heads % g == 0)


def heads_wanted(table_ref, row, ids_ref, asker, block):
    heads, capacity = ids_ref.shape[2], table_ref.shape[2]
    for c in range(2):
        for s in range(capacity):
            table_ref[row, c, s] = -1
        slot = jnp.int32(0)
        for h in range(heads):
            match = (ids_ref[asker, c, h] == block) & (slot < capacity)

            @pl.when(match)
            def _(slot=slot, h=h, c=c):
                table_ref[row, c, slot] = h

            slot = slot + match.astype(jnp.int32)


def copy_tiles(out_ref, list_ref, row, c, source_ref):
    for s in range(out_ref.shape[0]):
        cols = pl.ds(pl.multiple_of(jnp.maximum(list_ref[row, c, s], 0) * HD, HD), HD)
        out_ref[s, 0] = source_ref[0, :, cols]
        out_ref[s, 1] = source_ref[1, :, cols]


def pack_kernel(ids_ref, kv_ref, take_ref, out_ref, list_ref):
    me = lax.axis_index("dp")

    @pl.loop(0, ids_ref.shape[0])
    def _(other):
        far = jnp.abs(other - me) >= 2
        heads_wanted(take_ref, other, ids_ref, me, jnp.where(far, other, -1))
        heads_wanted(list_ref, 0, ids_ref, other, jnp.where(far, me, -1))
        for c in range(2):
            copy_tiles(out_ref.at[other, c], list_ref, 0, c, kv_ref.at[:, c])


def local_kernel(heads_step, ids_ref, len_ref, q_ref, kv_ref, gkv_ref, acc_ref, max_ref, sum_ref):
    me = lax.axis_index("dp")
    c = pl.program_id(0)
    g = pl.program_id(1)
    glob = gkv_ref.shape[2]
    lane = lax.broadcasted_iota(jnp.int32, (1, glob + BLK), 1)
    batch = head_batch(heads_step)
    for start in range(0, heads_step, batch):
        cols = [slice(n * HD, (n + 1) * HD) for n in range(start, start + batch)]
        scores, values = [], []
        for n, col in zip(range(start, start + batch), cols):
            k = jnp.concatenate([gkv_ref[0, 0, :, col], kv_ref[0, 0, :, col]], axis=0)
            values.append(jnp.concatenate([gkv_ref[1, 0, :, col], kv_ref[1, 0, :, col]], axis=0))
            twice = jnp.where(ids_ref[me, c, g * heads_step + n] == me, 1.0, 0.0)
            bias = jnp.where(lane < glob, 0.0, jnp.where(me < len_ref[c], twice, NEG))
            scores.append(dot_nt(q_ref[0, :, col], k) * SCALE + bias)
        tops = [jnp.max(s, axis=1, keepdims=True) for s in scores]
        weights = [jnp.exp2(s - m).astype(jnp.bfloat16) for s, m in zip(scores, tops)]
        sums = [dot_nn(p, with_ones(v)) for p, v in zip(weights, values)]
        for col, m, pv in zip(cols, tops, sums):
            acc_ref[0, :, col] = pv[:, :HD]
            sum_ref[0, :, col] = pv[:, HD:]
            max_ref[0, :, col] = jnp.broadcast_to(m, (BLK, HD))


def merge(scores, olds, values):
    tops = [jnp.maximum(old[0], jnp.max(s, axis=1, keepdims=True)) for s, old in zip(scores, olds)]
    weights = [jnp.exp2(s - m[:, : s.shape[1]]).astype(jnp.bfloat16) for s, m in zip(scores, tops)]
    alphas = [jnp.exp2(old[0] - m) for old, m in zip(olds, tops)]
    added = [dot_nn(p, with_ones(v)) for p, v in zip(weights, values)]
    return [
        (m, alpha * old[1] + pv[:, HD:], alpha * old[2] + pv[:, :HD])
        for m, alpha, old, pv in zip(tops, alphas, olds, added)
    ]


def window_kernel(ids_ref, len_ref, q_ref, up_ref, down_ref, res_ref, acc_ref, max_ref, sum_ref, new_acc_ref, new_max_ref, new_sum_ref, out_ref, sq_ref):
    me = lax.axis_index("dp")
    heads = q_ref.shape[2] // HD
    batch = head_batch(heads)
    lane = lax.broadcasted_iota(jnp.int32, (1, 2 * BLK), 1)
    for c in range(2):
        length = len_ref[c]
        alive = me < length
        up_live = (me >= 1) & (me - 1 < length)
        down_live = me + 1 < length

        def step(g, squares, c=c, alive=alive, up_live=up_live, down_live=down_live):
            cols = [pl.ds(pl.multiple_of((g * batch + n) * HD, HD), HD) for n in range(batch)]
            blocks = [ids_ref[me, c, g * batch + n] for n in range(batch)]
            scores, values = [], []
            for block, col in zip(blocks, cols):
                up_bias = jnp.where(up_live, jnp.where(block == me - 1, 1.0, 0.0), NEG)
                down_bias = jnp.where(down_live, jnp.where(block == me + 1, 1.0, 0.0), NEG)
                bias = jnp.where(lane < BLK, up_bias, down_bias)
                k = jnp.concatenate([up_ref[0, c, :, col], down_ref[0, c, :, col]], axis=0)
                values.append(jnp.concatenate([up_ref[1, c, :, col], down_ref[1, c, :, col]], axis=0))
                scores.append(dot_nt(q_ref[c, :, col], k) * SCALE + bias)
            olds = [(max_ref[c, :, col], sum_ref[c, :, col], acc_ref[c, :, col]) for col in cols]
            residuals = [res_ref[c, :, col].astype(jnp.float32) for col in cols]
            news = merge(scores, olds, values)
            updates = [
                (res + jnp.where(alive, acc / l, 0.0)).astype(jnp.bfloat16) for res, (_, l, acc) in zip(residuals, news)
            ]
            for block, col, (m, l, acc), updated in zip(blocks, cols, news, updates):
                new_max_ref[c, :, col] = m
                new_sum_ref[c, :, col] = l
                new_acc_ref[c, :, col] = acc
                out_ref[c, :, col] = updated
                wide = updated.astype(jnp.float32)
                squares = squares + wide * wide * jnp.where(jnp.abs(block - me) < 2, 1.0, 0.0)
            return squares

        sq_ref[c] = lax.fori_loop(0, heads // batch, step, jnp.zeros((BLK, HD), jnp.float32))


def far_kernel(ids_ref, take_ref, len_ref, tile_ref, q_ref, res_ref, acc_ref, max_ref, sum_ref, old_ref, old_sq_ref, out_ref, sq_ref):
    del old_ref
    me = lax.axis_index("dp")
    owners, _, capacity = take_ref.shape
    sq_ref[...] = old_sq_ref[...]

    def one_owner(owner):
        places = [(c, s) for c in range(2) for s in range(capacity)]
        taken = [take_ref[owner, c, s] for c, s in places]
        chosen = [jnp.maximum(h, 0) for h in taken]
        cols = [pl.ds(pl.multiple_of(h * HD, HD), HD) for h in chosen]
        live = [(t >= 0) & (ids_ref[me, c, h] < len_ref[c]) for (c, _), t, h in zip(places, taken, chosen)]
        scores = [
            dot_nt(q_ref[c, :, col], tile_ref[owner, c, s, 0]) * SCALE + jnp.where(ok, 0.0, NEG)
            for (c, s), col, ok in zip(places, cols, live)
        ]
        olds = [(max_ref[c, :, col], sum_ref[c, :, col], acc_ref[c, :, col]) for (c, _), col in zip(places, cols)]
        residuals = [res_ref[c, :, col].astype(jnp.float32) for (c, _), col in zip(places, cols)]
        news = merge(scores, olds, [tile_ref[owner, c, s, 1] for c, s in places])
        updates = [
            (res + jnp.where(me < len_ref[c], acc / l, 0.0)).astype(jnp.bfloat16)
            for (c, _), res, (_, l, acc) in zip(places, residuals, news)
        ]
        squares = [jnp.zeros((BLK, HD), jnp.float32)] * 2
        for (c, _), t, updated in zip(places, taken, updates):
            wide = updated.astype(jnp.float32)
            squares[c] = squares[c] + wide * wide * jnp.where(t >= 0, 1.0, 0.0)
        for c in range(2):
            sq_ref[c] += squares[c]
        for (c, _), t, col, updated in zip(places, taken, cols, updates):

            @pl.when(t >= 0)
            def _(c=c, col=col, updated=updated):
                out_ref[c, :, col] = updated

    pl.loop(0, owners)(one_owner)


def smem():
    return pl.BlockSpec(memory_space=pltpu.SMEM)


def vmem():
    return pl.BlockSpec(memory_space=pltpu.VMEM)


def body_any(residual, queries, keys_values, global_kv, block_ids, lengths, gain):
    width = residual.shape[-1]
    heads = width // HD
    dp_count = lax.axis_size("dp")
    pipe_count = lax.axis_size("pipe")
    tensor_count = lax.axis_size("tensor")
    group = head_group(heads)
    steps = heads // group
    lanes = group * HD
    capacity = (heads + dp_count - 1) // dp_count
    q = queries[0]
    res = residual[0]
    glob = global_kv[0]
    length = lengths[0]
    glob_count = glob.shape[2]
    params = pltpu.CompilerParams(vmem_limit_bytes=VMEM_LIMIT)

    ids = block_ids[0, :, 0]
    ids = lax.all_to_all(jnp.broadcast_to(ids, (dp_count,) + ids.shape), "dp", split_axis=0, concat_axis=0, tiled=True)
    kv, ids = lax.optimization_barrier((keys_values[0], ids))
    up = lax.ppermute(kv, "dp", [(i, i + 1) for i in range(dp_count - 1)])
    down = lax.ppermute(kv, "dp", [(i + 1, i) for i in range(dp_count - 1)])

    lines = [[(i + 1, i) for i in range(pipe_count - 1)], [(i, i + 1) for i in range(pipe_count - 1)]]
    gains = [lax.ppermute(gain[0, c], "pipe", [(j, i) for i, j in lines[c]]) for c in range(2)]
    q, gains = lax.optimization_barrier((q, gains))
    wide = jax.ShapeDtypeStruct((2, BLK, width), jnp.float32)
    row_spec = pl.BlockSpec((1, BLK, lanes), lambda c, g: (c, 0, g))
    pair_spec = pl.BlockSpec((2, 1, BLK, lanes), lambda c, g: (0, c, 0, g))
    acc, maxes, sums = pl.pallas_call(
        functools.partial(local_kernel, group),
        grid=(2, steps),
        out_shape=[wide] * 3,
        in_specs=[
            smem(),
            smem(),
            row_spec,
            pair_spec,
            pl.BlockSpec((2, 1, glob_count, lanes), lambda c, g: (0, c, 0, g)),
        ],
        out_specs=[row_spec] * 3,
        compiler_params=params,
        cost_estimate=pl.CostEstimate(
            flops=4 * 2 * BLK * width * (glob_count + BLK), bytes_accessed=14 * 2**20, transcendentals=0
        ),
    )(ids, length, q, kv, glob)

    kv, acc = lax.optimization_barrier((kv, acc))

    tile = (2, capacity, 2, BLK, HD)
    take, tiles_all = pl.pallas_call(
        pack_kernel,
        out_shape=[
            jax.ShapeDtypeStruct((dp_count, 2, capacity), jnp.int32),
            jax.ShapeDtypeStruct((dp_count,) + tile, jnp.bfloat16),
        ],
        in_specs=[smem(), vmem()],
        out_specs=[smem(), vmem()],
        scratch_shapes=[pltpu.SMEM((1, 2, capacity), jnp.int32)],
        compiler_params=params,
    )(ids, kv)
    far = [(take, lax.all_to_all(tiles_all, "dp", split_axis=0, concat_axis=0, tiled=True))]

    acc, maxes, sums, updated, squares = pl.pallas_call(
        window_kernel,
        out_shape=[wide] * 3
        + [jax.ShapeDtypeStruct((2, BLK, width), jnp.bfloat16), jax.ShapeDtypeStruct((2, BLK, HD), jnp.float32)],
        in_specs=[smem(), smem()] + [vmem()] * 7,
        out_specs=[vmem()] * 5,
        compiler_params=params,
        cost_estimate=pl.CostEstimate(
            flops=4 * 2 * BLK * width * 2 * BLK, bytes_accessed=9 * 2**20, transcendentals=0
        ),
    )(ids, length, q, up, down, res, acc, maxes, sums)

    for heads_taken, tiles_got in far:
        updated, squares = pl.pallas_call(
            far_kernel,
            out_shape=[
                jax.ShapeDtypeStruct((2, BLK, width), jnp.bfloat16),
                jax.ShapeDtypeStruct((2, BLK, HD), jnp.float32),
            ],
            in_specs=[smem(), smem(), smem()] + [vmem()] * 8,
            out_specs=[vmem()] * 2,
            input_output_aliases={9: 0},
            compiler_params=params,
        )(ids, heads_taken, length, tiles_got, q, res, acc, maxes, sums, updated, squares)

    total = lax.psum(jnp.sum(squares, axis=2), "tensor")
    inverse = lax.rsqrt(total / D + epsilon)
    normed = [
        (updated[c].astype(jnp.float32) * inverse[c][:, None] * gains[c].astype(jnp.float32)).astype(jnp.bfloat16)
        for c in range(2)
    ]
    return jnp.stack([lax.ppermute(normed[c], "pipe", lines[c]) for c in range(2)])[None]


def pair_queries(first, second):
    none = jnp.zeros_like(first)
    return jnp.concatenate(
        [jnp.concatenate([first, none], axis=1), jnp.concatenate([none, second], axis=1)], axis=0
    )


def pair_rows(first, second, lanes):
    return jnp.concatenate([jnp.broadcast_to(first, (BLK, lanes)), jnp.broadcast_to(second, (BLK, lanes))], axis=0)


def pair_context(weights, values):
    both = dot_nn(weights.astype(jnp.bfloat16), values)
    return jnp.concatenate([both[:BLK, :HD], both[BLK:, HD:]], axis=0)


LENGTH = 32


def sent_in(turn):
    parity = lax.rem(lax.axis_index("pipe"), 2)
    return parity if turn == 0 else 1 - parity


def copy_heads(out_ref, list_ref, row, source_ref):
    for s in range(out_ref.shape[0]):
        cols = pl.ds(pl.multiple_of(jnp.maximum(list_ref[row, s], 0) * HD, HD), HD)
        out_ref[s, 0] = source_ref[0, :, cols]
        out_ref[s, 1] = source_ref[1, :, cols]


def list_heads(list_ref, row, heads, block, block_of):
    capacity = list_ref.shape[1]
    for s in range(capacity):
        list_ref[row, s] = 0
    slot = jnp.int32(0)
    for h in range(heads):
        match = (block_of(h) == block) & (slot < capacity)

        @pl.when(match)
        def _(slot=slot, h=h):
            list_ref[row, slot] = h

        slot = slot + match.astype(jnp.int32)


def distant_kernel(ids_ref, kv0_ref, kv1_ref, tile0_ref, tile1_ref, list_ref):
    me = lax.axis_index("dp")
    heads = ids_ref.shape[1]

    @pl.when((me == 0) | (me == 3))
    def _():
        for turn, (kv_ref, tile_ref) in enumerate(((kv0_ref, tile0_ref), (kv1_ref, tile1_ref))):
            c = sent_in(turn)
            list_heads(list_ref, 0, heads, me, lambda h, c=c: ids_ref[c, h])
            copy_heads(tile_ref, list_ref, 0, kv_ref)


def forward_kernel(turn, ids_ref, up_ids_ref, down_ids_ref, kv_ref, up_ref, down_ref, tile_ref, list_ref):
    me = lax.axis_index("dp")
    heads = ids_ref.shape[1]
    c = sent_in(turn)
    edge = (me == 0) | (me == 3)
    list_heads(
        list_ref,
        0,
        heads,
        jnp.where(edge, me, 3 - me),
        lambda h: jnp.where(edge, ids_ref[c, h], jnp.where(me == 1, up_ids_ref[h], down_ids_ref[h])),
    )
    pl.when(edge)(lambda: copy_heads(tile_ref, list_ref, 0, kv_ref))
    pl.when(me == 1)(lambda: copy_heads(tile_ref, list_ref, 0, down_ref))
    pl.when(me == 2)(lambda: copy_heads(tile_ref, list_ref, 0, up_ref))


def message_kernel(turn, order_ref, ids_ref, len_ref, q_ref, res_ref, kv_ref, gkv_ref, out_ref, glob_ref, sems):
    me = lax.axis_index("dp")
    c = order_ref[turn]
    glob = gkv_ref.shape[2]
    width = out_ref.shape[1] - HD
    heads = width // HD
    copies = [pltpu.make_async_copy(gkv_ref.at[n, c], glob_ref.at[n], sems.at[n]) for n in range(2)]
    for copy in copies:
        copy.start()
    place = lax.broadcasted_iota(jnp.int32, (1, HD), 1)
    note = jnp.where(place == LENGTH, len_ref[c], 0)
    for h in range(heads):
        note = jnp.where(place == h, ids_ref[c, h], note)
    out_ref[:BLK, width:] = jnp.broadcast_to(note.astype(jnp.float32), (BLK, HD)).astype(jnp.bfloat16)
    out_ref[BLK : 2 * BLK, width:] = jnp.zeros((BLK, HD), jnp.bfloat16)
    out_ref[:BLK, :width] = q_ref[c]
    out_ref[BLK : 2 * BLK, :width] = res_ref[c]
    own_live = me < len_ref[c]

    def score(n):
        both = slice(n * HD, (n + 2) * HD)
        q = pair_queries(q_ref[c, :, n * HD : (n + 1) * HD], q_ref[c, :, (n + 1) * HD : (n + 2) * HD])
        k = jnp.concatenate([glob_ref[0, :, both], kv_ref[0, c, :, both]], axis=0)
        own = [jnp.where(own_live, jnp.where(ids_ref[c, n + i] == me, 1.0, 0.0), NEG) for i in range(2)]
        s = dot_nt(q, k) * SCALE
        return jnp.concatenate([s[:, :glob], s[:, glob:] + pair_rows(*own, BLK)], axis=1)

    def weigh(s):
        m = jnp.max(s, axis=1, keepdims=True)
        p = jnp.exp2(s - m)
        l = jnp.sum(p, axis=1, keepdims=True)
        return p.astype(jnp.bfloat16), l, m + jnp.log2(l)

    def finish(n, p, l):
        both = slice(n * HD, (n + 2) * HD)
        v = jnp.concatenate([glob_ref[1, :, both], kv_ref[1, c, :, both]], axis=0)
        return (pair_context(p, v) / l).astype(jnp.bfloat16)

    state = jnp.zeros((BLK, HD), jnp.float32)
    pairs = heads // 2
    scored = weighed = None
    for t in range(pairs + 2):
        fresh = ready = None
        if t < pairs:
            if t == 0:
                copies[0].wait()
            fresh = score(2 * t)
        if scored is not None:
            p, l, level = weigh(scored)
            ready = (p, l)
            high = level.astype(jnp.bfloat16).astype(jnp.float32)
            middle = (level - high).astype(jnp.bfloat16).astype(jnp.float32)
            low = level - high - middle
            for i in range(2):
                rows = slice(i * BLK, (i + 1) * BLK)
                at = place - (2 * (t - 1) + i)
                state = jnp.where(
                    at == 0, high[rows], jnp.where(at == 32, middle[rows], jnp.where(at == 64, low[rows], state))
                )
        if weighed is not None:
            if t == 2:
                copies[1].wait()
            h = 2 * (t - 2)
            context = finish(h, *weighed)
            for i in range(2):
                out_ref[2 * BLK :, (h + i) * HD : (h + i + 1) * HD] = context[i * BLK : (i + 1) * BLK]
        scored, weighed = fresh, ready
    out_ref[2 * BLK :, width:] = state.astype(jnp.bfloat16)


def near_kernel(info_ref, message_ref, up_ref, down_ref, acc_ref, max_ref, sum_ref, out_ref, sq_ref, take_ref):
    me = lax.axis_index("dp")
    width = out_ref.shape[1]
    heads = width // HD
    batch = head_batch(heads)
    length = info_ref[LENGTH]
    alive = me < length
    up_live = (me >= 1) & (me - 1 < length)
    down_live = me + 1 < length
    list_heads(take_ref, 0, heads, jnp.where(me < 2, me + 2, me - 2), lambda h: info_ref[h])
    list_heads(take_ref, 1, heads, 3 - me, lambda h: info_ref[h])
    lane = lax.broadcasted_iota(jnp.int32, (1, 2 * BLK), 1)
    state = message_ref[2 * BLK :, width:].astype(jnp.float32)
    state = state + pltpu.roll(state, 96, 1) + pltpu.roll(state, 64, 1)
    squares = jnp.zeros((BLK, HD), jnp.float32)

    def score(numbers):
        items = []
        for h in numbers:
            col = slice(h * HD, (h + 1) * HD)
            block = info_ref[h]
            up_bias = jnp.where(up_live, jnp.where(block == me - 1, 1.0, 0.0), NEG)
            down_bias = jnp.where(down_live, jnp.where(block == me + 1, 1.0, 0.0), NEG)
            bias = jnp.where(lane < BLK, up_bias, down_bias)
            k = jnp.concatenate([up_ref[0, :, col], down_ref[0, :, col]], axis=0)
            v = jnp.concatenate([up_ref[1, :, col], down_ref[1, :, col]], axis=0)
            s = dot_nt(message_ref[:BLK, col], k) * SCALE + bias
            level = jnp.broadcast_to(state[:, h : h + 1], (BLK, HD))
            near = jnp.where(jnp.abs(block - me) < 2, 1.0, 0.0)
            items.append((col, s, v, level, message_ref[BLK : 2 * BLK, col], message_ref[2 * BLK :, col], near))
        return items

    def weigh(items):
        outs = []
        for col, s, v, level, res, context, near in items:
            m = jnp.maximum(level, jnp.max(s, axis=1, keepdims=True))
            p = jnp.exp2(s - m).astype(jnp.bfloat16)
            outs.append((col, m, p, v, jnp.exp2(level - m), res, context, near))
        return outs

    def finish(items, squares):
        outs = []
        for col, m, p, v, alpha, res, context, near in items:
            pv = dot_nn(p, with_ones(v))
            l = alpha + pv[:, HD:]
            acc = alpha * context.astype(jnp.float32) + pv[:, :HD]
            updated = (res.astype(jnp.float32) + jnp.where(alive, acc / l, 0.0)).astype(jnp.bfloat16)
            wide = updated.astype(jnp.float32)
            squares = squares + wide * wide * near
            outs.append((col, m, l, acc, updated))
        for col, m, l, acc, updated in outs:
            max_ref[:, col] = m
            sum_ref[:, col] = l
            acc_ref[:, col] = acc
            out_ref[:, col] = updated
        return squares

    batches = [range(start, start + batch) for start in range(0, heads, batch)]
    scored = weighed = None
    for turn in range(len(batches) + 2):
        fresh = score(batches[turn]) if turn < len(batches) else None
        ready = weigh(scored) if scored else None
        if weighed:
            squares = finish(weighed, squares)
        scored, weighed = fresh, ready
    sq_ref[...] = squares


def tile_kernel(row, last, *refs):
    infos, takes, messages, tiles, accs, maxes, sums, olds, old_sqs = [refs[2 * n : 2 * n + 2] for n in range(9)]
    me = lax.axis_index("dp")
    if last:
        outs = [refs[18].at[1 - sent_in(turn)] for turn in range(2)]
        sqs = [refs[19].at[1 - sent_in(turn)] for turn in range(2)]
        for turn in range(2):
            outs[turn][...] = olds[turn][...]
    else:
        outs, sqs = refs[18:20], refs[20:22]

    def work():
        places = [(t, s) for t in range(2) for s in range(tiles[0].shape[0])]
        chosen = [takes[t][row, s] for t, s in places]
        cols = [pl.ds(pl.multiple_of(h * HD, HD), HD) for h in chosen]
        live = [infos[t][h] < infos[t][LENGTH] for (t, _), h in zip(places, chosen)]
        scores = [
            dot_nt(messages[t][:BLK, col], tiles[t][s, 0]) * SCALE + jnp.where(ok, 0.0, NEG)
            for (t, s), col, ok in zip(places, cols, live)
        ]
        before = [(maxes[t][:, col], sums[t][:, col], accs[t][:, col]) for (t, _), col in zip(places, cols)]
        residuals = [messages[t][BLK : 2 * BLK, col].astype(jnp.float32) for (t, _), col in zip(places, cols)]
        news = merge(scores, before, [tiles[t][s, 1] for t, s in places])
        updates = [
            (res + jnp.where(me < infos[t][LENGTH], acc / l, 0.0)).astype(jnp.bfloat16)
            for (t, _), res, (_, l, acc) in zip(places, residuals, news)
        ]
        squares = [old_sqs[t][...] for t in range(2)]
        for (t, _), col, updated in zip(places, cols, updates):
            outs[t][:, col] = updated
            wide = updated.astype(jnp.float32)
            squares[t] = squares[t] + wide * wide
        for t in range(2):
            sqs[t][...] = squares[t]

    if last:
        work()
    else:
        for t in range(2):
            sqs[t][...] = old_sqs[t][...]
        pl.when((me == 0) | (me == 3))(work)


def body_chain(residual, queries, keys_values, global_kv, block_ids, lengths, gain):
    width = residual.shape[-1]
    heads = width // HD
    pipe_count = lax.axis_size("pipe")
    capacity = heads // 4
    q, res, glob, kv, length = queries[0], residual[0], global_kv[0], keys_values[0], lengths[0]
    own_ids = block_ids[0, :, 0]
    glob_count = glob.shape[2]
    params = pltpu.CompilerParams(vmem_limit_bytes=VMEM_LIMIT)
    order = jnp.stack([sent_in(0), sent_in(1)])

    def send(array, turn, moves):
        pairs = []
        for p in range(pipe_count):
            other = p ^ 1 if turn == 1 else ((p + 1) ^ 1) - 1
            if 0 <= other < pipe_count:
                pairs += [
                    ((i * pipe_count + p) if direct else (i * pipe_count + other), j * pipe_count + other)
                    for i, j, direct in moves
                ]
        return lax.ppermute(array, ("dp", "pipe"), pairs)

    ids_3 = lax.ppermute(own_ids, "dp", [(0, 3), (3, 0)])
    ids_2 = lax.ppermute(own_ids, "dp", [(2, 0), (1, 3)])
    kvs, ups, downs = [], [], []
    for turn in range(2):
        c = order[turn]
        note = jnp.pad(lax.dynamic_index_in_dim(own_ids, c, 0, keepdims=False), (0, HD - heads)).astype(jnp.bfloat16)
        note = jnp.broadcast_to(note, (2, BLK, HD))
        kvs.append(jnp.concatenate([lax.dynamic_index_in_dim(kv, c, 1, keepdims=False), note], axis=2))
    kv, ids_3, ids_2, *kvs = lax.optimization_barrier((kv, ids_3, ids_2, *kvs))
    same = [(i, i, True) for i in range(4)]
    crossed = send(kvs[0], 0, same)
    own_kv = kv
    kv, crossed = lax.optimization_barrier((kv, crossed))
    for turn, source in enumerate((crossed, kvs[1])):
        ups.append(send(source, turn, [(i, i + 1, turn == 1) for i in range(3)]))
        downs.append(send(source, turn, [(i + 1, i, turn == 1) for i in range(3)]))

    message = jax.ShapeDtypeStruct((3 * BLK, width + HD), jnp.bfloat16)

    def local_part(turn, kv):
        return pl.pallas_call(
            functools.partial(message_kernel, turn),
            out_shape=message,
            in_specs=[smem()] * 3 + [vmem()] * 3 + [pl.BlockSpec(memory_space=pl.ANY)],
            out_specs=vmem(),
            scratch_shapes=[
                pltpu.VMEM((2, glob_count, width), jnp.bfloat16),
                pltpu.SemaphoreType.DMA((2,)),
            ],
            compiler_params=pltpu.CompilerParams(vmem_limit_bytes=LOCAL_LIMIT),
        )(order, own_ids, length, q, res, kv, glob)

    messages = [local_part(0, own_kv), local_part(1, kv)]
    messages = list(lax.optimization_barrier(tuple(messages)))
    messages = [send(messages[turn], turn, same) for turn in range(2)]
    tiles = jax.ShapeDtypeStruct((capacity, 2, BLK, HD), jnp.bfloat16)
    distant = pl.pallas_call(
        distant_kernel,
        out_shape=[tiles, tiles],
        in_specs=[smem(), vmem(), vmem()],
        out_specs=[vmem(), vmem()],
        scratch_shapes=[pltpu.SMEM((1, capacity), jnp.int32)],
        compiler_params=params,
    )(ids_3, *kvs)
    far_3 = [send(distant[turn], turn, [(0, 3, True), (3, 0, True)]) for turn in range(2)]

    far_2 = []
    for turn in range(2):
        array = pl.pallas_call(
            functools.partial(forward_kernel, turn),
            out_shape=tiles,
            in_specs=[smem()] * 3 + [vmem()] * 3,
            out_specs=vmem(),
            scratch_shapes=[pltpu.SMEM((1, capacity), jnp.int32)],
            compiler_params=params,
        )(
            ids_2,
            ups[turn][0, 0, width:].astype(jnp.int32),
            downs[turn][0, 0, width:].astype(jnp.int32),
            kvs[turn],
            ups[turn],
            downs[turn],
        )
        far_2.append(send(array, turn, [(0, 2, True), (3, 1, True), (2, 3, False), (1, 0, False)]))

    wide = jax.ShapeDtypeStruct((BLK, width), jnp.float32)
    row = jax.ShapeDtypeStruct((BLK, width), jnp.bfloat16)
    square = jax.ShapeDtypeStruct((BLK, HD), jnp.float32)
    near, infos = [None, None], [None, None]
    for turn in (1, 0):
        if turn == 0:
            messages[0], near[1][4] = lax.optimization_barrier((messages[0], near[1][4]))
        infos[turn] = messages[turn][0, width:].astype(jnp.int32)
        near[turn] = list(
            pl.pallas_call(
                near_kernel,
                out_shape=[wide, wide, wide, row, square, jax.ShapeDtypeStruct((2, capacity), jnp.int32)],
                in_specs=[smem()] + [vmem()] * 3,
                out_specs=[vmem()] * 5 + [smem()],
                compiler_params=params,
            )(infos[turn], messages[turn], ups[turn], downs[turn])
        )
    accs, maxes, sums, updates, squares, takes = [list(items) for items in zip(*near)]
    for index, got, last in ((1, far_3, False), (0, far_2, True)):
        pair = [jax.ShapeDtypeStruct((2,) + kind.shape, kind.dtype) for kind in (row, square)]
        results = pl.pallas_call(
            functools.partial(tile_kernel, index, last),
            out_shape=pair if last else [row, row, square, square],
            in_specs=[smem()] * 4 + [vmem()] * 14,
            out_specs=[vmem()] * (2 if last else 4),
            input_output_aliases={} if last else {14: 0, 15: 1},
            compiler_params=params,
        )(*infos, *takes, *messages, *got, *accs, *maxes, *sums, *updates, *squares)
        if not last:
            updates, squares = results[:2], results[2:]

    updated, squares = results
    total = lax.psum(jnp.sum(squares, axis=2), "tensor")
    inverse = lax.rsqrt(total / D + epsilon)
    normed = updated.astype(jnp.float32) * inverse[:, :, None] * gain[0][:, None, :].astype(jnp.float32)
    return normed.astype(jnp.bfloat16)[None]


def body(*arrays):
    heads = arrays[0].shape[-1] // HD
    chain = lax.axis_size("dp") == 4 and lax.axis_size("pipe") % 2 == 0 and heads % 8 == 0 and heads <= 32
    return (body_chain if chain else body_any)(*arrays)


def solution(mesh):
    in_specs = (
        P("pipe", None, "dp", "tensor"),
        P("pipe", None, "dp", "tensor"),
        P("pipe", None, None, "dp", "tensor"),
        P("pipe", None, None, None, "tensor"),
        P("pipe", None, "dp", "tensor"),
        P("pipe", None),
        P("pipe", None, "tensor"),
    )
    out_specs = P("pipe", None, "dp", "tensor")
    return jax.shard_map(body, mesh=mesh, in_specs=in_specs, out_specs=out_specs, check_vma=False)
```

```python
import functools

import jax
import jax.numpy as jnp
from jax import lax
from jax.experimental import pallas as pl
from jax.experimental.pallas import tpu as pltpu
from jax.sharding import PartitionSpec as P

D = 6144
HD = 128
BLK = 64
LOG2E = 1.4426950408889634
SCALE = HD ** (-0.5) * LOG2E
NEG = -1e30
VMEM_LIMIT = 20 * 1024 * 1024
LOCAL_LIMIT = 52 * 1024 * 1024

epsilon = 1e-05


def dot_nt(a, b):
    return lax.dot_general(a, b, (((1,), (1,)), ((), ())), preferred_element_type=jnp.float32)


def dot_nn(a, b):
    return lax.dot_general(a, b, (((1,), (0,)), ((), ())), preferred_element_type=jnp.float32)


def with_ones(v):
    return jnp.concatenate([v, jnp.ones((v.shape[0], HD), v.dtype)], axis=1)


def head_group(heads):
    return max(g for g in range(1, 9) if heads % g == 0)


def head_batch(heads):
    return max(g for g in range(1, 5) if heads % g == 0)


def heads_wanted(table_ref, row, ids_ref, asker, block):
    heads, capacity = ids_ref.shape[2], table_ref.shape[2]
    for c in range(2):
        for s in range(capacity):
            table_ref[row, c, s] = -1
        slot = jnp.int32(0)
        for h in range(heads):
            match = (ids_ref[asker, c, h] == block) & (slot < capacity)

            @pl.when(match)
            def _(slot=slot, h=h, c=c):
                table_ref[row, c, slot] = h

            slot = slot + match.astype(jnp.int32)


def copy_tiles(out_ref, list_ref, row, c, source_ref):
    for s in range(out_ref.shape[0]):
        cols = pl.ds(pl.multiple_of(jnp.maximum(list_ref[row, c, s], 0) * HD, HD), HD)
        out_ref[s, 0] = source_ref[0, :, cols]
        out_ref[s, 1] = source_ref[1, :, cols]


def pack_kernel(ids_ref, kv_ref, take_ref, out_ref, list_ref):
    me = lax.axis_index("dp")

    @pl.loop(0, ids_ref.shape[0])
    def _(other):
        far = jnp.abs(other - me) >= 2
        heads_wanted(take_ref, other, ids_ref, me, jnp.where(far, other, -1))
        heads_wanted(list_ref, 0, ids_ref, other, jnp.where(far, me, -1))
        for c in range(2):
            copy_tiles(out_ref.at[other, c], list_ref, 0, c, kv_ref.at[:, c])


def local_kernel(heads_step, ids_ref, len_ref, q_ref, kv_ref, gkv_ref, acc_ref, max_ref, sum_ref):
    me = lax.axis_index("dp")
    c = pl.program_id(0)
    g = pl.program_id(1)
    glob = gkv_ref.shape[2]
    lane = lax.broadcasted_iota(jnp.int32, (1, glob + BLK), 1)
    batch = head_batch(heads_step)
    for start in range(0, heads_step, batch):
        cols = [slice(n * HD, (n + 1) * HD) for n in range(start, start + batch)]
        scores, values = [], []
        for n, col in zip(range(start, start + batch), cols):
            k = jnp.concatenate([gkv_ref[0, 0, :, col], kv_ref[0, 0, :, col]], axis=0)
            values.append(jnp.concatenate([gkv_ref[1, 0, :, col], kv_ref[1, 0, :, col]], axis=0))
            twice = jnp.where(ids_ref[me, c, g * heads_step + n] == me, 1.0, 0.0)
            bias = jnp.where(lane < glob, 0.0, jnp.where(me < len_ref[c], twice, NEG))
            scores.append(dot_nt(q_ref[0, :, col], k) * SCALE + bias)
        tops = [jnp.max(s, axis=1, keepdims=True) for s in scores]
        weights = [jnp.exp2(s - m).astype(jnp.bfloat16) for s, m in zip(scores, tops)]
        sums = [dot_nn(p, with_ones(v)) for p, v in zip(weights, values)]
        for col, m, pv in zip(cols, tops, sums):
            acc_ref[0, :, col] = pv[:, :HD]
            sum_ref[0, :, col] = pv[:, HD:]
            max_ref[0, :, col] = jnp.broadcast_to(m, (BLK, HD))


def merge(scores, olds, values):
    tops = [jnp.maximum(old[0], jnp.max(s, axis=1, keepdims=True)) for s, old in zip(scores, olds)]
    weights = [jnp.exp2(s - m[:, : s.shape[1]]).astype(jnp.bfloat16) for s, m in zip(scores, tops)]
    alphas = [jnp.exp2(old[0] - m) for old, m in zip(olds, tops)]
    added = [dot_nn(p, with_ones(v)) for p, v in zip(weights, values)]
    return [
        (m, alpha * old[1] + pv[:, HD:], alpha * old[2] + pv[:, :HD])
        for m, alpha, old, pv in zip(tops, alphas, olds, added)
    ]


def window_kernel(ids_ref, len_ref, q_ref, up_ref, down_ref, res_ref, acc_ref, max_ref, sum_ref, new_acc_ref, new_max_ref, new_sum_ref, out_ref, sq_ref):
    me = lax.axis_index("dp")
    heads = q_ref.shape[2] // HD
    batch = head_batch(heads)
    lane = lax.broadcasted_iota(jnp.int32, (1, 2 * BLK), 1)
    for c in range(2):
        length = len_ref[c]
        alive = me < length
        up_live = (me >= 1) & (me - 1 < length)
        down_live = me + 1 < length

        def step(g, squares, c=c, alive=alive, up_live=up_live, down_live=down_live):
            cols = [pl.ds(pl.multiple_of((g * batch + n) * HD, HD), HD) for n in range(batch)]
            blocks = [ids_ref[me, c, g * batch + n] for n in range(batch)]
            scores, values = [], []
            for block, col in zip(blocks, cols):
                up_bias = jnp.where(up_live, jnp.where(block == me - 1, 1.0, 0.0), NEG)
                down_bias = jnp.where(down_live, jnp.where(block == me + 1, 1.0, 0.0), NEG)
                bias = jnp.where(lane < BLK, up_bias, down_bias)
                k = jnp.concatenate([up_ref[0, c, :, col], down_ref[0, c, :, col]], axis=0)
                values.append(jnp.concatenate([up_ref[1, c, :, col], down_ref[1, c, :, col]], axis=0))
                scores.append(dot_nt(q_ref[c, :, col], k) * SCALE + bias)
            olds = [(max_ref[c, :, col], sum_ref[c, :, col], acc_ref[c, :, col]) for col in cols]
            residuals = [res_ref[c, :, col].astype(jnp.float32) for col in cols]
            news = merge(scores, olds, values)
            updates = [
                (res + jnp.where(alive, acc / l, 0.0)).astype(jnp.bfloat16) for res, (_, l, acc) in zip(residuals, news)
            ]
            for block, col, (m, l, acc), updated in zip(blocks, cols, news, updates):
                new_max_ref[c, :, col] = m
                new_sum_ref[c, :, col] = l
                new_acc_ref[c, :, col] = acc
                out_ref[c, :, col] = updated
                wide = updated.astype(jnp.float32)
                squares = squares + wide * wide * jnp.where(jnp.abs(block - me) < 2, 1.0, 0.0)
            return squares

        sq_ref[c] = lax.fori_loop(0, heads // batch, step, jnp.zeros((BLK, HD), jnp.float32))


def far_kernel(ids_ref, take_ref, len_ref, tile_ref, q_ref, res_ref, acc_ref, max_ref, sum_ref, old_ref, old_sq_ref, out_ref, sq_ref):
    del old_ref
    me = lax.axis_index("dp")
    owners, _, capacity = take_ref.shape
    sq_ref[...] = old_sq_ref[...]

    def one_owner(owner):
        places = [(c, s) for c in range(2) for s in range(capacity)]
        taken = [take_ref[owner, c, s] for c, s in places]
        chosen = [jnp.maximum(h, 0) for h in taken]
        cols = [pl.ds(pl.multiple_of(h * HD, HD), HD) for h in chosen]
        live = [(t >= 0) & (ids_ref[me, c, h] < len_ref[c]) for (c, _), t, h in zip(places, taken, chosen)]
        scores = [
            dot_nt(q_ref[c, :, col], tile_ref[owner, c, s, 0]) * SCALE + jnp.where(ok, 0.0, NEG)
            for (c, s), col, ok in zip(places, cols, live)
        ]
        olds = [(max_ref[c, :, col], sum_ref[c, :, col], acc_ref[c, :, col]) for (c, _), col in zip(places, cols)]
        residuals = [res_ref[c, :, col].astype(jnp.float32) for (c, _), col in zip(places, cols)]
        news = merge(scores, olds, [tile_ref[owner, c, s, 1] for c, s in places])
        updates = [
            (res + jnp.where(me < len_ref[c], acc / l, 0.0)).astype(jnp.bfloat16)
            for (c, _), res, (_, l, acc) in zip(places, residuals, news)
        ]
        squares = [jnp.zeros((BLK, HD), jnp.float32)] * 2
        for (c, _), t, updated in zip(places, taken, updates):
            wide = updated.astype(jnp.float32)
            squares[c] = squares[c] + wide * wide * jnp.where(t >= 0, 1.0, 0.0)
        for c in range(2):
            sq_ref[c] += squares[c]
        for (c, _), t, col, updated in zip(places, taken, cols, updates):

            @pl.when(t >= 0)
            def _(c=c, col=col, updated=updated):
                out_ref[c, :, col] = updated

    pl.loop(0, owners)(one_owner)


def smem():
    return pl.BlockSpec(memory_space=pltpu.SMEM)


def vmem():
    return pl.BlockSpec(memory_space=pltpu.VMEM)


def body_any(residual, queries, keys_values, global_kv, block_ids, lengths, gain):
    width = residual.shape[-1]
    heads = width // HD
    dp_count = lax.axis_size("dp")
    pipe_count = lax.axis_size("pipe")
    tensor_count = lax.axis_size("tensor")
    group = head_group(heads)
    steps = heads // group
    lanes = group * HD
    capacity = (heads + dp_count - 1) // dp_count
    q = queries[0]
    res = residual[0]
    glob = global_kv[0]
    length = lengths[0]
    glob_count = glob.shape[2]
    params = pltpu.CompilerParams(vmem_limit_bytes=VMEM_LIMIT)

    ids = block_ids[0, :, 0]
    ids = lax.all_to_all(jnp.broadcast_to(ids, (dp_count,) + ids.shape), "dp", split_axis=0, concat_axis=0, tiled=True)
    kv, ids = lax.optimization_barrier((keys_values[0], ids))
    up = lax.ppermute(kv, "dp", [(i, i + 1) for i in range(dp_count - 1)])
    down = lax.ppermute(kv, "dp", [(i + 1, i) for i in range(dp_count - 1)])

    lines = [[(i + 1, i) for i in range(pipe_count - 1)], [(i, i + 1) for i in range(pipe_count - 1)]]
    gains = [lax.ppermute(gain[0, c], "pipe", [(j, i) for i, j in lines[c]]) for c in range(2)]
    q, gains = lax.optimization_barrier((q, gains))
    wide = jax.ShapeDtypeStruct((2, BLK, width), jnp.float32)
    row_spec = pl.BlockSpec((1, BLK, lanes), lambda c, g: (c, 0, g))
    pair_spec = pl.BlockSpec((2, 1, BLK, lanes), lambda c, g: (0, c, 0, g))
    acc, maxes, sums = pl.pallas_call(
        functools.partial(local_kernel, group),
        grid=(2, steps),
        out_shape=[wide] * 3,
        in_specs=[
            smem(),
            smem(),
            row_spec,
            pair_spec,
            pl.BlockSpec((2, 1, glob_count, lanes), lambda c, g: (0, c, 0, g)),
        ],
        out_specs=[row_spec] * 3,
        compiler_params=params,
        cost_estimate=pl.CostEstimate(
            flops=4 * 2 * BLK * width * (glob_count + BLK), bytes_accessed=14 * 2**20, transcendentals=0
        ),
    )(ids, length, q, kv, glob)

    kv, acc = lax.optimization_barrier((kv, acc))

    tile = (2, capacity, 2, BLK, HD)
    take, tiles_all = pl.pallas_call(
        pack_kernel,
        out_shape=[
            jax.ShapeDtypeStruct((dp_count, 2, capacity), jnp.int32),
            jax.ShapeDtypeStruct((dp_count,) + tile, jnp.bfloat16),
        ],
        in_specs=[smem(), vmem()],
        out_specs=[smem(), vmem()],
        scratch_shapes=[pltpu.SMEM((1, 2, capacity), jnp.int32)],
        compiler_params=params,
    )(ids, kv)
    far = [(take, lax.all_to_all(tiles_all, "dp", split_axis=0, concat_axis=0, tiled=True))]

    acc, maxes, sums, updated, squares = pl.pallas_call(
        window_kernel,
        out_shape=[wide] * 3
        + [jax.ShapeDtypeStruct((2, BLK, width), jnp.bfloat16), jax.ShapeDtypeStruct((2, BLK, HD), jnp.float32)],
        in_specs=[smem(), smem()] + [vmem()] * 7,
        out_specs=[vmem()] * 5,
        compiler_params=params,
        cost_estimate=pl.CostEstimate(
            flops=4 * 2 * BLK * width * 2 * BLK, bytes_accessed=9 * 2**20, transcendentals=0
        ),
    )(ids, length, q, up, down, res, acc, maxes, sums)

    for heads_taken, tiles_got in far:
        updated, squares = pl.pallas_call(
            far_kernel,
            out_shape=[
                jax.ShapeDtypeStruct((2, BLK, width), jnp.bfloat16),
                jax.ShapeDtypeStruct((2, BLK, HD), jnp.float32),
            ],
            in_specs=[smem(), smem(), smem()] + [vmem()] * 8,
            out_specs=[vmem()] * 2,
            input_output_aliases={9: 0},
            compiler_params=params,
        )(ids, heads_taken, length, tiles_got, q, res, acc, maxes, sums, updated, squares)

    total = lax.psum(jnp.sum(squares, axis=2), "tensor")
    inverse = lax.rsqrt(total / D + epsilon)
    normed = [
        (updated[c].astype(jnp.float32) * inverse[c][:, None] * gains[c].astype(jnp.float32)).astype(jnp.bfloat16)
        for c in range(2)
    ]
    return jnp.stack([lax.ppermute(normed[c], "pipe", lines[c]) for c in range(2)])[None]


def pair_queries(first, second):
    none = jnp.zeros_like(first)
    return jnp.concatenate(
        [jnp.concatenate([first, none], axis=1), jnp.concatenate([none, second], axis=1)], axis=0
    )


def pair_rows(first, second, lanes):
    return jnp.concatenate([jnp.broadcast_to(first, (BLK, lanes)), jnp.broadcast_to(second, (BLK, lanes))], axis=0)


def pair_context(weights, values):
    both = dot_nn(weights.astype(jnp.bfloat16), values)
    return jnp.concatenate([both[:BLK, :HD], both[BLK:, HD:]], axis=0)


LENGTH = 32


def sent_in(turn):
    parity = lax.rem(lax.axis_index("pipe"), 2)
    return parity if turn == 0 else 1 - parity


def copy_heads(out_ref, list_ref, row, source_ref):
    for s in range(out_ref.shape[0]):
        cols = pl.ds(pl.multiple_of(jnp.maximum(list_ref[row, s], 0) * HD, HD), HD)
        out_ref[s, 0] = source_ref[0, :, cols]
        out_ref[s, 1] = source_ref[1, :, cols]


def list_heads(list_ref, row, heads, block, block_of):
    capacity = list_ref.shape[1]
    for s in range(capacity):
        list_ref[row, s] = 0
    slot = jnp.int32(0)
    for h in range(heads):
        match = (block_of(h) == block) & (slot < capacity)

        @pl.when(match)
        def _(slot=slot, h=h):
            list_ref[row, slot] = h

        slot = slot + match.astype(jnp.int32)


def distant_kernel(ids_ref, kv0_ref, kv1_ref, tile0_ref, tile1_ref, list_ref):
    me = lax.axis_index("dp")
    heads = ids_ref.shape[1]

    @pl.when((me == 0) | (me == 3))
    def _():
        for turn, (kv_ref, tile_ref) in enumerate(((kv0_ref, tile0_ref), (kv1_ref, tile1_ref))):
            c = sent_in(turn)
            list_heads(list_ref, 0, heads, me, lambda h, c=c: ids_ref[c, h])
            copy_heads(tile_ref, list_ref, 0, kv_ref)


def forward_kernel(turn, ids_ref, up_ids_ref, down_ids_ref, kv_ref, up_ref, down_ref, tile_ref, list_ref):
    me = lax.axis_index("dp")
    heads = ids_ref.shape[1]
    c = sent_in(turn)
    edge = (me == 0) | (me == 3)
    list_heads(
        list_ref,
        0,
        heads,
        jnp.where(edge, me, 3 - me),
        lambda h: jnp.where(edge, ids_ref[c, h], jnp.where(me == 1, up_ids_ref[h], down_ids_ref[h])),
    )
    pl.when(edge)(lambda: copy_heads(tile_ref, list_ref, 0, kv_ref))
    pl.when(me == 1)(lambda: copy_heads(tile_ref, list_ref, 0, down_ref))
    pl.when(me == 2)(lambda: copy_heads(tile_ref, list_ref, 0, up_ref))


def message_kernel(turn, order_ref, ids_ref, len_ref, q_ref, res_ref, kv_ref, gkv_ref, out_ref, glob_ref, sems):
    me = lax.axis_index("dp")
    c = order_ref[turn]
    glob = gkv_ref.shape[2]
    width = out_ref.shape[1] - HD
    heads = width // HD
    copies = [pltpu.make_async_copy(gkv_ref.at[n, c], glob_ref.at[n], sems.at[n]) for n in range(2)]
    for copy in copies:
        copy.start()
    place = lax.broadcasted_iota(jnp.int32, (1, HD), 1)
    note = jnp.where(place == LENGTH, len_ref[c], 0)
    for h in range(heads):
        note = jnp.where(place == h, ids_ref[c, h], note)
    out_ref[:BLK, width:] = jnp.broadcast_to(note.astype(jnp.float32), (BLK, HD)).astype(jnp.bfloat16)
    out_ref[BLK : 2 * BLK, width:] = jnp.zeros((BLK, HD), jnp.bfloat16)
    out_ref[:BLK, :width] = q_ref[c]
    out_ref[BLK : 2 * BLK, :width] = res_ref[c]
    own_live = me < len_ref[c]

    def score(n):
        both = slice(n * HD, (n + 2) * HD)
        q = pair_queries(q_ref[c, :, n * HD : (n + 1) * HD], q_ref[c, :, (n + 1) * HD : (n + 2) * HD])
        k = jnp.concatenate([glob_ref[0, :, both], kv_ref[0, c, :, both]], axis=0)
        own = [jnp.where(own_live, jnp.where(ids_ref[c, n + i] == me, 1.0, 0.0), NEG) for i in range(2)]
        s = dot_nt(q, k) * SCALE
        return jnp.concatenate([s[:, :glob], s[:, glob:] + pair_rows(*own, BLK)], axis=1)

    def weigh(s):
        m = jnp.max(s, axis=1, keepdims=True)
        p = jnp.exp2(s - m)
        l = jnp.sum(p, axis=1, keepdims=True)
        return p.astype(jnp.bfloat16), l, m + jnp.log2(l)

    def finish(n, p, l):
        both = slice(n * HD, (n + 2) * HD)
        v = jnp.concatenate([glob_ref[1, :, both], kv_ref[1, c, :, both]], axis=0)
        return (pair_context(p, v) / l).astype(jnp.bfloat16)

    state = jnp.zeros((BLK, HD), jnp.float32)
    group = 4
    for first in range(0, heads // 2, group):
        contexts, levels = [], []
        scored = weighed = None
        for t in range(group + 2):
            fresh = ready = None
            if t < group:
                if first == 0 and t == 0:
                    copies[0].wait()
                fresh = score(2 * (first + t))
            if scored is not None:
                p, l, level = weigh(scored)
                ready = (p, l)
                levels.append(level)
            if weighed is not None:
                if first == 0 and t == 2:
                    copies[1].wait()
                contexts.append(finish(2 * (first + t - 2), *weighed))
            scored, weighed = fresh, ready
        for n, (context, level) in enumerate(zip(contexts, levels)):
            high = level.astype(jnp.bfloat16).astype(jnp.float32)
            middle = (level - high).astype(jnp.bfloat16).astype(jnp.float32)
            low = level - high - middle
            for i in range(2):
                rows = slice(i * BLK, (i + 1) * BLK)
                head = 2 * (first + n) + i
                at = place - head
                state = jnp.where(
                    at == 0, high[rows], jnp.where(at == 32, middle[rows], jnp.where(at == 64, low[rows], state))
                )
                out_ref[2 * BLK :, head * HD : (head + 1) * HD] = context[rows]
    out_ref[2 * BLK :, width:] = state.astype(jnp.bfloat16)


def near_kernel(info_ref, message_ref, up_ref, down_ref, acc_ref, max_ref, sum_ref, out_ref, sq_ref, take_ref):
    me = lax.axis_index("dp")
    width = out_ref.shape[1]
    heads = width // HD
    batch = head_batch(heads)
    length = info_ref[LENGTH]
    alive = me < length
    up_live = (me >= 1) & (me - 1 < length)
    down_live = me + 1 < length
    list_heads(take_ref, 0, heads, jnp.where(me < 2, me + 2, me - 2), lambda h: info_ref[h])
    list_heads(take_ref, 1, heads, 3 - me, lambda h: info_ref[h])
    lane = lax.broadcasted_iota(jnp.int32, (1, 2 * BLK), 1)
    state = message_ref[2 * BLK :, width:].astype(jnp.float32)
    state = state + pltpu.roll(state, 96, 1) + pltpu.roll(state, 64, 1)
    squares = jnp.zeros((BLK, HD), jnp.float32)

    def score(numbers):
        items = []
        for h in numbers:
            col = slice(h * HD, (h + 1) * HD)
            block = info_ref[h]
            up_bias = jnp.where(up_live, jnp.where(block == me - 1, 1.0, 0.0), NEG)
            down_bias = jnp.where(down_live, jnp.where(block == me + 1, 1.0, 0.0), NEG)
            bias = jnp.where(lane < BLK, up_bias, down_bias)
            k = jnp.concatenate([up_ref[0, :, col], down_ref[0, :, col]], axis=0)
            v = jnp.concatenate([up_ref[1, :, col], down_ref[1, :, col]], axis=0)
            s = dot_nt(message_ref[:BLK, col], k) * SCALE + bias
            level = jnp.broadcast_to(state[:, h : h + 1], (BLK, HD))
            near = jnp.where(jnp.abs(block - me) < 2, 1.0, 0.0)
            items.append((col, s, v, level, message_ref[BLK : 2 * BLK, col], message_ref[2 * BLK :, col], near))
        return items

    def weigh(items):
        outs = []
        for col, s, v, level, res, context, near in items:
            m = jnp.maximum(level, jnp.max(s, axis=1, keepdims=True))
            p = jnp.exp2(s - m).astype(jnp.bfloat16)
            outs.append((col, m, p, v, jnp.exp2(level - m), res, context, near))
        return outs

    def finish(items, squares):
        outs = []
        for col, m, p, v, alpha, res, context, near in items:
            pv = dot_nn(p, with_ones(v))
            l = alpha + pv[:, HD:]
            acc = alpha * context.astype(jnp.float32) + pv[:, :HD]
            updated = (res.astype(jnp.float32) + jnp.where(alive, acc / l, 0.0)).astype(jnp.bfloat16)
            wide = updated.astype(jnp.float32)
            squares = squares + wide * wide * near
            outs.append((col, m, l, acc, updated))
        for col, m, l, acc, updated in outs:
            max_ref[:, col] = m
            sum_ref[:, col] = l
            acc_ref[:, col] = acc
            out_ref[:, col] = updated
        return squares

    batches = [range(start, start + batch) for start in range(0, heads, batch)]
    scored = weighed = None
    for turn in range(len(batches) + 2):
        fresh = score(batches[turn]) if turn < len(batches) else None
        ready = weigh(scored) if scored else None
        if weighed:
            squares = finish(weighed, squares)
        scored, weighed = fresh, ready
    sq_ref[...] = squares


def tile_kernel(row, last, *refs):
    infos, takes, messages, tiles, accs, maxes, sums, olds, old_sqs = [refs[2 * n : 2 * n + 2] for n in range(9)]
    me = lax.axis_index("dp")
    if last:
        outs = [refs[18].at[1 - sent_in(turn)] for turn in range(2)]
        sqs = [refs[19].at[1 - sent_in(turn)] for turn in range(2)]
        for turn in range(2):
            outs[turn][...] = olds[turn][...]
    else:
        outs, sqs = refs[18:20], refs[20:22]

    def work():
        places = [(t, s) for t in range(2) for s in range(tiles[0].shape[0])]
        chosen = [takes[t][row, s] for t, s in places]
        cols = [pl.ds(pl.multiple_of(h * HD, HD), HD) for h in chosen]
        live = [infos[t][h] < infos[t][LENGTH] for (t, _), h in zip(places, chosen)]
        scores = [
            dot_nt(messages[t][:BLK, col], tiles[t][s, 0]) * SCALE + jnp.where(ok, 0.0, NEG)
            for (t, s), col, ok in zip(places, cols, live)
        ]
        before = [(maxes[t][:, col], sums[t][:, col], accs[t][:, col]) for (t, _), col in zip(places, cols)]
        residuals = [messages[t][BLK : 2 * BLK, col].astype(jnp.float32) for (t, _), col in zip(places, cols)]
        news = merge(scores, before, [tiles[t][s, 1] for t, s in places])
        updates = [
            (res + jnp.where(me < infos[t][LENGTH], acc / l, 0.0)).astype(jnp.bfloat16)
            for (t, _), res, (_, l, acc) in zip(places, residuals, news)
        ]
        squares = [old_sqs[t][...] for t in range(2)]
        for (t, _), col, updated in zip(places, cols, updates):
            outs[t][:, col] = updated
            wide = updated.astype(jnp.float32)
            squares[t] = squares[t] + wide * wide
        for t in range(2):
            sqs[t][...] = squares[t]

    if last:
        work()
    else:
        for t in range(2):
            sqs[t][...] = old_sqs[t][...]
        pl.when((me == 0) | (me == 3))(work)


def body_chain(residual, queries, keys_values, global_kv, block_ids, lengths, gain):
    width = residual.shape[-1]
    heads = width // HD
    pipe_count = lax.axis_size("pipe")
    capacity = heads // 4
    q, res, glob, kv, length = queries[0], residual[0], global_kv[0], keys_values[0], lengths[0]
    own_ids = block_ids[0, :, 0]
    glob_count = glob.shape[2]
    params = pltpu.CompilerParams(vmem_limit_bytes=VMEM_LIMIT)
    order = jnp.stack([sent_in(0), sent_in(1)])

    def send(array, turn, moves):
        pairs = []
        for p in range(pipe_count):
            other = p ^ 1 if turn == 1 else ((p + 1) ^ 1) - 1
            if 0 <= other < pipe_count:
                pairs += [
                    ((i * pipe_count + p) if direct else (i * pipe_count + other), j * pipe_count + other)
                    for i, j, direct in moves
                ]
        return lax.ppermute(array, ("dp", "pipe"), pairs)

    ids_3 = lax.ppermute(own_ids, "dp", [(0, 3), (3, 0)])
    ids_2 = lax.ppermute(own_ids, "dp", [(2, 0), (1, 3)])
    kvs, ups, downs = [], [], []
    for turn in range(2):
        c = order[turn]
        note = jnp.pad(lax.dynamic_index_in_dim(own_ids, c, 0, keepdims=False), (0, HD - heads)).astype(jnp.bfloat16)
        note = jnp.broadcast_to(note, (2, BLK, HD))
        kvs.append(jnp.concatenate([lax.dynamic_index_in_dim(kv, c, 1, keepdims=False), note], axis=2))
    kv, ids_3, ids_2, *kvs = lax.optimization_barrier((kv, ids_3, ids_2, *kvs))
    same = [(i, i, True) for i in range(4)]
    crossed = send(kvs[0], 0, same)
    own_kv = kv
    kv, crossed = lax.optimization_barrier((kv, crossed))
    for turn, source in enumerate((crossed, kvs[1])):
        ups.append(send(source, turn, [(i, i + 1, turn == 1) for i in range(3)]))
        downs.append(send(source, turn, [(i + 1, i, turn == 1) for i in range(3)]))

    message = jax.ShapeDtypeStruct((3 * BLK, width + HD), jnp.bfloat16)

    def local_part(turn, kv):
        return pl.pallas_call(
            functools.partial(message_kernel, turn),
            out_shape=message,
            in_specs=[smem()] * 3 + [vmem()] * 3 + [pl.BlockSpec(memory_space=pl.ANY)],
            out_specs=vmem(),
            scratch_shapes=[
                pltpu.VMEM((2, glob_count, width), jnp.bfloat16),
                pltpu.SemaphoreType.DMA((2,)),
            ],
            compiler_params=pltpu.CompilerParams(vmem_limit_bytes=LOCAL_LIMIT),
        )(order, own_ids, length, q, res, kv, glob)

    messages = [local_part(0, own_kv), local_part(1, kv)]
    messages = list(lax.optimization_barrier(tuple(messages)))
    messages = [send(messages[turn], turn, same) for turn in range(2)]
    tiles = jax.ShapeDtypeStruct((capacity, 2, BLK, HD), jnp.bfloat16)
    distant = pl.pallas_call(
        distant_kernel,
        out_shape=[tiles, tiles],
        in_specs=[smem(), vmem(), vmem()],
        out_specs=[vmem(), vmem()],
        scratch_shapes=[pltpu.SMEM((1, capacity), jnp.int32)],
        compiler_params=params,
    )(ids_3, *kvs)
    far_3 = [send(distant[turn], turn, [(0, 3, True), (3, 0, True)]) for turn in range(2)]

    far_2 = []
    for turn in range(2):
        array = pl.pallas_call(
            functools.partial(forward_kernel, turn),
            out_shape=tiles,
            in_specs=[smem()] * 3 + [vmem()] * 3,
            out_specs=vmem(),
            scratch_shapes=[pltpu.SMEM((1, capacity), jnp.int32)],
            compiler_params=params,
        )(
            ids_2,
            ups[turn][0, 0, width:].astype(jnp.int32),
            downs[turn][0, 0, width:].astype(jnp.int32),
            kvs[turn],
            ups[turn],
            downs[turn],
        )
        far_2.append(send(array, turn, [(0, 2, True), (3, 1, True), (2, 3, False), (1, 0, False)]))

    wide = jax.ShapeDtypeStruct((BLK, width), jnp.float32)
    row = jax.ShapeDtypeStruct((BLK, width), jnp.bfloat16)
    square = jax.ShapeDtypeStruct((BLK, HD), jnp.float32)
    near, infos = [None, None], [None, None]
    for turn in (1, 0):
        if turn == 0:
            messages[0], near[1][4] = lax.optimization_barrier((messages[0], near[1][4]))
        infos[turn] = messages[turn][0, width:].astype(jnp.int32)
        near[turn] = list(
            pl.pallas_call(
                near_kernel,
                out_shape=[wide, wide, wide, row, square, jax.ShapeDtypeStruct((2, capacity), jnp.int32)],
                in_specs=[smem()] + [vmem()] * 3,
                out_specs=[vmem()] * 5 + [smem()],
                compiler_params=params,
            )(infos[turn], messages[turn], ups[turn], downs[turn])
        )
    accs, maxes, sums, updates, squares, takes = [list(items) for items in zip(*near)]
    for index, got, last in ((1, far_3, False), (0, far_2, True)):
        pair = [jax.ShapeDtypeStruct((2,) + kind.shape, kind.dtype) for kind in (row, square)]
        results = pl.pallas_call(
            functools.partial(tile_kernel, index, last),
            out_shape=pair if last else [row, row, square, square],
            in_specs=[smem()] * 4 + [vmem()] * 14,
            out_specs=[vmem()] * (2 if last else 4),
            input_output_aliases={} if last else {14: 0, 15: 1},
            compiler_params=params,
        )(*infos, *takes, *messages, *got, *accs, *maxes, *sums, *updates, *squares)
        if not last:
            updates, squares = results[:2], results[2:]

    updated, squares = results
    total = lax.psum(jnp.sum(squares, axis=2), "tensor")
    inverse = lax.rsqrt(total / D + epsilon)
    normed = updated.astype(jnp.float32) * inverse[:, :, None] * gain[0][:, None, :].astype(jnp.float32)
    return normed.astype(jnp.bfloat16)[None]


def body(*arrays):
    heads = arrays[0].shape[-1] // HD
    chain = lax.axis_size("dp") == 4 and lax.axis_size("pipe") % 2 == 0 and heads % 8 == 0 and heads <= 32
    return (body_chain if chain else body_any)(*arrays)


def solution(mesh):
    in_specs = (
        P("pipe", None, "dp", "tensor"),
        P("pipe", None, "dp", "tensor"),
        P("pipe", None, None, "dp", "tensor"),
        P("pipe", None, None, None, "tensor"),
        P("pipe", None, "dp", "tensor"),
        P("pipe", None),
        P("pipe", None, "tensor"),
    )
    out_specs = P("pipe", None, "dp", "tensor")
    return jax.shard_map(body, mesh=mesh, in_specs=in_specs, out_specs=out_specs, check_vma=False)
```

```python
import functools

import jax
import jax.numpy as jnp
from jax import lax
from jax.experimental import pallas as pl
from jax.experimental.pallas import tpu as pltpu
from jax.sharding import PartitionSpec as P

D = 6144
HD = 128
BLK = 64
LOG2E = 1.4426950408889634
SCALE = HD ** (-0.5) * LOG2E
NEG = -1e30
VMEM_LIMIT = 20 * 1024 * 1024

epsilon = 1e-05


def dot_nt(a, b):
    return lax.dot_general(a, b, (((1,), (1,)), ((), ())), preferred_element_type=jnp.float32)


def dot_nn(a, b):
    return lax.dot_general(a, b, (((1,), (0,)), ((), ())), preferred_element_type=jnp.float32)


def with_ones(v):
    return jnp.concatenate([v, jnp.ones((v.shape[0], HD), v.dtype)], axis=1)


def head_group(heads):
    return max(g for g in range(1, 9) if heads % g == 0)


def head_batch(heads):
    return max(g for g in range(1, 5) if heads % g == 0)


def heads_wanted(table_ref, row, ids_ref, asker, block):
    heads, capacity = ids_ref.shape[2], table_ref.shape[2]
    for c in range(2):
        for s in range(capacity):
            table_ref[row, c, s] = -1
        slot = jnp.int32(0)
        for h in range(heads):
            match = (ids_ref[asker, c, h] == block) & (slot < capacity)

            @pl.when(match)
            def _(slot=slot, h=h, c=c):
                table_ref[row, c, slot] = h

            slot = slot + match.astype(jnp.int32)


def copy_tiles(out_ref, list_ref, row, c, source_ref):
    for s in range(out_ref.shape[0]):
        cols = pl.ds(pl.multiple_of(jnp.maximum(list_ref[row, c, s], 0) * HD, HD), HD)
        out_ref[s, 0] = source_ref[0, :, cols]
        out_ref[s, 1] = source_ref[1, :, cols]


def pack_kernel(ids_ref, kv_ref, take_ref, out_ref, list_ref):
    me = lax.axis_index("dp")

    @pl.loop(0, ids_ref.shape[0])
    def _(other):
        far = jnp.abs(other - me) >= 2
        heads_wanted(take_ref, other, ids_ref, me, jnp.where(far, other, -1))
        heads_wanted(list_ref, 0, ids_ref, other, jnp.where(far, me, -1))
        for c in range(2):
            copy_tiles(out_ref.at[other, c], list_ref, 0, c, kv_ref.at[:, c])


def local_kernel(heads_step, ids_ref, len_ref, q_ref, kv_ref, gkv_ref, acc_ref, max_ref, sum_ref):
    me = lax.axis_index("dp")
    c = pl.program_id(0)
    g = pl.program_id(1)
    glob = gkv_ref.shape[2]
    lane = lax.broadcasted_iota(jnp.int32, (1, glob + BLK), 1)
    batch = head_batch(heads_step)
    for start in range(0, heads_step, batch):
        cols = [slice(n * HD, (n + 1) * HD) for n in range(start, start + batch)]
        scores, values = [], []
        for n, col in zip(range(start, start + batch), cols):
            k = jnp.concatenate([gkv_ref[0, 0, :, col], kv_ref[0, 0, :, col]], axis=0)
            values.append(jnp.concatenate([gkv_ref[1, 0, :, col], kv_ref[1, 0, :, col]], axis=0))
            twice = jnp.where(ids_ref[me, c, g * heads_step + n] == me, 1.0, 0.0)
            bias = jnp.where(lane < glob, 0.0, jnp.where(me < len_ref[c], twice, NEG))
            scores.append(dot_nt(q_ref[0, :, col], k) * SCALE + bias)
        tops = [jnp.max(s, axis=1, keepdims=True) for s in scores]
        weights = [jnp.exp2(s - m).astype(jnp.bfloat16) for s, m in zip(scores, tops)]
        sums = [dot_nn(p, with_ones(v)) for p, v in zip(weights, values)]
        for col, m, pv in zip(cols, tops, sums):
            acc_ref[0, :, col] = pv[:, :HD]
            sum_ref[0, :, col] = pv[:, HD:]
            max_ref[0, :, col] = jnp.broadcast_to(m, (BLK, HD))


def merge(scores, olds, values):
    tops = [jnp.maximum(old[0], jnp.max(s, axis=1, keepdims=True)) for s, old in zip(scores, olds)]
    weights = [jnp.exp2(s - m[:, : s.shape[1]]).astype(jnp.bfloat16) for s, m in zip(scores, tops)]
    alphas = [jnp.exp2(old[0] - m) for old, m in zip(olds, tops)]
    added = [dot_nn(p, with_ones(v)) for p, v in zip(weights, values)]
    return [
        (m, alpha * old[1] + pv[:, HD:], alpha * old[2] + pv[:, :HD])
        for m, alpha, old, pv in zip(tops, alphas, olds, added)
    ]


def window_kernel(ids_ref, len_ref, q_ref, up_ref, down_ref, res_ref, acc_ref, max_ref, sum_ref, new_acc_ref, new_max_ref, new_sum_ref, out_ref, sq_ref):
    me = lax.axis_index("dp")
    heads = q_ref.shape[2] // HD
    batch = head_batch(heads)
    lane = lax.broadcasted_iota(jnp.int32, (1, 2 * BLK), 1)
    for c in range(2):
        length = len_ref[c]
        alive = me < length
        up_live = (me >= 1) & (me - 1 < length)
        down_live = me + 1 < length

        def step(g, squares, c=c, alive=alive, up_live=up_live, down_live=down_live):
            cols = [pl.ds(pl.multiple_of((g * batch + n) * HD, HD), HD) for n in range(batch)]
            blocks = [ids_ref[me, c, g * batch + n] for n in range(batch)]
            scores, values = [], []
            for block, col in zip(blocks, cols):
                up_bias = jnp.where(up_live, jnp.where(block == me - 1, 1.0, 0.0), NEG)
                down_bias = jnp.where(down_live, jnp.where(block == me + 1, 1.0, 0.0), NEG)
                bias = jnp.where(lane < BLK, up_bias, down_bias)
                k = jnp.concatenate([up_ref[0, c, :, col], down_ref[0, c, :, col]], axis=0)
                values.append(jnp.concatenate([up_ref[1, c, :, col], down_ref[1, c, :, col]], axis=0))
                scores.append(dot_nt(q_ref[c, :, col], k) * SCALE + bias)
            olds = [(max_ref[c, :, col], sum_ref[c, :, col], acc_ref[c, :, col]) for col in cols]
            residuals = [res_ref[c, :, col].astype(jnp.float32) for col in cols]
            news = merge(scores, olds, values)
            updates = [
                (res + jnp.where(alive, acc / l, 0.0)).astype(jnp.bfloat16) for res, (_, l, acc) in zip(residuals, news)
            ]
            for block, col, (m, l, acc), updated in zip(blocks, cols, news, updates):
                new_max_ref[c, :, col] = m
                new_sum_ref[c, :, col] = l
                new_acc_ref[c, :, col] = acc
                out_ref[c, :, col] = updated
                wide = updated.astype(jnp.float32)
                squares = squares + wide * wide * jnp.where(jnp.abs(block - me) < 2, 1.0, 0.0)
            return squares

        sq_ref[c] = lax.fori_loop(0, heads // batch, step, jnp.zeros((BLK, HD), jnp.float32))


def far_kernel(ids_ref, take_ref, len_ref, tile_ref, q_ref, res_ref, acc_ref, max_ref, sum_ref, old_ref, old_sq_ref, out_ref, sq_ref):
    del old_ref
    me = lax.axis_index("dp")
    owners, _, capacity = take_ref.shape
    sq_ref[...] = old_sq_ref[...]

    def one_owner(owner):
        places = [(c, s) for c in range(2) for s in range(capacity)]
        taken = [take_ref[owner, c, s] for c, s in places]
        chosen = [jnp.maximum(h, 0) for h in taken]
        cols = [pl.ds(pl.multiple_of(h * HD, HD), HD) for h in chosen]
        live = [(t >= 0) & (ids_ref[me, c, h] < len_ref[c]) for (c, _), t, h in zip(places, taken, chosen)]
        scores = [
            dot_nt(q_ref[c, :, col], tile_ref[owner, c, s, 0]) * SCALE + jnp.where(ok, 0.0, NEG)
            for (c, s), col, ok in zip(places, cols, live)
        ]
        olds = [(max_ref[c, :, col], sum_ref[c, :, col], acc_ref[c, :, col]) for (c, _), col in zip(places, cols)]
        residuals = [res_ref[c, :, col].astype(jnp.float32) for (c, _), col in zip(places, cols)]
        news = merge(scores, olds, [tile_ref[owner, c, s, 1] for c, s in places])
        updates = [
            (res + jnp.where(me < len_ref[c], acc / l, 0.0)).astype(jnp.bfloat16)
            for (c, _), res, (_, l, acc) in zip(places, residuals, news)
        ]
        squares = [jnp.zeros((BLK, HD), jnp.float32)] * 2
        for (c, _), t, updated in zip(places, taken, updates):
            wide = updated.astype(jnp.float32)
            squares[c] = squares[c] + wide * wide * jnp.where(t >= 0, 1.0, 0.0)
        for c in range(2):
            sq_ref[c] += squares[c]
        for (c, _), t, col, updated in zip(places, taken, cols, updates):

            @pl.when(t >= 0)
            def _(c=c, col=col, updated=updated):
                out_ref[c, :, col] = updated

    pl.loop(0, owners)(one_owner)


def smem():
    return pl.BlockSpec(memory_space=pltpu.SMEM)


def vmem():
    return pl.BlockSpec(memory_space=pltpu.VMEM)


def body_any(residual, queries, keys_values, global_kv, block_ids, lengths, gain):
    width = residual.shape[-1]
    heads = width // HD
    dp_count = lax.axis_size("dp")
    pipe_count = lax.axis_size("pipe")
    tensor_count = lax.axis_size("tensor")
    group = head_group(heads)
    steps = heads // group
    lanes = group * HD
    capacity = (heads + dp_count - 1) // dp_count
    q = queries[0]
    res = residual[0]
    glob = global_kv[0]
    length = lengths[0]
    glob_count = glob.shape[2]
    params = pltpu.CompilerParams(vmem_limit_bytes=VMEM_LIMIT)

    ids = block_ids[0, :, 0]
    ids = lax.all_to_all(jnp.broadcast_to(ids, (dp_count,) + ids.shape), "dp", split_axis=0, concat_axis=0, tiled=True)
    kv, ids = lax.optimization_barrier((keys_values[0], ids))
    up = lax.ppermute(kv, "dp", [(i, i + 1) for i in range(dp_count - 1)])
    down = lax.ppermute(kv, "dp", [(i + 1, i) for i in range(dp_count - 1)])

    lines = [[(i + 1, i) for i in range(pipe_count - 1)], [(i, i + 1) for i in range(pipe_count - 1)]]
    gains = [lax.ppermute(gain[0, c], "pipe", [(j, i) for i, j in lines[c]]) for c in range(2)]
    q, gains = lax.optimization_barrier((q, gains))
    wide = jax.ShapeDtypeStruct((2, BLK, width), jnp.float32)
    row_spec = pl.BlockSpec((1, BLK, lanes), lambda c, g: (c, 0, g))
    pair_spec = pl.BlockSpec((2, 1, BLK, lanes), lambda c, g: (0, c, 0, g))
    acc, maxes, sums = pl.pallas_call(
        functools.partial(local_kernel, group),
        grid=(2, steps),
        out_shape=[wide] * 3,
        in_specs=[
            smem(),
            smem(),
            row_spec,
            pair_spec,
            pl.BlockSpec((2, 1, glob_count, lanes), lambda c, g: (0, c, 0, g)),
        ],
        out_specs=[row_spec] * 3,
        compiler_params=params,
        cost_estimate=pl.CostEstimate(
            flops=4 * 2 * BLK * width * (glob_count + BLK), bytes_accessed=14 * 2**20, transcendentals=0
        ),
    )(ids, length, q, kv, glob)

    kv, acc = lax.optimization_barrier((kv, acc))

    tile = (2, capacity, 2, BLK, HD)
    take, tiles_all = pl.pallas_call(
        pack_kernel,
        out_shape=[
            jax.ShapeDtypeStruct((dp_count, 2, capacity), jnp.int32),
            jax.ShapeDtypeStruct((dp_count,) + tile, jnp.bfloat16),
        ],
        in_specs=[smem(), vmem()],
        out_specs=[smem(), vmem()],
        scratch_shapes=[pltpu.SMEM((1, 2, capacity), jnp.int32)],
        compiler_params=params,
    )(ids, kv)
    far = [(take, lax.all_to_all(tiles_all, "dp", split_axis=0, concat_axis=0, tiled=True))]

    acc, maxes, sums, updated, squares = pl.pallas_call(
        window_kernel,
        out_shape=[wide] * 3
        + [jax.ShapeDtypeStruct((2, BLK, width), jnp.bfloat16), jax.ShapeDtypeStruct((2, BLK, HD), jnp.float32)],
        in_specs=[smem(), smem()] + [vmem()] * 7,
        out_specs=[vmem()] * 5,
        compiler_params=params,
        cost_estimate=pl.CostEstimate(
            flops=4 * 2 * BLK * width * 2 * BLK, bytes_accessed=9 * 2**20, transcendentals=0
        ),
    )(ids, length, q, up, down, res, acc, maxes, sums)

    for heads_taken, tiles_got in far:
        updated, squares = pl.pallas_call(
            far_kernel,
            out_shape=[
                jax.ShapeDtypeStruct((2, BLK, width), jnp.bfloat16),
                jax.ShapeDtypeStruct((2, BLK, HD), jnp.float32),
            ],
            in_specs=[smem(), smem(), smem()] + [vmem()] * 8,
            out_specs=[vmem()] * 2,
            input_output_aliases={9: 0},
            compiler_params=params,
        )(ids, heads_taken, length, tiles_got, q, res, acc, maxes, sums, updated, squares)

    total = lax.psum(jnp.sum(squares, axis=2), "tensor")
    inverse = lax.rsqrt(total / D + epsilon)
    normed = [
        (updated[c].astype(jnp.float32) * inverse[c][:, None] * gains[c].astype(jnp.float32)).astype(jnp.bfloat16)
        for c in range(2)
    ]
    return jnp.stack([lax.ppermute(normed[c], "pipe", lines[c]) for c in range(2)])[None]


def pair_queries(first, second):
    none = jnp.zeros_like(first)
    return jnp.concatenate(
        [jnp.concatenate([first, none], axis=1), jnp.concatenate([none, second], axis=1)], axis=0
    )


def pair_rows(first, second, lanes):
    return jnp.concatenate([jnp.broadcast_to(first, (BLK, lanes)), jnp.broadcast_to(second, (BLK, lanes))], axis=0)


def pair_context(weights, values):
    both = dot_nn(weights.astype(jnp.bfloat16), values)
    return jnp.concatenate([both[:BLK, :HD], both[BLK:, HD:]], axis=0)


LENGTH = 32


def sent_in(turn):
    parity = lax.rem(lax.axis_index("pipe"), 2)
    return parity if turn == 0 else 1 - parity


def copy_heads(out_ref, list_ref, row, source_ref):
    for s in range(out_ref.shape[0]):
        cols = pl.ds(pl.multiple_of(jnp.maximum(list_ref[row, s], 0) * HD, HD), HD)
        out_ref[s, 0] = source_ref[0, :, cols]
        out_ref[s, 1] = source_ref[1, :, cols]


def list_heads(list_ref, row, heads, block, block_of):
    capacity = list_ref.shape[1]
    for s in range(capacity):
        list_ref[row, s] = 0
    slot = jnp.int32(0)
    for h in range(heads):
        match = (block_of(h) == block) & (slot < capacity)

        @pl.when(match)
        def _(slot=slot, h=h):
            list_ref[row, slot] = h

        slot = slot + match.astype(jnp.int32)


def distant_kernel(ids_ref, kv0_ref, kv1_ref, tile0_ref, tile1_ref, list_ref):
    me = lax.axis_index("dp")
    heads = ids_ref.shape[1]

    @pl.when((me == 0) | (me == 3))
    def _():
        for turn, (kv_ref, tile_ref) in enumerate(((kv0_ref, tile0_ref), (kv1_ref, tile1_ref))):
            c = sent_in(turn)
            list_heads(list_ref, 0, heads, me, lambda h, c=c: ids_ref[c, h])
            copy_heads(tile_ref, list_ref, 0, kv_ref)


def forward_kernel(turn, ids_ref, up_ids_ref, down_ids_ref, kv_ref, up_ref, down_ref, tile_ref, list_ref):
    me = lax.axis_index("dp")
    heads = ids_ref.shape[1]
    c = sent_in(turn)
    edge = (me == 0) | (me == 3)
    list_heads(
        list_ref,
        0,
        heads,
        jnp.where(edge, me, 3 - me),
        lambda h: jnp.where(edge, ids_ref[c, h], jnp.where(me == 1, up_ids_ref[h], down_ids_ref[h])),
    )
    pl.when(edge)(lambda: copy_heads(tile_ref, list_ref, 0, kv_ref))
    pl.when(me == 1)(lambda: copy_heads(tile_ref, list_ref, 0, down_ref))
    pl.when(me == 2)(lambda: copy_heads(tile_ref, list_ref, 0, up_ref))


def message_kernel(turn, heads_step, order_ref, ids_ref, len_ref, q_ref, res_ref, kv_ref, gkv_ref, out_ref):
    me = lax.axis_index("dp")
    g = pl.program_id(0)
    c = order_ref[turn]
    glob = gkv_ref.shape[2]
    width = out_ref.shape[1] - HD
    heads = width // HD
    place = lax.broadcasted_iota(jnp.int32, (1, HD), 1)

    @pl.when(g == 0)
    def _():
        note = jnp.where(place == LENGTH, len_ref[c], 0)
        for h in range(heads):
            note = jnp.where(place == h, ids_ref[c, h], note)
        note = jnp.broadcast_to(note.astype(jnp.float32), (BLK, HD)).astype(jnp.bfloat16)
        out_ref[:BLK, width:] = note
        out_ref[BLK:, width:] = jnp.zeros((2 * BLK, HD), jnp.bfloat16)

    state = out_ref[2 * BLK :, width:].astype(jnp.float32)
    own_live = me < len_ref[c]
    numbers = range(0, heads_step, 2)
    scores, values = [], []
    for n in numbers:
        both = slice(n * HD, (n + 2) * HD)
        q = pair_queries(q_ref[0, :, n * HD : (n + 1) * HD], q_ref[0, :, (n + 1) * HD : (n + 2) * HD])
        k = jnp.concatenate([gkv_ref[0, 0, :, both], kv_ref[0, 0, :, both]], axis=0)
        values.append(jnp.concatenate([gkv_ref[1, 0, :, both], kv_ref[1, 0, :, both]], axis=0))
        own = [
            jnp.where(own_live, jnp.where(ids_ref[c, g * heads_step + n + i] == me, 1.0, 0.0), NEG) for i in range(2)
        ]
        s = dot_nt(q, k) * SCALE
        scores.append(jnp.concatenate([s[:, :glob], s[:, glob:] + pair_rows(*own, BLK)], axis=1))
    tops = [jnp.max(s, axis=1, keepdims=True) for s in scores]
    weights = [jnp.exp2(s - m) for s, m in zip(scores, tops)]
    sums = [jnp.sum(p, axis=1, keepdims=True) for p in weights]
    contexts = [(pair_context(p, v) / l).astype(jnp.bfloat16) for p, v, l in zip(weights, values, sums)]
    levels = [m + jnp.log2(l) for m, l in zip(tops, sums)]
    for n, context, level in zip(numbers, contexts, levels):
        high = level.astype(jnp.bfloat16).astype(jnp.float32)
        middle = (level - high).astype(jnp.bfloat16).astype(jnp.float32)
        low = level - high - middle
        for i in range(2):
            rows = slice(i * BLK, (i + 1) * BLK)
            head = g * heads_step + n + i
            at = place - head
            state = jnp.where(at == 0, high[rows], jnp.where(at == 32, middle[rows], jnp.where(at == 64, low[rows], state)))
            col = slice((n + i) * HD, (n + i + 1) * HD)
            out = pl.ds(pl.multiple_of(head * HD, HD), HD)
            out_ref[:BLK, out] = q_ref[0, :, col]
            out_ref[BLK : 2 * BLK, out] = res_ref[0, :, col]
            out_ref[2 * BLK :, out] = context[rows]
    out_ref[2 * BLK :, width:] = state.astype(jnp.bfloat16)


def near_kernel(info_ref, message_ref, up_ref, down_ref, acc_ref, max_ref, sum_ref, out_ref, sq_ref, take_ref):
    me = lax.axis_index("dp")
    width = out_ref.shape[1]
    heads = width // HD
    batch = head_batch(heads)
    length = info_ref[LENGTH]
    alive = me < length
    up_live = (me >= 1) & (me - 1 < length)
    down_live = me + 1 < length
    list_heads(take_ref, 0, heads, jnp.where(me < 2, me + 2, me - 2), lambda h: info_ref[h])
    list_heads(take_ref, 1, heads, 3 - me, lambda h: info_ref[h])
    lane = lax.broadcasted_iota(jnp.int32, (1, 2 * BLK), 1)
    state = message_ref[2 * BLK :, width:].astype(jnp.float32)
    state = state + pltpu.roll(state, 96, 1) + pltpu.roll(state, 64, 1)
    squares = jnp.zeros((BLK, HD), jnp.float32)

    def score(numbers):
        items = []
        for h in numbers:
            col = slice(h * HD, (h + 1) * HD)
            block = info_ref[h]
            up_bias = jnp.where(up_live, jnp.where(block == me - 1, 1.0, 0.0), NEG)
            down_bias = jnp.where(down_live, jnp.where(block == me + 1, 1.0, 0.0), NEG)
            bias = jnp.where(lane < BLK, up_bias, down_bias)
            k = jnp.concatenate([up_ref[0, :, col], down_ref[0, :, col]], axis=0)
            v = jnp.concatenate([up_ref[1, :, col], down_ref[1, :, col]], axis=0)
            s = dot_nt(message_ref[:BLK, col], k) * SCALE + bias
            level = jnp.broadcast_to(state[:, h : h + 1], (BLK, HD))
            near = jnp.where(jnp.abs(block - me) < 2, 1.0, 0.0)
            items.append((col, s, v, level, message_ref[BLK : 2 * BLK, col], message_ref[2 * BLK :, col], near))
        return items

    def weigh(items):
        outs = []
        for col, s, v, level, res, context, near in items:
            m = jnp.maximum(level, jnp.max(s, axis=1, keepdims=True))
            p = jnp.exp2(s - m).astype(jnp.bfloat16)
            outs.append((col, m, p, v, jnp.exp2(level - m), res, context, near))
        return outs

    def finish(items, squares):
        outs = []
        for col, m, p, v, alpha, res, context, near in items:
            pv = dot_nn(p, with_ones(v))
            l = alpha + pv[:, HD:]
            acc = alpha * context.astype(jnp.float32) + pv[:, :HD]
            updated = (res.astype(jnp.float32) + jnp.where(alive, acc / l, 0.0)).astype(jnp.bfloat16)
            wide = updated.astype(jnp.float32)
            squares = squares + wide * wide * near
            outs.append((col, m, l, acc, updated))
        for col, m, l, acc, updated in outs:
            max_ref[:, col] = m
            sum_ref[:, col] = l
            acc_ref[:, col] = acc
            out_ref[:, col] = updated
        return squares

    batches = [range(start, start + batch) for start in range(0, heads, batch)]
    scored = weighed = None
    for turn in range(len(batches) + 2):
        fresh = score(batches[turn]) if turn < len(batches) else None
        ready = weigh(scored) if scored else None
        if weighed:
            squares = finish(weighed, squares)
        scored, weighed = fresh, ready
    sq_ref[...] = squares


def tile_kernel(row, last, *refs):
    infos, takes, messages, tiles, accs, maxes, sums, olds, old_sqs = [refs[2 * n : 2 * n + 2] for n in range(9)]
    me = lax.axis_index("dp")
    if last:
        outs = [refs[18].at[1 - sent_in(turn)] for turn in range(2)]
        sqs = [refs[19].at[1 - sent_in(turn)] for turn in range(2)]
        for turn in range(2):
            outs[turn][...] = olds[turn][...]
    else:
        outs, sqs = refs[18:20], refs[20:22]

    def work():
        places = [(t, s) for t in range(2) for s in range(tiles[0].shape[0])]
        chosen = [takes[t][row, s] for t, s in places]
        cols = [pl.ds(pl.multiple_of(h * HD, HD), HD) for h in chosen]
        live = [infos[t][h] < infos[t][LENGTH] for (t, _), h in zip(places, chosen)]
        scores = [
            dot_nt(messages[t][:BLK, col], tiles[t][s, 0]) * SCALE + jnp.where(ok, 0.0, NEG)
            for (t, s), col, ok in zip(places, cols, live)
        ]
        before = [(maxes[t][:, col], sums[t][:, col], accs[t][:, col]) for (t, _), col in zip(places, cols)]
        residuals = [messages[t][BLK : 2 * BLK, col].astype(jnp.float32) for (t, _), col in zip(places, cols)]
        news = merge(scores, before, [tiles[t][s, 1] for t, s in places])
        updates = [
            (res + jnp.where(me < infos[t][LENGTH], acc / l, 0.0)).astype(jnp.bfloat16)
            for (t, _), res, (_, l, acc) in zip(places, residuals, news)
        ]
        squares = [old_sqs[t][...] for t in range(2)]
        for (t, _), col, updated in zip(places, cols, updates):
            outs[t][:, col] = updated
            wide = updated.astype(jnp.float32)
            squares[t] = squares[t] + wide * wide
        for t in range(2):
            sqs[t][...] = squares[t]

    if last:
        work()
    else:
        for t in range(2):
            sqs[t][...] = old_sqs[t][...]
        pl.when((me == 0) | (me == 3))(work)


def body_chain(residual, queries, keys_values, global_kv, block_ids, lengths, gain):
    width = residual.shape[-1]
    heads = width // HD
    pipe_count = lax.axis_size("pipe")
    group = head_group(heads)
    steps = heads // group
    lanes = group * HD
    capacity = heads // 4
    q, res, glob, kv, length = queries[0], residual[0], global_kv[0], keys_values[0], lengths[0]
    own_ids = block_ids[0, :, 0]
    glob_count = glob.shape[2]
    params = pltpu.CompilerParams(vmem_limit_bytes=VMEM_LIMIT)
    order = jnp.stack([sent_in(0), sent_in(1)])

    def send(array, turn, moves):
        pairs = []
        for p in range(pipe_count):
            other = p ^ 1 if turn == 1 else ((p + 1) ^ 1) - 1
            if 0 <= other < pipe_count:
                pairs += [
                    ((i * pipe_count + p) if direct else (i * pipe_count + other), j * pipe_count + other)
                    for i, j, direct in moves
                ]
        return lax.ppermute(array, ("dp", "pipe"), pairs)

    ids_3 = lax.ppermute(own_ids, "dp", [(0, 3), (3, 0)])
    ids_2 = lax.ppermute(own_ids, "dp", [(2, 0), (1, 3)])
    kvs, ups, downs = [], [], []
    for turn in range(2):
        c = order[turn]
        note = jnp.pad(lax.dynamic_index_in_dim(own_ids, c, 0, keepdims=False), (0, HD - heads)).astype(jnp.bfloat16)
        note = jnp.broadcast_to(note, (2, BLK, HD))
        kvs.append(jnp.concatenate([lax.dynamic_index_in_dim(kv, c, 1, keepdims=False), note], axis=2))
    kv, ids_3, ids_2, *kvs = lax.optimization_barrier((kv, ids_3, ids_2, *kvs))
    same = [(i, i, True) for i in range(4)]
    crossed = send(kvs[0], 0, same)
    own_kv = kv
    kv, crossed = lax.optimization_barrier((kv, crossed))
    for turn, source in enumerate((crossed, kvs[1])):
        ups.append(send(source, turn, [(i, i + 1, turn == 1) for i in range(3)]))
        downs.append(send(source, turn, [(i + 1, i, turn == 1) for i in range(3)]))

    message = jax.ShapeDtypeStruct((3 * BLK, width + HD), jnp.bfloat16)

    def local_part(turn, kv):
        return pl.pallas_call(
            functools.partial(message_kernel, turn, group),
            grid_spec=pltpu.PrefetchScalarGridSpec(
                num_scalar_prefetch=3,
                grid=(steps,),
                in_specs=[
                    pl.BlockSpec((1, BLK, lanes), lambda g, order, ids, length: (order[turn], 0, g)),
                    pl.BlockSpec((1, BLK, lanes), lambda g, order, ids, length: (order[turn], 0, g)),
                    pl.BlockSpec((2, 1, BLK, lanes), lambda g, order, ids, length: (0, order[turn], 0, g)),
                    pl.BlockSpec((2, 1, glob_count, lanes), lambda g, order, ids, length: (0, order[turn], 0, g)),
                ],
                out_specs=vmem(),
            ),
            out_shape=message,
            compiler_params=params,
        )(order, own_ids, length, q, res, kv, glob)

    messages = [local_part(0, own_kv), local_part(1, kv)]
    messages = list(lax.optimization_barrier(tuple(messages)))
    messages = [send(messages[turn], turn, same) for turn in range(2)]
    tiles = jax.ShapeDtypeStruct((capacity, 2, BLK, HD), jnp.bfloat16)
    distant = pl.pallas_call(
        distant_kernel,
        out_shape=[tiles, tiles],
        in_specs=[smem(), vmem(), vmem()],
        out_specs=[vmem(), vmem()],
        scratch_shapes=[pltpu.SMEM((1, capacity), jnp.int32)],
        compiler_params=params,
    )(ids_3, *kvs)
    far_3 = [send(distant[turn], turn, [(0, 3, True), (3, 0, True)]) for turn in range(2)]

    far_2 = []
    for turn in range(2):
        array = pl.pallas_call(
            functools.partial(forward_kernel, turn),
            out_shape=tiles,
            in_specs=[smem()] * 3 + [vmem()] * 3,
            out_specs=vmem(),
            scratch_shapes=[pltpu.SMEM((1, capacity), jnp.int32)],
            compiler_params=params,
        )(
            ids_2,
            ups[turn][0, 0, width:].astype(jnp.int32),
            downs[turn][0, 0, width:].astype(jnp.int32),
            kvs[turn],
            ups[turn],
            downs[turn],
        )
        far_2.append(send(array, turn, [(0, 2, True), (3, 1, True), (2, 3, False), (1, 0, False)]))

    wide = jax.ShapeDtypeStruct((BLK, width), jnp.float32)
    row = jax.ShapeDtypeStruct((BLK, width), jnp.bfloat16)
    square = jax.ShapeDtypeStruct((BLK, HD), jnp.float32)
    near, infos = [None, None], [None, None]
    for turn in (1, 0):
        if turn == 0:
            messages[0], near[1][4] = lax.optimization_barrier((messages[0], near[1][4]))
        infos[turn] = messages[turn][0, width:].astype(jnp.int32)
        near[turn] = list(
            pl.pallas_call(
                near_kernel,
                out_shape=[wide, wide, wide, row, square, jax.ShapeDtypeStruct((2, capacity), jnp.int32)],
                in_specs=[smem()] + [vmem()] * 3,
                out_specs=[vmem()] * 5 + [smem()],
                compiler_params=params,
            )(infos[turn], messages[turn], ups[turn], downs[turn])
        )
    accs, maxes, sums, updates, squares, takes = [list(items) for items in zip(*near)]
    for index, got, last in ((1, far_3, False), (0, far_2, True)):
        pair = [jax.ShapeDtypeStruct((2,) + kind.shape, kind.dtype) for kind in (row, square)]
        results = pl.pallas_call(
            functools.partial(tile_kernel, index, last),
            out_shape=pair if last else [row, row, square, square],
            in_specs=[smem()] * 4 + [vmem()] * 14,
            out_specs=[vmem()] * (2 if last else 4),
            input_output_aliases={} if last else {14: 0, 15: 1},
            compiler_params=params,
        )(*infos, *takes, *messages, *got, *accs, *maxes, *sums, *updates, *squares)
        if not last:
            updates, squares = results[:2], results[2:]

    updated, squares = results
    total = lax.psum(jnp.sum(squares, axis=2), "tensor")
    inverse = lax.rsqrt(total / D + epsilon)
    normed = updated.astype(jnp.float32) * inverse[:, :, None] * gain[0][:, None, :].astype(jnp.float32)
    return normed.astype(jnp.bfloat16)[None]


def body(*arrays):
    heads = arrays[0].shape[-1] // HD
    chain = lax.axis_size("dp") == 4 and lax.axis_size("pipe") % 2 == 0 and heads % 8 == 0 and heads <= 32
    return (body_chain if chain else body_any)(*arrays)


def solution(mesh):
    in_specs = (
        P("pipe", None, "dp", "tensor"),
        P("pipe", None, "dp", "tensor"),
        P("pipe", None, None, "dp", "tensor"),
        P("pipe", None, None, None, "tensor"),
        P("pipe", None, "dp", "tensor"),
        P("pipe", None),
        P("pipe", None, "tensor"),
    )
    out_specs = P("pipe", None, "dp", "tensor")
    return jax.shard_map(body, mesh=mesh, in_specs=in_specs, out_specs=out_specs, check_vma=False)
```

```python
import functools

import jax
import jax.numpy as jnp
from jax import lax
from jax.experimental import pallas as pl
from jax.experimental.pallas import tpu as pltpu
from jax.sharding import PartitionSpec as P

D = 6144
HD = 128
BLK = 64
LOG2E = 1.4426950408889634
SCALE = HD ** (-0.5) * LOG2E
NEG = -1e30
VMEM_LIMIT = 20 * 1024 * 1024

epsilon = 1e-05


def dot_nt(a, b):
    return lax.dot_general(a, b, (((1,), (1,)), ((), ())), preferred_element_type=jnp.float32)


def dot_nn(a, b):
    return lax.dot_general(a, b, (((1,), (0,)), ((), ())), preferred_element_type=jnp.float32)


def with_ones(v):
    return jnp.concatenate([v, jnp.ones((v.shape[0], HD), v.dtype)], axis=1)


def head_group(heads):
    return max(g for g in range(1, 9) if heads % g == 0)


def head_batch(heads):
    return max(g for g in range(1, 5) if heads % g == 0)


def heads_wanted(table_ref, row, ids_ref, asker, block):
    heads, capacity = ids_ref.shape[2], table_ref.shape[2]
    for c in range(2):
        for s in range(capacity):
            table_ref[row, c, s] = -1
        slot = jnp.int32(0)
        for h in range(heads):
            match = (ids_ref[asker, c, h] == block) & (slot < capacity)

            @pl.when(match)
            def _(slot=slot, h=h, c=c):
                table_ref[row, c, slot] = h

            slot = slot + match.astype(jnp.int32)


def copy_tiles(out_ref, list_ref, row, c, source_ref):
    for s in range(out_ref.shape[0]):
        cols = pl.ds(pl.multiple_of(jnp.maximum(list_ref[row, c, s], 0) * HD, HD), HD)
        out_ref[s, 0] = source_ref[0, :, cols]
        out_ref[s, 1] = source_ref[1, :, cols]


def pack_kernel(ids_ref, kv_ref, take_ref, out_ref, list_ref):
    me = lax.axis_index("dp")

    @pl.loop(0, ids_ref.shape[0])
    def _(other):
        far = jnp.abs(other - me) >= 2
        heads_wanted(take_ref, other, ids_ref, me, jnp.where(far, other, -1))
        heads_wanted(list_ref, 0, ids_ref, other, jnp.where(far, me, -1))
        for c in range(2):
            copy_tiles(out_ref.at[other, c], list_ref, 0, c, kv_ref.at[:, c])


def local_kernel(heads_step, ids_ref, len_ref, q_ref, kv_ref, gkv_ref, acc_ref, max_ref, sum_ref):
    me = lax.axis_index("dp")
    c = pl.program_id(0)
    g = pl.program_id(1)
    glob = gkv_ref.shape[2]
    lane = lax.broadcasted_iota(jnp.int32, (1, glob + BLK), 1)
    batch = head_batch(heads_step)
    for start in range(0, heads_step, batch):
        cols = [slice(n * HD, (n + 1) * HD) for n in range(start, start + batch)]
        scores, values = [], []
        for n, col in zip(range(start, start + batch), cols):
            k = jnp.concatenate([gkv_ref[0, 0, :, col], kv_ref[0, 0, :, col]], axis=0)
            values.append(jnp.concatenate([gkv_ref[1, 0, :, col], kv_ref[1, 0, :, col]], axis=0))
            twice = jnp.where(ids_ref[me, c, g * heads_step + n] == me, 1.0, 0.0)
            bias = jnp.where(lane < glob, 0.0, jnp.where(me < len_ref[c], twice, NEG))
            scores.append(dot_nt(q_ref[0, :, col], k) * SCALE + bias)
        tops = [jnp.max(s, axis=1, keepdims=True) for s in scores]
        weights = [jnp.exp2(s - m).astype(jnp.bfloat16) for s, m in zip(scores, tops)]
        sums = [dot_nn(p, with_ones(v)) for p, v in zip(weights, values)]
        for col, m, pv in zip(cols, tops, sums):
            acc_ref[0, :, col] = pv[:, :HD]
            sum_ref[0, :, col] = pv[:, HD:]
            max_ref[0, :, col] = jnp.broadcast_to(m, (BLK, HD))


def merge(scores, olds, values):
    tops = [jnp.maximum(old[0], jnp.max(s, axis=1, keepdims=True)) for s, old in zip(scores, olds)]
    weights = [jnp.exp2(s - m[:, : s.shape[1]]).astype(jnp.bfloat16) for s, m in zip(scores, tops)]
    alphas = [jnp.exp2(old[0] - m) for old, m in zip(olds, tops)]
    added = [dot_nn(p, with_ones(v)) for p, v in zip(weights, values)]
    return [
        (m, alpha * old[1] + pv[:, HD:], alpha * old[2] + pv[:, :HD])
        for m, alpha, old, pv in zip(tops, alphas, olds, added)
    ]


def window_kernel(ids_ref, len_ref, q_ref, up_ref, down_ref, res_ref, acc_ref, max_ref, sum_ref, new_acc_ref, new_max_ref, new_sum_ref, out_ref, sq_ref):
    me = lax.axis_index("dp")
    heads = q_ref.shape[2] // HD
    batch = head_batch(heads)
    lane = lax.broadcasted_iota(jnp.int32, (1, 2 * BLK), 1)
    for c in range(2):
        length = len_ref[c]
        alive = me < length
        up_live = (me >= 1) & (me - 1 < length)
        down_live = me + 1 < length

        def step(g, squares, c=c, alive=alive, up_live=up_live, down_live=down_live):
            cols = [pl.ds(pl.multiple_of((g * batch + n) * HD, HD), HD) for n in range(batch)]
            blocks = [ids_ref[me, c, g * batch + n] for n in range(batch)]
            scores, values = [], []
            for block, col in zip(blocks, cols):
                up_bias = jnp.where(up_live, jnp.where(block == me - 1, 1.0, 0.0), NEG)
                down_bias = jnp.where(down_live, jnp.where(block == me + 1, 1.0, 0.0), NEG)
                bias = jnp.where(lane < BLK, up_bias, down_bias)
                k = jnp.concatenate([up_ref[0, c, :, col], down_ref[0, c, :, col]], axis=0)
                values.append(jnp.concatenate([up_ref[1, c, :, col], down_ref[1, c, :, col]], axis=0))
                scores.append(dot_nt(q_ref[c, :, col], k) * SCALE + bias)
            olds = [(max_ref[c, :, col], sum_ref[c, :, col], acc_ref[c, :, col]) for col in cols]
            residuals = [res_ref[c, :, col].astype(jnp.float32) for col in cols]
            news = merge(scores, olds, values)
            updates = [
                (res + jnp.where(alive, acc / l, 0.0)).astype(jnp.bfloat16) for res, (_, l, acc) in zip(residuals, news)
            ]
            for block, col, (m, l, acc), updated in zip(blocks, cols, news, updates):
                new_max_ref[c, :, col] = m
                new_sum_ref[c, :, col] = l
                new_acc_ref[c, :, col] = acc
                out_ref[c, :, col] = updated
                wide = updated.astype(jnp.float32)
                squares = squares + wide * wide * jnp.where(jnp.abs(block - me) < 2, 1.0, 0.0)
            return squares

        sq_ref[c] = lax.fori_loop(0, heads // batch, step, jnp.zeros((BLK, HD), jnp.float32))


def far_kernel(ids_ref, take_ref, len_ref, tile_ref, q_ref, res_ref, acc_ref, max_ref, sum_ref, old_ref, old_sq_ref, out_ref, sq_ref):
    del old_ref
    me = lax.axis_index("dp")
    owners, _, capacity = take_ref.shape
    sq_ref[...] = old_sq_ref[...]

    def one_owner(owner):
        places = [(c, s) for c in range(2) for s in range(capacity)]
        taken = [take_ref[owner, c, s] for c, s in places]
        chosen = [jnp.maximum(h, 0) for h in taken]
        cols = [pl.ds(pl.multiple_of(h * HD, HD), HD) for h in chosen]
        live = [(t >= 0) & (ids_ref[me, c, h] < len_ref[c]) for (c, _), t, h in zip(places, taken, chosen)]
        scores = [
            dot_nt(q_ref[c, :, col], tile_ref[owner, c, s, 0]) * SCALE + jnp.where(ok, 0.0, NEG)
            for (c, s), col, ok in zip(places, cols, live)
        ]
        olds = [(max_ref[c, :, col], sum_ref[c, :, col], acc_ref[c, :, col]) for (c, _), col in zip(places, cols)]
        residuals = [res_ref[c, :, col].astype(jnp.float32) for (c, _), col in zip(places, cols)]
        news = merge(scores, olds, [tile_ref[owner, c, s, 1] for c, s in places])
        updates = [
            (res + jnp.where(me < len_ref[c], acc / l, 0.0)).astype(jnp.bfloat16)
            for (c, _), res, (_, l, acc) in zip(places, residuals, news)
        ]
        squares = [jnp.zeros((BLK, HD), jnp.float32)] * 2
        for (c, _), t, updated in zip(places, taken, updates):
            wide = updated.astype(jnp.float32)
            squares[c] = squares[c] + wide * wide * jnp.where(t >= 0, 1.0, 0.0)
        for c in range(2):
            sq_ref[c] += squares[c]
        for (c, _), t, col, updated in zip(places, taken, cols, updates):

            @pl.when(t >= 0)
            def _(c=c, col=col, updated=updated):
                out_ref[c, :, col] = updated

    pl.loop(0, owners)(one_owner)


def smem():
    return pl.BlockSpec(memory_space=pltpu.SMEM)


def vmem():
    return pl.BlockSpec(memory_space=pltpu.VMEM)


def body_any(residual, queries, keys_values, global_kv, block_ids, lengths, gain):
    width = residual.shape[-1]
    heads = width // HD
    dp_count = lax.axis_size("dp")
    pipe_count = lax.axis_size("pipe")
    tensor_count = lax.axis_size("tensor")
    group = head_group(heads)
    steps = heads // group
    lanes = group * HD
    capacity = (heads + dp_count - 1) // dp_count
    q = queries[0]
    res = residual[0]
    glob = global_kv[0]
    length = lengths[0]
    glob_count = glob.shape[2]
    params = pltpu.CompilerParams(vmem_limit_bytes=VMEM_LIMIT)

    ids = block_ids[0, :, 0]
    ids = lax.all_to_all(jnp.broadcast_to(ids, (dp_count,) + ids.shape), "dp", split_axis=0, concat_axis=0, tiled=True)
    kv, ids = lax.optimization_barrier((keys_values[0], ids))
    up = lax.ppermute(kv, "dp", [(i, i + 1) for i in range(dp_count - 1)])
    down = lax.ppermute(kv, "dp", [(i + 1, i) for i in range(dp_count - 1)])

    lines = [[(i + 1, i) for i in range(pipe_count - 1)], [(i, i + 1) for i in range(pipe_count - 1)]]
    gains = [lax.ppermute(gain[0, c], "pipe", [(j, i) for i, j in lines[c]]) for c in range(2)]
    q, gains = lax.optimization_barrier((q, gains))
    wide = jax.ShapeDtypeStruct((2, BLK, width), jnp.float32)
    row_spec = pl.BlockSpec((1, BLK, lanes), lambda c, g: (c, 0, g))
    pair_spec = pl.BlockSpec((2, 1, BLK, lanes), lambda c, g: (0, c, 0, g))
    acc, maxes, sums = pl.pallas_call(
        functools.partial(local_kernel, group),
        grid=(2, steps),
        out_shape=[wide] * 3,
        in_specs=[
            smem(),
            smem(),
            row_spec,
            pair_spec,
            pl.BlockSpec((2, 1, glob_count, lanes), lambda c, g: (0, c, 0, g)),
        ],
        out_specs=[row_spec] * 3,
        compiler_params=params,
        cost_estimate=pl.CostEstimate(
            flops=4 * 2 * BLK * width * (glob_count + BLK), bytes_accessed=14 * 2**20, transcendentals=0
        ),
    )(ids, length, q, kv, glob)

    kv, acc = lax.optimization_barrier((kv, acc))

    tile = (2, capacity, 2, BLK, HD)
    take, tiles_all = pl.pallas_call(
        pack_kernel,
        out_shape=[
            jax.ShapeDtypeStruct((dp_count, 2, capacity), jnp.int32),
            jax.ShapeDtypeStruct((dp_count,) + tile, jnp.bfloat16),
        ],
        in_specs=[smem(), vmem()],
        out_specs=[smem(), vmem()],
        scratch_shapes=[pltpu.SMEM((1, 2, capacity), jnp.int32)],
        compiler_params=params,
    )(ids, kv)
    far = [(take, lax.all_to_all(tiles_all, "dp", split_axis=0, concat_axis=0, tiled=True))]

    acc, maxes, sums, updated, squares = pl.pallas_call(
        window_kernel,
        out_shape=[wide] * 3
        + [jax.ShapeDtypeStruct((2, BLK, width), jnp.bfloat16), jax.ShapeDtypeStruct((2, BLK, HD), jnp.float32)],
        in_specs=[smem(), smem()] + [vmem()] * 7,
        out_specs=[vmem()] * 5,
        compiler_params=params,
        cost_estimate=pl.CostEstimate(
            flops=4 * 2 * BLK * width * 2 * BLK, bytes_accessed=9 * 2**20, transcendentals=0
        ),
    )(ids, length, q, up, down, res, acc, maxes, sums)

    for heads_taken, tiles_got in far:
        updated, squares = pl.pallas_call(
            far_kernel,
            out_shape=[
                jax.ShapeDtypeStruct((2, BLK, width), jnp.bfloat16),
                jax.ShapeDtypeStruct((2, BLK, HD), jnp.float32),
            ],
            in_specs=[smem(), smem(), smem()] + [vmem()] * 8,
            out_specs=[vmem()] * 2,
            input_output_aliases={9: 0},
            compiler_params=params,
        )(ids, heads_taken, length, tiles_got, q, res, acc, maxes, sums, updated, squares)

    total = lax.psum(jnp.sum(squares, axis=2), "tensor")
    inverse = lax.rsqrt(total / D + epsilon)
    normed = [
        (updated[c].astype(jnp.float32) * inverse[c][:, None] * gains[c].astype(jnp.float32)).astype(jnp.bfloat16)
        for c in range(2)
    ]
    return jnp.stack([lax.ppermute(normed[c], "pipe", lines[c]) for c in range(2)])[None]


def pair_queries(first, second):
    none = jnp.zeros_like(first)
    return jnp.concatenate(
        [jnp.concatenate([first, none], axis=1), jnp.concatenate([none, second], axis=1)], axis=0
    )


def pair_rows(first, second, lanes):
    return jnp.concatenate([jnp.broadcast_to(first, (BLK, lanes)), jnp.broadcast_to(second, (BLK, lanes))], axis=0)


def pair_context(weights, values):
    both = dot_nn(weights.astype(jnp.bfloat16), values)
    return jnp.concatenate([both[:BLK, :HD], both[BLK:, HD:]], axis=0)


LENGTH = 32


def sent_in(turn):
    parity = lax.rem(lax.axis_index("pipe"), 2)
    return parity if turn == 0 else 1 - parity


def copy_heads(out_ref, list_ref, row, source_ref):
    for s in range(out_ref.shape[0]):
        cols = pl.ds(pl.multiple_of(jnp.maximum(list_ref[row, s], 0) * HD, HD), HD)
        out_ref[s, 0] = source_ref[0, :, cols]
        out_ref[s, 1] = source_ref[1, :, cols]


def list_heads(list_ref, row, heads, block, block_of):
    capacity = list_ref.shape[1]
    for s in range(capacity):
        list_ref[row, s] = 0
    slot = jnp.int32(0)
    for h in range(heads):
        match = (block_of(h) == block) & (slot < capacity)

        @pl.when(match)
        def _(slot=slot, h=h):
            list_ref[row, slot] = h

        slot = slot + match.astype(jnp.int32)


def distant_kernel(ids_ref, kv0_ref, kv1_ref, tile0_ref, tile1_ref, list_ref):
    me = lax.axis_index("dp")
    heads = ids_ref.shape[1]

    @pl.when((me == 0) | (me == 3))
    def _():
        for turn, (kv_ref, tile_ref) in enumerate(((kv0_ref, tile0_ref), (kv1_ref, tile1_ref))):
            c = sent_in(turn)
            list_heads(list_ref, 0, heads, me, lambda h, c=c: ids_ref[c, h])
            copy_heads(tile_ref, list_ref, 0, kv_ref)


def forward_kernel(turn, ids_ref, up_ids_ref, down_ids_ref, kv_ref, up_ref, down_ref, tile_ref, list_ref):
    me = lax.axis_index("dp")
    heads = ids_ref.shape[1]
    c = sent_in(turn)
    edge = (me == 0) | (me == 3)
    list_heads(
        list_ref,
        0,
        heads,
        jnp.where(edge, me, 3 - me),
        lambda h: jnp.where(edge, ids_ref[c, h], jnp.where(me == 1, up_ids_ref[h], down_ids_ref[h])),
    )
    pl.when(edge)(lambda: copy_heads(tile_ref, list_ref, 0, kv_ref))
    pl.when(me == 1)(lambda: copy_heads(tile_ref, list_ref, 0, down_ref))
    pl.when(me == 2)(lambda: copy_heads(tile_ref, list_ref, 0, up_ref))


def message_kernel(turn, heads_step, order_ref, ids_ref, len_ref, q_ref, res_ref, kv_ref, gkv_ref, out_ref):
    me = lax.axis_index("dp")
    g = pl.program_id(0)
    c = order_ref[turn]
    glob = gkv_ref.shape[2]
    width = out_ref.shape[1] - HD
    heads = width // HD
    place = lax.broadcasted_iota(jnp.int32, (1, HD), 1)

    @pl.when(g == 0)
    def _():
        note = jnp.where(place == LENGTH, len_ref[c], 0)
        for h in range(heads):
            note = jnp.where(place == h, ids_ref[c, h], note)
        note = jnp.broadcast_to(note.astype(jnp.float32), (BLK, HD)).astype(jnp.bfloat16)
        out_ref[:BLK, width:] = note
        out_ref[BLK:, width:] = jnp.zeros((2 * BLK, HD), jnp.bfloat16)

    state = out_ref[2 * BLK :, width:].astype(jnp.float32)
    own_live = me < len_ref[c]
    numbers = range(0, heads_step, 2)
    scores, values = [], []
    for n in numbers:
        both = slice(n * HD, (n + 2) * HD)
        q = pair_queries(q_ref[0, :, n * HD : (n + 1) * HD], q_ref[0, :, (n + 1) * HD : (n + 2) * HD])
        k = jnp.concatenate([gkv_ref[0, 0, :, both], kv_ref[0, 0, :, both]], axis=0)
        values.append(jnp.concatenate([gkv_ref[1, 0, :, both], kv_ref[1, 0, :, both]], axis=0))
        own = [
            jnp.where(own_live, jnp.where(ids_ref[c, g * heads_step + n + i] == me, 1.0, 0.0), NEG) for i in range(2)
        ]
        s = dot_nt(q, k) * SCALE
        scores.append(jnp.concatenate([s[:, :glob], s[:, glob:] + pair_rows(*own, BLK)], axis=1))
    tops = [jnp.max(s, axis=1, keepdims=True) for s in scores]
    weights = [jnp.exp2(s - m) for s, m in zip(scores, tops)]
    sums = [jnp.sum(p, axis=1, keepdims=True) for p in weights]
    contexts = [(pair_context(p, v) / l).astype(jnp.bfloat16) for p, v, l in zip(weights, values, sums)]
    levels = [m + jnp.log2(l) for m, l in zip(tops, sums)]
    for n, context, level in zip(numbers, contexts, levels):
        high = level.astype(jnp.bfloat16).astype(jnp.float32)
        middle = (level - high).astype(jnp.bfloat16).astype(jnp.float32)
        low = level - high - middle
        for i in range(2):
            rows = slice(i * BLK, (i + 1) * BLK)
            head = g * heads_step + n + i
            at = place - head
            state = jnp.where(at == 0, high[rows], jnp.where(at == 32, middle[rows], jnp.where(at == 64, low[rows], state)))
            col = slice((n + i) * HD, (n + i + 1) * HD)
            out = pl.ds(pl.multiple_of(head * HD, HD), HD)
            out_ref[:BLK, out] = q_ref[0, :, col]
            out_ref[BLK : 2 * BLK, out] = res_ref[0, :, col]
            out_ref[2 * BLK :, out] = context[rows]
    out_ref[2 * BLK :, width:] = state.astype(jnp.bfloat16)


def near_kernel(info_ref, message_ref, up_ref, down_ref, acc_ref, max_ref, sum_ref, out_ref, sq_ref, take_ref):
    me = lax.axis_index("dp")
    width = out_ref.shape[1]
    heads = width // HD
    batch = head_batch(heads)
    length = info_ref[LENGTH]
    alive = me < length
    up_live = (me >= 1) & (me - 1 < length)
    down_live = me + 1 < length
    list_heads(take_ref, 0, heads, jnp.where(me < 2, me + 2, me - 2), lambda h: info_ref[h])
    list_heads(take_ref, 1, heads, 3 - me, lambda h: info_ref[h])
    lane = lax.broadcasted_iota(jnp.int32, (1, 2 * BLK), 1)
    state = message_ref[2 * BLK :, width:].astype(jnp.float32)
    state = state + pltpu.roll(state, 96, 1) + pltpu.roll(state, 64, 1)
    squares = jnp.zeros((BLK, HD), jnp.float32)

    def score(numbers):
        items = []
        for h in numbers:
            col = slice(h * HD, (h + 1) * HD)
            block = info_ref[h]
            up_bias = jnp.where(up_live, jnp.where(block == me - 1, 1.0, 0.0), NEG)
            down_bias = jnp.where(down_live, jnp.where(block == me + 1, 1.0, 0.0), NEG)
            bias = jnp.where(lane < BLK, up_bias, down_bias)
            k = jnp.concatenate([up_ref[0, :, col], down_ref[0, :, col]], axis=0)
            v = jnp.concatenate([up_ref[1, :, col], down_ref[1, :, col]], axis=0)
            s = dot_nt(message_ref[:BLK, col], k) * SCALE + bias
            level = jnp.broadcast_to(state[:, h : h + 1], (BLK, HD))
            near = jnp.where(jnp.abs(block - me) < 2, 1.0, 0.0)
            items.append((col, s, v, level, message_ref[BLK : 2 * BLK, col], message_ref[2 * BLK :, col], near))
        return items

    def weigh(items):
        outs = []
        for col, s, v, level, res, context, near in items:
            m = jnp.maximum(level, jnp.max(s, axis=1, keepdims=True))
            p = jnp.exp2(s - m).astype(jnp.bfloat16)
            outs.append((col, m, p, v, jnp.exp2(level - m), res, context, near))
        return outs

    def finish(items, squares):
        outs = []
        for col, m, p, v, alpha, res, context, near in items:
            pv = dot_nn(p, with_ones(v))
            l = alpha + pv[:, HD:]
            acc = alpha * context.astype(jnp.float32) + pv[:, :HD]
            updated = (res.astype(jnp.float32) + jnp.where(alive, acc / l, 0.0)).astype(jnp.bfloat16)
            wide = updated.astype(jnp.float32)
            squares = squares + wide * wide * near
            outs.append((col, m, l, acc, updated))
        for col, m, l, acc, updated in outs:
            max_ref[:, col] = m
            sum_ref[:, col] = l
            acc_ref[:, col] = acc
            out_ref[:, col] = updated
        return squares

    batches = [range(start, start + batch) for start in range(0, heads, batch)]
    scored = weighed = None
    for turn in range(len(batches) + 2):
        fresh = score(batches[turn]) if turn < len(batches) else None
        ready = weigh(scored) if scored else None
        if weighed:
            squares = finish(weighed, squares)
        scored, weighed = fresh, ready
    sq_ref[...] = squares


def tile_kernel(row, last, *refs):
    infos, takes, messages, tiles, accs, maxes, sums, olds, old_sqs = [refs[2 * n : 2 * n + 2] for n in range(9)]
    me = lax.axis_index("dp")
    if last:
        outs = [refs[18].at[1 - sent_in(turn)] for turn in range(2)]
        sqs = [refs[19].at[1 - sent_in(turn)] for turn in range(2)]
        for turn in range(2):
            outs[turn][...] = olds[turn][...]
    else:
        outs, sqs = refs[18:20], refs[20:22]

    def work():
        places = [(t, s) for t in range(2) for s in range(tiles[0].shape[0])]
        chosen = [takes[t][row, s] for t, s in places]
        cols = [pl.ds(pl.multiple_of(h * HD, HD), HD) for h in chosen]
        live = [infos[t][h] < infos[t][LENGTH] for (t, _), h in zip(places, chosen)]
        scores = [
            dot_nt(messages[t][:BLK, col], tiles[t][s, 0]) * SCALE + jnp.where(ok, 0.0, NEG)
            for (t, s), col, ok in zip(places, cols, live)
        ]
        before = [(maxes[t][:, col], sums[t][:, col], accs[t][:, col]) for (t, _), col in zip(places, cols)]
        residuals = [messages[t][BLK : 2 * BLK, col].astype(jnp.float32) for (t, _), col in zip(places, cols)]
        news = merge(scores, before, [tiles[t][s, 1] for t, s in places])
        updates = [
            (res + jnp.where(me < infos[t][LENGTH], acc / l, 0.0)).astype(jnp.bfloat16)
            for (t, _), res, (_, l, acc) in zip(places, residuals, news)
        ]
        squares = [old_sqs[t][...] for t in range(2)]
        for (t, _), col, updated in zip(places, cols, updates):
            outs[t][:, col] = updated
            wide = updated.astype(jnp.float32)
            squares[t] = squares[t] + wide * wide
        for t in range(2):
            sqs[t][...] = squares[t]

    if last:
        work()
    else:
        for t in range(2):
            sqs[t][...] = old_sqs[t][...]
        pl.when((me == 0) | (me == 3))(work)


def body_chain(residual, queries, keys_values, global_kv, block_ids, lengths, gain):
    width = residual.shape[-1]
    heads = width // HD
    pipe_count = lax.axis_size("pipe")
    group = head_group(heads)
    steps = heads // group
    lanes = group * HD
    capacity = heads // 4
    q, res, glob, kv, length = queries[0], residual[0], global_kv[0], keys_values[0], lengths[0]
    own_ids = block_ids[0, :, 0]
    glob_count = glob.shape[2]
    params = pltpu.CompilerParams(vmem_limit_bytes=VMEM_LIMIT)
    order = jnp.stack([sent_in(0), sent_in(1)])

    def send(array, turn, moves):
        pairs = []
        for p in range(pipe_count):
            other = p ^ 1 if turn == 1 else ((p + 1) ^ 1) - 1
            if 0 <= other < pipe_count:
                pairs += [
                    ((i * pipe_count + p) if direct else (i * pipe_count + other), j * pipe_count + other)
                    for i, j, direct in moves
                ]
        return lax.ppermute(array, ("dp", "pipe"), pairs)

    ids_3 = lax.ppermute(own_ids, "dp", [(0, 3), (3, 0)])
    ids_2 = lax.ppermute(own_ids, "dp", [(2, 0), (1, 3)])
    kvs, ups, downs = [], [], []
    for turn in range(2):
        c = order[turn]
        note = jnp.pad(lax.dynamic_index_in_dim(own_ids, c, 0, keepdims=False), (0, HD - heads)).astype(jnp.bfloat16)
        note = jnp.broadcast_to(note, (2, BLK, HD))
        kvs.append(jnp.concatenate([lax.dynamic_index_in_dim(kv, c, 1, keepdims=False), note], axis=2))
    kv, ids_3, ids_2, *kvs = lax.optimization_barrier((kv, ids_3, ids_2, *kvs))
    same = [(i, i, True) for i in range(4)]
    crossed = send(kvs[0], 0, same)
    own_kv = kv
    kv, crossed = lax.optimization_barrier((kv, crossed))
    for turn, source in enumerate((crossed, kvs[1])):
        ups.append(send(source, turn, [(i, i + 1, turn == 1) for i in range(3)]))
        downs.append(send(source, turn, [(i + 1, i, turn == 1) for i in range(3)]))

    message = jax.ShapeDtypeStruct((3 * BLK, width + HD), jnp.bfloat16)

    def local_part(turn, kv):
        return pl.pallas_call(
            functools.partial(message_kernel, turn, group),
            grid_spec=pltpu.PrefetchScalarGridSpec(
                num_scalar_prefetch=3,
                grid=(steps,),
                in_specs=[
                    pl.BlockSpec((1, BLK, lanes), lambda g, order, ids, length: (order[turn], 0, g)),
                    pl.BlockSpec((1, BLK, lanes), lambda g, order, ids, length: (order[turn], 0, g)),
                    pl.BlockSpec((2, 1, BLK, lanes), lambda g, order, ids, length: (0, order[turn], 0, g)),
                    pl.BlockSpec((2, 1, glob_count, lanes), lambda g, order, ids, length: (0, order[turn], 0, g)),
                ],
                out_specs=vmem(),
            ),
            out_shape=message,
            compiler_params=params,
        )(order, own_ids, length, q, res, kv, glob)

    messages = [local_part(0, own_kv), local_part(1, kv)]
    messages = list(lax.optimization_barrier(tuple(messages)))
    messages = [send(messages[turn], turn, same) for turn in range(2)]
    tiles = jax.ShapeDtypeStruct((capacity, 2, BLK, HD), jnp.bfloat16)
    distant = pl.pallas_call(
        distant_kernel,
        out_shape=[tiles, tiles],
        in_specs=[smem(), vmem(), vmem()],
        out_specs=[vmem(), vmem()],
        scratch_shapes=[pltpu.SMEM((1, capacity), jnp.int32)],
        compiler_params=params,
    )(ids_3, *kvs)
    far_3 = [send(distant[turn], turn, [(0, 3, True), (3, 0, True)]) for turn in range(2)]

    wide = jax.ShapeDtypeStruct((BLK, width), jnp.float32)
    row = jax.ShapeDtypeStruct((BLK, width), jnp.bfloat16)
    square = jax.ShapeDtypeStruct((BLK, HD), jnp.float32)
    far_2, near, infos = [None, None], [None, None], [None, None]
    for turn in (1, 0):
        if turn == 0:
            ups[0], near[1][4] = lax.optimization_barrier((ups[0], near[1][4]))
        array = pl.pallas_call(
            functools.partial(forward_kernel, turn),
            out_shape=tiles,
            in_specs=[smem()] * 3 + [vmem()] * 3,
            out_specs=vmem(),
            scratch_shapes=[pltpu.SMEM((1, capacity), jnp.int32)],
            compiler_params=params,
        )(
            ids_2,
            ups[turn][0, 0, width:].astype(jnp.int32),
            downs[turn][0, 0, width:].astype(jnp.int32),
            kvs[turn],
            ups[turn],
            downs[turn],
        )
        far_2[turn] = send(array, turn, [(0, 2, True), (3, 1, True), (2, 3, False), (1, 0, False)])
        infos[turn] = messages[turn][0, width:].astype(jnp.int32)
        near[turn] = list(
            pl.pallas_call(
                near_kernel,
                out_shape=[wide, wide, wide, row, square, jax.ShapeDtypeStruct((2, capacity), jnp.int32)],
                in_specs=[smem()] + [vmem()] * 3,
                out_specs=[vmem()] * 5 + [smem()],
                compiler_params=params,
            )(infos[turn], messages[turn], ups[turn], downs[turn])
        )
    accs, maxes, sums, updates, squares, takes = [list(items) for items in zip(*near)]
    for index, got, last in ((1, far_3, False), (0, far_2, True)):
        pair = [jax.ShapeDtypeStruct((2,) + kind.shape, kind.dtype) for kind in (row, square)]
        results = pl.pallas_call(
            functools.partial(tile_kernel, index, last),
            out_shape=pair if last else [row, row, square, square],
            in_specs=[smem()] * 4 + [vmem()] * 14,
            out_specs=[vmem()] * (2 if last else 4),
            input_output_aliases={} if last else {14: 0, 15: 1},
            compiler_params=params,
        )(*infos, *takes, *messages, *got, *accs, *maxes, *sums, *updates, *squares)
        if not last:
            updates, squares = results[:2], results[2:]

    updated, squares = results
    total = lax.psum(jnp.sum(squares, axis=2), "tensor")
    inverse = lax.rsqrt(total / D + epsilon)
    normed = updated.astype(jnp.float32) * inverse[:, :, None] * gain[0][:, None, :].astype(jnp.float32)
    return normed.astype(jnp.bfloat16)[None]


def body(*arrays):
    heads = arrays[0].shape[-1] // HD
    chain = lax.axis_size("dp") == 4 and lax.axis_size("pipe") % 2 == 0 and heads % 8 == 0 and heads <= 32
    return (body_chain if chain else body_any)(*arrays)


def solution(mesh):
    in_specs = (
        P("pipe", None, "dp", "tensor"),
        P("pipe", None, "dp", "tensor"),
        P("pipe", None, None, "dp", "tensor"),
        P("pipe", None, None, None, "tensor"),
        P("pipe", None, "dp", "tensor"),
        P("pipe", None),
        P("pipe", None, "tensor"),
    )
    out_specs = P("pipe", None, "dp", "tensor")
    return jax.shard_map(body, mesh=mesh, in_specs=in_specs, out_specs=out_specs, check_vma=False)
```
